128 devices in a mesh: shard: 4 (over y_lo, core), blk: 32 (over y_hi, z, x).
Axes of the slice: x: 4, y: 4 (y_hi: 2, y_lo: 2; y = y_hi * 2 + y_lo), z: 4, core: 2. Of those that a mesh axis runs over, the one named last changes fastest.
Arguments:
- hidden: float32 [4, 4096, 960], P('shard', 'blk'), may hold values from -6 to 6
- chosen: int32 [4, 4096], P('shard', 'blk'), may hold values from 0 to 1, as said below
- positions: int32 [4, 4096], P('shard', 'blk'), may hold values from 0 to 6142, as said below
- w_query: bfloat16 [960, 960], P('shard'), may hold values from -0.375 to 0.375
- w_key: bfloat16 [960, 320], P('shard'), may hold values from -0.1875 to 0.1875
- w_value: bfloat16 [960, 320], P('shard'), may hold values from -0.1875 to 0.1875
- w_output: bfloat16 [960, 960], P('shard'), may hold values from -6 to 6
- w_gate: bfloat16 [960, 2560], P('shard'), may hold values from -0.1875 to 0.1875
- w_up: bfloat16 [960, 2560], P('shard'), may hold values from -0.1875 to 0.1875
- w_down: bfloat16 [2560, 960], P('shard'), may hold values from -0.15625 to 0.15625
- gain_attn: bfloat16 [960], P('shard'), may hold values from 0.25 to 1.75
- gain_ffn: bfloat16 [960], P('shard'), may hold values from 0.25 to 1.75
- router: bfloat16 [960], P('shard'), may hold values from -0.1875 to 0.1875
- d_out: float32 [4, 4096, 960], P('shard', 'blk'), may hold values from -6 to 6
Outputs:
- output: float32 [4, 4096, 960], P('shard', 'blk')
- d_hidden: float32 [4, 4096, 960], P('shard', 'blk')
- g_query: float32 [960, 960], P('shard')
- g_key: float32 [960, 320], P('shard')
- g_value: float32 [960, 320], P('shard')
- g_output: float32 [960, 960], P('shard')
- g_gate: float32 [960, 2560], P('shard')
- g_up: float32 [960, 2560], P('shard')
- g_down: float32 [2560, 960], P('shard')
- g_gain_attn: float32 [960], P('shard')
- g_gain_ffn: float32 [960], P('shard')
- g_router: float32 [960], P('shard')
The draws below stay inside these ranges and needn't reach their ends.
Inputs may be any that keep to these rules, and one draw needn't show every extreme that they name: `chosen`: in each aligned block of 256 tokens of a sequence exactly 128 tokens are 1 and the others 0. Along each sequence the positions start at 0 and rise by 1 or 2 from token to token; the last token of every sequence has position 6142.
All inputs are finite; a program needn't handle non-finite values.
Results may differ from the reference program's by a relative error of at most 0.035.
Values may be sent and summed in bfloat16 or wider, within the bound.
A program may use at most 192 MiB of HBM per device.

```python
import math
import jax
import jax.numpy as jnp
from jax import lax

D = 960
HEADS = 15
KV_HEADS = 5
HEAD_DIM = 64
FF = 2560
BLOCK = 256
SEL = 128
SEQ_LEN = 4096
SEQS = 4


def draw_chosen(key, part):
    block_count = SEQS * (SEQ_LEN // BLOCK)
    block_keys = jax.random.split(key, block_count)
    orders = jax.vmap(lambda one_key: jax.random.permutation(one_key, BLOCK))(block_keys)
    return (orders < SEL).astype(jnp.int32).reshape(SEQS, SEQ_LEN)


def draw_positions(key, part):
    step_count = SEQ_LEN - 1
    seq_keys = jax.random.split(key, SEQS)
    orders = jax.vmap(lambda one_key: jax.random.permutation(one_key, step_count))(seq_keys)
    step_sizes = 1 + (orders < step_count // 2).astype(jnp.int32)
    starts = jnp.zeros((SEQS, 1), jnp.int32)
    return jnp.concatenate([starts, jnp.cumsum(step_sizes, axis=1).astype(jnp.int32)], axis=1).astype(jnp.int32)


def level_of(rng, dims, cuts, low, top_value):
    loudness, own = 1.0, jax.random.fold_in(rng, 6)
    for axis_at, blocks in cuts:
        draws = jnp.exp(jax.random.uniform(jax.random.fold_in(own, axis_at), (blocks,), jnp.float32, low / len(cuts), top_value / len(cuts)))
        loudness = loudness * jnp.repeat(draws, dims[axis_at] // blocks).reshape([-1 if axis == axis_at else 1 for axis in range(len(dims))])
    return loudness


def gaussian(own_key, dims, width, bound, pieces=(), dtype=jnp.bfloat16):
    values = jax.random.normal(own_key, dims, jnp.float32) * width
    if len(pieces) > 0:
        values = level_of(own_key, dims, pieces, -0.22, 0.18) * values
    return jnp.clip(values, min=-bound, max=bound).astype(dtype)


def setup_inputs(seed: int = 0) -> dict:
    key_list = jax.random.split(jax.random.key(seed), 15)
    hidden = gaussian(key_list[0], (SEQS, SEQ_LEN, D), 1.0, 6.0, ((0, 4), (1, 32)), jnp.float32)
    chosen = draw_chosen(jax.random.fold_in(key_list[14], 71), 0)
    positions = draw_positions(jax.random.fold_in(key_list[14], 71), 0)
    w_query = gaussian(key_list[3], (D, HEADS * HEAD_DIM), (D // 4) ** -0.5, 0.375, ((0, 4),))
    w_key = gaussian(key_list[4], (D, KV_HEADS * HEAD_DIM), D ** -0.5, 0.1875, ((0, 4),))
    w_value = gaussian(key_list[5], (D, KV_HEADS * HEAD_DIM), D ** -0.5, 0.1875, ((0, 4),))
    w_output = gaussian(key_list[6], (HEADS * HEAD_DIM, D), (max(1, HEADS * HEAD_DIM * 8 // SEQ_LEN)) ** -0.5, 6.0, ((0, 4),))
    w_gate = gaussian(key_list[7], (D, FF), D ** -0.5, 0.1875, ((0, 4),))
    w_up = gaussian(key_list[8], (D, FF), D ** -0.5, 0.1875, ((0, 4),))
    w_down = gaussian(key_list[9], (FF, D), (FF // 2) ** -0.5, 0.15625, ((0, 4),))
    gain_attn = jnp.clip(1.0 + 0.15 * jax.random.normal(key_list[10], (D,), jnp.float32), 0.25, 1.75).astype(jnp.bfloat16)
    gain_ffn = jnp.clip(1.0 + 0.15 * jax.random.normal(key_list[11], (D,), jnp.float32), 0.25, 1.75).astype(jnp.bfloat16)
    router = gaussian(key_list[12], (D,), D ** -0.5, 0.1875, ((0, 4),))
    d_out = gaussian(key_list[13], (SEQS, SEQ_LEN, D), 1.0, 6.0, ((0, 4), (1, 32)), jnp.float32)
    return {"hidden": hidden, "chosen": chosen, "positions": positions, "w_query": w_query, "w_key": w_key, "w_value": w_value, "w_output": w_output, "w_gate": w_gate, "w_up": w_up, "w_down": w_down, "gain_attn": gain_attn, "gain_ffn": gain_ffn, "router": router, "d_out": d_out}


EPS = 1e-05
THETA = 10000.0
NEGATIVE = -1e+30
HIGHEST_PRECISION = lax.Precision.HIGHEST

@jax.custom_vjp
def low(v):
    return lax.optimization_barrier(v.astype(jnp.bfloat16)).astype(jnp.float32)

@jax.custom_vjp
def low_back(v):
    return v

def low_keep(v):
    return (low(v), None)

def low_pass(kept, grad):
    return (grad,)

def back_keep(v):
    return (v, None)

def back_low(kept, grad):
    return (low(grad),)
low.defvjp(low_keep, low_pass)
low_back.defvjp(back_keep, back_low)

def rms_norm(values, gain_vector):
    inverse_rms = lax.rsqrt(lax.optimization_barrier(jnp.mean(values * values, axis=-1, keepdims=True)) + EPS)
    return values * inverse_rms * gain_vector

def angles_of(positions, head_dim):
    frequency = THETA ** (-jnp.arange(0, head_dim // 2).astype(jnp.float32) * 2.0 / head_dim)
    return positions.astype(jnp.float32)[:, None] * frequency[None, :]

def rotate(values, angles):
    half_dim = values.shape[-1] // 2
    cosine = jnp.cos(angles)[:, None, :]
    sine_part = jnp.sin(angles)[:, None, :]
    first_half = values[..., :half_dim]
    second_half = values[..., half_dim:]
    return jnp.concatenate([first_half * cosine - second_half * sine_part, second_half * cosine + first_half * sine_part], axis=-1)

def sequence_forward(state_in, seq_chosen, seq_positions, weight_set):
    w_query, w_key, w_value, w_output, w_gate, w_up, w_down, gain_attn, gain_ffn, router = weight_set
    length = state_in.shape[0]
    groups = HEADS // KV_HEADS
    angles = angles_of(seq_positions, HEAD_DIM)
    normed_first = low(rms_norm(state_in, gain_attn))
    query_pre = low_back(jnp.dot(normed_first, w_query, precision=HIGHEST_PRECISION)).reshape(length, HEADS, HEAD_DIM)
    queries = low(rotate(query_pre, angles)).reshape(length, KV_HEADS, groups, HEAD_DIM)
    key_pre = low_back(jnp.dot(normed_first, w_key, precision=HIGHEST_PRECISION)).reshape(length, KV_HEADS, HEAD_DIM)
    key_rows = low(rotate(key_pre, angles))
    value_rows = low(low_back(jnp.dot(normed_first, w_value, precision=HIGHEST_PRECISION))).reshape(length, KV_HEADS, HEAD_DIM)
    block_rows = math.gcd(length, 512)
    token_index = jnp.arange(length).astype(jnp.int32)
    key_ok = seq_chosen > 0

    def attend(row_start):
        query_block = lax.dynamic_slice_in_dim(queries, row_start, block_rows, 0)
        query_index = row_start + jnp.arange(block_rows).astype(jnp.int32)
        scores = jnp.einsum('tkgd,skd->kgts', query_block, key_rows, precision=HIGHEST_PRECISION) * HEAD_DIM ** (-0.5)
        scores = low_back(scores)
        earlier = (token_index // BLOCK)[None, :] <= (query_index // BLOCK)[:, None]
        allowed = earlier & key_ok[None, :] | (token_index[None, :] == query_index[:, None])
        scores = jnp.where(allowed, scores, NEGATIVE)
        top_score = lax.optimization_barrier(jnp.max(scores, axis=-1, keepdims=True))
        exponent = jnp.exp(scores - top_score)
        probability = low(exponent / lax.optimization_barrier(jnp.sum(exponent, axis=-1, keepdims=True)))
        return jnp.einsum('kgts,skd->tkgd', probability, value_rows, precision=HIGHEST_PRECISION)
    row_starts = jnp.arange(0, length, block_rows).astype(jnp.int32)
    mixture = lax.map(jax.checkpoint(attend), row_starts).reshape(length, HEADS * HEAD_DIM)
    mixture = low_back(low(mixture))
    attn_out = low_back(jnp.dot(mixture, w_output, precision=HIGHEST_PRECISION))
    middle = state_in + attn_out
    normed_second = low(rms_norm(middle, gain_ffn))
    gate_proj = low_back(jnp.dot(normed_second, w_gate, precision=HIGHEST_PRECISION))
    up_proj = low_back(jnp.dot(normed_second, w_up, precision=HIGHEST_PRECISION))
    inner = low(gate_proj * jax.nn.sigmoid(gate_proj) * up_proj)
    ffn_out = low_back(jnp.dot(inner, w_down, precision=HIGHEST_PRECISION))
    route_gate = jax.nn.sigmoid(jnp.dot(state_in, router, precision=HIGHEST_PRECISION))
    weight_row = seq_chosen.astype(jnp.float32) * route_gate
    return state_in + weight_row[:, None] * (attn_out + ffn_out)

def reference(hidden, chosen, positions, w_query, w_key, w_value, w_output, w_gate, w_up, w_down, gain_attn, gain_ffn, router, d_out):
    weight_set = tuple((member.astype(jnp.float32) for member in (w_query, w_key, w_value, w_output, w_gate, w_up, w_down, gain_attn, gain_ffn, router)))

    def per_sequence(running, sequence_item):
        seq_hidden, seq_chosen, seq_positions, seq_cotangent = sequence_item

        def forward(state_in, weights_in):
            return sequence_forward(state_in, seq_chosen, seq_positions, weights_in)
        result, pull_back = jax.vjp(forward, seq_hidden, weight_set)
        d_state, d_weights = pull_back(seq_cotangent)
        running = jax.tree.map(lambda left, right: left + right, running, d_weights)
        return (running, (result, d_state))
    zero_grads = jax.tree.map(jnp.zeros_like, weight_set)
    gradients, (output, d_hidden) = lax.scan(per_sequence, zero_grads, (hidden, chosen, positions, d_out))
    return (output, d_hidden, gradients[0], gradients[1], gradients[2], gradients[3], gradients[4], gradients[5], gradients[6], gradients[7], gradients[8], gradients[9])
```

```python
import functools

import jax
import jax.numpy as jnp
from jax import lax
from jax.experimental import pallas as pl
from jax.experimental.pallas import tpu as pltpu
from jax.sharding import Mesh
from jax.sharding import PartitionSpec as P

D = 960
HEADS = 15
KV_HEADS = 5
GROUPS = 3
HEAD_DIM = 64
FF = 2560
EPS = 1e-05
THETA = 10000.0
SCALE = HEAD_DIM ** (-0.5)
T = 64
PAIR = 128
SLOTS = 32
KEYS = SLOTS * T
AX = ("ylo", "core", "yhi", "z", "x")
DIMS = (2, 2, 2, 4, 4)
MESH = pl.DeviceIdType.MESH
BF = jnp.bfloat16
F32 = jnp.float32
VMEM_LIMIT = 56 * 2**20


def dot(a, b, dims=(((1,), (0,)), ((), ()))):
    return lax.dot_general(a, b, dims, preferred_element_type=F32)


NT = (((1,), (1,)), ((), ()))
TN = (((0,), (0,)), ((), ()))


def moved(place, dy, dcore, dz, dx):
    ylo, core, yhi, z, x = place
    y = (yhi * 2 + ylo + dy) % 4
    return (y % 2, (core + dcore) % 2, y // 2, (z + dz) % 4, (x + dx) % 4)


def flat(place):
    at = 0
    for size, c in zip(DIMS, place):
        at = at * size + c
    return at


def places():
    for ylo in range(2):
        for core in range(2):
            for yhi in range(2):
                for z in range(4):
                    for x in range(4):
                        yield (ylo, core, yhi, z, x)


def permute(value, dy=0, dcore=0, dz=0, dx=0):
    return lax.ppermute(value, AX, [(flat(p), flat(moved(p, dy, dcore, dz, dx))) for p in places()])


def swap_x(value):
    return lax.ppermute(
        value, AX, [(flat(p), flat(p[:4] + (p[4] ^ 1,))) for p in places()]
    )


def here():
    return tuple(lax.axis_index(a) for a in AX)


def neighbour(me, axis, step):
    ylo, core, yhi, z, x = me
    if axis == "z":
        z = lax.rem(z + step + 4, 4)
    elif axis == "x":
        x = lax.rem(x + step + 4, 4)
    else:
        yhi = 1 - yhi
    return (ylo, core, yhi, z, x)


FIVE = (("x", 1), ("x", -1), ("z", 1), ("z", -1), ("y", 1))


def greet(me):
    barrier = pltpu.get_barrier_semaphore()
    for axis, step in FIVE:
        pl.semaphore_signal(
            barrier, inc=1, device_id=neighbour(me, axis, step), device_id_type=MESH
        )
    pl.semaphore_wait(barrier, len(FIVE))


class Sends:
    def __init__(self, me, send_sems, recv_sems):
        self.me, self.send_sems, self.recv_sems, self.all = me, send_sems, recv_sems, []

    def start(self, src, dst, axis, step):
        k = len(self.all)
        copy = pltpu.make_async_remote_copy(
            src_ref=src,
            dst_ref=dst,
            send_sem=self.send_sems.at[k],
            recv_sem=self.recv_sems.at[k],
            device_id=neighbour(self.me, axis, step),
            device_id_type=MESH,
        )
        copy.start()
        self.all.append(copy)
        return copy

    def finish(self):
        for copy in self.all:
            copy.wait_send()


def gather_kernel(kv_ref, out_ref, send_sems, recv_sems):
    me = here()
    _, _, yh, z, x = me
    oy = 1 - yh
    greet(me)
    sends = Sends(me, send_sems, recv_sems)
    half, quarter = T // 2, T // 4
    streams = (("x", "z", 0), ("z", "x", half))

    def slot(y, axis, step, rows, count):
        zz = lax.rem(z + step + 4, 4) if axis == "z" else z
        xx = lax.rem(x + step + 4, 4) if axis == "x" else x
        return out_ref.at[y, zz, xx, pl.ds(rows, count)]

    def line(y, axis, step, rows, count):
        if axis == "z":
            return out_ref.at[y, lax.rem(z + step + 4, 4), :, pl.ds(rows, count)]
        return out_ref.at[y, :, lax.rem(x + step + 4, 4), pl.ds(rows, count)]

    own = out_ref.at[yh, z, x]
    own[...] = kv_ref[...]
    first = sends.start(kv_ref, own, "y", 1)
    got = {}
    for y, tag in ((yh, 0), (oy, 1)):
        if tag:
            first.wait_recv()
        for axis, _, row in streams:
            src = slot(y, axis, 0, row, half)
            for step in (1, -1):
                got[tag, row, step] = sends.start(src, src, axis, step)
    far = {}
    for y, tag in ((yh, 0), (oy, 1)):
        for axis, _, row in streams:
            for step, off in ((1, 0), (-1, quarter)):
                got[tag, row, step].wait_recv()
                src = slot(y, axis, -step, row + off, quarter)
                far[tag, row, step] = sends.start(src, src, axis, step)
    wide = {}
    for y, tag in ((yh, 0), (oy, 1)):
        for _, axis, row in streams:
            for step in (1, -1):
                far[tag, row, step].wait_recv()
            src = line(y, axis, 0, row, half)
            for step in (1, -1):
                wide[tag, row, step] = sends.start(src, src, axis, step)
    last = []
    for y, tag in ((yh, 0), (oy, 1)):
        for _, axis, row in streams:
            for step, off in ((1, 0), (-1, quarter)):
                wide[tag, row, step].wait_recv()
                src = line(y, axis, -step, row + off, quarter)
                last.append(sends.start(src, src, axis, step))
    for copy in last:
        copy.wait_recv()
    sends.finish()


def gather_keys(kv):
    count = 33
    return pl.pallas_call(
        gather_kernel,
        name="gather_keys",
        out_shape=jax.ShapeDtypeStruct((2, 4, 4, T, 640), BF),
        in_specs=[pl.BlockSpec(memory_space=pltpu.VMEM)],
        out_specs=pl.BlockSpec(memory_space=pltpu.VMEM),
        scratch_shapes=[pltpu.SemaphoreType.DMA((count,)), pltpu.SemaphoreType.DMA((count,))],
        compiler_params=pltpu.CompilerParams(
            collective_id=1, has_side_effects=True, vmem_limit_bytes=VMEM_LIMIT
        ),
        cost_estimate=pl.CostEstimate(flops=0, bytes_accessed=60_000_000, transcendentals=0),
    )(kv)


def plus(*terms):
    total = terms[0].astype(F32)
    for term in terms[1:]:
        total = total + term.astype(F32)
    return total


def scatter_kernel(part_ref, out_ref, low_a, low_b, fwd, full, out_b, sums, nar_low, nar_out, nar_full, y_in, send_sems, recv_sems):
    me = here()
    _, _, yh, z, x = me
    greet(me)
    sends = Sends(me, send_sems, recv_sems)
    half, quarter = T // 2, T // 4
    streams = (("x", "z", 0), ("z", "x", half))

    def line(axis, step, row, count):
        if axis == "z":
            return part_ref.at[:, lax.rem(z + step + 4, 4), :, pl.ds(row, count)]
        return part_ref.at[:, :, lax.rem(x + step + 4, 4), pl.ds(row, count)]

    near = {}
    for s, (axis, _, row) in enumerate(streams):
        near[s, 1] = sends.start(line(axis, 2, row, quarter), low_a.at[s], axis, 1)
        near[s, -1] = sends.start(line(axis, 2, row + quarter, quarter), low_b.at[s], axis, -1)
    whole = {}
    for s, (axis, _, row) in enumerate(streams):
        for d, (step, low) in enumerate(((1, low_a), (-1, low_b))):
            near[s, step].wait_recv()
            lo, hi = (0, quarter) if step == 1 else (quarter, 0)
            out_b[s, d, :, :, pl.ds(lo, quarter)] = plus(
                line(axis, step, row + lo, quarter)[...], low[s]
            ).astype(BF)
            out_b[s, d, :, :, pl.ds(hi, quarter)] = line(axis, step, row + hi, quarter)[...]
            whole[s, step] = sends.start(out_b.at[s, d], full.at[s, d], axis, step)
    near = {}
    for s, (axis, other, row) in enumerate(streams):
        for step in (1, -1):
            whole[s, step].wait_recv()
        sums[s] = plus(line(axis, 0, row, half)[...], full[s, 0], full[s, 1]).astype(BF)
        at = z if other == "z" else x
        far = lax.rem(at + 2, 4)
        near[s, 1] = sends.start(
            sums.at[s, :, far, pl.ds(0, quarter)], nar_low.at[s, 0], other, 1
        )
        near[s, -1] = sends.start(
            sums.at[s, :, far, pl.ds(quarter, quarter)], nar_low.at[s, 1], other, -1
        )
    for s, (axis, other, row) in enumerate(streams):
        at = z if other == "z" else x
        for d, step in enumerate((1, -1)):
            near[s, step].wait_recv()
            to = lax.rem(at + step + 4, 4)
            lo, hi = (0, quarter) if step == 1 else (quarter, 0)
            nar_out[s, d, :, pl.ds(lo, quarter)] = plus(
                sums[s, :, to, pl.ds(lo, quarter)], nar_low[s, d]
            ).astype(BF)
            nar_out[s, d, :, pl.ds(hi, quarter)] = sums[s, :, to, pl.ds(hi, quarter)]
            whole[s, step] = sends.start(nar_out.at[s, d], nar_full.at[s, d], other, step)
    swap = {}
    for s, (axis, other, row) in enumerate(streams):
        at = z if other == "z" else x
        for step in (1, -1):
            whole[s, step].wait_recv()
        fwd[s] = plus(sums[s, :, at], nar_full[s, 0], nar_full[s, 1]).astype(BF)
        swap[s] = sends.start(fwd.at[s, 1 - yh], y_in.at[s], "y", 1)
    for s, (axis, other, row) in enumerate(streams):
        swap[s].wait_recv()
        out_ref[pl.ds(row, half)] = plus(fwd[s, yh], y_in[s])
    sends.finish()


def scatter_keys(part):
    half, quarter, w = T // 2, T // 4, 640
    count = 18
    return pl.pallas_call(
        scatter_kernel,
        name="scatter_keys",
        out_shape=jax.ShapeDtypeStruct((T, w), F32),
        in_specs=[pl.BlockSpec(memory_space=pltpu.VMEM)],
        out_specs=pl.BlockSpec(memory_space=pltpu.VMEM),
        scratch_shapes=[
            pltpu.VMEM((2, 2, 4, quarter, w), BF),
            pltpu.VMEM((2, 2, 4, quarter, w), BF),
            pltpu.VMEM((2, 2, half, w), BF),
            pltpu.VMEM((2, 2, 2, 4, half, w), BF),
            pltpu.VMEM((2, 2, 2, 4, half, w), BF),
            pltpu.VMEM((2, 2, 4, half, w), BF),
            pltpu.VMEM((2, 2, 2, quarter, w), BF),
            pltpu.VMEM((2, 2, 2, half, w), BF),
            pltpu.VMEM((2, 2, 2, half, w), BF),
            pltpu.VMEM((2, half, w), BF),
            pltpu.SemaphoreType.DMA((count,)),
            pltpu.SemaphoreType.DMA((count,)),
        ],
        compiler_params=pltpu.CompilerParams(
            collective_id=2, has_side_effects=True, vmem_limit_bytes=VMEM_LIMIT
        ),
        cost_estimate=pl.CostEstimate(flops=0, bytes_accessed=80_000_000, transcendentals=0),
    )(part)


ROWS = 240
STREAMS = (("x", "z", 0, 128, 64), ("z", "x", 128, 112, 64))


def reduce_kernel(width, g_ref, out_ref, low, out_b, full, sums, nlow, nout, nfull, y_in, send_sems, recv_sems):
    me = here()
    _, _, yh, z, x = me
    greet(me)
    sends = Sends(me, send_sems, recv_sems)
    big, small = width // 4, width // 16
    pos = {"z": z, "x": x}

    def around(axis, step):
        return lax.rem(pos[axis] + step + 4, 4)

    def col(axis, step):
        return pl.ds(pl.multiple_of(around(axis, step) * big, 128), big)

    def sub(axis, step):
        return pl.ds(pl.multiple_of(around(axis, step) * small, 128), small)

    near, whole = {}, {}
    for s, (axis, _, row, rows, cut) in enumerate(STREAMS):
        c = col(axis, 2)
        near[s, 1] = sends.start(g_ref.at[pl.ds(row, cut), c], low.at[pl.ds(row, cut)], axis, 1)
        near[s, -1] = sends.start(
            g_ref.at[pl.ds(row + cut, rows - cut), c], low.at[pl.ds(row + cut, rows - cut)], axis, -1
        )
    for s, (axis, _, row, rows, cut) in enumerate(STREAMS):
        for d, step in enumerate((1, -1)):
            near[s, step].wait_recv()
            parts = ((row, cut), (row + cut, rows - cut))
            add, keep = parts if step == 1 else parts[::-1]
            c = col(axis, step)
            out_b[d, pl.ds(*add)] = plus(g_ref[pl.ds(*add), c], low[pl.ds(*add)]).astype(BF)
            out_b[d, pl.ds(*keep)] = g_ref[pl.ds(*keep), c]
            whole[s, step] = sends.start(
                out_b.at[d, pl.ds(row, rows)], full.at[d, pl.ds(row, rows)], axis, step
            )
    for s, (axis, other, row, rows, cut) in enumerate(STREAMS):
        for step in (1, -1):
            whole[s, step].wait_recv()
        r = pl.ds(row, rows)
        sums[r] = plus(g_ref[r, col(axis, 0)], full[0, r], full[1, r]).astype(BF)
        c = sub(other, 2)
        near[s, 1] = sends.start(sums.at[pl.ds(row, cut), c], nlow.at[pl.ds(row, cut)], other, 1)
        near[s, -1] = sends.start(
            sums.at[pl.ds(row + cut, rows - cut), c], nlow.at[pl.ds(row + cut, rows - cut)], other, -1
        )
    for s, (_, other, row, rows, cut) in enumerate(STREAMS):
        for d, step in enumerate((1, -1)):
            near[s, step].wait_recv()
            parts = ((row, cut), (row + cut, rows - cut))
            add, keep = parts if step == 1 else parts[::-1]
            c = sub(other, step)
            nout[d, pl.ds(*add)] = plus(sums[pl.ds(*add), c], nlow[pl.ds(*add)]).astype(BF)
            nout[d, pl.ds(*keep)] = sums[pl.ds(*keep), c]
            whole[s, step] = sends.start(
                nout.at[d, pl.ds(row, rows)], nfull.at[d, pl.ds(row, rows)], other, step
            )
    swap = {}
    for s, (axis, other, row, rows, cut) in enumerate(STREAMS):
        for step in (1, -1):
            whole[s, step].wait_recv()
        r = pl.ds(row, rows)
        y_in[0, r] = plus(sums[r, sub(other, 0)], nfull[0, r], nfull[1, r]).astype(BF)
        swap[s] = sends.start(y_in.at[0, r], y_in.at[1, r], "y", 1)

    def cell(axis, a, b):
        return pl.ds(pl.multiple_of(a * big + b * small, 128), small)

    for s, (axis, other, row, rows, cut) in enumerate(STREAMS):
        swap[s].wait_recv()
        r = pl.ds(row, rows)
        c = cell(axis, pos[axis], pos[other])
        out_ref[r, c] = plus(y_in[0, r], y_in[1, r]).astype(BF)
        for step in (1, -1):
            near[s, step] = sends.start(out_ref.at[r, c], out_ref.at[r, c], other, step)
    for s, (axis, other, row, rows, cut) in enumerate(STREAMS):
        parts = (pl.ds(row, cut), pl.ds(row + cut, rows - cut))
        for d, step in enumerate((1, -1)):
            near[s, step].wait_recv()
            c = cell(axis, pos[axis], around(other, -step))
            ref = out_ref.at[parts[d], c]
            whole[s, step] = sends.start(ref, ref, other, step)
    for s, (axis, other, row, rows, cut) in enumerate(STREAMS):
        for step in (1, -1):
            whole[s, step].wait_recv()
        ref = out_ref.at[pl.ds(row, rows), col(axis, 0)]
        for step in (1, -1):
            near[s, step] = sends.start(ref, ref, axis, step)
    last = []
    for s, (axis, other, row, rows, cut) in enumerate(STREAMS):
        parts = (pl.ds(row, cut), pl.ds(row + cut, rows - cut))
        for d, step in enumerate((1, -1)):
            near[s, step].wait_recv()
            ref = out_ref.at[parts[d], col(axis, -step)]
            last.append(sends.start(ref, ref, axis, step))
    for copy in last:
        copy.wait_recv()
    sends.finish()


def reduce_all(g, number):
    width = g.shape[1]
    big, small = width // 4, width // 16
    count = 34
    return pl.pallas_call(
        functools.partial(reduce_kernel, width),
        name=f"reduce_{width}",
        out_shape=jax.ShapeDtypeStruct((ROWS, width), BF),
        in_specs=[pl.BlockSpec(memory_space=pltpu.VMEM)],
        out_specs=pl.BlockSpec(memory_space=pltpu.VMEM),
        scratch_shapes=[
            pltpu.VMEM((ROWS, big), BF),
            pltpu.VMEM((2, ROWS, big), BF),
            pltpu.VMEM((2, ROWS, big), BF),
            pltpu.VMEM((ROWS, big), BF),
            pltpu.VMEM((ROWS, small), BF),
            pltpu.VMEM((2, ROWS, small), BF),
            pltpu.VMEM((2, ROWS, small), BF),
            pltpu.VMEM((2, ROWS, small), BF),
            pltpu.SemaphoreType.DMA((count,)),
            pltpu.SemaphoreType.DMA((count,)),
        ],
        compiler_params=pltpu.CompilerParams(
            collective_id=number, has_side_effects=True, vmem_limit_bytes=VMEM_LIMIT
        ),
        cost_estimate=pl.CostEstimate(flops=0, bytes_accessed=width * 20000, transcendentals=0),
    )(g)


def attend_kernel(limit_ref, q_ref, kv_ref, mix_ref, prob_ref):
    limit = limit_ref[0]
    tile = kv_ref[...].reshape(KEYS, 128)
    scores = dot(q_ref[0], tile, NT) * SCALE
    column = lax.broadcasted_iota(jnp.int32, scores.shape, 1)
    scores = jnp.where(column < limit, scores, -1e30)
    top = jnp.max(scores, axis=-1, keepdims=True)
    exponent = jnp.exp(scores - top)
    total = jnp.sum(exponent, axis=-1, keepdims=True)
    prob = (exponent * (1.0 / total)).astype(BF)
    prob_ref[0] = prob
    mix_ref[0] = dot(prob, tile)


def attend(limit, q, kv):
    rows = GROUPS * T
    return pl.pallas_call(
        attend_kernel,
        name="attend",
        grid=(KV_HEADS,),
        out_shape=(
            jax.ShapeDtypeStruct((KV_HEADS, rows, 128), F32),
            jax.ShapeDtypeStruct((KV_HEADS, rows, KEYS), BF),
        ),
        in_specs=[
            pl.BlockSpec(memory_space=pltpu.SMEM),
            pl.BlockSpec((1, rows, 128), lambda j: (j, 0, 0)),
            pl.BlockSpec((2, 4, 4, T, 128), lambda j: (0, 0, 0, 0, j)),
        ],
        out_specs=(
            pl.BlockSpec((1, rows, 128), lambda j: (j, 0, 0)),
            pl.BlockSpec((1, rows, KEYS), lambda j: (j, 0, 0)),
        ),
        compiler_params=pltpu.CompilerParams(vmem_limit_bytes=VMEM_LIMIT),
        cost_estimate=pl.CostEstimate(
            flops=4 * HEADS * T * KEYS * 128, bytes_accessed=8_000_000, transcendentals=HEADS * T * KEYS
        ),
    )(limit, q, kv)


def attend_back_kernel(q_ref, do_ref, mix_ref, prob_ref, kv_ref, dq_ref, dkv_ref):
    tile = kv_ref[...].reshape(KEYS, 128)
    prob = prob_ref[0]
    d_out = do_ref[0]
    d_prob = dot(d_out, tile, NT)
    delta = jnp.sum(d_out.astype(F32) * mix_ref[0], axis=-1, keepdims=True)
    d_score = (prob.astype(F32) * (d_prob - delta)).astype(BF)
    dq_ref[0] = dot(d_score, tile) * SCALE
    grad = dot(d_score, q_ref[0], TN) * SCALE + dot(prob, d_out, TN)
    dkv_ref[...] = grad.astype(BF).reshape(2, 4, 4, T, 128)


def attend_back(q, d_mix, mix, prob, kv):
    rows = GROUPS * T
    head = pl.BlockSpec((1, rows, 128), lambda j: (j, 0, 0))
    tile = pl.BlockSpec((2, 4, 4, T, 128), lambda j: (0, 0, 0, 0, j))
    return pl.pallas_call(
        attend_back_kernel,
        name="attend_back",
        grid=(KV_HEADS,),
        out_shape=(
            jax.ShapeDtypeStruct((KV_HEADS, rows, 128), F32),
            jax.ShapeDtypeStruct((2, 4, 4, T, 640), BF),
        ),
        in_specs=[head, head, head, pl.BlockSpec((1, rows, KEYS), lambda j: (j, 0, 0)), tile],
        out_specs=(head, tile),
        compiler_params=pltpu.CompilerParams(vmem_limit_bytes=VMEM_LIMIT),
        cost_estimate=pl.CostEstimate(
            flops=8 * HEADS * T * KEYS * 128, bytes_accessed=12_000_000, transcendentals=0
        ),
    )(q, d_mix, mix, prob, kv)


def by_shard(x, width):
    core, ylo = lax.axis_index("core") == 1, lax.axis_index("ylo") == 1
    p = [x[..., k * width : (k + 1) * width] for k in range(4)]
    return ordered(p)


def ordered(p):
    core, ylo = lax.axis_index("core") == 1, lax.axis_index("ylo") == 1
    p = [jnp.where(core, p[k ^ 1], p[k]) for k in range(4)]
    return [jnp.where(ylo, p[k ^ 2], p[k]) for k in range(4)]


def gathered(first, second):
    sib = (permute(first, dcore=1), permute(second, dcore=1))
    other = (permute(first, dy=1), permute(second, dy=-1))
    far = (permute(other[0], dcore=1), permute(other[1], dcore=1))
    return [(first, second), sib, other, far]


def angles_of(positions):
    frequency = THETA ** (-jnp.arange(0, HEAD_DIM // 2).astype(F32) * 2.0 / HEAD_DIM)
    return positions[:, None] * frequency[None, :]


def rotate(values, cosine, sine):
    a, b = values[..., : HEAD_DIM // 2], values[..., HEAD_DIM // 2 :]
    return jnp.concatenate([a * cosine - b * sine, b * cosine + a * sine], axis=-1)


def norm_back(z, r, gain, dy):
    dz = r * (gain * dy) - z * (r * r * r) * jnp.mean(gain * dy * z, axis=-1, keepdims=True)
    return dz, jnp.sum(dy * z * r, axis=0)


def everyone(rows, slices):
    half = T // 2
    far = jnp.concatenate([rows, slices[2], slices[3]], axis=1)
    near = permute(jnp.concatenate([rows, slices[1]], axis=1), dcore=1)
    got = jnp.concatenate([permute(far[:half], dy=1), permute(far[half:], dy=-1)], axis=0)
    n, m = rows.shape[1], slices[0].shape[1]
    relay = permute(jnp.concatenate([got[:, :n], got[:, n + m :]], axis=1), dcore=1)
    every = jnp.concatenate([rows, near[:, :n], got[:, :n], relay[:, :n]], axis=0)
    some = jnp.concatenate([slices[0], near[:, n:], got[:, n : n + m], relay[:, n:]], axis=0)
    return every, some


def per_device(hidden, chosen, positions, w_query, w_key, w_value, w_output, w_gate, w_up, w_down, gain_attn, gain_ffn, router, d_out):
    tokens, upstream = hidden[0], d_out[0]
    x_at = lax.axis_index("x")
    odd = lax.rem(x_at, 2) == 1
    block = (lax.axis_index("yhi") * 16 + lax.axis_index("z") * 4 + x_at) // 2

    vectors = jnp.stack([gain_attn, gain_ffn, router], axis=1)
    w_kv = jnp.concatenate([w_key, w_value, vectors, jnp.zeros((240, 61), BF)], axis=1)
    qkv = gathered(w_query, w_kv)

    flag = chosen[0] > 0
    count = jnp.cumsum(flag.astype(jnp.int32))
    rank = count - 1 + jnp.where(odd, PAIR - count[-1], 0)
    place = (lax.broadcasted_iota(jnp.int32, (PAIR, PAIR), 0) == rank[None, :]) & flag[None, :]
    place = place.astype(BF)
    pos = positions[0]
    pos_cols = jnp.stack([pos // 64, pos % 64], axis=1).astype(BF)
    packed = jnp.concatenate(
        [tokens.astype(BF), upstream.astype(BF), pos_cols, jnp.zeros((PAIR, 126), BF)], axis=1
    )
    compact = dot(place, packed).astype(BF)
    keep = jnp.where(odd, compact[T:], compact[:T])
    give = jnp.where(odd, compact[:T], compact[T:])
    mine = keep.astype(F32) + swap_x(give).astype(F32)
    h, up_c = mine[:, :D], mine[:, D : 2 * D]
    pos_c = mine[:, 2 * D] * 64.0 + mine[:, 2 * D + 1]

    out_w = gathered(w_output[:, :480], w_output[:, 480:])
    ffn_w = gathered(w_gate, w_up)
    down_w = gathered(w_down[:320], w_down[320:])

    vec = [jnp.concatenate(ordered([q[1][:, 640 + k] for q in qkv])) for k in range(3)]
    gain_a, gain_f, route_w = (v.astype(F32) for v in vec)

    r1 = lax.rsqrt(jnp.mean(h * h, axis=-1, keepdims=True) + EPS)
    x1 = (h * r1 * gain_a).astype(BF)
    x1_s = by_shard(x1, 240)
    q_pre = sum(dot(x1_s[k], qkv[k][0]) for k in range(4)).reshape(T, HEADS, HEAD_DIM)
    kv_pre = sum(dot(x1_s[k], qkv[k][1]) for k in range(4))
    angles = angles_of(pos_c)
    cosine, sine = jnp.cos(angles)[:, None, :], jnp.sin(angles)[:, None, :]
    q_rot = rotate(q_pre, cosine, sine).astype(BF)
    k_rot = rotate(kv_pre[:, :320].reshape(T, KV_HEADS, HEAD_DIM), cosine, sine).astype(BF)
    v_low = kv_pre[:, 320:640].astype(BF).reshape(T, KV_HEADS, HEAD_DIM)
    kv_all = gather_keys(jnp.concatenate([k_rot, v_low], axis=-1).reshape(T, 640))

    def heads_first(a):
        return a.reshape(T, KV_HEADS, GROUPS, HEAD_DIM).transpose(1, 2, 0, 3).reshape(KV_HEADS, GROUPS * T, HEAD_DIM)

    def tokens_first(a):
        return a.reshape(KV_HEADS, GROUPS, T, HEAD_DIM).transpose(2, 0, 1, 3).reshape(T, D)

    zero = jnp.zeros((KV_HEADS, GROUPS * T, HEAD_DIM), BF)
    q_heads = jnp.concatenate([heads_first(q_rot), zero], axis=-1)
    limit = ((block + 1) * PAIR).astype(jnp.int32).reshape(1)
    mix_heads, prob = attend(limit, q_heads, kv_all)
    mixture = tokens_first(mix_heads[..., HEAD_DIM:]).astype(BF)

    mix_s = by_shard(mixture, 240)
    attn_out = jnp.concatenate(
        [sum(dot(mix_s[k], out_w[k][p]) for k in range(4)) for p in range(2)], axis=1
    )
    middle = h + attn_out
    r2 = lax.rsqrt(jnp.mean(middle * middle, axis=-1, keepdims=True) + EPS)
    x2 = (middle * r2 * gain_f).astype(BF)
    x2_s = by_shard(x2, 240)
    gate = sum(dot(x2_s[k], ffn_w[k][0]) for k in range(4))
    up = sum(dot(x2_s[k], ffn_w[k][1]) for k in range(4))
    sg = jax.nn.sigmoid(gate)
    silu = gate * sg
    inner = (silu * up).astype(BF)
    inner_s = by_shard(inner, 640)
    ffn_out = sum(
        dot(inner_s[k][:, :320], down_w[k][0]) + dot(inner_s[k][:, 320:], down_w[k][1]) for k in range(4)
    )
    route = jax.nn.sigmoid(jnp.sum(h * route_w[None, :], axis=-1, keepdims=True))
    branch = attn_out + ffn_out
    out_c = route * branch
    d_branch = up_c * route
    d_logit = route * (1.0 - route) * jnp.sum(up_c * branch, axis=-1, keepdims=True)
    g_router = jnp.sum(d_logit * h, axis=0)

    d_ffn = d_branch.astype(BF)
    d_inner = jnp.concatenate(
        ordered(
            [
                jnp.concatenate([dot(d_ffn, down_w[k][0], NT), dot(d_ffn, down_w[k][1], NT)], axis=1)
                for k in range(4)
            ]
        ),
        axis=1,
    )
    d_gate = (d_inner * up * (sg + gate * sg * (1.0 - sg))).astype(BF)
    d_up = (d_inner * silu).astype(BF)
    d_x2 = jnp.concatenate(
        ordered([dot(d_gate, ffn_w[k][0], NT) + dot(d_up, ffn_w[k][1], NT) for k in range(4)]), axis=1
    )
    d_mid, g_gain_f = norm_back(middle, r2, gain_f, d_x2)
    d_attn = (d_branch + d_mid).astype(BF)
    d_mix = jnp.concatenate(
        ordered([dot(d_attn[:, :480], out_w[k][0], NT) + dot(d_attn[:, 480:], out_w[k][1], NT) for k in range(4)]),
        axis=1,
    ).astype(BF)

    rows_1, some_1 = everyone(
        jnp.concatenate([d_gate, d_up, d_ffn, d_attn], axis=1),
        [jnp.concatenate([x2_s[k], inner_s[k], mix_s[k]], axis=1) for k in range(4)],
    )
    g_gate_up = dot(some_1[:, :240], rows_1[:, : 2 * FF], TN)
    g_down_t = dot(rows_1[:, 2 * FF : 2 * FF + D], some_1[:, 240:880], TN)
    g_out = dot(some_1[:, 880:], rows_1[:, 2 * FF + D :], TN)
    g_one = jnp.concatenate(
        [g_gate_up.astype(BF)]
        + [g_down_t[240 * k : 240 * (k + 1)].astype(BF) for k in range(4)]
        + [g_out[:, :512].astype(BF)],
        axis=1,
    )

    d_mix_heads = jnp.concatenate([zero, heads_first(d_mix.reshape(T, HEADS, HEAD_DIM))], axis=-1)
    d_q_heads, d_kv = attend_back(q_heads, d_mix_heads, mix_heads, prob, kv_all)
    d_own = scatter_keys(d_kv).reshape(T, KV_HEADS, 2 * HEAD_DIM)
    d_q = rotate(tokens_first(d_q_heads[..., :HEAD_DIM]).reshape(T, HEADS, HEAD_DIM), cosine, -sine)
    d_q = d_q.reshape(T, D).astype(BF)
    d_k = rotate(d_own[..., :HEAD_DIM], cosine, -sine).reshape(T, 320).astype(BF)
    d_v = d_own[..., HEAD_DIM:].reshape(T, 320).astype(BF)
    d_kv_low = jnp.concatenate([d_k, d_v], axis=1)
    d_x1 = jnp.concatenate(
        ordered([dot(d_q, qkv[k][0], NT) + dot(d_kv_low, qkv[k][1][:, :640], NT) for k in range(4)]), axis=1
    )
    d_first, g_gain_a = norm_back(h, r1, gain_a, d_x1)
    d_h = d_mid + d_first + d_logit * route_w[None, :]

    back = jnp.concatenate([out_c, d_h], axis=1).astype(BF)
    other = swap_x(back)
    both = jnp.concatenate([jnp.where(odd, other, back), jnp.where(odd, back, other)], axis=0)
    spread = dot(place, both, TN)
    output = tokens + spread[:, :D]
    d_tokens = upstream + spread[:, D:]

    rows_2, some_2 = everyone(jnp.concatenate([d_q, d_kv_low], axis=1), x1_s)
    g_qkv = dot(some_2, rows_2, TN)
    g_two = jnp.concatenate([g_out[:, 512:].astype(BF), g_qkv.astype(BF)], axis=1)

    s_one = reduce_all(g_one, 3)
    s_two = reduce_all(g_two, 4)
    vector = lax.psum(jnp.stack([g_gain_a, g_gain_f, g_router]), AX)
    shard = lax.axis_index("ylo") * 2 + lax.axis_index("core")
    vector = lax.dynamic_slice_in_dim(vector, shard * 240, 240, axis=1)
    g_down = s_one[:, 2 * FF : 3 * FF].reshape(240, 4, 640).transpose(2, 1, 0).reshape(640, D)
    return (
        output[None],
        d_tokens[None],
        s_two[:, 448:1408].astype(F32),
        s_two[:, 1408:1728].astype(F32),
        s_two[:, 1728:].astype(F32),
        jnp.concatenate([s_one[:, 3 * FF :], s_two[:, :448]], axis=1).astype(F32),
        s_one[:, :FF].astype(F32),
        s_one[:, FF : 2 * FF].astype(F32),
        g_down.astype(F32),
        vector[0],
        vector[1],
        vector[2],
    )


def solution(mesh):
    finer = Mesh(mesh.devices.reshape(DIMS), AX)
    shard, blk = ("ylo", "core"), ("yhi", "z", "x")
    act, row, weight, vec = P(shard, blk, None), P(shard, blk), P(shard, None), P(shard)
    return jax.shard_map(
        per_device,
        mesh=finer,
        in_specs=(act, row, row) + (weight,) * 7 + (vec,) * 3 + (act,),
        out_specs=(act, act) + (weight,) * 7 + (vec,) * 3,
        check_vma=False,
    )
```

```python
import functools

import jax
import jax.numpy as jnp
from jax import lax
from jax.experimental import pallas as pl
from jax.experimental.pallas import tpu as pltpu
from jax.sharding import Mesh
from jax.sharding import PartitionSpec as P

D = 960
HEADS = 15
KV_HEADS = 5
GROUPS = 3
HEAD_DIM = 64
FF = 2560
EPS = 1e-05
THETA = 10000.0
SCALE = HEAD_DIM ** (-0.5)
T = 64
PAIR = 128
SLOTS = 32
KEYS = SLOTS * T
AX = ("ylo", "core", "yhi", "z", "x")
DIMS = (2, 2, 2, 4, 4)
MESH = pl.DeviceIdType.MESH
BF = jnp.bfloat16
F32 = jnp.float32
VMEM_LIMIT = 56 * 2**20


def dot(a, b, dims=(((1,), (0,)), ((), ()))):
    return lax.dot_general(a, b, dims, preferred_element_type=F32)


NT = (((1,), (1,)), ((), ()))
TN = (((0,), (0,)), ((), ()))


def moved(place, dy, dcore, dz, dx):
    ylo, core, yhi, z, x = place
    y = (yhi * 2 + ylo + dy) % 4
    return (y % 2, (core + dcore) % 2, y // 2, (z + dz) % 4, (x + dx) % 4)


def flat(place):
    at = 0
    for size, c in zip(DIMS, place):
        at = at * size + c
    return at


def places():
    for ylo in range(2):
        for core in range(2):
            for yhi in range(2):
                for z in range(4):
                    for x in range(4):
                        yield (ylo, core, yhi, z, x)


def permute(value, dy=0, dcore=0, dz=0, dx=0):
    return lax.ppermute(value, AX, [(flat(p), flat(moved(p, dy, dcore, dz, dx))) for p in places()])


def swap_x(value):
    return lax.ppermute(
        value, AX, [(flat(p), flat(p[:4] + (p[4] ^ 1,))) for p in places()]
    )


def here():
    return tuple(lax.axis_index(a) for a in AX)


def neighbour(me, axis, step):
    ylo, core, yhi, z, x = me
    if axis == "z":
        z = lax.rem(z + step + 4, 4)
    elif axis == "x":
        x = lax.rem(x + step + 4, 4)
    elif axis == "pair":
        x = x + 1 - 2 * lax.rem(x, 2)
    elif axis == "yhi":
        yhi = 1 - yhi
    elif axis == "ylo":
        ylo = 1 - ylo
    elif axis == "core":
        core = 1 - core
    else:
        y = lax.rem(yhi * 2 + ylo + step + 4, 4)
        ylo, yhi = lax.rem(y, 2), y // 2
    return (ylo, core, yhi, z, x)


NEAR = (("x", 1), ("x", -1), ("z", 1), ("z", -1), ("yhi", 1))
WEIGHT = (("y", 1), ("y", -1), ("core", 1))
SMALL = (("core", 1), ("ylo", 1), ("x", 2), ("z", 2))


def greet(me, partners):
    barrier = pltpu.get_barrier_semaphore()
    for axis, step in partners:
        pl.semaphore_signal(
            barrier, inc=1, device_id=neighbour(me, axis, step), device_id_type=MESH
        )
    pl.semaphore_wait(barrier, len(partners))


class Sends:
    def __init__(self, me, send_sems, recv_sems):
        self.me, self.send_sems, self.recv_sems, self.all = me, send_sems, recv_sems, []

    def start(self, src, dst, axis, step):
        k = len(self.all)
        copy = pltpu.make_async_remote_copy(
            src_ref=src,
            dst_ref=dst,
            send_sem=self.send_sems.at[k],
            recv_sem=self.recv_sems.at[k],
            device_id=neighbour(self.me, axis, step),
            device_id_type=MESH,
        )
        copy.start()
        self.all.append(copy)
        return copy

    def finish(self):
        for copy in self.all:
            copy.wait_send()


def together(*steps):
    steps = list(steps)
    while steps:
        for step in list(steps):
            try:
                next(step)
            except StopIteration:
                steps.remove(step)


def sems(count):
    return [pltpu.SemaphoreType.DMA((count,)), pltpu.SemaphoreType.DMA((count,))]


def plus(*terms):
    total = terms[0].astype(F32)
    for term in terms[1:]:
        total = total + term.astype(F32)
    return total


class Shards:
    def __init__(self, sends):
        self.sends, self.arrived, self.last = sends, [], []

    def near(self, own, out):
        self.last.append(self.sends.start(own, out.at[out.shape[0] - 3], "core", 1))

    def far(self, own, out, step, row, rows):
        r = pl.ds(row, rows)
        self.arrived.append((out, r, self.sends.start(own.at[r], out.at[out.shape[0] - 2, r], "y", step)))

    def relay(self):
        for out, r, copy in self.arrived:
            copy.wait_recv()
            self.last.append(self.sends.start(out.at[out.shape[0] - 2, r], out.at[out.shape[0] - 1, r], "core", 1))
        self.arrived = []

    def finish(self):
        self.relay()
        for copy in self.last:
            copy.wait_recv()
        self.last = []


def gather_steps(me, sends, kv_ref, out_ref):
    _, _, yh, z, x = me
    oy = 1 - yh
    half, quarter = T // 2, T // 4
    streams = (("x", "z", 0), ("z", "x", half))

    def slot(y, axis, step, rows, count):
        zz = lax.rem(z + step + 4, 4) if axis == "z" else z
        xx = lax.rem(x + step + 4, 4) if axis == "x" else x
        return out_ref.at[y, zz, xx, pl.ds(rows, count)]

    def line(y, axis, step, rows, count):
        if axis == "z":
            return out_ref.at[y, lax.rem(z + step + 4, 4), :, pl.ds(rows, count)]
        return out_ref.at[y, :, lax.rem(x + step + 4, 4), pl.ds(rows, count)]

    own = out_ref.at[yh, z, x]
    own[...] = kv_ref[...]
    first = sends.start(kv_ref, own, "yhi", 1)
    got = {}
    for y, tag in ((yh, 0), (oy, 1)):
        if tag:
            yield
            first.wait_recv()
        for axis, _, row in streams:
            src = slot(y, axis, 0, row, half)
            for step in (1, -1):
                got[tag, row, step] = sends.start(src, src, axis, step)
    far = {}
    for y, tag in ((yh, 0), (oy, 1)):
        yield
        for axis, _, row in streams:
            for step, off in ((1, 0), (-1, quarter)):
                got[tag, row, step].wait_recv()
                src = slot(y, axis, -step, row + off, quarter)
                far[tag, row, step] = sends.start(src, src, axis, step)
    wide = {}
    for y, tag in ((yh, 0), (oy, 1)):
        yield
        for _, axis, row in streams:
            for step in (1, -1):
                far[tag, row, step].wait_recv()
            src = line(y, axis, 0, row, half)
            for step in (1, -1):
                wide[tag, row, step] = sends.start(src, src, axis, step)
    last = []
    for y, tag in ((yh, 0), (oy, 1)):
        yield
        for _, axis, row in streams:
            for step, off in ((1, 0), (-1, quarter)):
                wide[tag, row, step].wait_recv()
                src = line(y, axis, -step, row + off, quarter)
                last.append(sends.start(src, src, axis, step))
    yield
    for copy in last:
        copy.wait_recv()


def swapped(x):
    lane = lax.broadcasted_iota(jnp.int32, x.shape, 1)
    return jnp.where(lane < HEAD_DIM // 2, pltpu.roll(x, 96, 1), pltpu.roll(x, 32, 1))


def front_kernel(
    hidden_ref, d_out_ref, chosen_ref, pos_ref, freq_ref, vec_ref, wq_ref, wk_ref, wv_ref,
    wo_ref, wg_ref, wu_ref, wd_ref,
    mix_ref, prob_ref, q_ref, kv_ref, h_ref, up_ref, x1_ref, cos_ref, sin_ref, place_ref, vec_out_ref,
    wq, wk, wv, wos_ref, wgs_ref, wus_ref, wds_ref,
    compact_h, compact_d, compact_p, got_h, got_d, got_p, vecs, q_pre, kv_own,
    load_sems, send_sems, recv_sems,
):
    me = here()
    yhi, z, x = me[2:]
    loads = []
    for k, (own, to) in enumerate(((wq_ref, wq), (wk_ref, wk), (wv_ref, wv))):
        loads.append(pltpu.make_async_copy(own, to.at[0], load_sems.at[k]))
        loads[-1].start()
    greet(me, NEAR + WEIGHT + (("pair", 1),))
    sends = Sends(me, send_sems, recv_sems)
    early, late = Shards(sends), Shards(sends)
    vec_far = sends.start(vec_ref, vecs.at[2], "y", 1)
    for own, to in ((wq_ref, wq), (wk_ref, wk), (wv_ref, wv)):
        early.far(own, to, 1, 0, 128)
        early.far(own, to, -1, 128, 112)
    vec_near = sends.start(vec_ref, vecs.at[1], "core", 1)
    for own, to in ((wq_ref, wq), (wk_ref, wk), (wv_ref, wv)):
        early.near(own, to)
    vecs[0] = vec_ref[...]

    odd = lax.rem(x, 2)
    flag = jnp.where(chosen_ref[...] > 0, 1.0, 0.0)
    token = lax.broadcasted_iota(jnp.int32, (PAIR, PAIR), 0)
    lane = lax.broadcasted_iota(jnp.int32, (PAIR, PAIR), 1)
    upto = jnp.where(token <= lane, 1.0, 0.0).astype(BF)
    count = dot(jnp.broadcast_to(flag, (16, PAIR)).astype(BF), upto)[0:1]
    total = jnp.sum(flag, axis=1, keepdims=True)
    rank = count - 1.0 + jnp.where(odd == 1, PAIR - total, 0.0)
    place = jnp.where(token.astype(F32) == rank, flag, 0.0)
    place_low = place.astype(BF)
    place_ref[...] = place_low
    compact_p[...] = jnp.broadcast_to(
        jnp.sum(place * pos_ref[...].astype(F32), axis=1, keepdims=True), (PAIR, PAIR)
    )
    compact_h[...] = dot(place_low, hidden_ref[...].astype(BF)).astype(BF)
    compact_d[...] = dot(place_low, d_out_ref[...].astype(BF)).astype(BF)
    give = pl.ds(pl.multiple_of((1 - odd) * T, T), T)
    keep = pl.ds(pl.multiple_of(odd * T, T), T)
    swaps = [
        sends.start(c.at[give], g, "pair", 1)
        for c, g in ((compact_h, got_h), (compact_p, got_p), (compact_d, got_d))
    ]
    vec_far.wait_recv()
    vec_last = sends.start(vecs.at[2], vecs.at[3], "core", 1)
    swaps[0].wait_recv()
    h = plus(compact_h[keep], got_h[...])
    h_ref[...] = h
    swaps[1].wait_recv()
    angle = (compact_p[keep] + got_p[...]) * freq_ref[...]
    turn = lax.broadcasted_iota(jnp.int32, (T, PAIR), 1)
    cosine = jnp.where(turn < HEAD_DIM, jnp.cos(angle), 1.0)
    sine = jnp.sin(angle)
    sine = jnp.where(turn < HEAD_DIM // 2, -sine, jnp.where(turn < HEAD_DIM, sine, 0.0))
    cos_ref[...], sin_ref[...] = cosine, sine
    vec_near.wait_recv()
    vec_last.wait_recv()
    vec_out_ref[...] = jnp.zeros_like(vec_out_ref)
    for k, v in enumerate(our_order(me, [vecs[k, :, :240] for k in range(4)])):
        vec_out_ref[:, 240 * k : 240 * (k + 1)] = v
    r1 = lax.rsqrt(jnp.mean(h * h, axis=-1, keepdims=True) + EPS)
    x1_ref[...] = (h * r1 * vec_out_ref[0:1, :D]).astype(BF)
    x1_k = our_order(me, cut_four(x1_ref))
    for copy in loads:
        copy.wait()
    early.relay()
    late.far(wo_ref, wos_ref, 1, 0, 128)
    late.far(wo_ref, wos_ref, -1, 128, 112)
    late.far(wg_ref, wgs_ref, 1, 0, 64)
    late.far(wg_ref, wgs_ref, -1, 128, 64)
    late.near(wo_ref, wos_ref)
    swaps[2].wait_recv()
    up_ref[...] = plus(compact_d[keep], got_d[...])
    early.finish()
    k_pre = sum(dot(x1_k[k], wk[k]) for k in range(4))
    v_pre = sum(dot(x1_k[k], wv[k]) for k in range(4))
    for j in range(KV_HEADS):
        run = slice(HEAD_DIM * j, HEAD_DIM * (j + 1))
        tile = jnp.concatenate([k_pre[:, run], v_pre[:, run]], axis=1)
        kv_own[:, 128 * j : 128 * (j + 1)] = (tile * cosine + swapped(tile) * sine).astype(BF)
    gather = gather_steps(me, sends, kv_own, kv_ref)
    next(gather)
    q_pre[...] = sum(dot(x1_k[k], wq[k]) for k in range(4))
    zero = jnp.zeros((T, HEAD_DIM), F32)
    for j in range(KV_HEADS):
        for g in range(GROUPS):
            at = HEAD_DIM * (GROUPS * j + g)
            tile = jnp.concatenate([q_pre[:, at : at + HEAD_DIM], zero], axis=1)
            q_ref[j, g * T : (g + 1) * T] = (tile * cosine + swapped(tile) * sine).astype(BF)
    next(gather)
    late.far(wg_ref, wgs_ref, 1, 64, 64)
    late.far(wg_ref, wgs_ref, -1, 192, 48)
    late.far(wu_ref, wus_ref, 1, 0, 128)
    late.far(wu_ref, wus_ref, -1, 128, 112)
    late.far(wd_ref, wds_ref, 1, 0, 320)
    late.far(wd_ref, wds_ref, -1, 320, 320)
    for own, out in ((wg_ref, wgs_ref), (wu_ref, wus_ref), (wd_ref, wds_ref)):
        late.near(own, out)
    together(gather)
    limit = ((yhi * 16 + z * 4 + x) // 2 + 1) * PAIR

    @pl.loop(0, KV_HEADS)
    def _(j):
        c = pl.ds(pl.multiple_of(j * 128, 128), 128)
        tile = kv_ref[:, :, :, :, c].reshape(KEYS, 128)
        scores = dot(q_ref[j], tile, NT) * SCALE
        column = lax.broadcasted_iota(jnp.int32, scores.shape, 1)
        scores = jnp.where(column < limit, scores, -1e30)
        exponent = jnp.exp(scores - jnp.max(scores, axis=-1, keepdims=True))
        prob = (exponent * (1.0 / jnp.sum(exponent, axis=-1, keepdims=True))).astype(BF)
        prob_ref[j] = prob
        mix_ref[j] = dot(prob, tile)

    late.finish()
    sends.finish()


def front(hidden, d_out, chosen, pos, freq, vec, w_query, w_key, w_value, *later):
    vmem, hbm = pl.BlockSpec(memory_space=pltpu.VMEM), pl.BlockSpec(memory_space=pl.ANY)
    rows = GROUPS * T
    return pl.pallas_call(
        front_kernel,
        name="front",
        out_shape=(
            jax.ShapeDtypeStruct((KV_HEADS, rows, 128), F32),
            jax.ShapeDtypeStruct((KV_HEADS, rows, KEYS), BF),
            jax.ShapeDtypeStruct((KV_HEADS, rows, 128), BF),
            jax.ShapeDtypeStruct((2, 4, 4, T, 640), BF),
            jax.ShapeDtypeStruct((T, D), F32),
            jax.ShapeDtypeStruct((T, D), F32),
            jax.ShapeDtypeStruct((T, D), BF),
            jax.ShapeDtypeStruct((T, 128), F32),
            jax.ShapeDtypeStruct((T, 128), F32),
            jax.ShapeDtypeStruct((PAIR, PAIR), BF),
            jax.ShapeDtypeStruct((8, 1024), F32),
            jax.ShapeDtypeStruct((4, 240, 960), BF),
            jax.ShapeDtypeStruct((4, 240, 320), BF),
            jax.ShapeDtypeStruct((4, 240, 320), BF),
        )
        + tuple(jax.ShapeDtypeStruct((3,) + w.shape, BF) for w in later),
        in_specs=[vmem] * 6 + [hbm] * 7,
        out_specs=(vmem,) * 14 + (hbm,) * 4,
        scratch_shapes=[
            pltpu.VMEM((PAIR, D), BF),
            pltpu.VMEM((PAIR, D), BF),
            pltpu.VMEM((PAIR, PAIR), F32),
            pltpu.VMEM((T, D), BF),
            pltpu.VMEM((T, D), BF),
            pltpu.VMEM((T, PAIR), F32),
            pltpu.VMEM((4, 8, 256), F32),
            pltpu.VMEM((T, D), F32),
            pltpu.VMEM((T, 640), BF),
            pltpu.SemaphoreType.DMA((3,)),
        ]
        + sems(84),
        compiler_params=pltpu.CompilerParams(
            collective_id=1, has_side_effects=True, vmem_limit_bytes=VMEM_LIMIT
        ),
        cost_estimate=pl.CostEstimate(flops=5_000_000_000, bytes_accessed=90_000_000, transcendentals=0),
    )(hidden, d_out, chosen, pos, freq, vec, w_query, w_key, w_value, *later)


def key_steps(me, sends, part_ref, out_ref, low, out_b, full, sums, nlow, nout, nfull, mine, y_in):
    _, _, yh, z, x = me
    half, quarter = T // 2, T // 4
    streams = (("x", "z", 0), ("z", "x", half))

    def line(axis, step, row, count):
        if axis == "z":
            return part_ref.at[:, lax.rem(z + step + 4, 4), :, pl.ds(row, count)]
        return part_ref.at[:, :, lax.rem(x + step + 4, 4), pl.ds(row, count)]

    near = {}
    for s, (axis, _, row) in enumerate(streams):
        near[s, 1] = sends.start(line(axis, 2, row, quarter), low.at[s, 0], axis, 1)
        near[s, -1] = sends.start(line(axis, 2, row + quarter, quarter), low.at[s, 1], axis, -1)
    whole = {}
    yield
    for s, (axis, _, row) in enumerate(streams):
        for d, step in enumerate((1, -1)):
            near[s, step].wait_recv()
            lo, hi = (0, quarter) if step == 1 else (quarter, 0)
            out_b[s, d, :, :, pl.ds(lo, quarter)] = plus(
                line(axis, step, row + lo, quarter)[...], low[s, d]
            ).astype(BF)
            out_b[s, d, :, :, pl.ds(hi, quarter)] = line(axis, step, row + hi, quarter)[...]
            whole[s, step] = sends.start(out_b.at[s, d], full.at[s, d], axis, step)
    yield
    near = {}
    for s, (axis, other, row) in enumerate(streams):
        for step in (1, -1):
            whole[s, step].wait_recv()
        sums[s] = plus(line(axis, 0, row, half)[...], full[s, 0], full[s, 1]).astype(BF)
        far = lax.rem((z if other == "z" else x) + 2, 4)
        near[s, 1] = sends.start(sums.at[s, :, far, pl.ds(0, quarter)], nlow.at[s, 0], other, 1)
        near[s, -1] = sends.start(
            sums.at[s, :, far, pl.ds(quarter, quarter)], nlow.at[s, 1], other, -1
        )
    yield
    for s, (axis, other, row) in enumerate(streams):
        at = z if other == "z" else x
        for d, step in enumerate((1, -1)):
            near[s, step].wait_recv()
            to = lax.rem(at + step + 4, 4)
            lo, hi = (0, quarter) if step == 1 else (quarter, 0)
            nout[s, d, :, pl.ds(lo, quarter)] = plus(
                sums[s, :, to, pl.ds(lo, quarter)], nlow[s, d]
            ).astype(BF)
            nout[s, d, :, pl.ds(hi, quarter)] = sums[s, :, to, pl.ds(hi, quarter)]
            whole[s, step] = sends.start(nout.at[s, d], nfull.at[s, d], other, step)
    yield
    swap = {}
    for s, (axis, other, row) in enumerate(streams):
        at = z if other == "z" else x
        for step in (1, -1):
            whole[s, step].wait_recv()
        mine[s] = plus(sums[s, :, at], nfull[s, 0], nfull[s, 1]).astype(BF)
        swap[s] = sends.start(mine.at[s, 1 - yh], y_in.at[s], "yhi", 1)
    yield
    for s, (axis, other, row) in enumerate(streams):
        swap[s].wait_recv()
        out_ref[pl.ds(row, half)] = plus(mine[s, yh], y_in[s])


def key_scratch():
    half, quarter, w = T // 2, T // 4, 640
    return [
        pltpu.VMEM((2, 2, 2, 4, quarter, w), BF),
        pltpu.VMEM((2, 2, 2, 4, half, w), BF),
        pltpu.VMEM((2, 2, 2, 4, half, w), BF),
        pltpu.VMEM((2, 2, 4, half, w), BF),
        pltpu.VMEM((2, 2, 2, quarter, w), BF),
        pltpu.VMEM((2, 2, 2, half, w), BF),
        pltpu.VMEM((2, 2, 2, half, w), BF),
        pltpu.VMEM((2, 2, half, w), BF),
        pltpu.VMEM((2, half, w), BF),
    ]


ROWS = 256
HALF = ROWS // 2
STREAMS = (("x", "z", 0), ("z", "x", HALF))
RUN = HALF // 4
CUT = HALF // 2


def spots(me):
    return {"z": me[3], "x": me[4]}


def around(me, axis, step):
    return lax.rem(spots(me)[axis] + step + 4, 4)


def columns(me, axis, step, big):
    return pl.ds(pl.multiple_of(around(me, axis, step) * big, 128), big)


def sum_steps(me, sends, g_ref, mine, low, out_b, full, sums, nlow, nout, nfull, y_in):
    big = mine.shape[-1]
    near, whole = {}, {}

    def parts(step):
        return (0, CUT) if step == 1 else (CUT, 0)

    for s, (axis, _, row) in enumerate(STREAMS):
        c = columns(me, axis, 2, big)
        for step in (1, -1):
            r = pl.ds(row + parts(step)[0], CUT)
            near[s, step] = sends.start(g_ref.at[r, c], low.at[r], axis, step)
    yield
    for s, (axis, _, row) in enumerate(STREAMS):
        for d, step in enumerate((1, -1)):
            near[s, step].wait_recv()
            add, keep = (pl.ds(row + p, CUT) for p in parts(step))
            c = columns(me, axis, step, big)
            out_b[d, add] = plus(g_ref[add, c], low[add]).astype(BF)
            out_b[d, keep] = g_ref[keep, c]
            r = pl.ds(row, HALF)
            whole[s, step] = sends.start(out_b.at[d, r], full.at[d, r], axis, step)
    yield
    half = RUN // 2

    def run(row, other, step, off, count):
        return pl.ds(pl.multiple_of(row + around(me, other, step) * RUN + off, 16), count)

    for s, (axis, other, row) in enumerate(STREAMS):
        for step in (1, -1):
            whole[s, step].wait_recv()
        r = pl.ds(row, HALF)
        sums[r] = plus(g_ref[r, columns(me, axis, 0, big)], full[0, r], full[1, r]).astype(BF)
        for d, step in enumerate((1, -1)):
            near[s, step] = sends.start(
                sums.at[run(row, other, 2, d * half, half)], nlow.at[s, d], other, step
            )
    yield
    for s, (axis, other, row) in enumerate(STREAMS):
        for d, step in enumerate((1, -1)):
            near[s, step].wait_recv()
            add, keep = (0, half) if step == 1 else (half, 0)
            nout[s, d, pl.ds(add, half)] = plus(
                sums[run(row, other, step, add, half)], nlow[s, d]
            ).astype(BF)
            nout[s, d, pl.ds(keep, half)] = sums[run(row, other, step, keep, half)]
            whole[s, step] = sends.start(nout.at[s, d], nfull.at[s, d], other, step)
    yield
    swap = {}
    for s, (axis, other, row) in enumerate(STREAMS):
        for step in (1, -1):
            whole[s, step].wait_recv()
        y_in[0, s] = plus(sums[run(row, other, 0, 0, RUN)], nfull[s, 0], nfull[s, 1]).astype(BF)
        swap[s] = sends.start(y_in.at[0, s], y_in.at[1, s], "yhi", 1)
    yield
    for s in range(2):
        swap[s].wait_recv()
        mine[s] = plus(y_in[0, s], y_in[1, s]).astype(BF)


def sum_scratch(width):
    big = width // 4
    return [
        pltpu.VMEM((ROWS, big), BF),
        pltpu.VMEM((2, ROWS, big), BF),
        pltpu.VMEM((2, ROWS, big), BF),
        pltpu.VMEM((ROWS, big), BF),
        pltpu.VMEM((2, 2, RUN // 2, big), BF),
        pltpu.VMEM((2, 2, RUN, big), BF),
        pltpu.VMEM((2, 2, RUN, big), BF),
        pltpu.VMEM((2, 2, RUN, big), BF),
    ]


def spread_steps(me, sends, mine, out_ref):
    big = mine.shape[-1]
    half = RUN // 2
    near, whole = {}, {}

    def run(row, other, step, off, count):
        return pl.ds(pl.multiple_of(row + around(me, other, step) * RUN + off, 16), count)

    for s, (axis, other, row) in enumerate(STREAMS):
        ref = out_ref.at[run(row, other, 0, 0, RUN), columns(me, axis, 0, big)]
        ref[...] = mine[s]
        for step in (1, -1):
            near[s, step] = sends.start(ref, ref, other, step)
    yield
    for s, (axis, other, row) in enumerate(STREAMS):
        for d, step in enumerate((1, -1)):
            near[s, step].wait_recv()
            ref = out_ref.at[run(row, other, -step, d * half, half), columns(me, axis, 0, big)]
            whole[s, step] = sends.start(ref, ref, other, step)
    yield
    for s, (axis, other, row) in enumerate(STREAMS):
        for step in (1, -1):
            whole[s, step].wait_recv()
        ref = out_ref.at[pl.ds(row, HALF), columns(me, axis, 0, big)]
        for step in (1, -1):
            near[s, step] = sends.start(ref, ref, axis, step)
    yield
    last = []
    for s, (axis, other, row) in enumerate(STREAMS):
        for d, step in enumerate((1, -1)):
            near[s, step].wait_recv()
            ref = out_ref.at[pl.ds(row + d * CUT, CUT), columns(me, axis, -step, big)]
            last.append(sends.start(ref, ref, axis, step))
    yield
    for copy in last:
        copy.wait_recv()


def vector_steps(sends, vec_ref, out_ref, keep, got):
    rounds = ((("core", 1),), (("ylo", 1),), (("x", 1), ("x", -1), ("x", 2)), (("z", 1), ("z", -1), ("z", 2)), (("yhi", 1),))
    keep[0] = vec_ref[...]
    k = 0
    for at, partners in enumerate(rounds):
        copies = []
        for axis, step in partners:
            copies.append((k, sends.start(keep.at[at], got.at[k], axis, step)))
            k += 1
        yield
        total = keep[at]
        for slot, copy in copies:
            copy.wait_recv()
            total = total + got[slot]
        keep[at + 1] = total
    out_ref[...] = keep[len(rounds)]


KEY_N, SUM_N = 9, 8


def scatter_kernel(part_ref, g_ref, own_ref, mine_ref, *scratch):
    me = here()
    greet(me, NEAR)
    sends = Sends(me, *scratch[-2:])
    together(
        key_steps(me, sends, part_ref, own_ref, *scratch[:KEY_N]),
        sum_steps(me, sends, g_ref, mine_ref, *scratch[KEY_N:-2]),
    )
    sends.finish()


def scatter_keys(part, g):
    vmem = pl.BlockSpec(memory_space=pltpu.VMEM)
    width = g.shape[1]
    return pl.pallas_call(
        scatter_kernel,
        name="scatter_keys",
        out_shape=(
            jax.ShapeDtypeStruct((T, 640), F32),
            jax.ShapeDtypeStruct((2, RUN, width // 4), BF),
        ),
        in_specs=[vmem, vmem],
        out_specs=(vmem, vmem),
        scratch_shapes=key_scratch() + sum_scratch(width) + sems(36),
        compiler_params=pltpu.CompilerParams(
            collective_id=2, has_side_effects=True, vmem_limit_bytes=VMEM_LIMIT
        ),
        cost_estimate=pl.CostEstimate(flops=0, bytes_accessed=120_000_000, transcendentals=0),
    )(part, g)


def last_kernel(mine_ref, g_ref, vec_ref, one_ref, two_ref, out_vec_ref, keep, got, own, *scratch):
    me = here()
    greet(me, NEAR + SMALL)
    sends = Sends(me, *scratch[-2:])

    def second():
        yield from sum_steps(me, sends, g_ref, own, *scratch[:-2])
        yield from spread_steps(me, sends, own, two_ref)

    together(
        vector_steps(sends, vec_ref, out_vec_ref, keep, got),
        second(),
        spread_steps(me, sends, mine_ref, one_ref),
    )
    sends.finish()


def reduce_last(mine, g, vec):
    vmem = pl.BlockSpec(memory_space=pltpu.VMEM)
    width = g.shape[1]
    return pl.pallas_call(
        last_kernel,
        name="reduce_last",
        out_shape=(
            jax.ShapeDtypeStruct((ROWS, mine.shape[2] * 4), BF),
            jax.ShapeDtypeStruct(g.shape, BF),
            jax.ShapeDtypeStruct(vec.shape, F32),
        ),
        in_specs=[vmem] * 3,
        out_specs=(vmem,) * 3,
        scratch_shapes=[
            pltpu.VMEM((6,) + vec.shape, F32),
            pltpu.VMEM((9,) + vec.shape, F32),
            pltpu.VMEM((2, RUN, width // 4), BF),
        ]
        + sum_scratch(width)
        + sems(64),
        compiler_params=pltpu.CompilerParams(
            collective_id=3, has_side_effects=True, vmem_limit_bytes=VMEM_LIMIT
        ),
        cost_estimate=pl.CostEstimate(flops=0, bytes_accessed=120_000_000, transcendentals=0),
    )(mine, g, vec)


def shard_of(me, k):
    ylo, core = me[0], me[1]
    return (ylo if k < 2 else 1 - ylo) * 2 + (core if k % 2 == 0 else 1 - core)


def our_order(me, p):
    core, ylo = me[1] == 1, me[0] == 1
    p = [jnp.where(core, p[k ^ 1], p[k]) for k in range(4)]
    return [jnp.where(ylo, p[k ^ 2], p[k]) for k in range(4)]


def cut_four(ref):
    return [ref[:, 240 * k : 240 * (k + 1)] for k in range(4)]


def norm_back_rows(z, r, gain, dy):
    dz = r * (gain * dy) - z * (r * r * r) * jnp.mean(gain * dy * z, axis=-1, keepdims=True)
    return dz, jnp.sum(dy * z * r, axis=0, keepdims=True)


def everyone_steps(sends, pieces):
    half = T // 2
    arrived, last = [], []
    for kind, source, whole, relay in pieces:
        near = source if kind == "all" else source[1]
        last.append(sends.start(near, whole.at[pl.ds(T, T)], "core", 1))
    for step, at in ((1, 0), (-1, half)):
        r = pl.ds(at, half)
        for kind, source, whole, relay in pieces:
            far = source if kind == "all" else source[2]
            arrived.append((sends.start(far.at[r], whole.at[pl.ds(2 * T + at, half)], "y", step), None))
            if kind == "all":
                arrived[-1] = (arrived[-1][0], (whole.at[pl.ds(2 * T + at, half)], whole.at[pl.ds(3 * T + at, half)]))
            else:
                copy = sends.start(source[3].at[r], relay.at[r], "y", step)
                arrived.append((copy, (relay.at[r], whole.at[pl.ds(3 * T + at, half)])))
    yield
    for copy, onward in arrived:
        copy.wait_recv()
        if onward is not None:
            last.append(sends.start(onward[0], onward[1], "core", 1))
    yield
    for copy in last:
        copy.wait_recv()


def dense_kernel(
    mix_ref, q_ref, prob_ref, kv_ref, h_ref, up_ref, vec_ref,
    wo_ref, wg_ref, wu_ref, wd_ref, wos_ref, wgs_ref, wus_ref, wds_ref,
    dq_ref, dkv_ref, g_ref, d_attn_ref, mixture_ref, d_mid_ref, out_ref, logit_ref, vec_out_ref,
    wo, wg, wu, wd, mixf, gate_s, up_s, inner, dgu, dffn, xs, do_s, d_mix_s,
    dgu_all, dffn_all, xs_all, inner_all, xs_relay, inner_relay,
    load_sems, send_sems, recv_sems,
):
    me = here()
    loads = []
    for k, (own, rest, to) in enumerate(
        ((wo_ref, wos_ref, wo), (wg_ref, wgs_ref, wg), (wu_ref, wus_ref, wu), (wd_ref, wds_ref, wd))
    ):
        pair = (
            pltpu.make_async_copy(own, to.at[0], load_sems.at[2 * k]),
            pltpu.make_async_copy(rest, to.at[pl.ds(1, 3)], load_sems.at[2 * k + 1]),
        )
        for copy in pair:
            copy.start()
        loads.append(pair)
    greet(me, WEIGHT)
    sends = Sends(me, send_sems, recv_sems)
    shards = [shard_of(me, k) for k in range(4)]

    def run640(k):
        return pl.ds(pl.multiple_of(shards[k] * 640, 128), 640)

    def run640_up(k):
        return pl.ds(pl.multiple_of(FF + shards[k] * 640, 128), 640)

    def loaded(k):
        for copy in loads[k]:
            copy.wait()

    for j in range(KV_HEADS):
        for g in range(GROUPS):
            h = GROUPS * j + g
            mixf[:, HEAD_DIM * h : HEAD_DIM * (h + 1)] = mix_ref[j, g * T : (g + 1) * T, HEAD_DIM:]
    mixture_ref[...] = mixf[...].astype(BF)
    mix_k = our_order(me, cut_four(mixture_ref))
    loaded(0)
    attn_out = sum(dot(mix_k[k], wo[k]) for k in range(4))
    hidden = h_ref[...]
    gain_f = vec_ref[1:2, :D]
    route_w = vec_ref[2:3, :D]
    middle = hidden + attn_out
    r2 = lax.rsqrt(jnp.mean(middle * middle, axis=-1, keepdims=True) + EPS)
    x2 = middle * r2 * gain_f
    x2_k = our_order(me, [x2[:, 240 * k : 240 * (k + 1)].astype(BF) for k in range(4)])
    xs[...] = jnp.zeros_like(xs)
    for k in range(4):
        xs[k, :, :240] = x2_k[k]
    loaded(1)
    gate_s[...] = sum(dot(x2_k[k], wg[k]) for k in range(4))
    loaded(2)
    up_s[...] = sum(dot(x2_k[k], wu[k]) for k in range(4))
    gate = gate_s[...]
    inner[...] = (gate * jax.nn.sigmoid(gate) * up_s[...]).astype(BF)
    loaded(3)
    ffn_out = sum(dot(inner[:, run640(k)], wd[k]) for k in range(4))
    route = jax.nn.sigmoid(jnp.sum(hidden * route_w, axis=-1, keepdims=True))
    branch = attn_out + ffn_out
    out_ref[...] = (route * branch).astype(BF)
    upstream = up_ref[...]
    d_branch = upstream * route
    d_logit = route * (1.0 - route) * jnp.sum(upstream * branch, axis=-1, keepdims=True)
    logit_ref[...] = jnp.broadcast_to(d_logit, logit_ref.shape)
    vec_out_ref[...] = jnp.zeros_like(vec_out_ref)
    vec_out_ref[2:3, :D] = jnp.sum(d_logit * hidden, axis=0, keepdims=True)
    d_ffn = d_branch.astype(BF)
    dffn[...] = jnp.zeros_like(dffn)
    for k in range(4):
        dffn[:, 256 * k : 256 * k + 240] = d_branch[:, 240 * k : 240 * (k + 1)].astype(BF)
    for k in range(4):
        d_inner = dot(d_ffn, wd[k], NT)
        gate, up = gate_s[:, run640(k)], up_s[:, run640(k)]
        sg = jax.nn.sigmoid(gate)
        dgu[:, run640(k)] = (d_inner * up * (sg + gate * sg * (1.0 - sg))).astype(BF)
        dgu[:, run640_up(k)] = (d_inner * (gate * sg)).astype(BF)
    pieces = (
        ("all", dgu, dgu_all, None),
        ("all", dffn, dffn_all, None),
        ("one", [xs.at[k] for k in range(4)], xs_all, xs_relay),
        ("one", [inner.at[:, run640(k)] for k in range(4)], inner_all, inner_relay),
    )
    share = everyone_steps(sends, pieces)
    next(share)
    own = pl.ds(0, T)
    dgu_all[own], dffn_all[own] = dgu[...], dffn[...]
    xs_all[own], inner_all[own] = xs[0], inner[:, run640(0)]
    d_gate, d_up = dgu[:, :FF], dgu[:, FF:]
    d_x2 = jnp.concatenate(
        our_order(me, [dot(d_gate, wg[k], NT) + dot(d_up, wu[k], NT) for k in range(4)]), axis=1
    )
    d_mid, g_gain_f = norm_back_rows(middle, r2, gain_f, d_x2)
    d_mid_ref[...] = d_mid
    vec_out_ref[1:2, :D] = g_gain_f
    d_attn = (d_branch + d_mid).astype(BF)
    d_attn_ref[...] = d_attn
    d_mix_s[...] = jnp.concatenate(our_order(me, [dot(d_attn, wo[k], NT) for k in range(4)]), axis=1)
    do_s[...] = jnp.zeros_like(do_s)
    for j in range(KV_HEADS):
        for g in range(GROUPS):
            h = GROUPS * j + g
            do_s[j, g * T : (g + 1) * T, HEAD_DIM:] = d_mix_s[:, HEAD_DIM * h : HEAD_DIM * (h + 1)].astype(BF)

    @pl.loop(0, KV_HEADS)
    def _(j):
        c = pl.ds(pl.multiple_of(j * 128, 128), 128)
        tile = kv_ref[:, :, :, :, c].reshape(KEYS, 128)
        prob, d_out = prob_ref[j], do_s[j]
        d_prob = dot(d_out, tile, NT)
        delta = jnp.sum(d_out.astype(F32) * mix_ref[j], axis=-1, keepdims=True)
        d_score = (prob.astype(F32) * (d_prob - delta)).astype(BF)
        dq_ref[j] = dot(d_score, tile) * SCALE
        grad = dot(d_score, q_ref[j], TN) * SCALE + dot(prob, d_out, TN)
        dkv_ref[:, :, :, :, c] = grad.astype(BF).reshape(2, 4, 4, T, 128)

    together(share)
    for c in range(0, 2 * FF, 1280):
        g_ref[:, c : c + 1280] = dot(xs_all[...], dgu_all[:, c : c + 1280], TN).astype(BF)
    for k in range(4):
        g_ref[:, 2 * FF + 640 * k : 2 * FF + 640 * (k + 1)] = dot(
            dffn_all[:, 256 * k : 256 * (k + 1)], inner_all[...], TN
        ).astype(BF)
    sends.finish()


def dense(mix, q, prob, kv, h, up_c, vec, own, rest):
    vmem, hbm = pl.BlockSpec(memory_space=pltpu.VMEM), pl.BlockSpec(memory_space=pl.ANY)
    rows = GROUPS * T
    return pl.pallas_call(
        dense_kernel,
        name="dense",
        out_shape=(
            jax.ShapeDtypeStruct((KV_HEADS, rows, 128), F32),
            jax.ShapeDtypeStruct((2, 4, 4, T, 640), BF),
            jax.ShapeDtypeStruct((ROWS, 3 * FF), BF),
            jax.ShapeDtypeStruct((T, D), BF),
            jax.ShapeDtypeStruct((T, D), BF),
            jax.ShapeDtypeStruct((T, D), F32),
            jax.ShapeDtypeStruct((T, D), BF),
            jax.ShapeDtypeStruct((T, 128), F32),
            jax.ShapeDtypeStruct((8, 1024), F32),
        ),
        in_specs=[vmem] * 7 + [hbm] * 8,
        out_specs=(vmem,) * 9,
        scratch_shapes=[
            pltpu.VMEM((4, 240, D), BF),
            pltpu.VMEM((4, 240, FF), BF),
            pltpu.VMEM((4, 240, FF), BF),
            pltpu.VMEM((4, 640, D), BF),
            pltpu.VMEM((T, D), F32),
            pltpu.VMEM((T, FF), F32),
            pltpu.VMEM((T, FF), F32),
            pltpu.VMEM((T, FF), BF),
            pltpu.VMEM((T, 2 * FF), BF),
            pltpu.VMEM((T, 1024), BF),
            pltpu.VMEM((4, T, 256), BF),
            pltpu.VMEM((KV_HEADS, rows, 128), BF),
            pltpu.VMEM((T, D), F32),
            pltpu.VMEM((4 * T, 2 * FF), BF),
            pltpu.VMEM((4 * T, 1024), BF),
            pltpu.VMEM((4 * T, 256), BF),
            pltpu.VMEM((4 * T, 640), BF),
            pltpu.VMEM((T, 256), BF),
            pltpu.VMEM((T, 640), BF),
            pltpu.SemaphoreType.DMA((8,)),
        ]
        + sems(28),
        compiler_params=pltpu.CompilerParams(
            collective_id=4, has_side_effects=True, vmem_limit_bytes=VMEM_LIMIT
        ),
        cost_estimate=pl.CostEstimate(
            flops=20_000_000_000, bytes_accessed=40_000_000, transcendentals=0
        ),
    )(mix, q, prob, kv, h, up_c, vec, *own, *rest)


def by_shard(x, width):
    core, ylo = lax.axis_index("core") == 1, lax.axis_index("ylo") == 1
    p = [x[..., k * width : (k + 1) * width] for k in range(4)]
    return ordered(p)


def ordered(p):
    core, ylo = lax.axis_index("core") == 1, lax.axis_index("ylo") == 1
    p = [jnp.where(core, p[k ^ 1], p[k]) for k in range(4)]
    return [jnp.where(ylo, p[k ^ 2], p[k]) for k in range(4)]


def rotate(values, cosine, sine):
    a, b = values[..., : HEAD_DIM // 2], values[..., HEAD_DIM // 2 :]
    return jnp.concatenate([a * cosine - b * sine, b * cosine + a * sine], axis=-1)


def norm_back(z, r, gain, dy):
    dz = r * (gain * dy) - z * (r * r * r) * jnp.mean(gain * dy * z, axis=-1, keepdims=True)
    return dz, jnp.sum(dy * z * r, axis=0)


def everyone(rows, slices):
    half = T // 2
    far = jnp.concatenate([rows, slices[2], slices[3]], axis=1)
    near = permute(jnp.concatenate([rows, slices[1]], axis=1), dcore=1)
    got = jnp.concatenate([permute(far[:half], dy=1), permute(far[half:], dy=-1)], axis=0)
    n, m = rows.shape[1], slices[0].shape[1]
    relay = permute(jnp.concatenate([got[:, :n], got[:, n + m :]], axis=1), dcore=1)
    every = jnp.concatenate([rows, near[:, :n], got[:, :n], relay[:, :n]], axis=0)
    some = jnp.concatenate([slices[0], near[:, n:], got[:, n : n + m], relay[:, n:]], axis=0)
    return every, some


def padded(a):
    return jnp.pad(a, ((0, 0), (0, ROWS - a.shape[1])))


def per_device(hidden, chosen, positions, w_query, w_key, w_value, w_output, w_gate, w_up, w_down, gain_attn, gain_ffn, router, d_out):
    tokens, upstream = hidden[0], d_out[0]
    odd = lax.rem(lax.axis_index("x"), 2) == 1
    own_w = (w_output, w_gate, w_up, w_down)
    frequency = THETA ** (-jnp.arange(0, HEAD_DIM // 2).astype(F32) * 2.0 / HEAD_DIM)
    vec = jnp.stack([gain_attn, gain_ffn, router]).astype(F32)
    vec = jnp.pad(vec, ((0, 5), (0, 16)))
    (
        mix_heads, prob, q_heads, kv_all, h, up_c, x1, cosine, sine, place, vec_in, wq, wk, wv, *rest_w
    ) = front(
        tokens, upstream, chosen, positions, jnp.tile(frequency, 4)[None, :], vec,
        w_query, w_key, w_value, *own_w
    )
    gain_a, route_w = vec_in[0, :D], vec_in[2, :D]
    r1 = lax.rsqrt(jnp.mean(h * h, axis=-1, keepdims=True) + EPS)
    x1_s = by_shard(x1, 240)
    cosine, sine = cosine[:, None, : HEAD_DIM // 2], -sine[:, None, : HEAD_DIM // 2]

    def tokens_first(a):
        return a.reshape(KV_HEADS, GROUPS, T, HEAD_DIM).transpose(2, 0, 1, 3).reshape(T, D)

    d_q_heads, d_kv, g_one, d_attn, mixture, d_mid, out_c, d_logit, vec_out = dense(
        mix_heads, q_heads, prob, kv_all, h, up_c, vec_in, own_w, rest_w
    )
    d_logit = d_logit[:, :1]
    mix_s = by_shard(mixture, 240)
    d_own, mine_one = scatter_keys(d_kv, g_one)
    d_own = d_own.reshape(T, KV_HEADS, 2 * HEAD_DIM)
    d_q = rotate(tokens_first(d_q_heads[..., :HEAD_DIM]).reshape(T, HEADS, HEAD_DIM), cosine, -sine)
    d_q = d_q.reshape(T, D).astype(BF)
    d_k = rotate(d_own[..., :HEAD_DIM], cosine, -sine).reshape(T, 320).astype(BF)
    d_v = d_own[..., HEAD_DIM:].reshape(T, 320).astype(BF)
    d_kv_low = jnp.concatenate([d_k, d_v], axis=1)
    d_x1 = jnp.concatenate(
        ordered([dot(d_q, wq[k], NT) + dot(d_k, wk[k], NT) + dot(d_v, wv[k], NT) for k in range(4)]), axis=1
    )
    d_first, g_gain_a = norm_back(h, r1, gain_a, d_x1)
    d_h = d_mid + d_first + d_logit * route_w[None, :]

    back = jnp.concatenate([out_c, d_h.astype(BF)], axis=1)
    other = swap_x(back)
    both = jnp.concatenate([jnp.where(odd, other, back), jnp.where(odd, back, other)], axis=0)
    spread = dot(place, both, TN)
    output = tokens + spread[:, :D]
    d_tokens = upstream + spread[:, D:]

    rows_2, some_2 = everyone(
        jnp.concatenate([d_q, d_kv_low, d_attn], axis=1),
        [jnp.concatenate([x1_s[k], mix_s[k]], axis=1) for k in range(4)],
    )
    g_two = jnp.concatenate(
        [
            dot(padded(some_2[:, :240]), rows_2[:, :1600], TN).astype(BF),
            dot(padded(some_2[:, 240:]), rows_2[:, 1600:], TN).astype(BF),
        ],
        axis=1,
    )
    vector = vec_out.at[0, :D].set(g_gain_a)
    s_one, s_two, vector = reduce_last(mine_one, g_two, vector)
    shard = lax.axis_index("ylo") * 2 + lax.axis_index("core")
    vector = lax.dynamic_slice_in_dim(vector, shard * 240, 240, axis=1)
    s_one, s_two = s_one[:240], s_two[:240]
    g_down = s_one[:, 2 * FF :].reshape(240, 4, 640).transpose(2, 1, 0).reshape(640, D)
    return (
        output[None],
        d_tokens[None],
        s_two[:, :960].astype(F32),
        s_two[:, 960:1280].astype(F32),
        s_two[:, 1280:1600].astype(F32),
        s_two[:, 1600:].astype(F32),
        s_one[:, :FF].astype(F32),
        s_one[:, FF : 2 * FF].astype(F32),
        g_down.astype(F32),
        vector[0],
        vector[1],
        vector[2],
    )


def solution(mesh):
    finer = Mesh(mesh.devices.reshape(DIMS), AX)
    shard, blk = ("ylo", "core"), ("yhi", "z", "x")
    act, row, weight, vec = P(shard, blk, None), P(shard, blk), P(shard, None), P(shard)
    return jax.shard_map(
        per_device,
        mesh=finer,
        in_specs=(act, row, row) + (weight,) * 7 + (vec,) * 3 + (act,),
        out_specs=(act, act) + (weight,) * 7 + (vec,) * 3,
        check_vma=False,
    )
```

```python
import functools

import jax
import jax.numpy as jnp
from jax import lax
from jax.experimental import pallas as pl
from jax.experimental.pallas import tpu as pltpu
from jax.sharding import Mesh
from jax.sharding import PartitionSpec as P

D = 960
HEADS = 15
KV_HEADS = 5
GROUPS = 3
HEAD_DIM = 64
FF = 2560
EPS = 1e-05
THETA = 10000.0
SCALE = HEAD_DIM ** (-0.5)
T = 64
PAIR = 128
SLOTS = 32
KEYS = SLOTS * T
AX = ("ylo", "core", "yhi", "z", "x")
DIMS = (2, 2, 2, 4, 4)
MESH = pl.DeviceIdType.MESH
BF = jnp.bfloat16
F32 = jnp.float32
VMEM_LIMIT = 56 * 2**20


def dot(a, b, dims=(((1,), (0,)), ((), ()))):
    return lax.dot_general(a, b, dims, preferred_element_type=F32)


NT = (((1,), (1,)), ((), ()))
TN = (((0,), (0,)), ((), ()))


def here():
    return tuple(lax.axis_index(a) for a in AX)


def neighbour(me, axis, step):
    ylo, core, yhi, z, x = me
    if axis == "z":
        z = lax.rem(z + step + 4, 4)
    elif axis == "x":
        x = lax.rem(x + step + 4, 4)
    elif axis == "pair":
        x = x + 1 - 2 * lax.rem(x, 2)
    elif axis == "yhi":
        yhi = 1 - yhi
    elif axis == "ylo":
        ylo = 1 - ylo
    elif axis == "core":
        core = 1 - core
    else:
        y = lax.rem(yhi * 2 + ylo + step + 4, 4)
        ylo, yhi = lax.rem(y, 2), y // 2
    return (ylo, core, yhi, z, x)


NEAR = (("x", 1), ("x", -1), ("z", 1), ("z", -1), ("yhi", 1))
WEIGHT = (("y", 1), ("y", -1), ("core", 1))
SMALL = (("core", 1), ("ylo", 1), ("x", 2), ("z", 2))


def greet(me, partners):
    barrier = pltpu.get_barrier_semaphore()
    for axis, step in partners:
        pl.semaphore_signal(
            barrier, inc=1, device_id=neighbour(me, axis, step), device_id_type=MESH
        )
    pl.semaphore_wait(barrier, len(partners))


class Sends:
    def __init__(self, me, send_sems, recv_sems):
        self.me, self.send_sems, self.recv_sems, self.all = me, send_sems, recv_sems, []

    def start(self, src, dst, axis, step):
        k = len(self.all)
        copy = pltpu.make_async_remote_copy(
            src_ref=src,
            dst_ref=dst,
            send_sem=self.send_sems.at[k],
            recv_sem=self.recv_sems.at[k],
            device_id=neighbour(self.me, axis, step),
            device_id_type=MESH,
        )
        copy.start()
        self.all.append(copy)
        return copy

    def finish(self):
        for copy in self.all:
            copy.wait_send()


def together(*steps):
    steps = list(steps)
    while steps:
        for step in list(steps):
            try:
                next(step)
            except StopIteration:
                steps.remove(step)


def sems(count):
    return [pltpu.SemaphoreType.DMA((count,)), pltpu.SemaphoreType.DMA((count,))]


def plus(*terms):
    total = terms[0].astype(F32)
    for term in terms[1:]:
        total = total + term.astype(F32)
    return total


class Shards:
    def __init__(self, sends):
        self.sends, self.arrived, self.last = sends, [], []
        self.color = lax.rem(sends.me[3] + sends.me[4], 2)

    def near(self, own, out):
        self.last.append(self.sends.start(own, out.at[out.shape[0] - 3], "core", 1))

    def far(self, own, out, cut):
        for step, row, rows in ((1, 0, cut), (-1, cut, own.shape[0] - cut)):
            r = pl.ds(row, rows)
            ref = out.at[out.shape[0] - 2, r]
            self.arrived.append((ref, out.at[out.shape[0] - 1, r], self.sends.start(own.at[r], ref, "y", step)))

    def relay(self):
        for ref, to, copy in self.arrived:
            copy.wait_recv()
            self.last.append(self.sends.start(ref, to, "core", 1))
        self.arrived = []

    def finish(self):
        self.relay()
        for copy in self.last:
            copy.wait_recv()
        self.last = []

    def half(self, own, out, block, cuts):
        rows, slots = own.shape[0], out.shape[0]
        sub = block // 2
        mine = self.color * (rows - block)

        def part(slot, start, count):
            return out.at[slot, pl.ds(pl.multiple_of(start, 16), count)]

        copies = []
        for step, off in ((1, 0), (-1, sub)):
            src = own.at[pl.ds(pl.multiple_of(mine + off, 16), sub)]
            copies.append(self.sends.start(src, part(slots - 2, mine + off, sub), "y", step))
        yield
        for copy in copies:
            copy.wait_recv()
        copies, off = [], 0
        for (axis, step), count in zip((("x", 1), ("x", -1), ("z", 1), ("z", -1)), cuts):
            ref = part(slots - 2, self.color * block + off, count)
            copies.append(self.sends.start(ref, ref, axis, step))
            off += count
        self.last.append(self.sends.start(part(slots - 2, mine, block), part(slots - 1, mine, block), "core", 1))
        yield
        for copy in copies:
            copy.wait_recv()
        rest = (1 - self.color) * block
        self.last.append(
            self.sends.start(part(slots - 2, rest, rows - block), part(slots - 1, rest, rows - block), "core", 1)
        )


def gather_steps(me, sends, kv_ref, out_ref):
    _, _, yh, z, x = me
    oy = 1 - yh
    half, quarter = T // 2, T // 4
    streams = (("x", "z", 0), ("z", "x", half))

    def slot(y, axis, step, rows, count):
        zz = lax.rem(z + step + 4, 4) if axis == "z" else z
        xx = lax.rem(x + step + 4, 4) if axis == "x" else x
        return out_ref.at[y, zz, xx, pl.ds(rows, count)]

    def line(y, axis, step, rows, count):
        if axis == "z":
            return out_ref.at[y, lax.rem(z + step + 4, 4), :, pl.ds(rows, count)]
        return out_ref.at[y, :, lax.rem(x + step + 4, 4), pl.ds(rows, count)]

    own = out_ref.at[yh, z, x]
    own[...] = kv_ref[...]
    first = sends.start(kv_ref, own, "yhi", 1)
    got = {}
    for y, tag in ((yh, 0), (oy, 1)):
        if tag:
            yield
            first.wait_recv()
        for axis, _, row in streams:
            src = slot(y, axis, 0, row, half)
            for step in (1, -1):
                got[tag, row, step] = sends.start(src, src, axis, step)
    far = {}
    for y, tag in ((yh, 0), (oy, 1)):
        yield
        for axis, _, row in streams:
            for step, off in ((1, 0), (-1, quarter)):
                got[tag, row, step].wait_recv()
                src = slot(y, axis, -step, row + off, quarter)
                far[tag, row, step] = sends.start(src, src, axis, step)
    wide = {}
    for y, tag in ((yh, 0), (oy, 1)):
        yield
        for _, axis, row in streams:
            for step in (1, -1):
                far[tag, row, step].wait_recv()
            src = line(y, axis, 0, row, half)
            for step in (1, -1):
                wide[tag, row, step] = sends.start(src, src, axis, step)
    last = []
    for y, tag in ((yh, 0), (oy, 1)):
        yield
        for _, axis, row in streams:
            for step, off in ((1, 0), (-1, quarter)):
                wide[tag, row, step].wait_recv()
                src = line(y, axis, -step, row + off, quarter)
                last.append(sends.start(src, src, axis, step))
    yield
    for copy in last:
        copy.wait_recv()


def swapped(x):
    lane = lax.broadcasted_iota(jnp.int32, x.shape, 1)
    return jnp.where(lane < HEAD_DIM // 2, pltpu.roll(x, 96, 1), pltpu.roll(x, 32, 1))


def front_kernel(
    hidden_ref, d_out_ref, chosen_ref, pos_ref, freq_ref, vec_ref, wq_ref, wk_ref, wv_ref,
    wo_ref, wg_ref, wu_ref, wd_ref,
    mix_ref, prob_ref, q_ref, kv_ref, h_ref, up_ref, x1_ref, cos_ref, sin_ref, place_ref, vec_out_ref,
    wq, wk, wv, wos_ref, wgs_ref, wus_ref, wds_ref,
    compact_h, compact_d, compact_p, got_h, got_d, got_p, vecs, q_pre, kv_own,
    load_sems, send_sems, recv_sems,
):
    me = here()
    yhi, z, x = me[2:]
    loads = []
    for k, (own, to) in enumerate(((wq_ref, wq), (wk_ref, wk), (wv_ref, wv))):
        loads.append(pltpu.make_async_copy(own, to.at[0], load_sems.at[k]))
        loads[-1].start()
    greet(me, NEAR + WEIGHT + (("pair", 1),))
    sends = Sends(me, send_sems, recv_sems)
    early, query, late = Shards(sends), Shards(sends), Shards(sends)
    vec_far = sends.start(vec_ref, vecs.at[2], "y", 1)
    early.far(wk_ref, wk, 160)
    early.far(wv_ref, wv, 160)
    vec_near = sends.start(vec_ref, vecs.at[1], "core", 1)
    early.near(wk_ref, wk)
    early.near(wv_ref, wv)
    query.far(wq_ref, wq, 128)
    query.near(wq_ref, wq)
    vecs[0] = vec_ref[...]

    odd = lax.rem(x, 2)
    flag = jnp.where(chosen_ref[...] > 0, 1.0, 0.0)
    token = lax.broadcasted_iota(jnp.int32, (PAIR, PAIR), 0)
    lane = lax.broadcasted_iota(jnp.int32, (PAIR, PAIR), 1)
    upto = jnp.where(token <= lane, 1.0, 0.0).astype(BF)
    count = dot(jnp.broadcast_to(flag, (16, PAIR)).astype(BF), upto)[0:1]
    total = jnp.sum(flag, axis=1, keepdims=True)
    rank = count - 1.0 + jnp.where(odd == 1, PAIR - total, 0.0)
    place = jnp.where(token.astype(F32) == rank, flag, 0.0)
    place_low = place.astype(BF)
    place_ref[...] = place_low
    compact_p[...] = jnp.broadcast_to(
        jnp.sum(place * pos_ref[...].astype(F32), axis=1, keepdims=True), (PAIR, PAIR)
    )
    compact_h[...] = dot(place_low, hidden_ref[...].astype(BF), NT).astype(BF)
    compact_d[...] = dot(place_low, d_out_ref[...].astype(BF), NT).astype(BF)
    give = pl.ds(pl.multiple_of((1 - odd) * T, T), T)
    keep = pl.ds(pl.multiple_of(odd * T, T), T)
    swaps = [
        sends.start(c.at[give], g, "pair", 1)
        for c, g in ((compact_h, got_h), (compact_p, got_p), (compact_d, got_d))
    ]
    vec_far.wait_recv()
    vec_last = sends.start(vecs.at[2], vecs.at[3], "core", 1)
    swaps[0].wait_recv()
    h = plus(compact_h[keep], got_h[...])
    h_ref[...] = h
    swaps[1].wait_recv()
    angle = (compact_p[keep] + got_p[...]) * freq_ref[...]
    turn = lax.broadcasted_iota(jnp.int32, (T, PAIR), 1)
    cosine = jnp.where(turn < HEAD_DIM, jnp.cos(angle), 1.0)
    sine = jnp.sin(angle)
    sine = jnp.where(turn < HEAD_DIM // 2, -sine, jnp.where(turn < HEAD_DIM, sine, 0.0))
    cos_ref[...], sin_ref[...] = cosine, sine
    vec_near.wait_recv()
    vec_last.wait_recv()
    vec_out_ref[...] = jnp.zeros_like(vec_out_ref)
    for k, v in enumerate(our_order(me, [vecs[k, :, :240] for k in range(4)])):
        vec_out_ref[:, 240 * k : 240 * (k + 1)] = v
    r1 = lax.rsqrt(jnp.mean(h * h, axis=-1, keepdims=True) + EPS)
    x1_ref[...] = (h * r1 * vec_out_ref[0:1, :D]).astype(BF)
    x1_k = our_order(me, cut_four(x1_ref))
    for copy in loads:
        copy.wait()
    early.finish()
    k_pre = sum(dot(x1_k[k], wk[k], NT) for k in range(4))
    v_pre = sum(dot(x1_k[k], wv[k], NT) for k in range(4))
    for j in range(KV_HEADS):
        run = slice(HEAD_DIM * j, HEAD_DIM * (j + 1))
        tile = jnp.concatenate([k_pre[:, run], v_pre[:, run]], axis=1)
        kv_own[:, 128 * j : 128 * (j + 1)] = (tile * cosine + swapped(tile) * sine).astype(BF)
    gather = gather_steps(me, sends, kv_own, kv_ref)
    next(gather)
    query.finish()
    swaps[2].wait_recv()
    up_ref[...] = plus(compact_d[keep], got_d[...])
    q_pre[...] = sum(dot(x1_k[k], wq[k]) for k in range(4))
    zero = jnp.zeros((T, HEAD_DIM), F32)
    for j in range(KV_HEADS):
        for g in range(GROUPS):
            at = HEAD_DIM * (GROUPS * j + g)
            tile = jnp.concatenate([q_pre[:, at : at + HEAD_DIM], zero], axis=1)
            q_ref[j, g * T : (g + 1) * T] = (tile * cosine + swapped(tile) * sine).astype(BF)
    next(gather)
    small, large = (128, (32, 32, 32, 16)), (480, (128, 128, 112, 112))
    out_w = late.half(wo_ref, wos_ref, *small)
    gate_w = late.half(wg_ref, wgs_ref, *small)
    up_w = late.half(wu_ref, wus_ref, *small)
    down_w = late.half(wd_ref, wds_ref, *large)
    for w in (out_w, gate_w, up_w, down_w):
        next(w)
    for own, out in ((wo_ref, wos_ref), (wg_ref, wgs_ref), (wu_ref, wus_ref), (wd_ref, wds_ref)):
        late.near(own, out)
    next(gather)
    next(gather)
    next(out_w)
    next(gather)
    next(gather)
    next(gate_w)
    together(gather)
    next(up_w)
    together(out_w)
    together(gate_w)
    limit = ((yhi * 16 + z * 4 + x) // 2 + 1) * PAIR

    @pl.loop(0, KV_HEADS)
    def _(j):
        c = pl.ds(pl.multiple_of(j * 128, 128), 128)
        tile = kv_ref[:, :, :, :, c].reshape(KEYS, 128)
        scores = dot(q_ref[j], tile, NT) * SCALE
        column = lax.broadcasted_iota(jnp.int32, scores.shape, 1)
        scores = jnp.where(column < limit, scores, -1e30)
        exponent = jnp.exp(scores - jnp.max(scores, axis=-1, keepdims=True))
        prob = (exponent * (1.0 / jnp.sum(exponent, axis=-1, keepdims=True))).astype(BF)
        prob_ref[j] = prob
        mix_ref[j] = dot(prob, tile)

    next(down_w)
    together(up_w)
    together(down_w)
    late.finish()
    sends.finish()


def front(hidden, d_out, chosen, pos, freq, vec, w_query, w_key, w_value, *later):
    vmem, hbm = pl.BlockSpec(memory_space=pltpu.VMEM), pl.BlockSpec(memory_space=pl.ANY)
    rows = GROUPS * T
    return pl.pallas_call(
        front_kernel,
        name="front",
        out_shape=(
            jax.ShapeDtypeStruct((KV_HEADS, rows, 128), F32),
            jax.ShapeDtypeStruct((KV_HEADS, rows, KEYS), BF),
            jax.ShapeDtypeStruct((KV_HEADS, rows, 128), BF),
            jax.ShapeDtypeStruct((2, 4, 4, T, 640), BF),
            jax.ShapeDtypeStruct((T, D), F32),
            jax.ShapeDtypeStruct((T, D), F32),
            jax.ShapeDtypeStruct((T, D), BF),
            jax.ShapeDtypeStruct((T, 128), F32),
            jax.ShapeDtypeStruct((T, 128), F32),
            jax.ShapeDtypeStruct((PAIR, PAIR), BF),
            jax.ShapeDtypeStruct((8, 1024), F32),
            jax.ShapeDtypeStruct((4, 240, 960), BF),
            jax.ShapeDtypeStruct((4, 320, 240), BF),
            jax.ShapeDtypeStruct((4, 320, 240), BF),
        )
        + tuple(jax.ShapeDtypeStruct((3,) + w.shape, BF) for w in later),
        in_specs=[vmem] * 6 + [hbm] * 7,
        out_specs=(vmem,) * 14 + (hbm,) * 4,
        scratch_shapes=[
            pltpu.VMEM((PAIR, D), BF),
            pltpu.VMEM((PAIR, D), BF),
            pltpu.VMEM((PAIR, PAIR), F32),
            pltpu.VMEM((T, D), BF),
            pltpu.VMEM((T, D), BF),
            pltpu.VMEM((T, PAIR), F32),
            pltpu.VMEM((4, 8, 256), F32),
            pltpu.VMEM((T, D), F32),
            pltpu.VMEM((T, 640), BF),
            pltpu.SemaphoreType.DMA((3,)),
        ]
        + sems(90),
        compiler_params=pltpu.CompilerParams(
            collective_id=1, has_side_effects=True, vmem_limit_bytes=VMEM_LIMIT
        ),
        cost_estimate=pl.CostEstimate(flops=5_000_000_000, bytes_accessed=90_000_000, transcendentals=0),
    )(hidden, d_out, chosen, pos, freq, vec, w_query, w_key, w_value, *later)


def key_steps(me, sends, part_ref, out_ref, low, out_b, full, sums, nlow, nout, nfull, mine, y_in):
    _, _, yh, z, x = me
    half, quarter = T // 2, T // 4
    streams = (("x", "z", 0), ("z", "x", half))

    def line(axis, step, row, count):
        if axis == "z":
            return part_ref.at[:, lax.rem(z + step + 4, 4), :, pl.ds(row, count)]
        return part_ref.at[:, :, lax.rem(x + step + 4, 4), pl.ds(row, count)]

    near = {}
    for s, (axis, _, row) in enumerate(streams):
        near[s, 1] = sends.start(line(axis, 2, row, quarter), low.at[s, 0], axis, 1)
        near[s, -1] = sends.start(line(axis, 2, row + quarter, quarter), low.at[s, 1], axis, -1)
    whole = {}
    yield
    for s, (axis, _, row) in enumerate(streams):
        for d, step in enumerate((1, -1)):
            near[s, step].wait_recv()
            lo, hi = (0, quarter) if step == 1 else (quarter, 0)
            out_b[s, d, :, :, pl.ds(lo, quarter)] = plus(
                line(axis, step, row + lo, quarter)[...], low[s, d]
            ).astype(BF)
            out_b[s, d, :, :, pl.ds(hi, quarter)] = line(axis, step, row + hi, quarter)[...]
            whole[s, step] = sends.start(out_b.at[s, d], full.at[s, d], axis, step)
    yield
    near = {}
    for s, (axis, other, row) in enumerate(streams):
        for step in (1, -1):
            whole[s, step].wait_recv()
        sums[s] = plus(line(axis, 0, row, half)[...], full[s, 0], full[s, 1]).astype(BF)
        far = lax.rem((z if other == "z" else x) + 2, 4)
        near[s, 1] = sends.start(sums.at[s, :, far, pl.ds(0, quarter)], nlow.at[s, 0], other, 1)
        near[s, -1] = sends.start(
            sums.at[s, :, far, pl.ds(quarter, quarter)], nlow.at[s, 1], other, -1
        )
    yield
    for s, (axis, other, row) in enumerate(streams):
        at = z if other == "z" else x
        for d, step in enumerate((1, -1)):
            near[s, step].wait_recv()
            to = lax.rem(at + step + 4, 4)
            lo, hi = (0, quarter) if step == 1 else (quarter, 0)
            nout[s, d, :, pl.ds(lo, quarter)] = plus(
                sums[s, :, to, pl.ds(lo, quarter)], nlow[s, d]
            ).astype(BF)
            nout[s, d, :, pl.ds(hi, quarter)] = sums[s, :, to, pl.ds(hi, quarter)]
            whole[s, step] = sends.start(nout.at[s, d], nfull.at[s, d], other, step)
    yield
    swap = {}
    for s, (axis, other, row) in enumerate(streams):
        at = z if other == "z" else x
        for step in (1, -1):
            whole[s, step].wait_recv()
        mine[s] = plus(sums[s, :, at], nfull[s, 0], nfull[s, 1]).astype(BF)
        swap[s] = sends.start(mine.at[s, 1 - yh], y_in.at[s], "yhi", 1)
    yield
    for s, (axis, other, row) in enumerate(streams):
        swap[s].wait_recv()
        out_ref[pl.ds(row, half)] = plus(mine[s, yh], y_in[s])


def key_scratch():
    half, quarter, w = T // 2, T // 4, 640
    return [
        pltpu.VMEM((2, 2, 2, 4, quarter, w), BF),
        pltpu.VMEM((2, 2, 2, 4, half, w), BF),
        pltpu.VMEM((2, 2, 2, 4, half, w), BF),
        pltpu.VMEM((2, 2, 4, half, w), BF),
        pltpu.VMEM((2, 2, 2, quarter, w), BF),
        pltpu.VMEM((2, 2, 2, half, w), BF),
        pltpu.VMEM((2, 2, 2, half, w), BF),
        pltpu.VMEM((2, 2, half, w), BF),
        pltpu.VMEM((2, half, w), BF),
    ]


ROWS = 256
HALF = ROWS // 2
STREAMS = (("x", "z", 0), ("z", "x", HALF))
RUN = HALF // 4
CUT = HALF // 2


def spots(me):
    return {"z": me[3], "x": me[4]}


def around(me, axis, step):
    return lax.rem(spots(me)[axis] + step + 4, 4)


def columns(me, axis, step, big):
    return pl.ds(pl.multiple_of(around(me, axis, step) * big, 128), big)


def sum_steps(me, sends, g_ref, mine, low, out_b, full, sums, nlow, nout, nfull, y_in):
    big = mine.shape[-1]
    near, whole = {}, {}

    def parts(step):
        return (0, CUT) if step == 1 else (CUT, 0)

    for s, (axis, _, row) in enumerate(STREAMS):
        c = columns(me, axis, 2, big)
        for step in (1, -1):
            r = pl.ds(row + parts(step)[0], CUT)
            near[s, step] = sends.start(g_ref.at[r, c], low.at[r], axis, step)
    yield
    for s, (axis, _, row) in enumerate(STREAMS):
        for d, step in enumerate((1, -1)):
            near[s, step].wait_recv()
            add, keep = (pl.ds(row + p, CUT) for p in parts(step))
            c = columns(me, axis, step, big)
            out_b[d, add] = plus(g_ref[add, c], low[add]).astype(BF)
            out_b[d, keep] = g_ref[keep, c]
            r = pl.ds(row, HALF)
            whole[s, step] = sends.start(out_b.at[d, r], full.at[d, r], axis, step)
    yield
    half = RUN // 2

    def run(row, other, step, off, count):
        return pl.ds(pl.multiple_of(row + around(me, other, step) * RUN + off, 16), count)

    for s, (axis, other, row) in enumerate(STREAMS):
        for step in (1, -1):
            whole[s, step].wait_recv()
        r = pl.ds(row, HALF)
        sums[r] = plus(g_ref[r, columns(me, axis, 0, big)], full[0, r], full[1, r]).astype(BF)
        for d, step in enumerate((1, -1)):
            near[s, step] = sends.start(
                sums.at[run(row, other, 2, d * half, half)], nlow.at[s, d], other, step
            )
    yield
    for s, (axis, other, row) in enumerate(STREAMS):
        for d, step in enumerate((1, -1)):
            near[s, step].wait_recv()
            add, keep = (0, half) if step == 1 else (half, 0)
            nout[s, d, pl.ds(add, half)] = plus(
                sums[run(row, other, step, add, half)], nlow[s, d]
            ).astype(BF)
            nout[s, d, pl.ds(keep, half)] = sums[run(row, other, step, keep, half)]
            whole[s, step] = sends.start(nout.at[s, d], nfull.at[s, d], other, step)
    yield
    swap = {}
    for s, (axis, other, row) in enumerate(STREAMS):
        for step in (1, -1):
            whole[s, step].wait_recv()
        y_in[0, s] = plus(sums[run(row, other, 0, 0, RUN)], nfull[s, 0], nfull[s, 1]).astype(BF)
        swap[s] = sends.start(y_in.at[0, s], y_in.at[1, s], "yhi", 1)
    yield
    for s in range(2):
        swap[s].wait_recv()
        mine[s] = plus(y_in[0, s], y_in[1, s]).astype(BF)


def sum_scratch(width):
    big = width // 4
    return [
        pltpu.VMEM((ROWS, big), BF),
        pltpu.VMEM((2, ROWS, big), BF),
        pltpu.VMEM((2, ROWS, big), BF),
        pltpu.VMEM((ROWS, big), BF),
        pltpu.VMEM((2, 2, RUN // 2, big), BF),
        pltpu.VMEM((2, 2, RUN, big), BF),
        pltpu.VMEM((2, 2, RUN, big), BF),
        pltpu.VMEM((2, 2, RUN, big), BF),
    ]


def spread_steps(me, sends, mine, out_ref):
    big = mine.shape[-1]
    half = RUN // 2
    near, whole = {}, {}

    def run(row, other, step, off, count):
        return pl.ds(pl.multiple_of(row + around(me, other, step) * RUN + off, 16), count)

    for s, (axis, other, row) in enumerate(STREAMS):
        ref = out_ref.at[run(row, other, 0, 0, RUN), columns(me, axis, 0, big)]
        ref[...] = mine[s]
        for step in (1, -1):
            near[s, step] = sends.start(ref, ref, other, step)
    yield
    for s, (axis, other, row) in enumerate(STREAMS):
        for d, step in enumerate((1, -1)):
            near[s, step].wait_recv()
            ref = out_ref.at[run(row, other, -step, d * half, half), columns(me, axis, 0, big)]
            whole[s, step] = sends.start(ref, ref, other, step)
    yield
    for s, (axis, other, row) in enumerate(STREAMS):
        for step in (1, -1):
            whole[s, step].wait_recv()
        ref = out_ref.at[pl.ds(row, HALF), columns(me, axis, 0, big)]
        for step in (1, -1):
            near[s, step] = sends.start(ref, ref, axis, step)
    yield
    last = []
    for s, (axis, other, row) in enumerate(STREAMS):
        for d, step in enumerate((1, -1)):
            near[s, step].wait_recv()
            ref = out_ref.at[pl.ds(row + d * CUT, CUT), columns(me, axis, -step, big)]
            last.append(sends.start(ref, ref, axis, step))
    yield
    for copy in last:
        copy.wait_recv()


def vector_steps(sends, vec_ref, out_ref, keep, got):
    rounds = ((("core", 1),), (("ylo", 1),), (("x", 1), ("x", -1), ("x", 2)), (("z", 1), ("z", -1), ("z", 2)), (("yhi", 1),))
    keep[0] = vec_ref[...]
    k = 0
    for at, partners in enumerate(rounds):
        copies = []
        for axis, step in partners:
            copies.append((k, sends.start(keep.at[at], got.at[k], axis, step)))
            k += 1
        yield
        total = keep[at]
        for slot, copy in copies:
            copy.wait_recv()
            total = total + got[slot]
        keep[at + 1] = total
    out_ref[...] = keep[len(rounds)]


def small_steps(me, sends, g_ref, out_ref, got_x, got_z, got_y, sum_z, sum_y):
    x, z = me[4], me[3]
    steps = (1, -1, 2)

    def rows(at, step, count, base=0):
        return pl.ds(pl.multiple_of(base + lax.rem(at + step + 4, 4) * count, 16), count)

    copies = [
        sends.start(g_ref.at[rows(x, step, 64)], got_x.at[k], "x", step) for k, step in enumerate(steps)
    ]
    yield
    for copy in copies:
        copy.wait_recv()
    sum_z[...] = plus(g_ref[rows(x, 0, 64)], got_x[0], got_x[1], got_x[2]).astype(BF)
    copies = [
        sends.start(sum_z.at[rows(z, step, 16)], got_z.at[k], "z", step) for k, step in enumerate(steps)
    ]
    yield
    for copy in copies:
        copy.wait_recv()
    sum_y[...] = plus(sum_z[rows(z, 0, 16)], got_z[0], got_z[1], got_z[2]).astype(BF)
    copy = sends.start(sum_y, got_y, "yhi", 1)
    yield
    copy.wait_recv()
    ref = out_ref.at[rows(z, 0, 16, x * 64)]
    ref[...] = plus(sum_y[...], got_y[...]).astype(BF)
    copies = [sends.start(ref, ref, "z", step) for step in steps]
    yield
    for copy in copies:
        copy.wait_recv()
    ref = out_ref.at[rows(x, 0, 64)]
    copies = [sends.start(ref, ref, "x", step) for step in steps]
    yield
    for copy in copies:
        copy.wait_recv()


KEY_N, SUM_N = 9, 8
WIDE, REST = 2 * FF, 4608


def back_kernel(
    part_ref, g_ref, dq_ref, d_attn_ref, mixture_ref, x1_ref, h_ref, d_mid_ref, out_ref, logit_ref, vec_ref, vec_part_ref,
    cos_ref, sin_ref, wq, wk, wv,
    one_ref, two_ref, three_ref, vec_out_ref, both_ref,
    own, ra, rb, xs, ra_all, rb_all, xs_all, xs_relay, g_two, g_three, d_x1_s, vec_all, keep_v, got_v,
    mine_one, mine_two, got_x, got_z, got_y, sum_z, sum_y,
    *scratch,
):
    me = here()
    key_scr, one_scr, two_scr = scratch[:KEY_N], scratch[KEY_N : KEY_N + SUM_N], scratch[KEY_N + SUM_N : -2]
    greet(me, NEAR + WEIGHT + SMALL + (("pair", 1),))
    sends = Sends(me, *scratch[-2:])
    odd = lax.rem(me[4], 2)
    keep = pl.ds(pl.multiple_of(odd * T, T), T)
    cosine, sine = cos_ref[...], sin_ref[...]
    mine = pl.ds(0, T)

    def turned_back(tile):
        return tile * cosine - swapped(tile) * sine

    def keys():
        yield from key_steps(me, sends, part_ref, own, *key_scr)
        for j in range(KV_HEADS):
            tile = turned_back(own[:, 128 * j : 128 * (j + 1)]).astype(BF)
            rb[:, HEAD_DIM * j : HEAD_DIM * (j + 1)] = tile[:, :HEAD_DIM]
            rb[:, 320 + HEAD_DIM * j : 320 + HEAD_DIM * (j + 1)] = tile[:, HEAD_DIM:]
        share = everyone_steps(sends, (("all", rb, rb_all, None),))
        next(share)
        rb_all[mine] = rb[...]
        d_k, d_v = rb[:, :320], rb[:, 320:]
        d_x1 = d_x1_s[...] + jnp.concatenate(
            our_order(me, [dot(d_k, wk[k]) + dot(d_v, wv[k]) for k in range(4)]), axis=1
        )
        h = h_ref[...]
        r1 = lax.rsqrt(jnp.mean(h * h, axis=-1, keepdims=True) + EPS)
        d_first, g_gain_a = norm_back_rows(h, r1, vec_ref[0:1, :D], d_x1)
        d_h = d_mid_ref[...] + d_first + logit_ref[:, 0:1] * vec_ref[2:3, :D]
        both_ref[keep, :D] = out_ref[...]
        both_ref[keep, D:] = d_h.astype(BF)
        swap = sends.start(both_ref.at[keep], both_ref.at[keep], "pair", 1)
        vec_all[...] = vec_part_ref[...]
        vec_all[0:1, :D] = g_gain_a
        vectors = vector_steps(sends, vec_all, vec_out_ref, keep_v, got_v)
        next(vectors)
        yield
        next(share)
        yield
        together(share)
        g_three[...] = dot(xs_all[:, :256], rb_all[...], TN).astype(BF)
        small = small_steps(me, sends, g_three, three_ref, got_x, got_z, got_y, sum_z, sum_y)
        while True:
            for step in (small, vectors):
                next(step, None)
            if small.gi_frame is None and vectors.gi_frame is None:
                break
            yield
        swap.wait_recv()

    def queries():
        for j in range(KV_HEADS):
            for g in range(GROUPS):
                at = HEAD_DIM * (GROUPS * j + g)
                ra[:, at : at + HEAD_DIM] = turned_back(dq_ref[j, g * T : (g + 1) * T]).astype(BF)[:, :HEAD_DIM]
        ra[:, D:] = d_attn_ref[...]
        xs[...] = jnp.zeros_like(xs)
        for k, (a, b) in enumerate(zip(our_order(me, cut_four(x1_ref)), our_order(me, cut_four(mixture_ref)))):
            xs[k, :, :240] = a
            xs[k, :, 256:496] = b
        share = everyone_steps(
            sends, (("all", ra, ra_all, None), ("one", [xs.at[k] for k in range(4)], xs_all, xs_relay))
        )
        next(share)
        ra_all[mine] = ra[...]
        xs_all[mine] = xs[0]
        d_q = ra[:, :D]
        d_x1_s[...] = jnp.concatenate(our_order(me, [dot(d_q, wq[k], NT) for k in range(4)]), axis=1)
        g_two[:, :FF] = g_ref[:, WIDE:]
        g_two[:, FF + 2 * D :] = jnp.zeros((ROWS, 128), BF)
        yield
        next(share)
        yield
        together(share)
        g_two[:, FF : FF + D] = dot(xs_all[:, :256], ra_all[:, :D], TN).astype(BF)
        g_two[:, FF + D : FF + 2 * D] = dot(xs_all[:, 256:], ra_all[:, D:], TN).astype(BF)
        yield from sum_steps(me, sends, g_two, mine_two, *two_scr)
        yield from spread_steps(me, sends, mine_two, two_ref)

    def wide():
        yield from sum_steps(me, sends, g_ref, mine_one, *one_scr)
        yield from spread_steps(me, sends, mine_one, one_ref)

    lanes = {"k": keys(), "q": queries(), "w": wide()}
    for c in ORDER:
        next(lanes[c], None)
    together(*(lanes[c] for c in "kwq"))
    sends.finish()


ORDER = "kwqkqqkwkkk"


def back(*args):
    vmem = pl.BlockSpec(memory_space=pltpu.VMEM)
    return pl.pallas_call(
        back_kernel,
        name="back",
        out_shape=(
            jax.ShapeDtypeStruct((ROWS, WIDE), BF),
            jax.ShapeDtypeStruct((ROWS, REST), BF),
            jax.ShapeDtypeStruct((ROWS, 640), BF),
            jax.ShapeDtypeStruct((8, 1024), F32),
            jax.ShapeDtypeStruct((PAIR, 2 * D), BF),
        ),
        in_specs=[vmem] * len(args),
        out_specs=(vmem,) * 5,
        scratch_shapes=[
            pltpu.VMEM((T, 640), F32),
            pltpu.VMEM((T, 2 * D), BF),
            pltpu.VMEM((T, 640), BF),
            pltpu.VMEM((4, T, 512), BF),
            pltpu.VMEM((4 * T, 2 * D), BF),
            pltpu.VMEM((4 * T, 640), BF),
            pltpu.VMEM((4 * T, 512), BF),
            pltpu.VMEM((T, 512), BF),
            pltpu.VMEM((ROWS, REST), BF),
            pltpu.VMEM((ROWS, 640), BF),
            pltpu.VMEM((T, D), F32),
            pltpu.VMEM((8, 1024), F32),
            pltpu.VMEM((6, 8, 1024), F32),
            pltpu.VMEM((9, 8, 1024), F32),
            pltpu.VMEM((2, RUN, WIDE // 4), BF),
            pltpu.VMEM((2, RUN, REST // 4), BF),
            pltpu.VMEM((3, 64, 640), BF),
            pltpu.VMEM((3, 16, 640), BF),
            pltpu.VMEM((16, 640), BF),
            pltpu.VMEM((64, 640), BF),
            pltpu.VMEM((16, 640), BF),
        ]
        + key_scratch()
        + sum_scratch(WIDE)
        + sum_scratch(REST)
        + sems(140),
        compiler_params=pltpu.CompilerParams(
            collective_id=2, has_side_effects=True, vmem_limit_bytes=VMEM_LIMIT
        ),
        cost_estimate=pl.CostEstimate(flops=2_000_000_000, bytes_accessed=200_000_000, transcendentals=0),
    )(*args)


def shard_of(me, k):
    ylo, core = me[0], me[1]
    return (ylo if k < 2 else 1 - ylo) * 2 + (core if k % 2 == 0 else 1 - core)


def our_order(me, p):
    core, ylo = me[1] == 1, me[0] == 1
    p = [jnp.where(core, p[k ^ 1], p[k]) for k in range(4)]
    return [jnp.where(ylo, p[k ^ 2], p[k]) for k in range(4)]


def cut_four(ref):
    return [ref[:, 240 * k : 240 * (k + 1)] for k in range(4)]


def norm_back_rows(z, r, gain, dy):
    dz = r * (gain * dy) - z * (r * r * r) * jnp.mean(gain * dy * z, axis=-1, keepdims=True)
    return dz, jnp.sum(dy * z * r, axis=0, keepdims=True)


def everyone_steps(sends, pieces):
    half = T // 2
    arrived, last = [], []
    for kind, source, whole, relay in pieces:
        near = source if kind == "all" else source[1]
        last.append(sends.start(near, whole.at[pl.ds(T, T)], "core", 1))
    for step, at in ((1, 0), (-1, half)):
        r = pl.ds(at, half)
        for kind, source, whole, relay in pieces:
            far = source if kind == "all" else source[2]
            arrived.append((sends.start(far.at[r], whole.at[pl.ds(2 * T + at, half)], "y", step), None))
            if kind == "all":
                arrived[-1] = (arrived[-1][0], (whole.at[pl.ds(2 * T + at, half)], whole.at[pl.ds(3 * T + at, half)]))
            else:
                copy = sends.start(source[3].at[r], relay.at[r], "y", step)
                arrived.append((copy, (relay.at[r], whole.at[pl.ds(3 * T + at, half)])))
    yield
    for copy, onward in arrived:
        copy.wait_recv()
        if onward is not None:
            last.append(sends.start(onward[0], onward[1], "core", 1))
    yield
    for copy in last:
        copy.wait_recv()


def dense_kernel(
    mix_ref, q_ref, prob_ref, kv_ref, h_ref, up_ref, vec_ref,
    wo_ref, wg_ref, wu_ref, wd_ref, wos_ref, wgs_ref, wus_ref, wds_ref,
    dq_ref, dkv_ref, g_ref, d_attn_ref, mixture_ref, d_mid_ref, out_ref, logit_ref, vec_out_ref,
    wo, wg, wu, wd, mixf, gate_s, up_s, inner, dgu, dffn, xs, do_s, d_mix_s,
    dgu_all, dffn_all, xs_all, inner_all, xs_relay, inner_relay,
    load_sems, send_sems, recv_sems,
):
    me = here()
    loads = []
    for k, (own, rest, to) in enumerate(
        ((wo_ref, wos_ref, wo), (wg_ref, wgs_ref, wg), (wu_ref, wus_ref, wu), (wd_ref, wds_ref, wd))
    ):
        pair = (
            pltpu.make_async_copy(own, to.at[0], load_sems.at[2 * k]),
            pltpu.make_async_copy(rest, to.at[pl.ds(1, 3)], load_sems.at[2 * k + 1]),
        )
        for copy in pair:
            copy.start()
        loads.append(pair)
    greet(me, WEIGHT)
    sends = Sends(me, send_sems, recv_sems)
    shards = [shard_of(me, k) for k in range(4)]

    def run640(k):
        return pl.ds(pl.multiple_of(shards[k] * 640, 128), 640)

    def run640_up(k):
        return pl.ds(pl.multiple_of(FF + shards[k] * 640, 128), 640)

    def loaded(k):
        for copy in loads[k]:
            copy.wait()

    for j in range(KV_HEADS):
        for g in range(GROUPS):
            h = GROUPS * j + g
            mixf[:, HEAD_DIM * h : HEAD_DIM * (h + 1)] = mix_ref[j, g * T : (g + 1) * T, HEAD_DIM:]
    mixture_ref[...] = mixf[...].astype(BF)
    mix_k = our_order(me, cut_four(mixture_ref))
    loaded(0)
    attn_out = sum(dot(mix_k[k], wo[k]) for k in range(4))
    hidden = h_ref[...]
    gain_f = vec_ref[1:2, :D]
    route_w = vec_ref[2:3, :D]
    middle = hidden + attn_out
    r2 = lax.rsqrt(jnp.mean(middle * middle, axis=-1, keepdims=True) + EPS)
    x2 = middle * r2 * gain_f
    x2_k = our_order(me, [x2[:, 240 * k : 240 * (k + 1)].astype(BF) for k in range(4)])
    xs[...] = jnp.zeros_like(xs)
    for k in range(4):
        xs[k, :, :240] = x2_k[k]
    loaded(1)
    gate_s[...] = sum(dot(x2_k[k], wg[k]) for k in range(4))
    loaded(2)
    up_s[...] = sum(dot(x2_k[k], wu[k]) for k in range(4))
    gate = gate_s[...]
    inner[...] = (gate * jax.nn.sigmoid(gate) * up_s[...]).astype(BF)
    loaded(3)
    ffn_out = sum(dot(inner[:, run640(k)], wd[k], NT) for k in range(4))
    route = jax.nn.sigmoid(jnp.sum(hidden * route_w, axis=-1, keepdims=True))
    branch = attn_out + ffn_out
    out_ref[...] = (route * branch).astype(BF)
    upstream = up_ref[...]
    d_branch = upstream * route
    d_logit = route * (1.0 - route) * jnp.sum(upstream * branch, axis=-1, keepdims=True)
    logit_ref[...] = jnp.broadcast_to(d_logit, logit_ref.shape)
    vec_out_ref[...] = jnp.zeros_like(vec_out_ref)
    vec_out_ref[2:3, :D] = jnp.sum(d_logit * hidden, axis=0, keepdims=True)
    d_ffn = d_branch.astype(BF)
    dffn[...] = jnp.zeros_like(dffn)
    for k in range(4):
        dffn[:, 256 * k : 256 * k + 240] = d_branch[:, 240 * k : 240 * (k + 1)].astype(BF)
    for k in range(4):
        d_inner = dot(d_ffn, wd[k])
        gate, up = gate_s[:, run640(k)], up_s[:, run640(k)]
        sg = jax.nn.sigmoid(gate)
        dgu[:, run640(k)] = (d_inner * up * (sg + gate * sg * (1.0 - sg))).astype(BF)
        dgu[:, run640_up(k)] = (d_inner * (gate * sg)).astype(BF)
    pieces = (
        ("all", dgu, dgu_all, None),
        ("all", dffn, dffn_all, None),
        ("one", [xs.at[k] for k in range(4)], xs_all, xs_relay),
        ("one", [inner.at[:, run640(k)] for k in range(4)], inner_all, inner_relay),
    )
    share = everyone_steps(sends, pieces)
    next(share)
    own = pl.ds(0, T)
    dgu_all[own], dffn_all[own] = dgu[...], dffn[...]
    xs_all[own], inner_all[own] = xs[0], inner[:, run640(0)]
    d_gate, d_up = dgu[:, :FF], dgu[:, FF:]
    d_x2 = jnp.concatenate(
        our_order(me, [dot(d_gate, wg[k], NT) + dot(d_up, wu[k], NT) for k in range(4)]), axis=1
    )
    d_mid, g_gain_f = norm_back_rows(middle, r2, gain_f, d_x2)
    d_mid_ref[...] = d_mid
    vec_out_ref[1:2, :D] = g_gain_f
    d_attn = (d_branch + d_mid).astype(BF)
    d_attn_ref[...] = d_attn
    d_mix_s[...] = jnp.concatenate(our_order(me, [dot(d_attn, wo[k], NT) for k in range(4)]), axis=1)
    do_s[...] = jnp.zeros_like(do_s)
    for j in range(KV_HEADS):
        for g in range(GROUPS):
            h = GROUPS * j + g
            do_s[j, g * T : (g + 1) * T, HEAD_DIM:] = d_mix_s[:, HEAD_DIM * h : HEAD_DIM * (h + 1)].astype(BF)

    @pl.loop(0, KV_HEADS)
    def _(j):
        c = pl.ds(pl.multiple_of(j * 128, 128), 128)
        tile = kv_ref[:, :, :, :, c].reshape(KEYS, 128)
        prob, d_out = prob_ref[j], do_s[j]
        d_prob = dot(d_out, tile, NT)
        delta = jnp.sum(d_out.astype(F32) * mix_ref[j], axis=-1, keepdims=True)
        d_score = (prob.astype(F32) * (d_prob - delta)).astype(BF)
        dq_ref[j] = dot(d_score, tile) * SCALE
        grad = dot(d_score, q_ref[j], TN) * SCALE + dot(prob, d_out, TN)
        dkv_ref[:, :, :, :, c] = grad.astype(BF).reshape(2, 4, 4, T, 128)

    together(share)
    for c in range(0, 2 * FF, 1280):
        g_ref[:, c : c + 1280] = dot(xs_all[...], dgu_all[:, c : c + 1280], TN).astype(BF)
    for k in range(4):
        g_ref[:, 2 * FF + 640 * k : 2 * FF + 640 * (k + 1)] = dot(
            dffn_all[:, 256 * k : 256 * (k + 1)], inner_all[...], TN
        ).astype(BF)
    sends.finish()


def dense(mix, q, prob, kv, h, up_c, vec, own, rest):
    vmem, hbm = pl.BlockSpec(memory_space=pltpu.VMEM), pl.BlockSpec(memory_space=pl.ANY)
    rows = GROUPS * T
    return pl.pallas_call(
        dense_kernel,
        name="dense",
        out_shape=(
            jax.ShapeDtypeStruct((KV_HEADS, rows, 128), F32),
            jax.ShapeDtypeStruct((2, 4, 4, T, 640), BF),
            jax.ShapeDtypeStruct((ROWS, 3 * FF), BF),
            jax.ShapeDtypeStruct((T, D), BF),
            jax.ShapeDtypeStruct((T, D), BF),
            jax.ShapeDtypeStruct((T, D), F32),
            jax.ShapeDtypeStruct((T, D), BF),
            jax.ShapeDtypeStruct((T, 128), F32),
            jax.ShapeDtypeStruct((8, 1024), F32),
        ),
        in_specs=[vmem] * 7 + [hbm] * 8,
        out_specs=(vmem,) * 9,
        scratch_shapes=[
            pltpu.VMEM((4, 240, D), BF),
            pltpu.VMEM((4, 240, FF), BF),
            pltpu.VMEM((4, 240, FF), BF),
            pltpu.VMEM((4, D, 640), BF),
            pltpu.VMEM((T, D), F32),
            pltpu.VMEM((T, FF), F32),
            pltpu.VMEM((T, FF), F32),
            pltpu.VMEM((T, FF), BF),
            pltpu.VMEM((T, 2 * FF), BF),
            pltpu.VMEM((T, 1024), BF),
            pltpu.VMEM((4, T, 256), BF),
            pltpu.VMEM((KV_HEADS, rows, 128), BF),
            pltpu.VMEM((T, D), F32),
            pltpu.VMEM((4 * T, 2 * FF), BF),
            pltpu.VMEM((4 * T, 1024), BF),
            pltpu.VMEM((4 * T, 256), BF),
            pltpu.VMEM((4 * T, 640), BF),
            pltpu.VMEM((T, 256), BF),
            pltpu.VMEM((T, 640), BF),
            pltpu.SemaphoreType.DMA((8,)),
        ]
        + sems(28),
        compiler_params=pltpu.CompilerParams(
            collective_id=4, has_side_effects=True, vmem_limit_bytes=VMEM_LIMIT
        ),
        cost_estimate=pl.CostEstimate(
            flops=20_000_000_000, bytes_accessed=40_000_000, transcendentals=0
        ),
    )(mix, q, prob, kv, h, up_c, vec, *own, *rest)


def per_device(hidden, chosen, positions, w_query, w_key, w_value, w_output, w_gate, w_up, w_down, gain_attn, gain_ffn, router, d_out):
    tokens, upstream = hidden[0], d_out[0]
    own_w = (w_output, w_gate, w_up, w_down.T)
    frequency = THETA ** (-jnp.arange(0, HEAD_DIM // 2).astype(F32) * 2.0 / HEAD_DIM)
    vec = jnp.stack([gain_attn, gain_ffn, router]).astype(F32)
    vec = jnp.pad(vec, ((0, 5), (0, 16)))
    (
        mix_heads, prob, q_heads, kv_all, h, up_c, x1, cosine, sine, place, vec_in, wq, wk, wv, *rest_w
    ) = front(
        tokens.T, upstream.T, chosen, positions, jnp.tile(frequency, 4)[None, :], vec,
        w_query, w_key.T, w_value.T, *own_w
    )
    d_q_heads, d_kv, g_one, d_attn, mixture, d_mid, out_c, d_logit, vec_out = dense(
        mix_heads, q_heads, prob, kv_all, h, up_c, vec_in, own_w, rest_w
    )
    s_one, s_two, s_three, vector, both = back(
        d_kv, g_one, d_q_heads, d_attn, mixture, x1, h, d_mid, out_c, d_logit, vec_in, vec_out, cosine, sine, wq, wk, wv
    )
    spread = dot(both, place, TN)
    output = (tokens.T + spread[:D]).T
    d_tokens = (upstream.T + spread[D:]).T
    shard = lax.axis_index("ylo") * 2 + lax.axis_index("core")
    vector = lax.dynamic_slice_in_dim(vector, shard * 240, 240, axis=1)
    s_one, s_two, s_three = s_one[:240], s_two[:240], s_three[:240]
    g_down = jnp.concatenate([s_two[:, 640 * k : 640 * (k + 1)] for k in range(4)], axis=0).astype(F32).T
    return (
        output[None],
        d_tokens[None],
        s_two[:, FF : FF + D].astype(F32),
        s_three[:, :320].astype(F32),
        s_three[:, 320:].astype(F32),
        s_two[:, FF + D : FF + 2 * D].astype(F32),
        s_one[:, :FF].astype(F32),
        s_one[:, FF:].astype(F32),
        g_down,
        vector[0],
        vector[1],
        vector[2],
    )


def solution(mesh):
    finer = Mesh(mesh.devices.reshape(DIMS), AX)
    shard, blk = ("ylo", "core"), ("yhi", "z", "x")
    act, row, weight, vec = P(shard, blk, None), P(shard, blk), P(shard, None), P(shard)
    return jax.shard_map(
        per_device,
        mesh=finer,
        in_specs=(act, row, row) + (weight,) * 7 + (vec,) * 3 + (act,),
        out_specs=(act, act) + (weight,) * 7 + (vec,) * 3,
        check_vma=False,
    )
```

```python
import functools

import jax
import jax.numpy as jnp
from jax import lax
from jax.experimental import pallas as pl
from jax.experimental.pallas import tpu as pltpu
from jax.sharding import Mesh
from jax.sharding import PartitionSpec as P

D = 960
HEADS = 15
KV_HEADS = 5
GROUPS = 3
HEAD_DIM = 64
FF = 2560
EPS = 1e-05
THETA = 10000.0
SCALE = HEAD_DIM ** (-0.5)
T = 64
PAIR = 128
SLOTS = 32
KEYS = SLOTS * T
AX = ("ylo", "core", "yhi", "z", "x")
DIMS = (2, 2, 2, 4, 4)
MESH = pl.DeviceIdType.MESH
BF = jnp.bfloat16
F32 = jnp.float32
VMEM_LIMIT = 56 * 2**20


def dot(a, b, dims=(((1,), (0,)), ((), ()))):
    return lax.dot_general(a, b, dims, preferred_element_type=F32)


NT = (((1,), (1,)), ((), ()))
TN = (((0,), (0,)), ((), ()))


def here():
    return tuple(lax.axis_index(a) for a in AX)


def neighbour(me, axis, step):
    ylo, core, yhi, z, x = me
    if axis == "z":
        z = lax.rem(z + step + 4, 4)
    elif axis == "x":
        x = lax.rem(x + step + 4, 4)
    elif axis == "pair":
        x = x + 1 - 2 * lax.rem(x, 2)
    elif axis == "yhi":
        yhi = 1 - yhi
    elif axis == "ylo":
        ylo = 1 - ylo
    elif axis == "core":
        core = 1 - core
    else:
        y = lax.rem(yhi * 2 + ylo + step + 4, 4)
        ylo, yhi = lax.rem(y, 2), y // 2
    return (ylo, core, yhi, z, x)


NEAR = (("x", 1), ("x", -1), ("z", 1), ("z", -1), ("yhi", 1))
WEIGHT = (("y", 1), ("y", -1), ("core", 1))
FAR = (("x", 2), ("z", 2))


def greet(me, partners):
    barrier = pltpu.get_barrier_semaphore()
    for axis, step in partners:
        pl.semaphore_signal(
            barrier, inc=1, device_id=neighbour(me, axis, step), device_id_type=MESH
        )
    pl.semaphore_wait(barrier, len(partners))


class Sends:
    def __init__(self, me, send_sems, recv_sems):
        self.me, self.send_sems, self.recv_sems, self.all = me, send_sems, recv_sems, []

    def start(self, src, dst, axis, step):
        k = len(self.all)
        copy = pltpu.make_async_remote_copy(
            src_ref=src,
            dst_ref=dst,
            send_sem=self.send_sems.at[k],
            recv_sem=self.recv_sems.at[k],
            device_id=neighbour(self.me, axis, step),
            device_id_type=MESH,
        )
        copy.start()
        self.all.append(copy)
        return copy

    def finish(self):
        for copy in self.all:
            copy.wait_send()


def together(*steps):
    steps = list(steps)
    while steps:
        for step in list(steps):
            try:
                next(step)
            except StopIteration:
                steps.remove(step)


def run_lanes(lanes, order):
    for c in order:
        next(lanes[c], None)
    together(*lanes.values())


def sems(count):
    return [pltpu.SemaphoreType.DMA((count,)), pltpu.SemaphoreType.DMA((count,))]


def plus(*terms):
    total = terms[0].astype(F32)
    for term in terms[1:]:
        total = total + term.astype(F32)
    return total


class Shards:
    def __init__(self, sends):
        self.sends, self.arrived, self.last = sends, [], []
        self.color = lax.rem(sends.me[3] + sends.me[4], 2)

    def near(self, own, out):
        self.last.append(self.sends.start(own, out.at[out.shape[0] - 3], "core", 1))

    def far(self, own, out, cut):
        for step, row, rows in ((1, 0, cut), (-1, cut, own.shape[0] - cut)):
            r = pl.ds(row, rows)
            ref = out.at[out.shape[0] - 2, r]
            self.arrived.append((ref, out.at[out.shape[0] - 1, r], self.sends.start(own.at[r], ref, "y", step)))

    def relay(self):
        for ref, to, copy in self.arrived:
            copy.wait_recv()
            self.last.append(self.sends.start(ref, to, "core", 1))
        self.arrived = []

    def finish(self):
        self.relay()
        for copy in self.last:
            copy.wait_recv()
        self.last = []

    def half(self, own, out, block, cuts):
        rows, slots = own.shape[0], out.shape[0]
        sub = block // 2
        mine = self.color * (rows - block)
        relay = slots > 1
        other = slots - 2 if relay else 0

        def part(slot, start, count):
            return out.at[slot, pl.ds(pl.multiple_of(start, 16), count)]

        copies = []
        for step, off in ((1, 0), (-1, sub)):
            src = own.at[pl.ds(pl.multiple_of(mine + off, 16), sub)]
            copies.append(self.sends.start(src, part(other, mine + off, sub), "y", step))
        if relay:
            self.near(own, out)
        yield
        for copy in copies:
            copy.wait_recv()
        copies, off = [], 0
        for (axis, step), count in zip((("x", 1), ("x", -1), ("z", 1), ("z", -1)), cuts):
            ref = part(other, self.color * block + off, count)
            copies.append(self.sends.start(ref, ref, axis, step))
            off += count
        if relay:
            self.last.append(self.sends.start(part(other, mine, block), part(slots - 1, mine, block), "core", 1))
        yield
        for copy in copies:
            copy.wait_recv()
        rest = (1 - self.color) * block
        if relay:
            self.last.append(
                self.sends.start(part(other, rest, rows - block), part(slots - 1, rest, rows - block), "core", 1)
            )


def gather_steps(me, sends, kv_ref, out_ref):
    _, _, yh, z, x = me
    oy = 1 - yh
    half, quarter = T // 2, T // 4
    streams = (("x", "z", 0), ("z", "x", half))

    def slot(y, axis, step, rows, count):
        zz = lax.rem(z + step + 4, 4) if axis == "z" else z
        xx = lax.rem(x + step + 4, 4) if axis == "x" else x
        return out_ref.at[y, zz, xx, pl.ds(rows, count)]

    def line(y, axis, step, rows, count):
        if axis == "z":
            return out_ref.at[y, lax.rem(z + step + 4, 4), :, pl.ds(rows, count)]
        return out_ref.at[y, :, lax.rem(x + step + 4, 4), pl.ds(rows, count)]

    own = out_ref.at[yh, z, x]
    own[...] = kv_ref[...]
    first = sends.start(kv_ref, own, "yhi", 1)
    got = {}
    for y, tag in ((yh, 0), (oy, 1)):
        if tag:
            yield
            first.wait_recv()
        for axis, _, row in streams:
            src = slot(y, axis, 0, row, half)
            for step in (1, -1):
                got[tag, row, step] = sends.start(src, src, axis, step)
    far = {}
    for y, tag in ((yh, 0), (oy, 1)):
        yield
        for axis, _, row in streams:
            for step, off in ((1, 0), (-1, quarter)):
                got[tag, row, step].wait_recv()
                src = slot(y, axis, -step, row + off, quarter)
                far[tag, row, step] = sends.start(src, src, axis, step)
    wide = {}
    for y, tag in ((yh, 0), (oy, 1)):
        yield
        for _, axis, row in streams:
            for step in (1, -1):
                far[tag, row, step].wait_recv()
            src = line(y, axis, 0, row, half)
            for step in (1, -1):
                wide[tag, row, step] = sends.start(src, src, axis, step)
    last = []
    for y, tag in ((yh, 0), (oy, 1)):
        yield
        for _, axis, row in streams:
            for step, off in ((1, 0), (-1, quarter)):
                wide[tag, row, step].wait_recv()
                src = line(y, axis, -step, row + off, quarter)
                last.append(sends.start(src, src, axis, step))
    yield
    for copy in last:
        copy.wait_recv()


def swapped(x):
    lane = lax.broadcasted_iota(jnp.int32, x.shape, 1)
    return jnp.where(lane < HEAD_DIM // 2, pltpu.roll(x, 96, 1), pltpu.roll(x, 32, 1))


def front_kernel(
    hidden_ref, d_out_ref, chosen_ref, pos_ref, freq_ref, vec_ref, wq_ref, wk_ref, wv_ref,
    wo_ref, wg_ref, wu_ref, wd_ref,
    mix_ref, prob_out, q_ref, kv_out, h_ref, up_ref, x1_ref, cos_ref, sin_ref, place_ref, vec_out_ref,
    wq_out, wk_out, wv_out, wos_ref, wgs_ref, wus_ref, wds_ref,
    compact_h, compact_d, compact_p, got_h, got_d, got_p, vecs, q_pre, kv_own,
    prob_ref, kv_ref, wq, wk, wv,
    load_sems, store_sems, send_sems, recv_sems,
):
    me = here()
    yhi, z, x = me[2:]
    loads = []
    for k, (own, to) in enumerate(((wq_ref, wq), (wk_ref, wk), (wv_ref, wv))):
        loads.append(pltpu.make_async_copy(own, to.at[0], load_sems.at[k]))
        loads[-1].start()
    greet(me, NEAR + WEIGHT)
    sends = Sends(me, send_sems, recv_sems)
    early, query, late = Shards(sends), Shards(sends), Shards(sends)
    odd = lax.rem(x, 2)
    give = pl.ds(pl.multiple_of((1 - odd) * T, T), T)
    keep = pl.ds(pl.multiple_of(odd * T, T), T)
    limit = ((yhi * 16 + z * 4 + x) // 2 + 1) * PAIR
    stores = []

    def store(a, b):
        stores.append(pltpu.make_async_copy(a, b, store_sems.at[len(stores)]))
        stores[-1].start()

    def main():
        vec_far = sends.start(vec_ref, vecs.at[2], "y", 1)
        early.far(wk_ref, wk, 160)
        early.far(wv_ref, wv, 160)
        vec_near = sends.start(vec_ref, vecs.at[1], "core", 1)
        early.near(wk_ref, wk)
        early.near(wv_ref, wv)
        query.far(wq_ref, wq, 128)
        query.near(wq_ref, wq)
        vecs[0] = vec_ref[...]
        flag = jnp.where(chosen_ref[...] > 0, 1.0, 0.0)
        token = lax.broadcasted_iota(jnp.int32, (PAIR, PAIR), 0)
        lane = lax.broadcasted_iota(jnp.int32, (PAIR, PAIR), 1)
        upto = jnp.where(token <= lane, 1.0, 0.0).astype(BF)
        count = dot(jnp.broadcast_to(flag, (16, PAIR)).astype(BF), upto)[0:1]
        total = jnp.sum(flag, axis=1, keepdims=True)
        rank = count - 1.0 + jnp.where(odd == 1, PAIR - total, 0.0)
        place = jnp.where(token.astype(F32) == rank, flag, 0.0)
        place_low = place.astype(BF)
        place_ref[...] = place_low
        compact_p[...] = jnp.broadcast_to(
            jnp.sum(place * pos_ref[...].astype(F32), axis=1, keepdims=True), (PAIR, PAIR)
        )
        compact_h[...] = dot(place_low, hidden_ref[...].astype(BF), NT).astype(BF)
        swaps = [sends.start(c.at[give], g, "pair", 1) for c, g in ((compact_h, got_h), (compact_p, got_p))]
        yield
        compact_d[...] = dot(place_low, d_out_ref[...].astype(BF), NT).astype(BF)
        vec_far.wait_recv()
        vec_last = sends.start(vecs.at[2], vecs.at[3], "core", 1)
        early.relay()
        yield
        swaps[0].wait_recv()
        h = plus(compact_h[keep], got_h[...])
        h_ref[...] = h
        swaps.append(sends.start(compact_d.at[give], got_d, "pair", 1))
        swaps[1].wait_recv()
        angle = (compact_p[keep] + got_p[...]) * freq_ref[...]
        turn = lax.broadcasted_iota(jnp.int32, (T, PAIR), 1)
        cosine = jnp.where(turn < HEAD_DIM, jnp.cos(angle), 1.0)
        sine = jnp.sin(angle)
        sine = jnp.where(turn < HEAD_DIM // 2, -sine, jnp.where(turn < HEAD_DIM, sine, 0.0))
        cos_ref[...], sin_ref[...] = cosine, sine
        vec_near.wait_recv()
        vec_last.wait_recv()
        vec_out_ref[...] = jnp.zeros_like(vec_out_ref)
        for k, v in enumerate(our_order(me, [vecs[k, :, :240] for k in range(4)])):
            vec_out_ref[:, 240 * k : 240 * (k + 1)] = v
        r1 = lax.rsqrt(jnp.mean(h * h, axis=-1, keepdims=True) + EPS)
        x1_ref[...] = (h * r1 * vec_out_ref[0:1, :D]).astype(BF)
        x1_k = our_order(me, cut_four(x1_ref))
        for copy in loads:
            copy.wait()
        early.finish()
        k_pre = sum(dot(x1_k[k], wk[k], NT) for k in range(4))
        v_pre = sum(dot(x1_k[k], wv[k], NT) for k in range(4))
        for j in range(KV_HEADS):
            run = slice(HEAD_DIM * j, HEAD_DIM * (j + 1))
            tile = jnp.concatenate([k_pre[:, run], v_pre[:, run]], axis=1)
            kv_own[:, 128 * j : 128 * (j + 1)] = (tile * cosine + swapped(tile) * sine).astype(BF)
        gather = gather_steps(me, sends, kv_own, kv_ref)
        next(gather)
        yield
        next(gather)
        yield
        query.relay()
        yield
        query.finish()
        swaps[2].wait_recv()
        up_ref[...] = plus(compact_d[keep], got_d[...])
        q_pre[...] = sum(dot(x1_k[k], wq[k]) for k in range(4))
        zero = jnp.zeros((T, HEAD_DIM), F32)
        for j in range(KV_HEADS):
            for g in range(GROUPS):
                at = HEAD_DIM * (GROUPS * j + g)
                tile = jnp.concatenate([q_pre[:, at : at + HEAD_DIM], zero], axis=1)
                q_ref[j, g * T : (g + 1) * T] = (tile * cosine + swapped(tile) * sine).astype(BF)
        yield
        yield from gather
        for a, b in ((kv_ref, kv_out), (wq, wq_out), (wk, wk_out), (wv, wv_out)):
            store(a, b)
        for j in range(KV_HEADS):
            tile = kv_ref[:, :, :, :, 128 * j : 128 * (j + 1)].reshape(KEYS, 128)
            scores = dot(q_ref[j], tile, NT) * SCALE
            column = lax.broadcasted_iota(jnp.int32, scores.shape, 1)
            scores = jnp.where(column < limit, scores, -1e30)
            exponent = jnp.exp(scores - jnp.max(scores, axis=-1, keepdims=True))
            prob = (exponent * (1.0 / jnp.sum(exponent, axis=-1, keepdims=True))).astype(BF)
            prob_ref[j] = prob
            store(prob_ref.at[j], prob_out.at[j])
            mix_ref[j] = dot(prob, tile)
            yield

    small, large = (128, (32, 32, 32, 16)), (480, (128, 128, 112, 112))
    lanes = {
        "m": main(),
        "o": late.half(wo_ref, wos_ref, *small),
        "t": late.half(wg_ref, wgs_ref, *small),
        "u": late.half(wu_ref, wus_ref, *small),
        "d": late.half(wd_ref, wds_ref, *large),
    }
    run_lanes(lanes, FRONT_ORDER)
    late.finish()
    for copy in stores:
        copy.wait()
    sends.finish()


FRONT_ORDER = (
    "mmmommtmmoumdmommmtummdmmtumdm"
)


def front(hidden, d_out, chosen, pos, freq, vec, w_query, w_key, w_value, *later):
    vmem, hbm = pl.BlockSpec(memory_space=pltpu.VMEM), pl.BlockSpec(memory_space=pl.ANY)
    rows = GROUPS * T
    return pl.pallas_call(
        front_kernel,
        name="front",
        out_shape=(
            jax.ShapeDtypeStruct((KV_HEADS, rows, 128), F32),
            jax.ShapeDtypeStruct((KV_HEADS, rows, KEYS), BF),
            jax.ShapeDtypeStruct((KV_HEADS, rows, 128), BF),
            jax.ShapeDtypeStruct((2, 4, 4, T, 640), BF),
            jax.ShapeDtypeStruct((T, D), F32),
            jax.ShapeDtypeStruct((T, D), F32),
            jax.ShapeDtypeStruct((T, D), BF),
            jax.ShapeDtypeStruct((T, 128), F32),
            jax.ShapeDtypeStruct((T, 128), F32),
            jax.ShapeDtypeStruct((PAIR, PAIR), BF),
            jax.ShapeDtypeStruct((8, 1024), F32),
            jax.ShapeDtypeStruct((4, 240, 960), BF),
            jax.ShapeDtypeStruct((4, 320, 240), BF),
            jax.ShapeDtypeStruct((4, 320, 240), BF),
        )
        + tuple(jax.ShapeDtypeStruct((3,) + w.shape, BF) for w in later[:3])
        + (jax.ShapeDtypeStruct((1,) + later[3].shape, BF),),
        in_specs=[vmem] * 6 + [hbm] * 7,
        out_specs=(vmem, hbm, vmem, hbm) + (vmem,) * 7 + (hbm,) * 7,
        scratch_shapes=[
            pltpu.VMEM((PAIR, D), BF),
            pltpu.VMEM((PAIR, D), BF),
            pltpu.VMEM((PAIR, PAIR), F32),
            pltpu.VMEM((T, D), BF),
            pltpu.VMEM((T, D), BF),
            pltpu.VMEM((T, PAIR), F32),
            pltpu.VMEM((4, 8, 256), F32),
            pltpu.VMEM((T, D), F32),
            pltpu.VMEM((T, 640), BF),
            pltpu.VMEM((KV_HEADS, rows, KEYS), BF),
            pltpu.VMEM((2, 4, 4, T, 640), BF),
            pltpu.VMEM((4, 240, 960), BF),
            pltpu.VMEM((4, 320, 240), BF),
            pltpu.VMEM((4, 320, 240), BF),
            pltpu.SemaphoreType.DMA((3,)),
            pltpu.SemaphoreType.DMA((9,)),
        ]
        + sems(90),
        compiler_params=pltpu.CompilerParams(
            collective_id=1, has_side_effects=True, vmem_limit_bytes=VMEM_LIMIT
        ),
        cost_estimate=pl.CostEstimate(flops=5_000_000_000, bytes_accessed=90_000_000, transcendentals=0),
    )(hidden, d_out, chosen, pos, freq, vec, w_query, w_key, w_value, *later)


def key_steps(me, sends, part_ref, out_ref, low, out_b, full, sums, nlow, nout, nfull, mine, y_in):
    _, _, yh, z, x = me
    half, quarter = T // 2, T // 4
    streams = (("x", "z", 0), ("z", "x", half))

    def line(axis, step, row, count):
        if axis == "z":
            return part_ref.at[:, lax.rem(z + step + 4, 4), :, pl.ds(row, count)]
        return part_ref.at[:, :, lax.rem(x + step + 4, 4), pl.ds(row, count)]

    near = {}
    for s, (axis, _, row) in enumerate(streams):
        near[s, 1] = sends.start(line(axis, 2, row, quarter), low.at[s, 0], axis, 1)
        near[s, -1] = sends.start(line(axis, 2, row + quarter, quarter), low.at[s, 1], axis, -1)
    whole = {}
    for s, (axis, _, row) in enumerate(streams):
        yield
        for d, step in enumerate((1, -1)):
            near[s, step].wait_recv()
            lo, hi = (0, quarter) if step == 1 else (quarter, 0)
            out_b[s, d, :, :, pl.ds(lo, quarter)] = plus(
                line(axis, step, row + lo, quarter)[...], low[s, d]
            ).astype(BF)
            out_b[s, d, :, :, pl.ds(hi, quarter)] = line(axis, step, row + hi, quarter)[...]
            whole[s, step] = sends.start(out_b.at[s, d], full.at[s, d], axis, step)
    near = {}
    for s, (axis, other, row) in enumerate(streams):
        yield
        for step in (1, -1):
            whole[s, step].wait_recv()
        sums[s] = plus(line(axis, 0, row, half)[...], full[s, 0], full[s, 1]).astype(BF)
        far = lax.rem((z if other == "z" else x) + 2, 4)
        near[s, 1] = sends.start(sums.at[s, :, far, pl.ds(0, quarter)], nlow.at[s, 0], other, 1)
        near[s, -1] = sends.start(
            sums.at[s, :, far, pl.ds(quarter, quarter)], nlow.at[s, 1], other, -1
        )
    for s, (axis, other, row) in enumerate(streams):
        yield
        at = z if other == "z" else x
        for d, step in enumerate((1, -1)):
            near[s, step].wait_recv()
            to = lax.rem(at + step + 4, 4)
            lo, hi = (0, quarter) if step == 1 else (quarter, 0)
            nout[s, d, :, pl.ds(lo, quarter)] = plus(
                sums[s, :, to, pl.ds(lo, quarter)], nlow[s, d]
            ).astype(BF)
            nout[s, d, :, pl.ds(hi, quarter)] = sums[s, :, to, pl.ds(hi, quarter)]
            whole[s, step] = sends.start(nout.at[s, d], nfull.at[s, d], other, step)
    swap = {}
    for s, (axis, other, row) in enumerate(streams):
        yield
        at = z if other == "z" else x
        for step in (1, -1):
            whole[s, step].wait_recv()
        mine[s] = plus(sums[s, :, at], nfull[s, 0], nfull[s, 1]).astype(BF)
        swap[s] = sends.start(mine.at[s, 1 - yh], y_in.at[s], "yhi", 1)
    yield
    for s, (axis, other, row) in enumerate(streams):
        swap[s].wait_recv()
        out_ref[pl.ds(row, half)] = plus(mine[s, yh], y_in[s])


def key_scratch():
    half, quarter, w = T // 2, T // 4, 640
    return [
        pltpu.VMEM((2, 2, 2, 4, quarter, w), BF),
        pltpu.VMEM((2, 2, 2, 4, half, w), BF),
        pltpu.VMEM((2, 2, 2, 4, half, w), BF),
        pltpu.VMEM((2, 2, 4, half, w), BF),
        pltpu.VMEM((2, 2, 2, quarter, w), BF),
        pltpu.VMEM((2, 2, 2, half, w), BF),
        pltpu.VMEM((2, 2, 2, half, w), BF),
        pltpu.VMEM((2, 2, half, w), BF),
        pltpu.VMEM((2, half, w), BF),
    ]


ROWS = 256
HALF = ROWS // 2
STREAMS = (("x", "z"), ("z", "x"))


def spots(me):
    return {"z": me[3], "x": me[4]}


def around(me, axis, step):
    return lax.rem(spots(me)[axis] + step + 4, 4)


def columns(me, axis, step, big):
    return pl.ds(pl.multiple_of(around(me, axis, step) * big, 128), big)


def halves(big):
    cut = (big // 2 + 127) // 128 * 128
    return (0, cut), (cut, big - cut)


def sum_steps(me, sends, g_ref, mine, swap_y, low, out_b, full, sums, nlow, nout, nfull, y_in):
    run, big = mine.shape[-2:]
    h = 4 * run
    cut = h // 2
    near, whole = {}, {}

    def parts(step):
        return (0, cut) if step == 1 else (cut, 0)

    for s, (axis, _) in enumerate(STREAMS):
        c = columns(me, axis, 2, big)
        for step in (1, -1):
            r = pl.ds(s * h + parts(step)[0], cut)
            near[s, step] = sends.start(g_ref.at[r, c], low.at[r], axis, step)
    for s, (axis, _) in enumerate(STREAMS):
        yield
        for d, step in enumerate((1, -1)):
            near[s, step].wait_recv()
            add, keep = (pl.ds(s * h + p, cut) for p in parts(step))
            c = columns(me, axis, step, big)
            out_b[d, add] = plus(g_ref[add, c], low[add]).astype(BF)
            out_b[d, keep] = g_ref[keep, c]
            r = pl.ds(s * h, h)
            whole[s, step] = sends.start(out_b.at[d, r], full.at[d, r], axis, step)

    def rows(s, other, step):
        return pl.ds(pl.multiple_of(s * h + around(me, other, step) * run, 16), run)

    for s, (axis, other) in enumerate(STREAMS):
        yield
        for step in (1, -1):
            whole[s, step].wait_recv()
        r = pl.ds(s * h, h)
        sums[r] = plus(g_ref[r, columns(me, axis, 0, big)], full[0, r], full[1, r]).astype(BF)
        for d, step in enumerate((1, -1)):
            c = pl.ds(*halves(big)[d])
            near[s, step] = sends.start(sums.at[rows(s, other, 2), c], nlow.at[s, :, c], other, step)
    for s, (axis, other) in enumerate(STREAMS):
        yield
        for d, step in enumerate((1, -1)):
            near[s, step].wait_recv()
            add, keep = pl.ds(*halves(big)[d]), pl.ds(*halves(big)[1 - d])
            r = rows(s, other, step)
            nout[s, d, :, add] = plus(sums[r, add], nlow[s, :, add]).astype(BF)
            nout[s, d, :, keep] = sums[r, keep]
            whole[s, step] = sends.start(nout.at[s, d], nfull.at[s, d], other, step)
    swap = {}
    for s, (axis, other) in enumerate(STREAMS):
        yield
        for step in (1, -1):
            whole[s, step].wait_recv()
        total = plus(sums[rows(s, other, 0)], nfull[s, 0], nfull[s, 1]).astype(BF)
        if swap_y:
            y_in[0, s] = total
            swap[s] = sends.start(y_in.at[0, s], y_in.at[1, s], "yhi", 1)
        else:
            mine[s] = total
    if swap_y:
        for s in range(2):
            yield
            swap[s].wait_recv()
            mine[s] = plus(y_in[0, s], y_in[1, s]).astype(BF)


def sum_scratch(width, h):
    big, run = width // 4, h // 4
    return [
        pltpu.VMEM((2 * h, big), BF),
        pltpu.VMEM((2, 2 * h, big), BF),
        pltpu.VMEM((2, 2 * h, big), BF),
        pltpu.VMEM((2 * h, big), BF),
        pltpu.VMEM((2, run, big), BF),
        pltpu.VMEM((2, 2, run, big), BF),
        pltpu.VMEM((2, 2, run, big), BF),
        pltpu.VMEM((2, 2, run, big), BF),
    ]


def spread_steps(me, sends, mine, out_ref, store_sems, to_y):
    run, big = mine.shape[-2:]
    h = 4 * run
    cut = h // 2
    near, whole, stored, last, over = {}, {}, [], {}, []

    def base(s):
        return s * HALF + (me[2] * h if to_y else 0)

    def rows(s, off, count):
        return pl.ds(pl.multiple_of(base(s) + off, 16), count)

    def block(s, axis, step, off, count):
        return out_ref.at[rows(s, off, count), columns(me, axis, step, big)]

    def on(ref):
        if to_y:
            over.append(sends.start(ref, ref, "yhi", 1))

    for s, (axis, other) in enumerate(STREAMS):
        ref = block(s, axis, 0, around(me, other, 0) * run, run)
        for step in (1, -1):
            near[s, step] = sends.start(mine.at[s], ref, other, step)
        stored.append(pltpu.make_async_copy(mine.at[s], ref, store_sems.at[s]))
        stored[-1].start()

    def narrow(s, axis, other, step, d):
        c0, n = halves(big)[d]
        c = pl.ds(pl.multiple_of(around(me, axis, 0) * big + c0, 128), n)
        return out_ref.at[rows(s, around(me, other, step) * run, run), c]

    for s, (axis, other) in enumerate(STREAMS):
        yield
        for d, step in enumerate((1, -1)):
            near[s, step].wait_recv()
            ref = narrow(s, axis, other, -step, d)
            whole[s, step] = sends.start(ref, ref, other, step)
    for s, (axis, other) in enumerate(STREAMS):
        yield
        for step in (1, -1):
            whole[s, step].wait_recv()
        stored[s].wait()
        ref = block(s, axis, 0, 0, h)
        for step in (1, -1):
            near[s, step] = sends.start(ref, ref, axis, step)
        on(ref)
    for s, (axis, other) in enumerate(STREAMS):
        yield
        for d, step in enumerate((1, -1)):
            near[s, step].wait_recv()
            ref = block(s, axis, -step, d * cut, cut)
            last[s, step] = sends.start(ref, ref, axis, step)
            on(block(s, axis, -step, 0, h))
    for s, (axis, other) in enumerate(STREAMS):
        yield
        for step in (1, -1):
            last[s, step].wait_recv()
        on(block(s, axis, 2, 0, h))
    if to_y:
        yield
        for copy in over:
            copy.wait_recv()


def halved_steps(me, sends, g_ref, mine, kept, got, out_ref, store_sems, *scratch):
    h = HALF // 2
    yh = me[2]
    copies = []
    for s in range(2):
        give = pl.ds(pl.multiple_of(s * HALF + (1 - yh) * h, 16), h)
        copies.append(sends.start(g_ref.at[give], got.at[pl.ds(s * h, h)], "yhi", 1))
    for s in range(2):
        yield
        copies[s].wait_recv()
        r = pl.ds(s * h, h)
        kept[r] = plus(g_ref[pl.ds(pl.multiple_of(s * HALF + yh * h, 16), h)], got[r]).astype(BF)
    yield
    yield from sum_steps(me, sends, kept, mine, False, *scratch)
    yield from spread_steps(me, sends, mine, out_ref, store_sems, True)


def vector_steps(sends, vec_ref, out_ref, keep, got):
    rounds = ((("core", 1),), (("ylo", 1),), (("x", 1), ("x", -1), ("x", 2)), (("z", 1), ("z", -1), ("z", 2)), (("yhi", 1),))
    keep[0] = vec_ref[...]
    k = 0
    for at, partners in enumerate(rounds):
        copies = []
        for axis, step in partners:
            copies.append((k, sends.start(keep.at[at], got.at[k], axis, step)))
            k += 1
        yield
        total = keep[at]
        for slot, copy in copies:
            copy.wait_recv()
            total = total + got[slot]
        keep[at + 1] = total
    out_ref[...] = keep[len(rounds)]


def small_steps(me, sends, g_ref, out_ref, got_x, got_z, got_y, sum_z, sum_y):
    x, z = me[4], me[3]
    steps = (1, -1, 2)

    def rows(at, step, count, base=0):
        return pl.ds(pl.multiple_of(base + lax.rem(at + step + 4, 4) * count, 16), count)

    copies = [
        sends.start(g_ref.at[rows(x, step, 64)], got_x.at[k], "x", step) for k, step in enumerate(steps)
    ]
    yield
    for copy in copies:
        copy.wait_recv()
    sum_z[...] = plus(g_ref[rows(x, 0, 64)], got_x[0], got_x[1], got_x[2]).astype(BF)
    copies = [
        sends.start(sum_z.at[rows(z, step, 16)], got_z.at[k], "z", step) for k, step in enumerate(steps)
    ]
    yield
    for copy in copies:
        copy.wait_recv()
    sum_y[...] = plus(sum_z[rows(z, 0, 16)], got_z[0], got_z[1], got_z[2]).astype(BF)
    copy = sends.start(sum_y, got_y, "yhi", 1)
    yield
    copy.wait_recv()
    ref = out_ref.at[rows(z, 0, 16, x * 64)]
    ref[...] = plus(sum_y[...], got_y[...]).astype(BF)
    copies = [sends.start(ref, ref, "z", step) for step in steps]
    yield
    for copy in copies:
        copy.wait_recv()
    ref = out_ref.at[rows(x, 0, 64)]
    copies = [sends.start(ref, ref, "x", step) for step in steps]
    yield
    for copy in copies:
        copy.wait_recv()


KEY_N, SUM_N = 9, 8
WIDE, REST = FF, 4608


def back_kernel(
    part_ref, g_in, dq_ref, d_attn_ref, mixture_ref, x1_ref, h_ref, d_mid_ref, out_ref, logit_ref, vec_ref, vec_part_ref,
    cos_ref, sin_ref, wq_in, wk_in, wv_in,
    gate_ref, up_ref, two_ref, three_ref, vec_out_ref, both_ref,
    own, ra, rb, xs, ra_all, rb_all, xs_all, xs_relay, g_two, g_three, d_x1_s, vec_all, keep_v, got_v,
    mine_gate, mine_up, mine_two, got_x, got_z, got_y, sum_z, sum_y,
    g_gate, g_up, kept, got_gate, wq, wk, wv, load_sems, store_sems,
    *scratch,
):
    me = here()
    key_scr, rest = scratch[:KEY_N], scratch[KEY_N:-2]
    gate_scr, up_scr, two_scr = rest[:SUM_N], rest[SUM_N : 2 * SUM_N], rest[2 * SUM_N :]
    loads = [
        pltpu.make_async_copy(a, b, load_sems.at[k])
        for k, (a, b) in enumerate(
            (
                (g_in.at[:, pl.ds(0, WIDE)], g_gate),
                (g_in.at[:, pl.ds(WIDE, WIDE)], g_up),
                (g_in.at[:, pl.ds(2 * WIDE, FF)], g_two.at[:, pl.ds(0, FF)]),
                (wq_in, wq),
                (wk_in, wk),
                (wv_in, wv),
            )
        )
    ]
    for copy in loads:
        copy.start()
    greet(me, NEAR + WEIGHT + FAR)
    sends = Sends(me, *scratch[-2:])
    odd = lax.rem(me[4], 2)
    keep = pl.ds(pl.multiple_of(odd * T, T), T)
    cosine, sine = cos_ref[...], sin_ref[...]
    mine = pl.ds(0, T)

    def turned_back(tile):
        return tile * cosine - swapped(tile) * sine

    def keys():
        yield from key_steps(me, sends, part_ref, own, *key_scr)
        for j in range(KV_HEADS):
            tile = turned_back(own[:, 128 * j : 128 * (j + 1)]).astype(BF)
            rb[:, HEAD_DIM * j : HEAD_DIM * (j + 1)] = tile[:, :HEAD_DIM]
            rb[:, 320 + HEAD_DIM * j : 320 + HEAD_DIM * (j + 1)] = tile[:, HEAD_DIM:]
        share = everyone_steps(sends, (("all", rb, rb_all, None),))
        next(share)
        rb_all[mine] = rb[...]
        d_k, d_v = rb[:, :320], rb[:, 320:]
        d_x1 = d_x1_s[...] + jnp.concatenate(
            our_order(me, [dot(d_k, wk[k]) + dot(d_v, wv[k]) for k in range(4)]), axis=1
        )
        h = h_ref[...]
        r1 = lax.rsqrt(jnp.mean(h * h, axis=-1, keepdims=True) + EPS)
        d_first, g_gain_a = norm_back_rows(h, r1, vec_ref[0:1, :D], d_x1)
        d_h = d_mid_ref[...] + d_first + logit_ref[:, 0:1] * vec_ref[2:3, :D]
        both_ref[keep, :D] = out_ref[...]
        both_ref[keep, D:] = d_h.astype(BF)
        swap = sends.start(both_ref.at[keep], both_ref.at[keep], "pair", 1)
        vec_all[...] = vec_part_ref[...]
        vec_all[0:1, :D] = g_gain_a
        vectors = vector_steps(sends, vec_all, vec_out_ref, keep_v, got_v)
        next(vectors)
        yield
        next(share)
        yield
        together(share)
        g_three[...] = dot(xs_all[:, :256], rb_all[...], TN).astype(BF)
        small = small_steps(me, sends, g_three, three_ref, got_x, got_z, got_y, sum_z, sum_y)
        while True:
            for step in (small, vectors):
                next(step, None)
            if small.gi_frame is None and vectors.gi_frame is None:
                break
            yield
        swap.wait_recv()

    def queries():
        for j in range(KV_HEADS):
            for g in range(GROUPS):
                at = HEAD_DIM * (GROUPS * j + g)
                ra[:, at : at + HEAD_DIM] = turned_back(dq_ref[j, g * T : (g + 1) * T]).astype(BF)[:, :HEAD_DIM]
        ra[:, D:] = d_attn_ref[...]
        xs[...] = jnp.zeros_like(xs)
        for k, (a, b) in enumerate(zip(our_order(me, cut_four(x1_ref)), our_order(me, cut_four(mixture_ref)))):
            xs[k, :, :240] = a
            xs[k, :, 256:496] = b
        share = everyone_steps(
            sends, (("all", ra, ra_all, None), ("one", [xs.at[k] for k in range(4)], xs_all, xs_relay))
        )
        next(share)
        ra_all[mine] = ra[...]
        xs_all[mine] = xs[0]
        d_q = ra[:, :D]
        for copy in loads[2:]:
            copy.wait()
        d_x1_s[...] = jnp.concatenate(our_order(me, [dot(d_q, wq[k], NT) for k in range(4)]), axis=1)
        g_two[:, FF + 2 * D :] = jnp.zeros((ROWS, 128), BF)
        yield
        next(share)
        yield
        together(share)
        g_two[:, FF : FF + D] = dot(xs_all[:, :256], ra_all[:, :D], TN).astype(BF)
        g_two[:, FF + D : FF + 2 * D] = dot(xs_all[:, 256:], ra_all[:, D:], TN).astype(BF)
        yield from sum_steps(me, sends, g_two, mine_two, True, *two_scr)
        yield from spread_steps(me, sends, mine_two, two_ref, store_sems.at[pl.ds(4, 2)], False)

    def gate():
        loads[0].wait()
        yield from halved_steps(
            me, sends, g_gate, mine_gate, kept, got_gate, gate_ref, store_sems.at[pl.ds(0, 2)], *gate_scr
        )

    def up():
        loads[1].wait()
        yield from sum_steps(me, sends, g_up, mine_up, True, *up_scr)
        yield from spread_steps(me, sends, mine_up, up_ref, store_sems.at[pl.ds(2, 2)], False)

    run_lanes({"k": keys(), "g": gate(), "u": up(), "q": queries()}, ORDER)
    sends.finish()


ORDER = (
    "kuqgkkuuqgkkqkkgguuqkkguugqukqgkguqkuguq"
    "gquqgukguqugqqgkgqqgukgqqkgguugqquqqgk"
)


def back(*args):
    vmem, hbm = pl.BlockSpec(memory_space=pltpu.VMEM), pl.BlockSpec(memory_space=pl.ANY)
    return pl.pallas_call(
        back_kernel,
        name="back",
        out_shape=(
            jax.ShapeDtypeStruct((ROWS, WIDE), BF),
            jax.ShapeDtypeStruct((ROWS, WIDE), BF),
            jax.ShapeDtypeStruct((ROWS, REST), BF),
            jax.ShapeDtypeStruct((ROWS, 640), BF),
            jax.ShapeDtypeStruct((8, 1024), F32),
            jax.ShapeDtypeStruct((PAIR, 2 * D), BF),
        ),
        in_specs=[vmem, hbm] + [vmem] * (len(args) - 5) + [hbm] * 3,
        out_specs=(hbm,) * 3 + (vmem,) * 3,
        scratch_shapes=[
            pltpu.VMEM((T, 640), F32),
            pltpu.VMEM((T, 2 * D), BF),
            pltpu.VMEM((T, 640), BF),
            pltpu.VMEM((4, T, 512), BF),
            pltpu.VMEM((4 * T, 2 * D), BF),
            pltpu.VMEM((4 * T, 640), BF),
            pltpu.VMEM((4 * T, 512), BF),
            pltpu.VMEM((T, 512), BF),
            pltpu.VMEM((ROWS, REST), BF),
            pltpu.VMEM((ROWS, 640), BF),
            pltpu.VMEM((T, D), F32),
            pltpu.VMEM((8, 1024), F32),
            pltpu.VMEM((6, 8, 1024), F32),
            pltpu.VMEM((9, 8, 1024), F32),
            pltpu.VMEM((2, HALF // 8, WIDE // 4), BF),
            pltpu.VMEM((2, HALF // 4, WIDE // 4), BF),
            pltpu.VMEM((2, HALF // 4, REST // 4), BF),
            pltpu.VMEM((3, 64, 640), BF),
            pltpu.VMEM((3, 16, 640), BF),
            pltpu.VMEM((16, 640), BF),
            pltpu.VMEM((64, 640), BF),
            pltpu.VMEM((16, 640), BF),
            pltpu.VMEM((ROWS, WIDE), BF),
            pltpu.VMEM((ROWS, WIDE), BF),
            pltpu.VMEM((HALF, WIDE), BF),
            pltpu.VMEM((HALF, WIDE), BF),
            pltpu.VMEM((4, 240, 960), BF),
            pltpu.VMEM((4, 320, 240), BF),
            pltpu.VMEM((4, 320, 240), BF),
            pltpu.SemaphoreType.DMA((6,)),
            pltpu.SemaphoreType.DMA((6,)),
        ]
        + key_scratch()
        + sum_scratch(WIDE, HALF // 2)
        + sum_scratch(WIDE, HALF)
        + sum_scratch(REST, HALF)
        + sems(190),
        compiler_params=pltpu.CompilerParams(
            collective_id=2, has_side_effects=True, vmem_limit_bytes=VMEM_LIMIT
        ),
        cost_estimate=pl.CostEstimate(flops=2_000_000_000, bytes_accessed=200_000_000, transcendentals=0),
    )(*args)


def finish_kernel(
    g_gate_ref, g_up_ref, two_ref, three_ref, vec_ref, both_ref, place_ref, hidden_ref, d_out_ref,
    out_ref, d_hidden_ref, query_ref, key_ref, value_ref, output_ref, gate_ref, up_ref, down_ref, vec_out_ref,
    low_one, low_two, low_three, wide_one, wide_two, wide_down, wide_kv, rows, load_sems, store_sems,
):
    keep = pl.ds(0, 240)
    runs_one = [pl.ds(1280 * k, 1280) for k in range(2)]
    runs_two = [pl.ds(640 * k, 640) for k in range(4)] + [pl.ds(FF, 2 * D)]
    loads = []
    for src, dst, runs in (
        (g_gate_ref, low_one.at[0], runs_one),
        (g_up_ref, low_one.at[1], runs_one),
        (two_ref, low_two, runs_two),
        (three_ref, low_three, [pl.ds(0, 640)]),
    ):
        for c in runs:
            loads.append(pltpu.make_async_copy(src.at[keep, c], dst.at[:, c], load_sems.at[len(loads)]))
            loads[-1].start()
    stores = []

    def store(a, b):
        stores.append(pltpu.make_async_copy(a, b, store_sems.at[len(stores)]))
        stores[-1].start()

    for k, (base, to) in enumerate(((hidden_ref, out_ref), (d_out_ref, d_hidden_ref))):
        rows[k] = base[...] + dot(both_ref[:, D * k : D * (k + 1)], place_ref[...], TN)
        store(rows.at[k], to)
    for k in range(4):
        loads[k].wait()
        c = runs_one[k % 2]
        wide_one[k // 2, :, c] = low_one[k // 2, :, c].astype(F32)
        store(wide_one.at[k // 2, :, c], (gate_ref, up_ref)[k // 2].at[:, c])
    for k in range(4):
        loads[4 + k].wait()
        r = pl.ds(240 * k, 240)
        wide_down[r] = low_two[:, runs_two[k]].astype(F32)
        store(wide_down.at[r], down_ref.at[r])
    loads[8].wait()
    for k, to in enumerate((query_ref, output_ref)):
        wide_two[k] = low_two[:, FF + D * k : FF + D * (k + 1)].astype(F32)
        store(wide_two.at[k], to)
    loads[9].wait()
    for k, to in enumerate((key_ref, value_ref)):
        wide_kv[k] = low_three[:, 320 * k : 320 * (k + 1)].astype(F32).T
        store(wide_kv.at[k], to)
    core, ylo = lax.axis_index("core") == 1, lax.axis_index("ylo") == 1
    p = [vec_ref[:, 240 * k : 240 * (k + 1)] for k in range(4)]
    vec_out_ref[...] = jnp.where(ylo, jnp.where(core, p[3], p[2]), jnp.where(core, p[1], p[0]))
    for copy in stores:
        copy.wait()


def finish(*args):
    vmem, hbm = pl.BlockSpec(memory_space=pltpu.VMEM), pl.BlockSpec(memory_space=pl.ANY)
    shapes = [(D, PAIR), (D, PAIR), (240, D), (320, 240), (320, 240), (240, D), (240, FF), (240, FF), (D, 640), (8, 240)]
    return pl.pallas_call(
        finish_kernel,
        name="finish",
        out_shape=tuple(jax.ShapeDtypeStruct(shape, F32) for shape in shapes),
        in_specs=[hbm] * 4 + [vmem] * 5,
        out_specs=(hbm,) * 9 + (vmem,),
        scratch_shapes=[
            pltpu.VMEM((2, 240, WIDE), BF),
            pltpu.VMEM((240, REST), BF),
            pltpu.VMEM((240, 640), BF),
            pltpu.VMEM((2, 240, WIDE), F32),
            pltpu.VMEM((2, 240, D), F32),
            pltpu.VMEM((D, 640), F32),
            pltpu.VMEM((2, 320, 240), F32),
            pltpu.VMEM((2, D, PAIR), F32),
            pltpu.SemaphoreType.DMA((10,)),
            pltpu.SemaphoreType.DMA((14,)),
        ],
        compiler_params=pltpu.CompilerParams(vmem_limit_bytes=VMEM_LIMIT),
        cost_estimate=pl.CostEstimate(flops=0, bytes_accessed=16_000_000, transcendentals=0),
    )(*args)


def shard_of(me, k):
    ylo, core = me[0], me[1]
    return (ylo if k < 2 else 1 - ylo) * 2 + (core if k % 2 == 0 else 1 - core)


def our_order(me, p):
    core, ylo = me[1] == 1, me[0] == 1
    p = [jnp.where(core, p[k ^ 1], p[k]) for k in range(4)]
    return [jnp.where(ylo, p[k ^ 2], p[k]) for k in range(4)]


def cut_four(ref):
    return [ref[:, 240 * k : 240 * (k + 1)] for k in range(4)]


def norm_back_rows(z, r, gain, dy):
    dz = r * (gain * dy) - z * (r * r * r) * jnp.mean(gain * dy * z, axis=-1, keepdims=True)
    return dz, jnp.sum(dy * z * r, axis=0, keepdims=True)


def everyone_steps(sends, pieces):
    half = T // 2
    arrived, last = [], []
    for kind, source, whole, relay in pieces:
        near = source if kind == "all" else source[1]
        last.append(sends.start(near, whole.at[pl.ds(T, T)], "core", 1))
    for step, at in ((1, 0), (-1, half)):
        r = pl.ds(at, half)
        for kind, source, whole, relay in pieces:
            far = source if kind == "all" else source[2]
            arrived.append((sends.start(far.at[r], whole.at[pl.ds(2 * T + at, half)], "y", step), None))
            if kind == "all":
                arrived[-1] = (arrived[-1][0], (whole.at[pl.ds(2 * T + at, half)], whole.at[pl.ds(3 * T + at, half)]))
            else:
                copy = sends.start(source[3].at[r], relay.at[r], "y", step)
                arrived.append((copy, (relay.at[r], whole.at[pl.ds(3 * T + at, half)])))
    yield
    for copy, onward in arrived:
        copy.wait_recv()
        if onward is not None:
            last.append(sends.start(onward[0], onward[1], "core", 1))
    yield
    for copy in last:
        copy.wait_recv()


def dense_kernel(
    mix_ref, q_ref, prob_in, kv_in, h_ref, up_ref, vec_ref,
    wo_ref, wg_ref, wu_ref, wd_ref, wos_ref, wgs_ref, wus_ref, wds_ref,
    dq_ref, dkv_out, g_out, d_attn_ref, mixture_ref, d_mid_ref, out_ref, logit_ref, vec_out_ref,
    wo, wg, wu, wd, mixf, gate_s, up_s, inner, dgu, dffn, xs, do_s, d_mix_s,
    dgu_all, dffn_all, xs_all, inner_all, xs_relay, inner_relay,
    prob_ref, kv_ref, dkv_ref, g_ref,
    load_sems, store_sems, send_sems, recv_sems,
):
    me = here()
    loads = []
    for k, (own, rest, to) in enumerate(
        ((wo_ref, wos_ref, wo), (wg_ref, wgs_ref, wg), (wu_ref, wus_ref, wu), (wd_ref, wds_ref, wd))
    ):
        there = to.at[pl.ds(1, 3)] if k < 3 else to.at[pl.ds(2, 1)]
        pair = (
            pltpu.make_async_copy(own, to.at[0], load_sems.at[2 * k]),
            pltpu.make_async_copy(rest, there, load_sems.at[2 * k + 1]),
        )
        for copy in pair:
            copy.start()
        loads.append(pair)
    loads.append(
        (
            pltpu.make_async_copy(prob_in, prob_ref, load_sems.at[8]),
            pltpu.make_async_copy(kv_in, kv_ref, load_sems.at[9]),
        )
    )
    for copy in loads[4]:
        copy.start()
    greet(me, WEIGHT)
    sends = Sends(me, send_sems, recv_sems)
    down = [
        sends.start(wd_ref, wd.at[1], "core", 1),
        sends.start(wds_ref.at[0], wd.at[3], "core", 1),
    ]
    shards = [shard_of(me, k) for k in range(4)]

    def run640(k):
        return pl.ds(pl.multiple_of(shards[k] * 640, 128), 640)

    def run640_up(k):
        return pl.ds(pl.multiple_of(FF + shards[k] * 640, 128), 640)

    def loaded(k):
        for copy in loads[k]:
            copy.wait()

    for j in range(KV_HEADS):
        for g in range(GROUPS):
            h = GROUPS * j + g
            mixf[:, HEAD_DIM * h : HEAD_DIM * (h + 1)] = mix_ref[j, g * T : (g + 1) * T, HEAD_DIM:]
    mixture_ref[...] = mixf[...].astype(BF)
    mix_k = our_order(me, cut_four(mixture_ref))
    loaded(0)
    attn_out = sum(dot(mix_k[k], wo[k]) for k in range(4))
    hidden = h_ref[...]
    gain_f = vec_ref[1:2, :D]
    route_w = vec_ref[2:3, :D]
    middle = hidden + attn_out
    r2 = lax.rsqrt(jnp.mean(middle * middle, axis=-1, keepdims=True) + EPS)
    x2 = middle * r2 * gain_f
    x2_k = our_order(me, [x2[:, 240 * k : 240 * (k + 1)].astype(BF) for k in range(4)])
    xs[...] = jnp.zeros_like(xs)
    for k in range(4):
        xs[k, :, :240] = x2_k[k]
    loaded(1)
    gate_s[...] = sum(dot(x2_k[k], wg[k]) for k in range(4))
    loaded(2)
    up_s[...] = sum(dot(x2_k[k], wu[k]) for k in range(4))
    gate = gate_s[...]
    inner[...] = (gate * jax.nn.sigmoid(gate) * up_s[...]).astype(BF)
    loaded(3)
    for copy in down:
        copy.wait_recv()
    ffn_out = sum(dot(inner[:, run640(k)], wd[k], NT) for k in range(4))
    route = jax.nn.sigmoid(jnp.sum(hidden * route_w, axis=-1, keepdims=True))
    branch = attn_out + ffn_out
    out_ref[...] = (route * branch).astype(BF)
    upstream = up_ref[...]
    d_branch = upstream * route
    d_logit = route * (1.0 - route) * jnp.sum(upstream * branch, axis=-1, keepdims=True)
    logit_ref[...] = jnp.broadcast_to(d_logit, logit_ref.shape)
    vec_out_ref[...] = jnp.zeros_like(vec_out_ref)
    vec_out_ref[2:3, :D] = jnp.sum(d_logit * hidden, axis=0, keepdims=True)
    d_ffn = d_branch.astype(BF)
    own = pl.ds(0, T)
    dffn[...] = jnp.zeros_like(dffn)
    for k in range(4):
        dffn[:, 256 * k : 256 * k + 240] = d_branch[:, 240 * k : 240 * (k + 1)].astype(BF)
    share_one = everyone_steps(
        sends,
        (
            ("all", dffn, dffn_all, None),
            ("one", [inner.at[:, run640(k)] for k in range(4)], inner_all, inner_relay),
            ("one", [xs.at[k] for k in range(4)], xs_all, xs_relay),
        ),
    )
    next(share_one)
    dffn_all[own], xs_all[own], inner_all[own] = dffn[...], xs[0], inner[:, run640(0)]
    for k in range(4):
        d_inner = dot(d_ffn, wd[k])
        gate, up = gate_s[:, run640(k)], up_s[:, run640(k)]
        sg = jax.nn.sigmoid(gate)
        dgu[:, run640(k)] = (d_inner * up * (sg + gate * sg * (1.0 - sg))).astype(BF)
        dgu[:, run640_up(k)] = (d_inner * (gate * sg)).astype(BF)
    share_two = everyone_steps(sends, (("all", dgu, dgu_all, None),))
    next(share_two)
    next(share_one)
    dgu_all[own] = dgu[...]
    d_gate, d_up = dgu[:, :FF], dgu[:, FF:]
    d_x2 = jnp.concatenate(
        our_order(me, [dot(d_gate, wg[k], NT) + dot(d_up, wu[k], NT) for k in range(4)]), axis=1
    )
    d_mid, g_gain_f = norm_back_rows(middle, r2, gain_f, d_x2)
    d_mid_ref[...] = d_mid
    vec_out_ref[1:2, :D] = g_gain_f
    d_attn = (d_branch + d_mid).astype(BF)
    d_attn_ref[...] = d_attn
    d_mix_s[...] = jnp.concatenate(our_order(me, [dot(d_attn, wo[k], NT) for k in range(4)]), axis=1)
    do_s[...] = jnp.zeros_like(do_s)
    for j in range(KV_HEADS):
        for g in range(GROUPS):
            h = GROUPS * j + g
            do_s[j, g * T : (g + 1) * T, HEAD_DIM:] = d_mix_s[:, HEAD_DIM * h : HEAD_DIM * (h + 1)].astype(BF)

    stores = []

    def store(a, b):
        stores.append(pltpu.make_async_copy(a, b, store_sems.at[KV_HEADS + len(stores)]))
        stores[-1].start()

    together(share_one)
    for k in range(4):
        c = pl.ds(2 * FF + 640 * k, 640)
        g_ref[:, c] = dot(dffn_all[:, 256 * k : 256 * (k + 1)], inner_all[...], TN).astype(BF)
        store(g_ref.at[:, c], g_out.at[:, c])
    loaded(4)

    @pl.loop(0, KV_HEADS)
    def _(j):
        c = pl.ds(pl.multiple_of(j * 128, 128), 128)
        tile = kv_ref[:, :, :, :, c].reshape(KEYS, 128)
        prob, d_out = prob_ref[j], do_s[j]
        d_prob = dot(d_out, tile, NT)
        delta = jnp.sum(d_out.astype(F32) * mix_ref[j], axis=-1, keepdims=True)
        d_score = (prob.astype(F32) * (d_prob - delta)).astype(BF)
        dq_ref[j] = dot(d_score, tile) * SCALE
        grad = dot(d_score, q_ref[j], TN) * SCALE + dot(prob, d_out, TN)
        dkv_ref[:, :, :, :, c] = grad.astype(BF).reshape(2, 4, 4, T, 128)
        pltpu.make_async_copy(dkv_ref.at[:, :, :, :, c], dkv_out.at[:, :, :, :, c], store_sems.at[j]).start()

    together(share_two)
    for at in range(0, 2 * FF, 1280):
        c = pl.ds(at, 1280)
        g_ref[:, c] = dot(xs_all[...], dgu_all[:, c], TN).astype(BF)
        store(g_ref.at[:, c], g_out.at[:, c])
    for j in range(KV_HEADS):
        c = pl.ds(j * 128, 128)
        pltpu.make_async_copy(dkv_ref.at[:, :, :, :, c], dkv_out.at[:, :, :, :, c], store_sems.at[j]).wait()
    for copy in stores:
        copy.wait()
    sends.finish()


def dense(mix, q, prob, kv, h, up_c, vec, own, rest):
    vmem, hbm = pl.BlockSpec(memory_space=pltpu.VMEM), pl.BlockSpec(memory_space=pl.ANY)
    rows = GROUPS * T
    return pl.pallas_call(
        dense_kernel,
        name="dense",
        out_shape=(
            jax.ShapeDtypeStruct((KV_HEADS, rows, 128), F32),
            jax.ShapeDtypeStruct((2, 4, 4, T, 640), BF),
            jax.ShapeDtypeStruct((ROWS, 3 * FF), BF),
            jax.ShapeDtypeStruct((T, D), BF),
            jax.ShapeDtypeStruct((T, D), BF),
            jax.ShapeDtypeStruct((T, D), F32),
            jax.ShapeDtypeStruct((T, D), BF),
            jax.ShapeDtypeStruct((T, 128), F32),
            jax.ShapeDtypeStruct((8, 1024), F32),
        ),
        in_specs=[vmem] * 2 + [hbm] * 2 + [vmem] * 3 + [hbm] * 8,
        out_specs=(vmem,) + (hbm,) * 2 + (vmem,) * 6,
        scratch_shapes=[
            pltpu.VMEM((4, 240, D), BF),
            pltpu.VMEM((4, 240, FF), BF),
            pltpu.VMEM((4, 240, FF), BF),
            pltpu.VMEM((4, D, 640), BF),
            pltpu.VMEM((T, D), F32),
            pltpu.VMEM((T, FF), F32),
            pltpu.VMEM((T, FF), F32),
            pltpu.VMEM((T, FF), BF),
            pltpu.VMEM((T, 2 * FF), BF),
            pltpu.VMEM((T, 1024), BF),
            pltpu.VMEM((4, T, 256), BF),
            pltpu.VMEM((KV_HEADS, rows, 128), BF),
            pltpu.VMEM((T, D), F32),
            pltpu.VMEM((4 * T, 2 * FF), BF),
            pltpu.VMEM((4 * T, 1024), BF),
            pltpu.VMEM((4 * T, 256), BF),
            pltpu.VMEM((4 * T, 640), BF),
            pltpu.VMEM((T, 256), BF),
            pltpu.VMEM((T, 640), BF),
            pltpu.VMEM((KV_HEADS, rows, KEYS), BF),
            pltpu.VMEM((2, 4, 4, T, 640), BF),
            pltpu.VMEM((2, 4, 4, T, 640), BF),
            pltpu.VMEM((ROWS, 3 * FF), BF),
            pltpu.SemaphoreType.DMA((10,)),
            pltpu.SemaphoreType.DMA((13,)),
        ]
        + sems(28),
        compiler_params=pltpu.CompilerParams(
            collective_id=4, has_side_effects=True, vmem_limit_bytes=VMEM_LIMIT
        ),
        cost_estimate=pl.CostEstimate(
            flops=20_000_000_000, bytes_accessed=40_000_000, transcendentals=0
        ),
    )(mix, q, prob, kv, h, up_c, vec, *own, *rest)


def per_device(hidden, chosen, positions, w_query, w_key, w_value, w_output, w_gate, w_up, w_down, gain_attn, gain_ffn, router, d_out):
    tokens, upstream = hidden[0], d_out[0]
    own_w = (w_output, w_gate, w_up, w_down.T)
    frequency = THETA ** (-jnp.arange(0, HEAD_DIM // 2).astype(F32) * 2.0 / HEAD_DIM)
    vec = jnp.stack([gain_attn, gain_ffn, router]).astype(F32)
    vec = jnp.pad(vec, ((0, 5), (0, 16)))
    (
        mix_heads, prob, q_heads, kv_all, h, up_c, x1, cosine, sine, place, vec_in, wq, wk, wv, *rest_w
    ) = front(
        tokens.T, upstream.T, chosen, positions, jnp.tile(frequency, 4)[None, :], vec,
        w_query, w_key.T, w_value.T, *own_w
    )
    d_q_heads, d_kv, g_one, d_attn, mixture, d_mid, out_c, d_logit, vec_out = dense(
        mix_heads, q_heads, prob, kv_all, h, up_c, vec_in, own_w, rest_w
    )
    s_gate, s_up, s_two, s_three, vector, both = back(
        d_kv, g_one, d_q_heads, d_attn, mixture, x1, h, d_mid, out_c, d_logit, vec_in, vec_out, cosine, sine, wq, wk, wv
    )
    output, d_tokens, g_query, g_key, g_value, g_output, g_gate, g_up, g_down, vectors = finish(
        s_gate, s_up, s_two, s_three, vector, both, place, tokens.T, upstream.T
    )
    return (
        output.T[None],
        d_tokens.T[None],
        g_query,
        g_key.T,
        g_value.T,
        g_output,
        g_gate,
        g_up,
        g_down.T,
        vectors[0],
        vectors[1],
        vectors[2],
    )


def solution(mesh):
    finer = Mesh(mesh.devices.reshape(DIMS), AX)
    shard, blk = ("ylo", "core"), ("yhi", "z", "x")
    act, row, weight, vec = P(shard, blk, None), P(shard, blk), P(shard, None), P(shard)
    return jax.shard_map(
        per_device,
        mesh=finer,
        in_specs=(act, row, row) + (weight,) * 7 + (vec,) * 3 + (act,),
        out_specs=(act, act) + (weight,) * 7 + (vec,) * 3,
        check_vma=False,
    )
```

```python
import functools

import jax
import jax.numpy as jnp
import numpy as np
from jax import lax
from jax.experimental import pallas as pl
from jax.experimental.pallas import tpu as pltpu
from jax.sharding import Mesh
from jax.sharding import PartitionSpec as P

D = 960
HEADS = 15
KV_HEADS = 5
GROUPS = 3
HEAD_DIM = 64
FF = 2560
EPS = 1e-05
THETA = 10000.0
SCALE = HEAD_DIM ** (-0.5)
T = 64
PAIR = 128
SLOTS = 32
KEYS = SLOTS * T
AX = ("ylo", "core", "yhi", "z", "x")
DIMS = (2, 2, 2, 4, 4)
MESH = pl.DeviceIdType.MESH
BF = jnp.bfloat16
F32 = jnp.float32
VMEM_LIMIT = 56 * 2**20


def dot(a, b, dims=(((1,), (0,)), ((), ()))):
    return lax.dot_general(a, b, dims, preferred_element_type=F32)


NT = (((1,), (1,)), ((), ()))
TN = (((0,), (0,)), ((), ()))


def here():
    return tuple(lax.axis_index(a) for a in AX)


def neighbour(me, axis, step):
    ylo, core, yhi, z, x = me
    if axis == "z":
        z = lax.rem(z + step + 4, 4)
    elif axis == "x":
        x = lax.rem(x + step + 4, 4)
    elif axis == "pair":
        x = x + 1 - 2 * lax.rem(x, 2)
    elif axis == "yhi":
        yhi = 1 - yhi
    elif axis == "ylo":
        ylo = 1 - ylo
    elif axis == "core":
        core = 1 - core
    else:
        y = lax.rem(yhi * 2 + ylo + step + 4, 4)
        ylo, yhi = lax.rem(y, 2), y // 2
    return (ylo, core, yhi, z, x)


NEAR = (("x", 1), ("x", -1), ("z", 1), ("z", -1), ("yhi", 1))
WEIGHT = (("y", 1), ("y", -1), ("core", 1))
FAR = (("x", 2), ("z", 2))


def greet(me, partners):
    barrier = pltpu.get_barrier_semaphore()
    for axis, step in partners:
        pl.semaphore_signal(
            barrier, inc=1, device_id=neighbour(me, axis, step), device_id_type=MESH
        )
    pl.semaphore_wait(barrier, len(partners))


class Sends:
    def __init__(self, me, send_sems, recv_sems):
        self.me, self.send_sems, self.recv_sems, self.all = me, send_sems, recv_sems, []

    def start(self, src, dst, axis, step):
        k = len(self.all)
        copy = pltpu.make_async_remote_copy(
            src_ref=src,
            dst_ref=dst,
            send_sem=self.send_sems.at[k],
            recv_sem=self.recv_sems.at[k],
            device_id=neighbour(self.me, axis, step),
            device_id_type=MESH,
        )
        copy.start()
        self.all.append(copy)
        return copy

    def finish(self):
        for copy in self.all:
            copy.wait_send()


def together(*steps):
    steps = list(steps)
    while steps:
        for step in list(steps):
            try:
                next(step)
            except StopIteration:
                steps.remove(step)


def run_lanes(lanes, order):
    for c in order:
        next(lanes[c], None)
    together(*lanes.values())


def sems(count):
    return [pltpu.SemaphoreType.DMA((count,)), pltpu.SemaphoreType.DMA((count,))]


def plus(*terms):
    total = terms[0].astype(F32)
    for term in terms[1:]:
        total = total + term.astype(F32)
    return total


class Shards:
    def __init__(self, sends):
        self.sends, self.arrived, self.last = sends, [], []
        self.color = lax.rem(sends.me[3] + sends.me[4], 2)

    def near(self, own, out):
        self.last.append(self.sends.start(own, out.at[out.shape[0] - 3], "core", 1))

    def far(self, own, out, cut):
        for step, row, rows in ((1, 0, cut), (-1, cut, own.shape[0] - cut)):
            r = pl.ds(row, rows)
            ref = out.at[out.shape[0] - 2, r]
            self.arrived.append((ref, out.at[out.shape[0] - 1, r], self.sends.start(own.at[r], ref, "y", step)))

    def relay(self):
        for ref, to, copy in self.arrived:
            copy.wait_recv()
            self.last.append(self.sends.start(ref, to, "core", 1))
        self.arrived = []

    def finish(self):
        self.relay()
        for copy in self.last:
            copy.wait_recv()
        self.last = []

    def half(self, own, out, block, cuts):
        rows, slots = own.shape[0], out.shape[0]
        sub = block // 2
        mine = self.color * (rows - block)
        relay = slots > 1
        other = slots - 2 if relay else 0

        def part(slot, start, count):
            return out.at[slot, pl.ds(pl.multiple_of(start, 16), count)]

        copies = []
        for step, off in ((1, 0), (-1, sub)):
            src = own.at[pl.ds(pl.multiple_of(mine + off, 16), sub)]
            copies.append(self.sends.start(src, part(other, mine + off, sub), "y", step))
        if relay:
            self.near(own, out)
        yield
        for copy in copies:
            copy.wait_recv()
        copies, off = [], 0
        for (axis, step), count in zip((("x", 1), ("x", -1), ("z", 1), ("z", -1)), cuts):
            ref = part(other, self.color * block + off, count)
            copies.append(self.sends.start(ref, ref, axis, step))
            off += count
        if relay:
            self.last.append(self.sends.start(part(other, mine, block), part(slots - 1, mine, block), "core", 1))
        yield
        for copy in copies:
            copy.wait_recv()
        rest = (1 - self.color) * block
        if relay:
            self.last.append(
                self.sends.start(part(other, rest, rows - block), part(slots - 1, rest, rows - block), "core", 1)
            )


def gather_steps(me, sends, kv_ref, out_ref):
    _, _, yh, z, x = me
    oy = 1 - yh
    half, quarter = T // 2, T // 4
    streams = (("x", "z", 0), ("z", "x", half))

    def slot(y, axis, step, rows, count):
        zz = lax.rem(z + step + 4, 4) if axis == "z" else z
        xx = lax.rem(x + step + 4, 4) if axis == "x" else x
        return out_ref.at[y, zz, xx, pl.ds(rows, count)]

    def line(y, axis, step, rows, count):
        if axis == "z":
            return out_ref.at[y, lax.rem(z + step + 4, 4), :, pl.ds(rows, count)]
        return out_ref.at[y, :, lax.rem(x + step + 4, 4), pl.ds(rows, count)]

    own = out_ref.at[yh, z, x]
    own[...] = kv_ref[...]
    first = sends.start(kv_ref, own, "yhi", 1)
    got = {}
    for y, tag in ((yh, 0), (oy, 1)):
        if tag:
            yield
            first.wait_recv()
        for axis, _, row in streams:
            src = slot(y, axis, 0, row, half)
            for step in (1, -1):
                got[tag, row, step] = sends.start(src, src, axis, step)
    far = {}
    for y, tag in ((yh, 0), (oy, 1)):
        yield
        for axis, _, row in streams:
            for step, off in ((1, 0), (-1, quarter)):
                got[tag, row, step].wait_recv()
                src = slot(y, axis, -step, row + off, quarter)
                far[tag, row, step] = sends.start(src, src, axis, step)
    wide = {}
    for y, tag in ((yh, 0), (oy, 1)):
        yield
        for _, axis, row in streams:
            for step in (1, -1):
                far[tag, row, step].wait_recv()
            src = line(y, axis, 0, row, half)
            for step in (1, -1):
                wide[tag, row, step] = sends.start(src, src, axis, step)
    last = []
    for y, tag in ((yh, 0), (oy, 1)):
        yield
        for _, axis, row in streams:
            for step, off in ((1, 0), (-1, quarter)):
                wide[tag, row, step].wait_recv()
                src = line(y, axis, -step, row + off, quarter)
                last.append(sends.start(src, src, axis, step))
    yield
    for copy in last:
        copy.wait_recv()


def swapped(x):
    lane = lax.broadcasted_iota(jnp.int32, x.shape, 1)
    return jnp.where(lane < HEAD_DIM // 2, pltpu.roll(x, 96, 1), pltpu.roll(x, 32, 1))


def front_kernel(
    hidden_ref, d_out_ref, chosen_ref, pos_ref, freq_ref, vec_ref, wq_ref, wk_ref, wv_ref,
    wo_ref, wg_ref, wu_ref, wd_ref,
    mix_ref, prob_out, q_ref, kv_out, h_ref, up_ref, x1_ref, cos_ref, sin_ref, place_ref, vec_out_ref,
    wq_out, wk_out, wv_out, wos_ref, wgs_ref, wus_ref, wds_ref,
    compact_h, compact_d, compact_p, got_h, got_d, got_p, vecs, q_pre, kv_own,
    prob_ref, kv_ref, wq, wk, wv,
    load_sems, store_sems, send_sems, recv_sems,
):
    me = here()
    yhi, z, x = me[2:]
    loads = []
    for k, (own, to) in enumerate(((wq_ref, wq), (wk_ref, wk), (wv_ref, wv))):
        loads.append(pltpu.make_async_copy(own, to.at[0], load_sems.at[k]))
        loads[-1].start()
    greet(me, NEAR + WEIGHT)
    sends = Sends(me, send_sems, recv_sems)
    early, query, late = Shards(sends), Shards(sends), Shards(sends)
    odd = lax.rem(x, 2)
    give = pl.ds(pl.multiple_of((1 - odd) * T, T), T)
    keep = pl.ds(pl.multiple_of(odd * T, T), T)
    limit = ((yhi * 16 + z * 4 + x) // 2 + 1) * PAIR
    stores = []

    def store(a, b):
        stores.append(pltpu.make_async_copy(a, b, store_sems.at[len(stores)]))
        stores[-1].start()

    def main():
        vec_far = sends.start(vec_ref, vecs.at[2], "y", 1)
        early.far(wk_ref, wk, 160)
        early.far(wv_ref, wv, 160)
        vec_near = sends.start(vec_ref, vecs.at[1], "core", 1)
        early.near(wk_ref, wk)
        early.near(wv_ref, wv)
        query.far(wq_ref, wq, 128)
        query.near(wq_ref, wq)
        vecs[0] = vec_ref[...]
        flag = jnp.where(chosen_ref[...] > 0, 1.0, 0.0)
        token = lax.broadcasted_iota(jnp.int32, (PAIR, PAIR), 0)
        lane = lax.broadcasted_iota(jnp.int32, (PAIR, PAIR), 1)
        upto = jnp.where(token <= lane, 1.0, 0.0).astype(BF)
        count = dot(jnp.broadcast_to(flag, (16, PAIR)).astype(BF), upto)[0:1]
        total = jnp.sum(flag, axis=1, keepdims=True)
        rank = count - 1.0 + jnp.where(odd == 1, PAIR - total, 0.0)
        place = jnp.where(token.astype(F32) == rank, flag, 0.0)
        place_low = place.astype(BF)
        place_ref[...] = place_low
        compact_p[...] = jnp.broadcast_to(
            jnp.sum(place * pos_ref[...].astype(F32), axis=1, keepdims=True), (PAIR, PAIR)
        )
        compact_h[...] = dot(place_low, hidden_ref[...].astype(BF), NT).astype(BF)
        swaps = [sends.start(c.at[give], g, "pair", 1) for c, g in ((compact_h, got_h), (compact_p, got_p))]
        yield
        compact_d[...] = dot(place_low, d_out_ref[...].astype(BF), NT).astype(BF)
        vec_far.wait_recv()
        vec_last = sends.start(vecs.at[2], vecs.at[3], "core", 1)
        early.relay()
        yield
        swaps[0].wait_recv()
        h = plus(compact_h[keep], got_h[...])
        h_ref[...] = h
        swaps.append(sends.start(compact_d.at[give], got_d, "pair", 1))
        swaps[1].wait_recv()
        angle = (compact_p[keep] + got_p[...]) * freq_ref[...]
        turn = lax.broadcasted_iota(jnp.int32, (T, PAIR), 1)
        cosine = jnp.where(turn < HEAD_DIM, jnp.cos(angle), 1.0)
        sine = jnp.sin(angle)
        sine = jnp.where(turn < HEAD_DIM // 2, -sine, jnp.where(turn < HEAD_DIM, sine, 0.0))
        cos_ref[...], sin_ref[...] = cosine, sine
        vec_near.wait_recv()
        vec_last.wait_recv()
        vec_out_ref[...] = jnp.zeros_like(vec_out_ref)
        for k, v in enumerate(our_order(me, [vecs[k, :, :240] for k in range(4)])):
            vec_out_ref[:, 240 * k : 240 * (k + 1)] = v
        r1 = lax.rsqrt(jnp.mean(h * h, axis=-1, keepdims=True) + EPS)
        x1_ref[...] = (h * r1 * vec_out_ref[0:1, :D]).astype(BF)
        x1_k = our_order(me, cut_four(x1_ref))
        for copy in loads:
            copy.wait()
        early.finish()
        k_pre = sum(dot(x1_k[k], wk[k], NT) for k in range(4))
        v_pre = sum(dot(x1_k[k], wv[k], NT) for k in range(4))
        for j in range(KV_HEADS):
            run = slice(HEAD_DIM * j, HEAD_DIM * (j + 1))
            tile = jnp.concatenate([k_pre[:, run], v_pre[:, run]], axis=1)
            kv_own[:, 128 * j : 128 * (j + 1)] = (tile * cosine + swapped(tile) * sine).astype(BF)
        gather = gather_steps(me, sends, kv_own, kv_ref)
        next(gather)
        yield
        next(gather)
        yield
        query.relay()
        yield
        query.finish()
        swaps[2].wait_recv()
        up_ref[...] = plus(compact_d[keep], got_d[...])
        q_pre[...] = sum(dot(x1_k[k], wq[k]) for k in range(4))
        zero = jnp.zeros((T, HEAD_DIM), F32)
        for j in range(KV_HEADS):
            for g in range(GROUPS):
                at = HEAD_DIM * (GROUPS * j + g)
                tile = jnp.concatenate([q_pre[:, at : at + HEAD_DIM], zero], axis=1)
                q_ref[j, g * T : (g + 1) * T] = (tile * cosine + swapped(tile) * sine).astype(BF)
        yield
        yield from gather
        for a, b in ((kv_ref, kv_out), (wq, wq_out), (wk, wk_out), (wv, wv_out)):
            store(a, b)
        for j in range(KV_HEADS):
            tile = kv_ref[:, :, :, :, 128 * j : 128 * (j + 1)].reshape(KEYS, 128)
            scores = dot(q_ref[j], tile, NT) * SCALE
            column = lax.broadcasted_iota(jnp.int32, scores.shape, 1)
            scores = jnp.where(column < limit, scores, -1e30)
            exponent = jnp.exp(scores - jnp.max(scores, axis=-1, keepdims=True))
            prob = (exponent * (1.0 / jnp.sum(exponent, axis=-1, keepdims=True))).astype(BF)
            prob_ref[j] = prob
            store(prob_ref.at[j], prob_out.at[j])
            mix_ref[j] = dot(prob, tile)
            yield

    small, large = (128, (32, 32, 32, 16)), (480, (128, 128, 112, 112))
    lanes = {
        "m": main(),
        "o": late.half(wo_ref, wos_ref, *small),
        "t": late.half(wg_ref, wgs_ref, *small),
        "u": late.half(wu_ref, wus_ref, *small),
        "d": late.half(wd_ref, wds_ref, *large),
    }
    run_lanes(lanes, "".join(FRONT_ORDER))
    late.finish()
    for copy in stores:
        copy.wait()
    sends.finish()


FRONT_ORDER = (
    "mmmommtmmoumdmommmtummdmmtumdm",
)


def front(hidden, d_out, chosen, pos, freq, vec, w_query, w_key, w_value, *later):
    vmem, hbm = pl.BlockSpec(memory_space=pltpu.VMEM), pl.BlockSpec(memory_space=pl.ANY)
    rows = GROUPS * T
    return pl.pallas_call(
        front_kernel,
        name="front",
        out_shape=(
            jax.ShapeDtypeStruct((KV_HEADS, rows, 128), F32),
            jax.ShapeDtypeStruct((KV_HEADS, rows, KEYS), BF),
            jax.ShapeDtypeStruct((KV_HEADS, rows, 128), BF),
            jax.ShapeDtypeStruct((2, 4, 4, T, 640), BF),
            jax.ShapeDtypeStruct((T, D), F32),
            jax.ShapeDtypeStruct((T, D), F32),
            jax.ShapeDtypeStruct((T, D), BF),
            jax.ShapeDtypeStruct((T, 128), F32),
            jax.ShapeDtypeStruct((T, 128), F32),
            jax.ShapeDtypeStruct((PAIR, PAIR), BF),
            jax.ShapeDtypeStruct((8, 1024), F32),
            jax.ShapeDtypeStruct((4, 240, 960), BF),
            jax.ShapeDtypeStruct((4, 320, 240), BF),
            jax.ShapeDtypeStruct((4, 320, 240), BF),
        )
        + tuple(jax.ShapeDtypeStruct((3,) + w.shape, BF) for w in later[:3])
        + (jax.ShapeDtypeStruct((1,) + later[3].shape, BF),),
        in_specs=[vmem] * 6 + [hbm] * 7,
        out_specs=(vmem, hbm, vmem, hbm) + (vmem,) * 7 + (hbm,) * 7,
        scratch_shapes=[
            pltpu.VMEM((PAIR, D), BF),
            pltpu.VMEM((PAIR, D), BF),
            pltpu.VMEM((PAIR, PAIR), F32),
            pltpu.VMEM((T, D), BF),
            pltpu.VMEM((T, D), BF),
            pltpu.VMEM((T, PAIR), F32),
            pltpu.VMEM((4, 8, 256), F32),
            pltpu.VMEM((T, D), F32),
            pltpu.VMEM((T, 640), BF),
            pltpu.VMEM((KV_HEADS, rows, KEYS), BF),
            pltpu.VMEM((2, 4, 4, T, 640), BF),
            pltpu.VMEM((4, 240, 960), BF),
            pltpu.VMEM((4, 320, 240), BF),
            pltpu.VMEM((4, 320, 240), BF),
            pltpu.SemaphoreType.DMA((3,)),
            pltpu.SemaphoreType.DMA((9,)),
        ]
        + sems(90),
        compiler_params=pltpu.CompilerParams(
            collective_id=1, has_side_effects=True, vmem_limit_bytes=VMEM_LIMIT
        ),
        cost_estimate=pl.CostEstimate(flops=5_000_000_000, bytes_accessed=90_000_000, transcendentals=0),
    )(hidden, d_out, chosen, pos, freq, vec, w_query, w_key, w_value, *later)


def key_steps(me, sends, part_ref, out_ref, low, out_b, full, sums, nlow, nout, nfull, mine, y_in):
    _, _, yh, z, x = me
    half, quarter = T // 2, T // 4
    streams = (("x", "z", 0), ("z", "x", half))

    def line(axis, step, row, count):
        if axis == "z":
            return part_ref.at[:, lax.rem(z + step + 4, 4), :, pl.ds(row, count)]
        return part_ref.at[:, :, lax.rem(x + step + 4, 4), pl.ds(row, count)]

    near = {}
    for s, (axis, _, row) in enumerate(streams):
        near[s, 1] = sends.start(line(axis, 2, row, quarter), low.at[s, 0], axis, 1)
        near[s, -1] = sends.start(line(axis, 2, row + quarter, quarter), low.at[s, 1], axis, -1)
    whole = {}
    for s, (axis, _, row) in enumerate(streams):
        yield
        for d, step in enumerate((1, -1)):
            near[s, step].wait_recv()
            lo, hi = (0, quarter) if step == 1 else (quarter, 0)
            out_b[s, d, :, :, pl.ds(lo, quarter)] = plus(
                line(axis, step, row + lo, quarter)[...], low[s, d]
            ).astype(BF)
            out_b[s, d, :, :, pl.ds(hi, quarter)] = line(axis, step, row + hi, quarter)[...]
            whole[s, step] = sends.start(out_b.at[s, d], full.at[s, d], axis, step)
    near = {}
    for s, (axis, other, row) in enumerate(streams):
        yield
        for step in (1, -1):
            whole[s, step].wait_recv()
        sums[s] = plus(line(axis, 0, row, half)[...], full[s, 0], full[s, 1]).astype(BF)
        far = lax.rem((z if other == "z" else x) + 2, 4)
        near[s, 1] = sends.start(sums.at[s, :, far, pl.ds(0, quarter)], nlow.at[s, 0], other, 1)
        near[s, -1] = sends.start(
            sums.at[s, :, far, pl.ds(quarter, quarter)], nlow.at[s, 1], other, -1
        )
    for s, (axis, other, row) in enumerate(streams):
        yield
        at = z if other == "z" else x
        for d, step in enumerate((1, -1)):
            near[s, step].wait_recv()
            to = lax.rem(at + step + 4, 4)
            lo, hi = (0, quarter) if step == 1 else (quarter, 0)
            nout[s, d, :, pl.ds(lo, quarter)] = plus(
                sums[s, :, to, pl.ds(lo, quarter)], nlow[s, d]
            ).astype(BF)
            nout[s, d, :, pl.ds(hi, quarter)] = sums[s, :, to, pl.ds(hi, quarter)]
            whole[s, step] = sends.start(nout.at[s, d], nfull.at[s, d], other, step)
    swap = {}
    for s, (axis, other, row) in enumerate(streams):
        yield
        at = z if other == "z" else x
        for step in (1, -1):
            whole[s, step].wait_recv()
        mine[s] = plus(sums[s, :, at], nfull[s, 0], nfull[s, 1]).astype(BF)
        swap[s] = sends.start(mine.at[s, 1 - yh], y_in.at[s], "yhi", 1)
    yield
    for s, (axis, other, row) in enumerate(streams):
        swap[s].wait_recv()
        out_ref[pl.ds(row, half)] = plus(mine[s, yh], y_in[s])


def key_scratch():
    half, quarter, w = T // 2, T // 4, 640
    return [
        pltpu.VMEM((2, 2, 2, 4, quarter, w), BF),
        pltpu.VMEM((2, 2, 2, 4, half, w), BF),
        pltpu.VMEM((2, 2, 2, 4, half, w), BF),
        pltpu.VMEM((2, 2, 4, half, w), BF),
        pltpu.VMEM((2, 2, 2, quarter, w), BF),
        pltpu.VMEM((2, 2, 2, half, w), BF),
        pltpu.VMEM((2, 2, 2, half, w), BF),
        pltpu.VMEM((2, 2, half, w), BF),
        pltpu.VMEM((2, half, w), BF),
    ]


ROWS = 256
HALF = ROWS // 2
STREAMS = (("x", "z"), ("z", "x"))


def spots(me):
    return {"z": me[3], "x": me[4]}


def around(me, axis, step):
    return lax.rem(spots(me)[axis] + step + 4, 4)


def columns(me, axis, step, big):
    return pl.ds(pl.multiple_of(around(me, axis, step) * big, 128), big)


def halves(big):
    cut = (big // 2 + 127) // 128 * 128
    return (0, cut), (cut, big - cut)


def wide_steps(me, sends, g_ref, low, out_b, full, sums):
    h, big = sums.shape[0] // 2, sums.shape[1]
    cut = h // 2
    near, whole = {}, {}

    def parts(step):
        return (0, cut) if step == 1 else (cut, 0)

    for s, (axis, _) in enumerate(STREAMS):
        c = columns(me, axis, 2, big)
        for step in (1, -1):
            r = pl.ds(s * h + parts(step)[0], cut)
            near[s, step] = sends.start(g_ref.at[r, c], low.at[r], axis, step)
    for s, (axis, _) in enumerate(STREAMS):
        yield
        for d, step in enumerate((1, -1)):
            near[s, step].wait_recv()
            add, keep = (pl.ds(s * h + p, cut) for p in parts(step))
            c = columns(me, axis, step, big)
            out_b[d, add] = plus(g_ref[add, c], low[add]).astype(BF)
            out_b[d, keep] = g_ref[keep, c]
            r = pl.ds(s * h, h)
            whole[s, step] = sends.start(out_b.at[d, r], full.at[d, r], axis, step)

    for s, (axis, _) in enumerate(STREAMS):
        yield
        for step in (1, -1):
            whole[s, step].wait_recv()
        r = pl.ds(s * h, h)
        sums[r] = plus(g_ref[r, columns(me, axis, 0, big)], full[0, r], full[1, r]).astype(BF)


def narrow_steps(me, sends, sums, mine, swap_y, nlow, nout, nfull, y_in):
    run, big = mine.shape[-2:]
    h = 4 * run
    near, whole = {}, {}

    def rows(s, other, step):
        return pl.ds(pl.multiple_of(s * h + around(me, other, step) * run, 16), run)

    for s, (axis, other) in enumerate(STREAMS):
        for d, step in enumerate((1, -1)):
            c = pl.ds(*halves(big)[d])
            near[s, step] = sends.start(sums.at[rows(s, other, 2), c], nlow.at[s, :, c], other, step)
    for s, (axis, other) in enumerate(STREAMS):
        yield
        for d, step in enumerate((1, -1)):
            near[s, step].wait_recv()
            add, keep = pl.ds(*halves(big)[d]), pl.ds(*halves(big)[1 - d])
            r = rows(s, other, step)
            nout[s, d, :, add] = plus(sums[r, add], nlow[s, :, add]).astype(BF)
            nout[s, d, :, keep] = sums[r, keep]
            whole[s, step] = sends.start(nout.at[s, d], nfull.at[s, d], other, step)
    swap = {}
    for s, (axis, other) in enumerate(STREAMS):
        yield
        for step in (1, -1):
            whole[s, step].wait_recv()
        total = plus(sums[rows(s, other, 0)], nfull[s, 0], nfull[s, 1]).astype(BF)
        if swap_y:
            y_in[0, s] = total
            swap[s] = sends.start(y_in.at[0, s], y_in.at[1, s], "yhi", 1)
        else:
            mine[s] = total
    if swap_y:
        for s in range(2):
            yield
            swap[s].wait_recv()
            mine[s] = plus(y_in[0, s], y_in[1, s]).astype(BF)


def sum_steps(me, sends, g_ref, mine, swap_y, low, out_b, full, sums, *narrow):
    yield from wide_steps(me, sends, g_ref, low, out_b, full, sums)
    yield from narrow_steps(me, sends, sums, mine, swap_y, *narrow)


def sum_scratch(width, h):
    big, run = width // 4, h // 4
    return [
        pltpu.VMEM((2 * h, big), BF),
        pltpu.VMEM((2, 2 * h, big), BF),
        pltpu.VMEM((2, 2 * h, big), BF),
        pltpu.VMEM((2 * h, big), BF),
        pltpu.VMEM((2, run, big), BF),
        pltpu.VMEM((2, 2, run, big), BF),
        pltpu.VMEM((2, 2, run, big), BF),
        pltpu.VMEM((2, 2, run, big), BF),
    ]


def spread_steps(me, sends, mine, out_ref, store_sems, to_y):
    run, big = mine.shape[-2:]
    h = 4 * run
    cut = h // 2
    near, whole, stored, last, over = {}, {}, [], {}, []

    def base(s):
        return s * HALF + (me[2] * h if to_y else 0)

    def rows(s, off, count):
        return pl.ds(pl.multiple_of(base(s) + off, 16), count)

    def block(s, axis, step, off, count):
        return out_ref.at[rows(s, off, count), columns(me, axis, step, big)]

    def on(ref):
        if to_y:
            over.append(sends.start(ref, ref, "yhi", 1))

    for s, (axis, other) in enumerate(STREAMS):
        ref = block(s, axis, 0, around(me, other, 0) * run, run)
        for step in (1, -1):
            near[s, step] = sends.start(mine.at[s], ref, other, step)
        stored.append(pltpu.make_async_copy(mine.at[s], ref, store_sems.at[s]))
        stored[-1].start()

    def narrow(s, axis, other, step, d):
        c0, n = halves(big)[d]
        c = pl.ds(pl.multiple_of(around(me, axis, 0) * big + c0, 128), n)
        return out_ref.at[rows(s, around(me, other, step) * run, run), c]

    for s, (axis, other) in enumerate(STREAMS):
        yield
        for d, step in enumerate((1, -1)):
            near[s, step].wait_recv()
            ref = narrow(s, axis, other, -step, d)
            whole[s, step] = sends.start(ref, ref, other, step)
    for s, (axis, other) in enumerate(STREAMS):
        yield
        for step in (1, -1):
            whole[s, step].wait_recv()
        stored[s].wait()
        ref = block(s, axis, 0, 0, h)
        for step in (1, -1):
            near[s, step] = sends.start(ref, ref, axis, step)
        on(ref)
    for s, (axis, other) in enumerate(STREAMS):
        yield
        for d, step in enumerate((1, -1)):
            near[s, step].wait_recv()
            ref = block(s, axis, -step, d * cut, cut)
            last[s, step] = sends.start(ref, ref, axis, step)
            on(block(s, axis, -step, 0, h))
    for s, (axis, other) in enumerate(STREAMS):
        yield
        for step in (1, -1):
            last[s, step].wait_recv()
        on(block(s, axis, 2, 0, h))
    if to_y:
        yield
        for copy in over:
            copy.wait_recv()


def halved_steps(me, sends, g_ref, mine, kept, got, out_ref, store_sems, *scratch):
    h = HALF // 2
    yh = me[2]
    copies = []
    for s in range(2):
        give = pl.ds(pl.multiple_of(s * HALF + (1 - yh) * h, 16), h)
        copies.append(sends.start(g_ref.at[give], got.at[pl.ds(s * h, h)], "yhi", 1))
    for s in range(2):
        yield
        copies[s].wait_recv()
        r = pl.ds(s * h, h)
        kept[r] = plus(g_ref[pl.ds(pl.multiple_of(s * HALF + yh * h, 16), h)], got[r]).astype(BF)
    yield
    yield from sum_steps(me, sends, kept, mine, False, *scratch)
    yield from spread_steps(me, sends, mine, out_ref, store_sems, True)


def vector_steps(sends, vec_ref, out_ref, keep, got):
    rounds = ((("core", 1),), (("ylo", 1),), (("x", 1), ("x", -1), ("x", 2)), (("z", 1), ("z", -1), ("z", 2)), (("yhi", 1),))
    keep[0] = vec_ref[...]
    k = 0
    for at, partners in enumerate(rounds):
        copies = []
        for axis, step in partners:
            copies.append((k, sends.start(keep.at[at], got.at[k], axis, step)))
            k += 1
        yield
        total = keep[at]
        for slot, copy in copies:
            copy.wait_recv()
            total = total + got[slot]
        keep[at + 1] = total
    out_ref[...] = keep[len(rounds)]


def small_steps(me, sends, g_ref, out_ref, got_x, got_z, got_y, sum_z, sum_y):
    x, z = me[3], me[4]
    steps = (1, -1, 2)

    def rows(at, step, count, base=0):
        return pl.ds(pl.multiple_of(base + lax.rem(at + step + 4, 4) * count, 16), count)

    copies = [
        sends.start(g_ref.at[rows(x, step, 64)], got_x.at[k], "z", step) for k, step in enumerate(steps)
    ]
    yield
    for copy in copies:
        copy.wait_recv()
    sum_z[...] = plus(g_ref[rows(x, 0, 64)], got_x[0], got_x[1], got_x[2]).astype(BF)
    copies = [
        sends.start(sum_z.at[rows(z, step, 16)], got_z.at[k], "x", step) for k, step in enumerate(steps)
    ]
    yield
    for copy in copies:
        copy.wait_recv()
    sum_y[...] = plus(sum_z[rows(z, 0, 16)], got_z[0], got_z[1], got_z[2]).astype(BF)
    copy = sends.start(sum_y, got_y, "yhi", 1)
    yield
    copy.wait_recv()
    ref = out_ref.at[rows(z, 0, 16, x * 64)]
    ref[...] = plus(sum_y[...], got_y[...]).astype(BF)
    copies = [sends.start(ref, ref, "x", step) for step in steps]
    yield
    for copy in copies:
        copy.wait_recv()
    ref = out_ref.at[rows(x, 0, 64)]
    copies = [sends.start(ref, ref, "z", step) for step in steps]
    yield
    for copy in copies:
        copy.wait_recv()


KEY_N, SUM_N = 9, 8
WIDE, REST = FF, 2048


def back_kernel(
    part_ref, g_in, sums_ref, dq_ref, d_attn_ref, mixture_ref, x1_ref, h_ref, d_mid_ref, out_ref, logit_ref, vec_ref, vec_part_ref,
    cos_ref, sin_ref, wq_in, wk_in, wv_in,
    gate_ref, up_ref, down_ref, two_ref, three_ref, vec_out_ref, both_ref,
    own, ra, rb, xs, ra_all, rb_all, xs_all, xs_relay, g_two, g_three, d_x1_s, vec_all, keep_v, got_v,
    mine_gate, mine_up, mine_down, mine_two, got_x, got_z, got_y, sum_z, sum_y,
    g_gate, g_up, kept, got_gate, wq, wk, wv, load_sems, store_sems,
    *scratch,
):
    me = here()
    key_scr, rest = scratch[:KEY_N], scratch[KEY_N:-2]
    gate_scr, up_scr, two_scr, down_scr = (rest[SUM_N * k : SUM_N * (k + 1)] for k in range(4))
    loads = [
        pltpu.make_async_copy(a, b, load_sems.at[k])
        for k, (a, b) in enumerate(
            (
                (g_in.at[:, pl.ds(0, WIDE)], g_gate),
                (g_in.at[:, pl.ds(WIDE, WIDE)], g_up),
                (wq_in, wq),
                (wk_in, wk),
                (wv_in, wv),
            )
        )
    ]
    for copy in loads:
        copy.start()
    greet(me, NEAR + WEIGHT + FAR)
    sends = Sends(me, *scratch[-2:])
    odd = lax.rem(me[4], 2)
    keep = pl.ds(pl.multiple_of(odd * T, T), T)
    cosine, sine = cos_ref[...], sin_ref[...]
    mine = pl.ds(0, T)

    def turned_back(tile):
        return tile * cosine - swapped(tile) * sine

    def keys():
        yield from key_steps(me, sends, part_ref, own, *key_scr)
        for j in range(KV_HEADS):
            tile = turned_back(own[:, 128 * j : 128 * (j + 1)]).astype(BF)
            rb[:, HEAD_DIM * j : HEAD_DIM * (j + 1)] = tile[:, :HEAD_DIM]
            rb[:, 320 + HEAD_DIM * j : 320 + HEAD_DIM * (j + 1)] = tile[:, HEAD_DIM:]
        share = everyone_steps(sends, (("all", rb, rb_all, None),))
        next(share)
        rb_all[mine] = rb[...]
        d_k, d_v = rb[:, :320], rb[:, 320:]
        d_x1 = d_x1_s[...] + jnp.concatenate(
            our_order(me, [dot(d_k, wk[k]) + dot(d_v, wv[k]) for k in range(4)]), axis=1
        )
        h = h_ref[...]
        r1 = lax.rsqrt(jnp.mean(h * h, axis=-1, keepdims=True) + EPS)
        d_first, g_gain_a = norm_back_rows(h, r1, vec_ref[0:1, :D], d_x1)
        d_h = d_mid_ref[...] + d_first + logit_ref[:, 0:1] * vec_ref[2:3, :D]
        both_ref[keep, :D] = out_ref[...]
        both_ref[keep, D:] = d_h.astype(BF)
        swap = sends.start(both_ref.at[keep], both_ref.at[keep], "pair", 1)
        vec_all[...] = vec_part_ref[...]
        vec_all[0:1, :D] = g_gain_a
        vectors = vector_steps(sends, vec_all, vec_out_ref, keep_v, got_v)
        next(vectors)
        yield
        next(share)
        yield
        together(share)
        g_three[...] = dot(xs_all[:, :256], rb_all[...], TN).astype(BF)
        small = small_steps(me, sends, g_three, three_ref, got_x, got_z, got_y, sum_z, sum_y)
        while True:
            for step in (small, vectors):
                next(step, None)
            if small.gi_frame is None and vectors.gi_frame is None:
                break
            yield
        swap.wait_recv()

    def queries():
        for j in range(KV_HEADS):
            for g in range(GROUPS):
                at = HEAD_DIM * (GROUPS * j + g)
                ra[:, at : at + HEAD_DIM] = turned_back(dq_ref[j, g * T : (g + 1) * T]).astype(BF)[:, :HEAD_DIM]
        ra[:, D:] = d_attn_ref[...]
        xs[...] = jnp.zeros_like(xs)
        for k, (a, b) in enumerate(zip(our_order(me, cut_four(x1_ref)), our_order(me, cut_four(mixture_ref)))):
            xs[k, :, :240] = a
            xs[k, :, 256:496] = b
        share = everyone_steps(
            sends, (("all", ra, ra_all, None), ("one", [xs.at[k] for k in range(4)], xs_all, xs_relay))
        )
        next(share)
        ra_all[mine] = ra[...]
        xs_all[mine] = xs[0]
        d_q = ra[:, :D]
        for copy in loads[2:]:
            copy.wait()
        d_x1_s[...] = jnp.concatenate(our_order(me, [dot(d_q, wq[k], NT) for k in range(4)]), axis=1)
        g_two[:, 2 * D :] = jnp.zeros((ROWS, 128), BF)
        yield
        next(share)
        yield
        together(share)
        g_two[:, :D] = dot(xs_all[:, :256], ra_all[:, :D], TN).astype(BF)
        g_two[:, D : 2 * D] = dot(xs_all[:, 256:], ra_all[:, D:], TN).astype(BF)
        yield from sum_steps(me, sends, g_two, mine_two, True, *two_scr)
        yield from spread_steps(me, sends, mine_two, two_ref, store_sems.at[pl.ds(6, 2)], False)

    def gate():
        loads[0].wait()
        yield from halved_steps(
            me, sends, g_gate, mine_gate, kept, got_gate, gate_ref, store_sems.at[pl.ds(0, 2)], *gate_scr
        )

    def up():
        loads[1].wait()
        yield from sum_steps(me, sends, g_up, mine_up, True, *up_scr)
        yield from spread_steps(me, sends, mine_up, up_ref, store_sems.at[pl.ds(2, 2)], False)

    def down():
        yield from narrow_steps(me, sends, sums_ref, mine_down, True, *down_scr)
        yield from spread_steps(me, sends, mine_down, down_ref, store_sems.at[pl.ds(4, 2)], False)

    run_lanes({"k": keys(), "g": gate(), "u": up(), "d": down(), "q": queries()}, "".join(ORDER))
    sends.finish()


ORDER = (
    "gkdqukddkuudgggkkuggqduqdkkuudggqqkududk",
    "ggqduqggukqgkukgqudgqgkuuqqqkddgqqgkuuqd",
    "qgkqudgqqgkuq",
)


def back(*args):
    vmem, hbm = pl.BlockSpec(memory_space=pltpu.VMEM), pl.BlockSpec(memory_space=pl.ANY)
    return pl.pallas_call(
        back_kernel,
        name="back",
        out_shape=(
            jax.ShapeDtypeStruct((ROWS, WIDE), BF),
            jax.ShapeDtypeStruct((ROWS, WIDE), BF),
            jax.ShapeDtypeStruct((ROWS, WIDE), BF),
            jax.ShapeDtypeStruct((ROWS, REST), BF),
            jax.ShapeDtypeStruct((ROWS, 640), BF),
            jax.ShapeDtypeStruct((8, 1024), F32),
            jax.ShapeDtypeStruct((PAIR, 2 * D), BF),
        ),
        in_specs=[vmem, hbm] + [vmem] * (len(args) - 5) + [hbm] * 3,
        out_specs=(hbm,) * 4 + (vmem,) * 3,
        scratch_shapes=[
            pltpu.VMEM((T, 640), F32),
            pltpu.VMEM((T, 2 * D), BF),
            pltpu.VMEM((T, 640), BF),
            pltpu.VMEM((4, T, 512), BF),
            pltpu.VMEM((4 * T, 2 * D), BF),
            pltpu.VMEM((4 * T, 640), BF),
            pltpu.VMEM((4 * T, 512), BF),
            pltpu.VMEM((T, 512), BF),
            pltpu.VMEM((ROWS, REST), BF),
            pltpu.VMEM((ROWS, 640), BF),
            pltpu.VMEM((T, D), F32),
            pltpu.VMEM((8, 1024), F32),
            pltpu.VMEM((6, 8, 1024), F32),
            pltpu.VMEM((9, 8, 1024), F32),
            pltpu.VMEM((2, HALF // 8, WIDE // 4), BF),
            pltpu.VMEM((2, HALF // 4, WIDE // 4), BF),
            pltpu.VMEM((2, HALF // 4, WIDE // 4), BF),
            pltpu.VMEM((2, HALF // 4, REST // 4), BF),
            pltpu.VMEM((3, 64, 640), BF),
            pltpu.VMEM((3, 16, 640), BF),
            pltpu.VMEM((16, 640), BF),
            pltpu.VMEM((64, 640), BF),
            pltpu.VMEM((16, 640), BF),
            pltpu.VMEM((ROWS, WIDE), BF),
            pltpu.VMEM((ROWS, WIDE), BF),
            pltpu.VMEM((HALF, WIDE), BF),
            pltpu.VMEM((HALF, WIDE), BF),
            pltpu.VMEM((4, 240, 960), BF),
            pltpu.VMEM((4, 320, 240), BF),
            pltpu.VMEM((4, 320, 240), BF),
            pltpu.SemaphoreType.DMA((6,)),
            pltpu.SemaphoreType.DMA((8,)),
        ]
        + key_scratch()
        + sum_scratch(WIDE, HALF // 2)
        + sum_scratch(WIDE, HALF)
        + sum_scratch(REST, HALF)
        + sum_scratch(WIDE, HALF)[4:]
        + sems(230),
        compiler_params=pltpu.CompilerParams(
            collective_id=2, has_side_effects=True, vmem_limit_bytes=VMEM_LIMIT
        ),
        cost_estimate=pl.CostEstimate(flops=2_000_000_000, bytes_accessed=200_000_000, transcendentals=0),
    )(*args)


def finish_kernel(
    g_gate_ref, g_up_ref, g_down_ref, two_ref, three_ref, vec_ref, both_ref, place_ref, hidden_ref, d_out_ref,
    out_ref, d_hidden_ref, query_ref, key_ref, value_ref, output_ref, gate_ref, up_ref, down_ref, vec_out_ref,
    low_one, low_down, low_two, low_three, wide_one, wide_two, wide_down, wide_kv, rows, load_sems, store_sems,
):
    keep = pl.ds(0, 240)
    runs_one = [pl.ds(1280 * k, 1280) for k in range(2)]
    runs_down = [pl.ds(640 * k, 640) for k in range(4)]
    loads = []
    for src, dst, runs in (
        (g_gate_ref, low_one.at[0], runs_one),
        (g_up_ref, low_one.at[1], runs_one),
        (g_down_ref, low_down, runs_down),
        (two_ref, low_two, [pl.ds(0, 2 * D)]),
        (three_ref, low_three, [pl.ds(0, 640)]),
    ):
        for c in runs:
            loads.append(pltpu.make_async_copy(src.at[keep, c], dst.at[:, c], load_sems.at[len(loads)]))
            loads[-1].start()
    stores = []

    def store(a, b):
        stores.append(pltpu.make_async_copy(a, b, store_sems.at[len(stores)]))
        stores[-1].start()

    for k, (base, to) in enumerate(((hidden_ref, out_ref), (d_out_ref, d_hidden_ref))):
        rows[k] = base[...] + dot(both_ref[:, D * k : D * (k + 1)], place_ref[...], TN)
        store(rows.at[k], to)
    for k in range(4):
        loads[k].wait()
        c = runs_one[k % 2]
        wide_one[k // 2, :, c] = low_one[k // 2, :, c].astype(F32)
        store(wide_one.at[k // 2, :, c], (gate_ref, up_ref)[k // 2].at[:, c])
    for k in range(4):
        loads[4 + k].wait()
        r = pl.ds(240 * k, 240)
        wide_down[r] = low_down[:, runs_down[k]].astype(F32)
        store(wide_down.at[r], down_ref.at[r])
    loads[8].wait()
    for k, to in enumerate((query_ref, output_ref)):
        wide_two[k] = low_two[:, D * k : D * (k + 1)].astype(F32)
        store(wide_two.at[k], to)
    loads[9].wait()
    for k, to in enumerate((key_ref, value_ref)):
        wide_kv[k] = low_three[:, 320 * k : 320 * (k + 1)].astype(F32).T
        store(wide_kv.at[k], to)
    core, ylo = lax.axis_index("core") == 1, lax.axis_index("ylo") == 1
    p = [vec_ref[:, 240 * k : 240 * (k + 1)] for k in range(4)]
    vec_out_ref[...] = jnp.where(ylo, jnp.where(core, p[3], p[2]), jnp.where(core, p[1], p[0]))
    for copy in stores:
        copy.wait()


def finish(*args):
    vmem, hbm = pl.BlockSpec(memory_space=pltpu.VMEM), pl.BlockSpec(memory_space=pl.ANY)
    shapes = [(D, PAIR), (D, PAIR), (240, D), (320, 240), (320, 240), (240, D), (240, FF), (240, FF), (D, 640), (8, 240)]
    return pl.pallas_call(
        finish_kernel,
        name="finish",
        out_shape=tuple(jax.ShapeDtypeStruct(shape, F32) for shape in shapes),
        in_specs=[hbm] * 5 + [vmem] * 5,
        out_specs=(hbm,) * 9 + (vmem,),
        scratch_shapes=[
            pltpu.VMEM((2, 240, WIDE), BF),
            pltpu.VMEM((240, WIDE), BF),
            pltpu.VMEM((240, REST), BF),
            pltpu.VMEM((240, 640), BF),
            pltpu.VMEM((2, 240, WIDE), F32),
            pltpu.VMEM((2, 240, D), F32),
            pltpu.VMEM((D, 640), F32),
            pltpu.VMEM((2, 320, 240), F32),
            pltpu.VMEM((2, D, PAIR), F32),
            pltpu.SemaphoreType.DMA((10,)),
            pltpu.SemaphoreType.DMA((14,)),
        ],
        compiler_params=pltpu.CompilerParams(vmem_limit_bytes=VMEM_LIMIT),
        cost_estimate=pl.CostEstimate(flops=0, bytes_accessed=16_000_000, transcendentals=0),
    )(*args)


def shard_of(me, k):
    ylo, core = me[0], me[1]
    return (ylo if k < 2 else 1 - ylo) * 2 + (core if k % 2 == 0 else 1 - core)


def our_order(me, p):
    core, ylo = me[1] == 1, me[0] == 1
    p = [jnp.where(core, p[k ^ 1], p[k]) for k in range(4)]
    return [jnp.where(ylo, p[k ^ 2], p[k]) for k in range(4)]


def cut_four(ref):
    return [ref[:, 240 * k : 240 * (k + 1)] for k in range(4)]


def norm_back_rows(z, r, gain, dy):
    dz = r * (gain * dy) - z * (r * r * r) * jnp.mean(gain * dy * z, axis=-1, keepdims=True)
    return dz, jnp.sum(dy * z * r, axis=0, keepdims=True)


def everyone_steps(sends, pieces):
    half = T // 2
    arrived, last = [], []
    for kind, source, whole, relay in pieces:
        near = source if kind == "all" else source[1]
        last.append(sends.start(near, whole.at[pl.ds(T, T)], "core", 1))
    for step, at in ((1, 0), (-1, half)):
        r = pl.ds(at, half)
        for kind, source, whole, relay in pieces:
            far = source if kind == "all" else source[2]
            arrived.append((sends.start(far.at[r], whole.at[pl.ds(2 * T + at, half)], "y", step), None))
            if kind == "all":
                arrived[-1] = (arrived[-1][0], (whole.at[pl.ds(2 * T + at, half)], whole.at[pl.ds(3 * T + at, half)]))
            else:
                copy = sends.start(source[3].at[r], relay.at[r], "y", step)
                arrived.append((copy, (relay.at[r], whole.at[pl.ds(3 * T + at, half)])))
    yield
    for copy, onward in arrived:
        copy.wait_recv()
        if onward is not None:
            last.append(sends.start(onward[0], onward[1], "core", 1))
    yield
    for copy in last:
        copy.wait_recv()


def dense_kernel(
    mix_ref, q_ref, prob_in, kv_in, h_ref, up_ref, vec_ref,
    wo_ref, wg_ref, wu_ref, wd_ref, wos_ref, wgs_ref, wus_ref, wds_ref,
    dq_ref, dkv_out, g_out, sums_ref, d_attn_ref, mixture_ref, d_mid_ref, out_ref, logit_ref, vec_out_ref,
    wo, wg, wu, wd, mixf, gate_s, up_s, inner, dgu, dffn, xs, do_s, d_mix_s,
    dgu_all, dffn_all, xs_all, inner_all, xs_relay, inner_relay,
    prob_ref, kv_ref, dkv_ref, g_ref, g_down, low, out_b, full,
    load_sems, store_sems, send_sems, recv_sems,
):
    me = here()
    loads = []
    for k, (own, rest, to) in enumerate(
        ((wo_ref, wos_ref, wo), (wg_ref, wgs_ref, wg), (wu_ref, wus_ref, wu), (wd_ref, wds_ref, wd))
    ):
        there = to.at[pl.ds(1, 3)] if k < 3 else to.at[pl.ds(2, 1)]
        pair = (
            pltpu.make_async_copy(own, to.at[0], load_sems.at[2 * k]),
            pltpu.make_async_copy(rest, there, load_sems.at[2 * k + 1]),
        )
        for copy in pair:
            copy.start()
        loads.append(pair)
    loads.append(
        (
            pltpu.make_async_copy(prob_in, prob_ref, load_sems.at[8]),
            pltpu.make_async_copy(kv_in, kv_ref, load_sems.at[9]),
        )
    )
    for copy in loads[4]:
        copy.start()
    greet(me, NEAR[:4] + WEIGHT)
    sends = Sends(me, send_sems, recv_sems)
    down = [
        sends.start(wd_ref, wd.at[1], "core", 1),
        sends.start(wds_ref.at[0], wd.at[3], "core", 1),
    ]
    shards = [shard_of(me, k) for k in range(4)]

    def run640(k):
        return pl.ds(pl.multiple_of(shards[k] * 640, 128), 640)

    def loaded(k):
        for copy in loads[k]:
            copy.wait()

    for j in range(KV_HEADS):
        for g in range(GROUPS):
            h = GROUPS * j + g
            mixf[:, HEAD_DIM * h : HEAD_DIM * (h + 1)] = mix_ref[j, g * T : (g + 1) * T, HEAD_DIM:]
    mixture_ref[...] = mixf[...].astype(BF)
    mix_k = our_order(me, cut_four(mixture_ref))
    loaded(0)
    attn_out = sum(dot(mix_k[k], wo[k]) for k in range(4))
    hidden = h_ref[...]
    gain_f = vec_ref[1:2, :D]
    route_w = vec_ref[2:3, :D]
    middle = hidden + attn_out
    r2 = lax.rsqrt(jnp.mean(middle * middle, axis=-1, keepdims=True) + EPS)
    x2 = middle * r2 * gain_f
    x2_k = our_order(me, [x2[:, 240 * k : 240 * (k + 1)].astype(BF) for k in range(4)])
    xs[...] = jnp.zeros_like(xs)
    for k in range(4):
        xs[k, :, :240] = x2_k[k]
    shares = [everyone_steps(sends, (("one", [xs.at[k] for k in range(4)], xs_all, xs_relay),))]
    next(shares[0])
    loaded(1)
    gate_s[...] = sum(dot(x2_k[k], wg[k]) for k in range(4))
    loaded(2)
    up_s[...] = sum(dot(x2_k[k], wu[k]) for k in range(4))
    gate = gate_s[...]
    inner[...] = (gate * jax.nn.sigmoid(gate) * up_s[...]).astype(BF)
    loaded(3)
    shares.append(
        everyone_steps(sends, (("one", [inner.at[:, run640(k)] for k in range(4)], inner_all, inner_relay),))
    )
    next(shares[1])
    for copy in down:
        copy.wait_recv()
    ffn_out = sum(dot(inner[:, run640(k)], wd[k], NT) for k in range(4))
    route = jax.nn.sigmoid(jnp.sum(hidden * route_w, axis=-1, keepdims=True))
    branch = attn_out + ffn_out
    out_ref[...] = (route * branch).astype(BF)
    upstream = up_ref[...]
    d_branch = upstream * route
    d_logit = route * (1.0 - route) * jnp.sum(upstream * branch, axis=-1, keepdims=True)
    logit_ref[...] = jnp.broadcast_to(d_logit, logit_ref.shape)
    vec_out_ref[...] = jnp.zeros_like(vec_out_ref)
    vec_out_ref[2:3, :D] = jnp.sum(d_logit * hidden, axis=0, keepdims=True)
    d_ffn = d_branch.astype(BF)
    own = pl.ds(0, T)
    dffn[...] = jnp.zeros_like(dffn)
    for k in range(4):
        dffn[:, 256 * k : 256 * k + 240] = d_branch[:, 240 * k : 240 * (k + 1)].astype(BF)
    shares.append(everyone_steps(sends, (("all", dffn, dffn_all, None),)))
    next(shares[2])
    dffn_all[own], xs_all[own], inner_all[own] = dffn[...], xs[0], inner[:, run640(0)]
    late = []
    for p in range(2):
        first = 2 * lax.rem(me[0] + p, 2)
        for b in range(2):
            at = (2 * p + (me[1] if b == 0 else 1 - me[1])) * 640
            run, run_up = (pl.ds(pl.multiple_of(c + at, 128), 640) for c in (0, FF))
            d_inner = dot(d_ffn, wd[first + b])
            gate, up = gate_s[:, run], up_s[:, run]
            sg = jax.nn.sigmoid(gate)
            dgu[:, run] = (d_inner * up * (sg + gate * sg * (1.0 - sg))).astype(BF)
            dgu[:, run_up] = (d_inner * (gate * sg)).astype(BF)
        cols = [pl.ds(c + 1280 * p, 1280) for c in (0, FF)]
        late.append(everyone_steps(sends, tuple(("all", dgu.at[:, c], dgu_all.at[:, c], None) for c in cols)))
        next(late[-1])
    for share in shares:
        next(share)
    dgu_all[own] = dgu[...]
    d_gate, d_up = dgu[:, :FF], dgu[:, FF:]
    d_x2 = jnp.concatenate(
        our_order(me, [dot(d_gate, wg[k], NT) + dot(d_up, wu[k], NT) for k in range(4)]), axis=1
    )
    d_mid, g_gain_f = norm_back_rows(middle, r2, gain_f, d_x2)
    d_mid_ref[...] = d_mid
    vec_out_ref[1:2, :D] = g_gain_f
    d_attn = (d_branch + d_mid).astype(BF)
    d_attn_ref[...] = d_attn
    d_mix_s[...] = jnp.concatenate(our_order(me, [dot(d_attn, wo[k], NT) for k in range(4)]), axis=1)
    do_s[...] = jnp.zeros_like(do_s)
    for j in range(KV_HEADS):
        for g in range(GROUPS):
            h = GROUPS * j + g
            do_s[j, g * T : (g + 1) * T, HEAD_DIM:] = d_mix_s[:, HEAD_DIM * h : HEAD_DIM * (h + 1)].astype(BF)

    stores = []

    def store(a, b):
        stores.append(pltpu.make_async_copy(a, b, store_sems.at[len(stores)]))
        stores[-1].start()

    together(*shares)
    for k in range(4):
        c = pl.ds(640 * k, 640)
        g_down[:, c] = dot(dffn_all[:, 256 * k : 256 * (k + 1)], inner_all[...], TN).astype(BF)
    wide = wide_steps(me, sends, g_down, low, out_b, full, sums_ref)
    next(wide)
    loaded(4)
    for j in range(KV_HEADS):
        c = pl.ds(j * 128, 128)
        tile = kv_ref[:, :, :, :, c].reshape(KEYS, 128)
        prob, d_out = prob_ref[j], do_s[j]
        d_prob = dot(d_out, tile, NT)
        delta = jnp.sum(d_out.astype(F32) * mix_ref[j], axis=-1, keepdims=True)
        d_score = (prob.astype(F32) * (d_prob - delta)).astype(BF)
        dq_ref[j] = dot(d_score, tile) * SCALE
        grad = dot(d_score, q_ref[j], TN) * SCALE + dot(prob, d_out, TN)
        dkv_ref[:, :, :, :, c] = grad.astype(BF).reshape(2, 4, 4, T, 128)
        store(dkv_ref.at[:, :, :, :, c], dkv_out.at[:, :, :, :, c])
        if j == 3:
            next(wide)
            next(wide)
    together(*late)
    for at in range(0, 2 * FF, 1280):
        c = pl.ds(at, 1280)
        g_ref[:, c] = dot(xs_all[...], dgu_all[:, c], TN).astype(BF)
        store(g_ref.at[:, c], g_out.at[:, c])
    together(wide)
    for copy in stores:
        copy.wait()
    sends.finish()


def dense(mix, q, prob, kv, h, up_c, vec, own, rest):
    vmem, hbm = pl.BlockSpec(memory_space=pltpu.VMEM), pl.BlockSpec(memory_space=pl.ANY)
    rows = GROUPS * T
    return pl.pallas_call(
        dense_kernel,
        name="dense",
        out_shape=(
            jax.ShapeDtypeStruct((KV_HEADS, rows, 128), F32),
            jax.ShapeDtypeStruct((2, 4, 4, T, 640), BF),
            jax.ShapeDtypeStruct((ROWS, 2 * FF), BF),
            jax.ShapeDtypeStruct((ROWS, FF // 4), BF),
            jax.ShapeDtypeStruct((T, D), BF),
            jax.ShapeDtypeStruct((T, D), BF),
            jax.ShapeDtypeStruct((T, D), F32),
            jax.ShapeDtypeStruct((T, D), BF),
            jax.ShapeDtypeStruct((T, 128), F32),
            jax.ShapeDtypeStruct((8, 1024), F32),
        ),
        in_specs=[vmem] * 2 + [hbm] * 2 + [vmem] * 3 + [hbm] * 8,
        out_specs=(vmem,) + (hbm,) * 2 + (vmem,) * 7,
        scratch_shapes=[
            pltpu.VMEM((4, 240, D), BF),
            pltpu.VMEM((4, 240, FF), BF),
            pltpu.VMEM((4, 240, FF), BF),
            pltpu.VMEM((4, D, 640), BF),
            pltpu.VMEM((T, D), F32),
            pltpu.VMEM((T, FF), F32),
            pltpu.VMEM((T, FF), F32),
            pltpu.VMEM((T, FF), BF),
            pltpu.VMEM((T, 2 * FF), BF),
            pltpu.VMEM((T, 1024), BF),
            pltpu.VMEM((4, T, 256), BF),
            pltpu.VMEM((KV_HEADS, rows, 128), BF),
            pltpu.VMEM((T, D), F32),
            pltpu.VMEM((4 * T, 2 * FF), BF),
            pltpu.VMEM((4 * T, 1024), BF),
            pltpu.VMEM((4 * T, 256), BF),
            pltpu.VMEM((4 * T, 640), BF),
            pltpu.VMEM((T, 256), BF),
            pltpu.VMEM((T, 640), BF),
            pltpu.VMEM((KV_HEADS, rows, KEYS), BF),
            pltpu.VMEM((2, 4, 4, T, 640), BF),
            pltpu.VMEM((2, 4, 4, T, 640), BF),
            pltpu.VMEM((ROWS, 2 * FF), BF),
            pltpu.VMEM((ROWS, FF), BF),
            *sum_scratch(FF, HALF)[:3],
            pltpu.SemaphoreType.DMA((10,)),
            pltpu.SemaphoreType.DMA((13,)),
        ]
        + sems(56),
        compiler_params=pltpu.CompilerParams(
            collective_id=4, has_side_effects=True, vmem_limit_bytes=VMEM_LIMIT
        ),
        cost_estimate=pl.CostEstimate(
            flops=20_000_000_000, bytes_accessed=40_000_000, transcendentals=0
        ),
    )(mix, q, prob, kv, h, up_c, vec, *own, *rest)


def per_device(hidden, chosen, positions, w_query, w_key, w_value, w_output, w_gate, w_up, w_down, gain_attn, gain_ffn, router, d_out):
    tokens, upstream = hidden[0], d_out[0]
    own_w = (w_output, w_gate, w_up, w_down.T)
    frequency = (THETA ** (-np.arange(0, HEAD_DIM // 2) * 2.0 / HEAD_DIM)).astype(np.float32)
    vec = jnp.stack([gain_attn, gain_ffn, router]).astype(F32)
    vec = jnp.pad(vec, ((0, 5), (0, 16)))
    (
        mix_heads, prob, q_heads, kv_all, h, up_c, x1, cosine, sine, place, vec_in, wq, wk, wv, *rest_w
    ) = front(
        tokens.T, upstream.T, chosen, positions, np.tile(frequency, 4)[None, :], vec,
        w_query, w_key.T, w_value.T, *own_w
    )
    d_q_heads, d_kv, g_one, sums_down, d_attn, mixture, d_mid, out_c, d_logit, vec_out = dense(
        mix_heads, q_heads, prob, kv_all, h, up_c, vec_in, own_w, rest_w
    )
    s_gate, s_up, s_down, s_two, s_three, vector, both = back(
        d_kv, g_one, sums_down, d_q_heads, d_attn, mixture, x1, h, d_mid, out_c, d_logit, vec_in, vec_out, cosine, sine, wq, wk, wv
    )
    output, d_tokens, g_query, g_key, g_value, g_output, g_gate, g_up, g_down, vectors = finish(
        s_gate, s_up, s_down, s_two, s_three, vector, both, place, tokens.T, upstream.T
    )
    return (
        output.T[None],
        d_tokens.T[None],
        g_query,
        g_key.T,
        g_value.T,
        g_output,
        g_gate,
        g_up,
        g_down.T,
        vectors[0],
        vectors[1],
        vectors[2],
    )


def solution(mesh):
    finer = Mesh(mesh.devices.reshape(DIMS), AX)
    shard, blk = ("ylo", "core"), ("yhi", "z", "x")
    act, row, weight, vec = P(shard, blk, None), P(shard, blk), P(shard, None), P(shard)
    return jax.shard_map(
        per_device,
        mesh=finer,
        in_specs=(act, row, row) + (weight,) * 7 + (vec,) * 3 + (act,),
        out_specs=(act, act) + (weight,) * 7 + (vec,) * 3,
        check_vma=False,
    )
```

```python
import functools

import jax
import jax.numpy as jnp
import numpy as np
from jax import lax
from jax.experimental import pallas as pl
from jax.experimental.pallas import tpu as pltpu
from jax.sharding import Mesh
from jax.sharding import PartitionSpec as P

D = 960
HEADS = 15
KV_HEADS = 5
GROUPS = 3
HEAD_DIM = 64
FF = 2560
EPS = 1e-05
THETA = 10000.0
SCALE = HEAD_DIM ** (-0.5)
T = 64
PAIR = 128
SLOTS = 32
KEYS = SLOTS * T
AX = ("ylo", "core", "yhi", "z", "x")
DIMS = (2, 2, 2, 4, 4)
MESH = pl.DeviceIdType.MESH
BF = jnp.bfloat16
F32 = jnp.float32
VMEM_LIMIT = 56 * 2**20


def dot(a, b, dims=(((1,), (0,)), ((), ()))):
    return lax.dot_general(a, b, dims, preferred_element_type=F32)


NT = (((1,), (1,)), ((), ()))
TN = (((0,), (0,)), ((), ()))


def here():
    return tuple(lax.axis_index(a) for a in AX)


def neighbour(me, axis, step):
    ylo, core, yhi, z, x = me
    if axis == "z":
        z = lax.rem(z + step + 4, 4)
    elif axis == "x":
        x = lax.rem(x + step + 4, 4)
    elif axis == "pair":
        x = x + 1 - 2 * lax.rem(x, 2)
    elif axis == "yhi":
        yhi = 1 - yhi
    elif axis == "ylo":
        ylo = 1 - ylo
    elif axis == "core":
        core = 1 - core
    else:
        y = lax.rem(yhi * 2 + ylo + step + 4, 4)
        ylo, yhi = lax.rem(y, 2), y // 2
    return (ylo, core, yhi, z, x)


NEAR = (("x", 1), ("x", -1), ("z", 1), ("z", -1), ("yhi", 1))
WEIGHT = (("y", 1), ("y", -1), ("core", 1))
FAR = (("x", 2), ("z", 2))


def hail(me, partners):
    barrier = pltpu.get_barrier_semaphore()
    for axis, step in partners:
        pl.semaphore_signal(
            barrier, inc=1, device_id=neighbour(me, axis, step), device_id_type=MESH
        )


def meet(partners):
    pl.semaphore_wait(pltpu.get_barrier_semaphore(), len(partners))


class Sends:
    def __init__(self, me, send_sems, recv_sems):
        self.me, self.send_sems, self.recv_sems, self.all = me, send_sems, recv_sems, []

    def start(self, src, dst, axis, step):
        k = len(self.all)
        copy = pltpu.make_async_remote_copy(
            src_ref=src,
            dst_ref=dst,
            send_sem=self.send_sems.at[k],
            recv_sem=self.recv_sems.at[k],
            device_id=neighbour(self.me, axis, step),
            device_id_type=MESH,
        )
        copy.start()
        self.all.append(copy)
        return copy

    def finish(self):
        for copy in self.all:
            copy.wait_send()


def together(*steps):
    steps = list(steps)
    while steps:
        for step in list(steps):
            try:
                next(step)
            except StopIteration:
                steps.remove(step)


def run_lanes(lanes, order):
    for c in order:
        next(lanes[c], None)
    together(*lanes.values())


def sems(count):
    return [pltpu.SemaphoreType.DMA((count,)), pltpu.SemaphoreType.DMA((count,))]


def plus(*terms):
    total = terms[0].astype(F32)
    for term in terms[1:]:
        total = total + term.astype(F32)
    return total


class Shards:
    def __init__(self, sends):
        self.sends, self.arrived, self.last = sends, [], []
        self.color = lax.rem(sends.me[3] + sends.me[4], 2)

    def near(self, own, out):
        self.last.append(self.sends.start(own, out.at[out.shape[0] - 3], "core", 1))

    def far(self, own, out, cut):
        for step, row, rows in ((1, 0, cut), (-1, cut, own.shape[0] - cut)):
            r = pl.ds(row, rows)
            ref = out.at[out.shape[0] - 2, r]
            self.arrived.append((ref, out.at[out.shape[0] - 1, r], self.sends.start(own.at[r], ref, "y", step)))

    def relay(self):
        for ref, to, copy in self.arrived:
            copy.wait_recv()
            self.last.append(self.sends.start(ref, to, "core", 1))
        self.arrived = []

    def finish(self):
        self.relay()
        for copy in self.last:
            copy.wait_recv()
        self.last = []

    def half(self, own, out, block, cuts):
        rows, slots = own.shape[0], out.shape[0]
        sub = block // 2
        mine = self.color * (rows - block)
        relay = slots > 1
        other = slots - 2 if relay else 0

        def part(slot, start, count):
            return out.at[slot, pl.ds(pl.multiple_of(start, 16), count)]

        copies = []
        for step, off in ((1, 0), (-1, sub)):
            src = own.at[pl.ds(pl.multiple_of(mine + off, 16), sub)]
            copies.append(self.sends.start(src, part(other, mine + off, sub), "y", step))
        if relay:
            self.near(own, out)
        yield
        for copy in copies:
            copy.wait_recv()
        copies, off = [], 0
        for (axis, step), count in zip((("x", 1), ("x", -1), ("z", 1), ("z", -1)), cuts):
            ref = part(other, self.color * block + off, count)
            copies.append(self.sends.start(ref, ref, axis, step))
            off += count
        if relay:
            self.last.append(self.sends.start(part(other, mine, block), part(slots - 1, mine, block), "core", 1))
        yield
        for copy in copies:
            copy.wait_recv()
        rest = (1 - self.color) * block
        if relay:
            self.last.append(
                self.sends.start(part(other, rest, rows - block), part(slots - 1, rest, rows - block), "core", 1)
            )


def gather_steps(me, sends, kv_ref, out_ref):
    _, _, yh, z, x = me
    oy = 1 - yh
    half, quarter = T // 2, T // 4
    streams = (("x", "z", 0), ("z", "x", half))

    def slot(y, axis, step, rows, count):
        zz = lax.rem(z + step + 4, 4) if axis == "z" else z
        xx = lax.rem(x + step + 4, 4) if axis == "x" else x
        return out_ref.at[y, zz, xx, pl.ds(rows, count)]

    def line(y, axis, step, rows, count):
        if axis == "z":
            return out_ref.at[y, lax.rem(z + step + 4, 4), :, pl.ds(rows, count)]
        return out_ref.at[y, :, lax.rem(x + step + 4, 4), pl.ds(rows, count)]

    own = out_ref.at[yh, z, x]
    own[...] = kv_ref[...]
    first = sends.start(kv_ref, own, "yhi", 1)
    got = {}
    for y, tag in ((yh, 0), (oy, 1)):
        if tag:
            yield
            first.wait_recv()
        for axis, _, row in streams:
            src = slot(y, axis, 0, row, half)
            for step in (1, -1):
                got[tag, row, step] = sends.start(src, src, axis, step)
    far = {}
    for y, tag in ((yh, 0), (oy, 1)):
        yield
        for axis, _, row in streams:
            for step, off in ((1, 0), (-1, quarter)):
                got[tag, row, step].wait_recv()
                src = slot(y, axis, -step, row + off, quarter)
                far[tag, row, step] = sends.start(src, src, axis, step)
    wide = {}
    for y, tag in ((yh, 0), (oy, 1)):
        yield
        for _, axis, row in streams:
            for step in (1, -1):
                far[tag, row, step].wait_recv()
            src = line(y, axis, 0, row, half)
            for step in (1, -1):
                wide[tag, row, step] = sends.start(src, src, axis, step)
    last = []
    for y, tag in ((yh, 0), (oy, 1)):
        yield
        for _, axis, row in streams:
            for step, off in ((1, 0), (-1, quarter)):
                wide[tag, row, step].wait_recv()
                src = line(y, axis, -step, row + off, quarter)
                last.append(sends.start(src, src, axis, step))
    yield
    for copy in last:
        copy.wait_recv()


def swapped(x):
    lane = lax.broadcasted_iota(jnp.int32, x.shape, 1)
    return jnp.where(lane < HEAD_DIM // 2, pltpu.roll(x, 96, 1), pltpu.roll(x, 32, 1))


def front_kernel(
    hidden_ref, d_out_ref, chosen_ref, pos_ref, freq_ref, gain_a_ref, gain_f_ref, router_ref, wq_ref, wk_ref, wv_ref,
    wo_ref, wg_ref, wu_ref, wd_ref,
    mix_ref, prob_out, q_ref, kv_out, h_ref, up_ref, x1_ref, cos_ref, sin_ref, place_ref, vec_out_ref,
    wq_out, wk_out, wv_out, wos_ref, wgs_ref, wus_ref, wds_ref,
    compact_h, compact_d, compact_p, got_h, got_d, got_p, vecs, q_pre, kv_own,
    prob_ref, kv_ref, wq, wk, wv,
    load_sems, store_sems, send_sems, recv_sems,
):
    me = here()
    yhi, z, x = me[2:]
    loads = []
    for k, (own, to) in enumerate(((wq_ref, wq), (wk_ref, wk), (wv_ref, wv))):
        loads.append(pltpu.make_async_copy(own, to.at[0], load_sems.at[k]))
        loads[-1].start()
    hail(me, NEAR + WEIGHT)
    sends = Sends(me, send_sems, recv_sems)
    early, query, late = Shards(sends), Shards(sends), Shards(sends)
    odd = lax.rem(x, 2)
    give = pl.ds(pl.multiple_of((1 - odd) * T, T), T)
    keep = pl.ds(pl.multiple_of(odd * T, T), T)
    limit = ((yhi * 16 + z * 4 + x) // 2 + 1) * PAIR
    stores = []

    def store(a, b):
        stores.append(pltpu.make_async_copy(a, b, store_sems.at[len(stores)]))
        stores[-1].start()

    def main():
        flag = jnp.where(chosen_ref[...] > 0, 1.0, 0.0)
        token = lax.broadcasted_iota(jnp.int32, (PAIR, PAIR), 0)
        lane = lax.broadcasted_iota(jnp.int32, (PAIR, PAIR), 1)
        upto = jnp.where(token <= lane, 1.0, 0.0).astype(BF)
        count = dot(jnp.broadcast_to(flag, (16, PAIR)).astype(BF), upto)[0:1]
        total = jnp.sum(flag, axis=1, keepdims=True)
        rank = count - 1.0 + jnp.where(odd == 1, PAIR - total, 0.0)
        place = jnp.where(token.astype(F32) == rank, flag, 0.0)
        place_low = place.astype(BF)
        place_ref[...] = place_low
        compact_p[...] = jnp.broadcast_to(
            jnp.sum(place * pos_ref[...].astype(F32), axis=1, keepdims=True), (PAIR, PAIR)
        )
        compact_h[...] = dot(place_low, hidden_ref[...].astype(BF), NT).astype(BF)
        vecs[0] = jnp.zeros((8, 256), F32)
        for k, ref in enumerate((gain_a_ref, gain_f_ref, router_ref)):
            vecs[0, k : k + 1, :240] = ref[...].astype(F32).reshape(1, 240)
        meet(NEAR + WEIGHT)
        vec_far = sends.start(vecs.at[0], vecs.at[2], "y", 1)
        early.far(wk_ref, wk, 160)
        early.far(wv_ref, wv, 160)
        vec_near = sends.start(vecs.at[0], vecs.at[1], "core", 1)
        early.near(wk_ref, wk)
        early.near(wv_ref, wv)
        query.far(wq_ref, wq, 128)
        query.near(wq_ref, wq)
        swaps = [sends.start(c.at[give], g, "pair", 1) for c, g in ((compact_h, got_h), (compact_p, got_p))]
        yield
        compact_d[...] = dot(place_low, d_out_ref[...].astype(BF), NT).astype(BF)
        vec_far.wait_recv()
        vec_last = sends.start(vecs.at[2], vecs.at[3], "core", 1)
        early.relay()
        yield
        swaps[0].wait_recv()
        h = plus(compact_h[keep], got_h[...])
        h_ref[...] = h
        swaps.append(sends.start(compact_d.at[give], got_d, "pair", 1))
        swaps[1].wait_recv()
        angle = (compact_p[keep] + got_p[...]) * freq_ref[...]
        turn = lax.broadcasted_iota(jnp.int32, (T, PAIR), 1)
        cosine = jnp.where(turn < HEAD_DIM, jnp.cos(angle), 1.0)
        sine = jnp.sin(angle)
        sine = jnp.where(turn < HEAD_DIM // 2, -sine, jnp.where(turn < HEAD_DIM, sine, 0.0))
        cos_ref[...], sin_ref[...] = cosine, sine
        vec_near.wait_recv()
        vec_last.wait_recv()
        vec_out_ref[...] = jnp.zeros_like(vec_out_ref)
        for k, v in enumerate(our_order(me, [vecs[k, :, :240] for k in range(4)])):
            vec_out_ref[:, 240 * k : 240 * (k + 1)] = v
        r1 = lax.rsqrt(jnp.mean(h * h, axis=-1, keepdims=True) + EPS)
        x1_ref[...] = (h * r1 * vec_out_ref[0:1, :D]).astype(BF)
        x1_k = our_order(me, cut_four(x1_ref))
        for copy in loads:
            copy.wait()
        early.finish()
        k_pre = sum(dot(x1_k[k], wk[k], NT) for k in range(4))
        v_pre = sum(dot(x1_k[k], wv[k], NT) for k in range(4))
        for j in range(KV_HEADS):
            run = slice(HEAD_DIM * j, HEAD_DIM * (j + 1))
            tile = jnp.concatenate([k_pre[:, run], v_pre[:, run]], axis=1)
            kv_own[:, 128 * j : 128 * (j + 1)] = (tile * cosine + swapped(tile) * sine).astype(BF)
        gather = gather_steps(me, sends, kv_own, kv_ref)
        next(gather)
        yield
        next(gather)
        yield
        query.relay()
        yield
        query.finish()
        swaps[2].wait_recv()
        up_ref[...] = plus(compact_d[keep], got_d[...])
        q_pre[...] = sum(dot(x1_k[k], wq[k]) for k in range(4))
        zero = jnp.zeros((T, HEAD_DIM), F32)
        for j in range(KV_HEADS):
            for g in range(GROUPS):
                at = HEAD_DIM * (GROUPS * j + g)
                tile = jnp.concatenate([q_pre[:, at : at + HEAD_DIM], zero], axis=1)
                q_ref[j, g * T : (g + 1) * T] = (tile * cosine + swapped(tile) * sine).astype(BF)
        yield
        yield from gather
        for a, b in ((kv_ref, kv_out), (wq, wq_out), (wk, wk_out), (wv, wv_out)):
            store(a, b)
        for j in range(KV_HEADS):
            tile = kv_ref[:, :, :, :, 128 * j : 128 * (j + 1)].reshape(KEYS, 128)
            scores = dot(q_ref[j], tile, NT) * SCALE
            column = lax.broadcasted_iota(jnp.int32, scores.shape, 1)
            scores = jnp.where(column < limit, scores, -1e30)
            exponent = jnp.exp(scores - jnp.max(scores, axis=-1, keepdims=True))
            prob = (exponent * (1.0 / jnp.sum(exponent, axis=-1, keepdims=True))).astype(BF)
            prob_ref[j] = prob
            store(prob_ref.at[j], prob_out.at[j])
            mix_ref[j] = dot(prob, tile)
            yield

    small, large = (128, (32, 32, 32, 16)), (480, (128, 128, 112, 112))
    lanes = {
        "m": main(),
        "o": late.half(wo_ref, wos_ref, *small),
        "t": late.half(wg_ref, wgs_ref, *small),
        "u": late.half(wu_ref, wus_ref, *small),
        "d": late.half(wd_ref, wds_ref, *large),
    }
    run_lanes(lanes, "".join(FRONT_ORDER))
    late.finish()
    for copy in stores:
        copy.wait()
    sends.finish()


FRONT_ORDER = (
    "mmmotmmummommmomdmtummtdmmumdm",
)


def front(hidden, d_out, chosen, pos, freq, gain_a, gain_f, router, w_query, w_key, w_value, *later):
    vmem, hbm = pl.BlockSpec(memory_space=pltpu.VMEM), pl.BlockSpec(memory_space=pl.ANY)
    rows = GROUPS * T
    return pl.pallas_call(
        front_kernel,
        name="front",
        out_shape=(
            jax.ShapeDtypeStruct((KV_HEADS, rows, 128), F32),
            jax.ShapeDtypeStruct((KV_HEADS, rows, KEYS), BF),
            jax.ShapeDtypeStruct((KV_HEADS, rows, 128), BF),
            jax.ShapeDtypeStruct((2, 4, 4, T, 640), BF),
            jax.ShapeDtypeStruct((T, D), F32),
            jax.ShapeDtypeStruct((T, D), F32),
            jax.ShapeDtypeStruct((T, D), BF),
            jax.ShapeDtypeStruct((T, 128), F32),
            jax.ShapeDtypeStruct((T, 128), F32),
            jax.ShapeDtypeStruct((PAIR, PAIR), BF),
            jax.ShapeDtypeStruct((8, 1024), F32),
            jax.ShapeDtypeStruct((4, 240, 960), BF),
            jax.ShapeDtypeStruct((4, 320, 240), BF),
            jax.ShapeDtypeStruct((4, 320, 240), BF),
        )
        + tuple(jax.ShapeDtypeStruct((3,) + w.shape, BF) for w in later[:3])
        + (jax.ShapeDtypeStruct((1,) + later[3].shape, BF),),
        in_specs=[vmem] * 8 + [hbm] * 7,
        out_specs=(vmem, hbm, vmem, hbm) + (vmem,) * 7 + (hbm,) * 7,
        scratch_shapes=[
            pltpu.VMEM((PAIR, D), BF),
            pltpu.VMEM((PAIR, D), BF),
            pltpu.VMEM((PAIR, PAIR), F32),
            pltpu.VMEM((T, D), BF),
            pltpu.VMEM((T, D), BF),
            pltpu.VMEM((T, PAIR), F32),
            pltpu.VMEM((4, 8, 256), F32),
            pltpu.VMEM((T, D), F32),
            pltpu.VMEM((T, 640), BF),
            pltpu.VMEM((KV_HEADS, rows, KEYS), BF),
            pltpu.VMEM((2, 4, 4, T, 640), BF),
            pltpu.VMEM((4, 240, 960), BF),
            pltpu.VMEM((4, 320, 240), BF),
            pltpu.VMEM((4, 320, 240), BF),
            pltpu.SemaphoreType.DMA((3,)),
            pltpu.SemaphoreType.DMA((9,)),
        ]
        + sems(90),
        compiler_params=pltpu.CompilerParams(
            collective_id=1, has_side_effects=True, vmem_limit_bytes=VMEM_LIMIT
        ),
        cost_estimate=pl.CostEstimate(flops=5_000_000_000, bytes_accessed=90_000_000, transcendentals=0),
    )(hidden, d_out, chosen, pos, freq, gain_a, gain_f, router, w_query, w_key, w_value, *later)


def key_steps(me, sends, part_ref, out_ref, low, out_b, full, sums, nlow, nout, nfull, mine, y_in):
    _, _, yh, z, x = me
    half, quarter = T // 2, T // 4
    streams = (("x", "z", 0), ("z", "x", half))

    def line(axis, step, row, count):
        if axis == "z":
            return part_ref.at[:, lax.rem(z + step + 4, 4), :, pl.ds(row, count)]
        return part_ref.at[:, :, lax.rem(x + step + 4, 4), pl.ds(row, count)]

    near = {}
    for s, (axis, _, row) in enumerate(streams):
        near[s, 1] = sends.start(line(axis, 2, row, quarter), low.at[s, 0], axis, 1)
        near[s, -1] = sends.start(line(axis, 2, row + quarter, quarter), low.at[s, 1], axis, -1)
    whole = {}
    for s, (axis, _, row) in enumerate(streams):
        yield
        for d, step in enumerate((1, -1)):
            near[s, step].wait_recv()
            lo, hi = (0, quarter) if step == 1 else (quarter, 0)
            out_b[s, d, :, :, pl.ds(lo, quarter)] = plus(
                line(axis, step, row + lo, quarter)[...], low[s, d]
            ).astype(BF)
            out_b[s, d, :, :, pl.ds(hi, quarter)] = line(axis, step, row + hi, quarter)[...]
            whole[s, step] = sends.start(out_b.at[s, d], full.at[s, d], axis, step)
    near = {}
    for s, (axis, other, row) in enumerate(streams):
        yield
        for step in (1, -1):
            whole[s, step].wait_recv()
        sums[s] = plus(line(axis, 0, row, half)[...], full[s, 0], full[s, 1]).astype(BF)
        far = lax.rem((z if other == "z" else x) + 2, 4)
        near[s, 1] = sends.start(sums.at[s, :, far, pl.ds(0, quarter)], nlow.at[s, 0], other, 1)
        near[s, -1] = sends.start(
            sums.at[s, :, far, pl.ds(quarter, quarter)], nlow.at[s, 1], other, -1
        )
    for s, (axis, other, row) in enumerate(streams):
        yield
        at = z if other == "z" else x
        for d, step in enumerate((1, -1)):
            near[s, step].wait_recv()
            to = lax.rem(at + step + 4, 4)
            lo, hi = (0, quarter) if step == 1 else (quarter, 0)
            nout[s, d, :, pl.ds(lo, quarter)] = plus(
                sums[s, :, to, pl.ds(lo, quarter)], nlow[s, d]
            ).astype(BF)
            nout[s, d, :, pl.ds(hi, quarter)] = sums[s, :, to, pl.ds(hi, quarter)]
            whole[s, step] = sends.start(nout.at[s, d], nfull.at[s, d], other, step)
    swap = {}
    for s, (axis, other, row) in enumerate(streams):
        yield
        at = z if other == "z" else x
        for step in (1, -1):
            whole[s, step].wait_recv()
        mine[s] = plus(sums[s, :, at], nfull[s, 0], nfull[s, 1]).astype(BF)
        swap[s] = sends.start(mine.at[s, 1 - yh], y_in.at[s], "yhi", 1)
    yield
    for s, (axis, other, row) in enumerate(streams):
        swap[s].wait_recv()
        out_ref[pl.ds(row, half)] = plus(mine[s, yh], y_in[s])


def key_scratch():
    half, quarter, w = T // 2, T // 4, 640
    return [
        pltpu.VMEM((2, 2, 2, 4, quarter, w), BF),
        pltpu.VMEM((2, 2, 2, 4, half, w), BF),
        pltpu.VMEM((2, 2, 2, 4, half, w), BF),
        pltpu.VMEM((2, 2, 4, half, w), BF),
        pltpu.VMEM((2, 2, 2, quarter, w), BF),
        pltpu.VMEM((2, 2, 2, half, w), BF),
        pltpu.VMEM((2, 2, 2, half, w), BF),
        pltpu.VMEM((2, 2, half, w), BF),
        pltpu.VMEM((2, half, w), BF),
    ]


ROWS = 256
HALF = ROWS // 2
STREAMS = (("x", "z"), ("z", "x"))


def spots(me):
    return {"z": me[3], "x": me[4]}


def around(me, axis, step):
    return lax.rem(spots(me)[axis] + step + 4, 4)


def columns(me, axis, step, big):
    return pl.ds(pl.multiple_of(around(me, axis, step) * big, 128), big)


def halves(big):
    cut = (big // 2 + 127) // 128 * 128
    return (0, cut), (cut, big - cut)


def wide_steps(me, sends, g_ref, low, out_b, full, sums):
    h, big = sums.shape[0] // 2, sums.shape[1]
    cut = h // 2
    near, whole = {}, {}

    def parts(step):
        return (0, cut) if step == 1 else (cut, 0)

    for s, (axis, _) in enumerate(STREAMS):
        c = columns(me, axis, 2, big)
        for step in (1, -1):
            r = pl.ds(s * h + parts(step)[0], cut)
            near[s, step] = sends.start(g_ref.at[r, c], low.at[r], axis, step)
    for s, (axis, _) in enumerate(STREAMS):
        yield
        for d, step in enumerate((1, -1)):
            near[s, step].wait_recv()
            add, keep = (pl.ds(s * h + p, cut) for p in parts(step))
            c = columns(me, axis, step, big)
            out_b[d, add] = plus(g_ref[add, c], low[add]).astype(BF)
            out_b[d, keep] = g_ref[keep, c]
            r = pl.ds(s * h, h)
            whole[s, step] = sends.start(out_b.at[d, r], full.at[d, r], axis, step)

    for s, (axis, _) in enumerate(STREAMS):
        yield
        for step in (1, -1):
            whole[s, step].wait_recv()
        r = pl.ds(s * h, h)
        sums[r] = plus(g_ref[r, columns(me, axis, 0, big)], full[0, r], full[1, r]).astype(BF)


def narrow_steps(me, sends, sums, mine, swap_y, nlow, nout, nfull, y_in):
    run, big = mine.shape[-2:]
    h = 4 * run
    near, whole = {}, {}

    def rows(s, other, step):
        return pl.ds(pl.multiple_of(s * h + around(me, other, step) * run, 16), run)

    for s, (axis, other) in enumerate(STREAMS):
        for d, step in enumerate((1, -1)):
            c = pl.ds(*halves(big)[d])
            near[s, step] = sends.start(sums.at[rows(s, other, 2), c], nlow.at[s, :, c], other, step)
    for s, (axis, other) in enumerate(STREAMS):
        yield
        for d, step in enumerate((1, -1)):
            near[s, step].wait_recv()
            add, keep = pl.ds(*halves(big)[d]), pl.ds(*halves(big)[1 - d])
            r = rows(s, other, step)
            nout[s, d, :, add] = plus(sums[r, add], nlow[s, :, add]).astype(BF)
            nout[s, d, :, keep] = sums[r, keep]
            whole[s, step] = sends.start(nout.at[s, d], nfull.at[s, d], other, step)
    swap = {}
    for s, (axis, other) in enumerate(STREAMS):
        yield
        for step in (1, -1):
            whole[s, step].wait_recv()
        total = plus(sums[rows(s, other, 0)], nfull[s, 0], nfull[s, 1]).astype(BF)
        if swap_y:
            y_in[0, s] = total
            swap[s] = sends.start(y_in.at[0, s], y_in.at[1, s], "yhi", 1)
        else:
            mine[s] = total
    if swap_y:
        for s in range(2):
            yield
            swap[s].wait_recv()
            mine[s] = plus(y_in[0, s], y_in[1, s]).astype(BF)


def sum_steps(me, sends, g_ref, mine, swap_y, low, out_b, full, sums, *narrow):
    yield from wide_steps(me, sends, g_ref, low, out_b, full, sums)
    yield from narrow_steps(me, sends, sums, mine, swap_y, *narrow)


def sum_scratch(width, h):
    big, run = width // 4, h // 4
    return [
        pltpu.VMEM((2 * h, big), BF),
        pltpu.VMEM((2, 2 * h, big), BF),
        pltpu.VMEM((2, 2 * h, big), BF),
        pltpu.VMEM((2 * h, big), BF),
        pltpu.VMEM((2, run, big), BF),
        pltpu.VMEM((2, 2, run, big), BF),
        pltpu.VMEM((2, 2, run, big), BF),
        pltpu.VMEM((2, 2, run, big), BF),
    ]


def spread_steps(me, sends, mine, out_ref, store_sems, to_y):
    run, big = mine.shape[-2:]
    h = 4 * run
    cut = h // 2
    near, whole, stored, last, over = {}, {}, [], {}, []

    def base(s):
        return s * HALF + (me[2] * h if to_y else 0)

    def rows(s, off, count):
        return pl.ds(pl.multiple_of(base(s) + off, 16), count)

    def block(s, axis, step, off, count):
        return out_ref.at[rows(s, off, count), columns(me, axis, step, big)]

    def on(ref):
        if to_y:
            over.append(sends.start(ref, ref, "yhi", 1))

    for s, (axis, other) in enumerate(STREAMS):
        ref = block(s, axis, 0, around(me, other, 0) * run, run)
        for step in (1, -1):
            near[s, step] = sends.start(mine.at[s], ref, other, step)
        stored.append(pltpu.make_async_copy(mine.at[s], ref, store_sems.at[s]))
        stored[-1].start()

    def narrow(s, axis, other, step, d):
        c0, n = halves(big)[d]
        c = pl.ds(pl.multiple_of(around(me, axis, 0) * big + c0, 128), n)
        return out_ref.at[rows(s, around(me, other, step) * run, run), c]

    for s, (axis, other) in enumerate(STREAMS):
        yield
        for d, step in enumerate((1, -1)):
            near[s, step].wait_recv()
            ref = narrow(s, axis, other, -step, d)
            whole[s, step] = sends.start(ref, ref, other, step)
    for s, (axis, other) in enumerate(STREAMS):
        yield
        for step in (1, -1):
            whole[s, step].wait_recv()
        stored[s].wait()
        ref = block(s, axis, 0, 0, h)
        for step in (1, -1):
            near[s, step] = sends.start(ref, ref, axis, step)
        on(ref)
    for s, (axis, other) in enumerate(STREAMS):
        yield
        for d, step in enumerate((1, -1)):
            near[s, step].wait_recv()
            ref = block(s, axis, -step, d * cut, cut)
            last[s, step] = sends.start(ref, ref, axis, step)
            on(block(s, axis, -step, 0, h))
    for s, (axis, other) in enumerate(STREAMS):
        yield
        for step in (1, -1):
            last[s, step].wait_recv()
        on(block(s, axis, 2, 0, h))
    if to_y:
        yield
        for copy in over:
            copy.wait_recv()


def halved_steps(me, sends, g_ref, mine, kept, got, out_ref, store_sems, *scratch):
    h = HALF // 2
    yh = me[2]
    copies = []
    for s in range(2):
        give = pl.ds(pl.multiple_of(s * HALF + (1 - yh) * h, 16), h)
        copies.append(sends.start(g_ref.at[give], got.at[pl.ds(s * h, h)], "yhi", 1))
    for s in range(2):
        yield
        copies[s].wait_recv()
        r = pl.ds(s * h, h)
        kept[r] = plus(g_ref[pl.ds(pl.multiple_of(s * HALF + yh * h, 16), h)], got[r]).astype(BF)
    yield
    yield from sum_steps(me, sends, kept, mine, False, *scratch)
    yield from spread_steps(me, sends, mine, out_ref, store_sems, True)


def vector_steps(sends, vec_ref, out_ref, keep, got):
    rounds = ((("core", 1),), (("ylo", 1),), (("x", 1), ("x", -1), ("x", 2)), (("z", 1), ("z", -1), ("z", 2)), (("yhi", 1),))
    keep[0] = vec_ref[...]
    k = 0
    for at, partners in enumerate(rounds):
        copies = []
        for axis, step in partners:
            copies.append((k, sends.start(keep.at[at], got.at[k], axis, step)))
            k += 1
        yield
        total = keep[at]
        for slot, copy in copies:
            copy.wait_recv()
            total = total + got[slot]
        keep[at + 1] = total
    out_ref[...] = keep[len(rounds)]


def small_steps(me, sends, g_ref, out_ref, got_x, got_z, got_y, sum_z, sum_y):
    x, z = me[3], me[4]
    steps = (1, -1, 2)

    def rows(at, step, count, base=0):
        return pl.ds(pl.multiple_of(base + lax.rem(at + step + 4, 4) * count, 16), count)

    copies = [
        sends.start(g_ref.at[rows(x, step, 64)], got_x.at[k], "z", step) for k, step in enumerate(steps)
    ]
    yield
    for copy in copies:
        copy.wait_recv()
    sum_z[...] = plus(g_ref[rows(x, 0, 64)], got_x[0], got_x[1], got_x[2]).astype(BF)
    copies = [
        sends.start(sum_z.at[rows(z, step, 16)], got_z.at[k], "x", step) for k, step in enumerate(steps)
    ]
    yield
    for copy in copies:
        copy.wait_recv()
    sum_y[...] = plus(sum_z[rows(z, 0, 16)], got_z[0], got_z[1], got_z[2]).astype(BF)
    copy = sends.start(sum_y, got_y, "yhi", 1)
    yield
    copy.wait_recv()
    ref = out_ref.at[rows(z, 0, 16, x * 64)]
    ref[...] = plus(sum_y[...], got_y[...]).astype(BF)
    copies = [sends.start(ref, ref, "x", step) for step in steps]
    yield
    for copy in copies:
        copy.wait_recv()
    ref = out_ref.at[rows(x, 0, 64)]
    copies = [sends.start(ref, ref, "z", step) for step in steps]
    yield
    for copy in copies:
        copy.wait_recv()


KEY_N, SUM_N = 9, 8
WIDE, REST = FF, 2048


def back_kernel(
    part_ref, g_in, sums_ref, dq_ref, d_attn_ref, mixture_ref, x1_ref, h_ref, d_mid_ref, logit_ref, vec_ref, vec_part_ref,
    cos_ref, sin_ref, wq_in, wk_in, wv_in,
    gate_ref, up_ref, down_ref, two_ref, three_ref, vec_out_ref, both_ref,
    own, ra, rb, xs, ra_all, rb_all, xs_all, xs_relay, g_two, g_three, d_x1_s, vec_all, keep_v, got_v,
    mine_gate, mine_up, mine_down, mine_two, got_x, got_z, got_y, sum_z, sum_y,
    g_gate, g_up, kept, got_gate, wq, wk, wv, load_sems, store_sems,
    *scratch,
):
    me = here()
    key_scr, rest = scratch[:KEY_N], scratch[KEY_N:-2]
    gate_scr, up_scr, two_scr, down_scr = (rest[SUM_N * k : SUM_N * (k + 1)] for k in range(4))
    loads = [
        pltpu.make_async_copy(a, b, load_sems.at[k])
        for k, (a, b) in enumerate(
            (
                (g_in.at[:, pl.ds(0, WIDE)], g_gate),
                (g_in.at[:, pl.ds(WIDE, WIDE)], g_up),
                (wq_in, wq),
                (wk_in, wk),
                (wv_in, wv),
            )
        )
    ]
    for copy in loads:
        copy.start()
    hail(me, NEAR + WEIGHT + FAR)
    sends = Sends(me, *scratch[-2:])
    odd = lax.rem(me[4], 2)
    keep = pl.ds(pl.multiple_of(odd * T, T), T)
    cosine, sine = cos_ref[...], sin_ref[...]
    mine = pl.ds(0, T)

    def turned_back(tile):
        return tile * cosine - swapped(tile) * sine

    for j in range(KV_HEADS):
        for g in range(GROUPS):
            at = HEAD_DIM * (GROUPS * j + g)
            ra[:, at : at + HEAD_DIM] = turned_back(dq_ref[j, g * T : (g + 1) * T]).astype(BF)[:, :HEAD_DIM]
    ra[:, D:] = d_attn_ref[...]
    xs[...] = jnp.zeros_like(xs)
    for k, (a, b) in enumerate(zip(our_order(me, cut_four(x1_ref)), our_order(me, cut_four(mixture_ref)))):
        xs[k, :, :240] = a
        xs[k, :, 256:496] = b
    meet(NEAR + WEIGHT + FAR)

    def keys():
        yield from key_steps(me, sends, part_ref, own, *key_scr)
        for j in range(KV_HEADS):
            tile = turned_back(own[:, 128 * j : 128 * (j + 1)]).astype(BF)
            rb[:, HEAD_DIM * j : HEAD_DIM * (j + 1)] = tile[:, :HEAD_DIM]
            rb[:, 320 + HEAD_DIM * j : 320 + HEAD_DIM * (j + 1)] = tile[:, HEAD_DIM:]
        share = everyone_steps(sends, (("all", rb, rb_all, None),))
        next(share)
        rb_all[mine] = rb[...]
        d_k, d_v = rb[:, :320], rb[:, 320:]
        d_x1 = d_x1_s[...] + jnp.concatenate(
            our_order(me, [dot(d_k, wk[k]) + dot(d_v, wv[k]) for k in range(4)]), axis=1
        )
        h = h_ref[...]
        r1 = lax.rsqrt(jnp.mean(h * h, axis=-1, keepdims=True) + EPS)
        d_first, g_gain_a = norm_back_rows(h, r1, vec_ref[0:1, :D], d_x1)
        d_h = d_mid_ref[...] + d_first + logit_ref[:, 0:1] * vec_ref[2:3, :D]
        both_ref[keep] = d_h.astype(BF)
        swap = sends.start(both_ref.at[keep], both_ref.at[keep], "pair", 1)
        vec_all[...] = vec_part_ref[...]
        vec_all[0:1, :D] = g_gain_a
        vectors = vector_steps(sends, vec_all, vec_out_ref, keep_v, got_v)
        next(vectors)
        yield
        next(share)
        yield
        together(share)
        g_three[...] = dot(xs_all[:, :256], rb_all[...], TN).astype(BF)
        small = small_steps(me, sends, g_three, three_ref, got_x, got_z, got_y, sum_z, sum_y)
        while True:
            for step in (small, vectors):
                next(step, None)
            if small.gi_frame is None and vectors.gi_frame is None:
                break
            yield
        swap.wait_recv()

    def queries():
        share = everyone_steps(
            sends, (("all", ra, ra_all, None), ("one", [xs.at[k] for k in range(4)], xs_all, xs_relay))
        )
        next(share)
        ra_all[mine] = ra[...]
        xs_all[mine] = xs[0]
        d_q = ra[:, :D]
        for copy in loads[2:]:
            copy.wait()
        d_x1_s[...] = jnp.concatenate(our_order(me, [dot(d_q, wq[k], NT) for k in range(4)]), axis=1)
        g_two[:, 2 * D :] = jnp.zeros((ROWS, 128), BF)
        yield
        next(share)
        yield
        together(share)
        g_two[:, :D] = dot(xs_all[:, :256], ra_all[:, :D], TN).astype(BF)
        g_two[:, D : 2 * D] = dot(xs_all[:, 256:], ra_all[:, D:], TN).astype(BF)
        yield from sum_steps(me, sends, g_two, mine_two, True, *two_scr)
        yield from spread_steps(me, sends, mine_two, two_ref, store_sems.at[pl.ds(6, 2)], False)

    def gate():
        loads[0].wait()
        yield from halved_steps(
            me, sends, g_gate, mine_gate, kept, got_gate, gate_ref, store_sems.at[pl.ds(0, 2)], *gate_scr
        )

    def up():
        loads[1].wait()
        yield from sum_steps(me, sends, g_up, mine_up, True, *up_scr)
        yield from spread_steps(me, sends, mine_up, up_ref, store_sems.at[pl.ds(2, 2)], False)

    def down():
        yield from narrow_steps(me, sends, sums_ref, mine_down, True, *down_scr)
        yield from spread_steps(me, sends, mine_down, down_ref, store_sems.at[pl.ds(4, 2)], False)

    run_lanes({"k": keys(), "g": gate(), "u": up(), "d": down(), "q": queries()}, "".join(ORDER))
    sends.finish()


ORDER = (
    "kgdukkquugkkgddguukkqdqgdukgkdqudqggkqdk",
    "qgkguqgdqugddqqgukguqqgugdudqqkuguqqdkuu",
    "gdgkuuqgqgqqk",
)


def back(*args):
    vmem, hbm = pl.BlockSpec(memory_space=pltpu.VMEM), pl.BlockSpec(memory_space=pl.ANY)
    return pl.pallas_call(
        back_kernel,
        name="back",
        out_shape=(
            jax.ShapeDtypeStruct((ROWS, WIDE), BF),
            jax.ShapeDtypeStruct((ROWS, WIDE), BF),
            jax.ShapeDtypeStruct((ROWS, WIDE), BF),
            jax.ShapeDtypeStruct((ROWS, REST), BF),
            jax.ShapeDtypeStruct((ROWS, 640), BF),
            jax.ShapeDtypeStruct((8, 1024), F32),
            jax.ShapeDtypeStruct((PAIR, D), BF),
        ),
        in_specs=[vmem, hbm] + [vmem] * (len(args) - 5) + [hbm] * 3,
        out_specs=(hbm,) * 4 + (vmem,) * 3,
        scratch_shapes=[
            pltpu.VMEM((T, 640), F32),
            pltpu.VMEM((T, 2 * D), BF),
            pltpu.VMEM((T, 640), BF),
            pltpu.VMEM((4, T, 512), BF),
            pltpu.VMEM((4 * T, 2 * D), BF),
            pltpu.VMEM((4 * T, 640), BF),
            pltpu.VMEM((4 * T, 512), BF),
            pltpu.VMEM((T, 512), BF),
            pltpu.VMEM((ROWS, REST), BF),
            pltpu.VMEM((ROWS, 640), BF),
            pltpu.VMEM((T, D), F32),
            pltpu.VMEM((8, 1024), F32),
            pltpu.VMEM((6, 8, 1024), F32),
            pltpu.VMEM((9, 8, 1024), F32),
            pltpu.VMEM((2, HALF // 8, WIDE // 4), BF),
            pltpu.VMEM((2, HALF // 4, WIDE // 4), BF),
            pltpu.VMEM((2, HALF // 4, WIDE // 4), BF),
            pltpu.VMEM((2, HALF // 4, REST // 4), BF),
            pltpu.VMEM((3, 64, 640), BF),
            pltpu.VMEM((3, 16, 640), BF),
            pltpu.VMEM((16, 640), BF),
            pltpu.VMEM((64, 640), BF),
            pltpu.VMEM((16, 640), BF),
            pltpu.VMEM((ROWS, WIDE), BF),
            pltpu.VMEM((ROWS, WIDE), BF),
            pltpu.VMEM((HALF, WIDE), BF),
            pltpu.VMEM((HALF, WIDE), BF),
            pltpu.VMEM((4, 240, 960), BF),
            pltpu.VMEM((4, 320, 240), BF),
            pltpu.VMEM((4, 320, 240), BF),
            pltpu.SemaphoreType.DMA((6,)),
            pltpu.SemaphoreType.DMA((8,)),
        ]
        + key_scratch()
        + sum_scratch(WIDE, HALF // 2)
        + sum_scratch(WIDE, HALF)
        + sum_scratch(REST, HALF)
        + sum_scratch(WIDE, HALF)[4:]
        + sems(230),
        compiler_params=pltpu.CompilerParams(
            collective_id=2, has_side_effects=True, vmem_limit_bytes=VMEM_LIMIT
        ),
        cost_estimate=pl.CostEstimate(flops=2_000_000_000, bytes_accessed=200_000_000, transcendentals=0),
    )(*args)


def finish_kernel(
    g_gate_ref, g_up_ref, g_down_ref, two_ref, three_ref, vec_ref, out_rows_ref, d_rows_ref, place_ref, hidden_ref, d_out_ref,
    out_ref, d_hidden_ref, query_ref, key_ref, value_ref, output_ref, gate_ref, up_ref, down_ref, vec_a_ref, vec_f_ref, vec_r_ref,
    low_one, low_down, low_two, low_three, wide_one, wide_two, wide_down, wide_kv, rows, load_sems, store_sems,
):
    keep = pl.ds(0, 240)
    runs_one = [pl.ds(1280 * k, 1280) for k in range(2)]
    runs_down = [pl.ds(640 * k, 640) for k in range(4)]
    loads = []
    for src, dst, runs in (
        (g_gate_ref, low_one.at[0], runs_one),
        (g_up_ref, low_one.at[1], runs_one),
        (g_down_ref, low_down, runs_down),
        (two_ref, low_two, [pl.ds(0, 2 * D)]),
        (three_ref, low_three, [pl.ds(0, 640)]),
    ):
        for c in runs:
            loads.append(pltpu.make_async_copy(src.at[keep, c], dst.at[:, c], load_sems.at[len(loads)]))
            loads[-1].start()
    stores = []

    def store(a, b):
        stores.append(pltpu.make_async_copy(a, b, store_sems.at[len(stores)]))
        stores[-1].start()

    for k, (base, at_rank, to) in enumerate(
        ((hidden_ref, out_rows_ref, out_ref), (d_out_ref, d_rows_ref, d_hidden_ref))
    ):
        rows[k] = base[...] + dot(at_rank[...], place_ref[...], TN)
        store(rows.at[k], to)
    for k in range(4):
        loads[k].wait()
        c = runs_one[k % 2]
        wide_one[k // 2, :, c] = low_one[k // 2, :, c].astype(F32)
        store(wide_one.at[k // 2, :, c], (gate_ref, up_ref)[k // 2].at[:, c])
    for k in range(4):
        loads[4 + k].wait()
        r = pl.ds(240 * k, 240)
        wide_down[r] = low_down[:, runs_down[k]].astype(F32)
        store(wide_down.at[r], down_ref.at[r])
    loads[8].wait()
    for k, to in enumerate((query_ref, output_ref)):
        wide_two[k] = low_two[:, D * k : D * (k + 1)].astype(F32)
        store(wide_two.at[k], to)
    loads[9].wait()
    for k, to in enumerate((key_ref, value_ref)):
        wide_kv[k] = low_three[:, 320 * k : 320 * (k + 1)].astype(F32).T
        store(wide_kv.at[k], to)
    core, ylo = lax.axis_index("core") == 1, lax.axis_index("ylo") == 1
    p = [vec_ref[:, 240 * k : 240 * (k + 1)] for k in range(4)]
    p = jnp.where(ylo, jnp.where(core, p[3], p[2]), jnp.where(core, p[1], p[0]))
    for k, ref in enumerate((vec_a_ref, vec_f_ref, vec_r_ref)):
        ref[...] = p[k : k + 1].reshape(240)
    for copy in stores:
        copy.wait()


def finish(*args):
    vmem, hbm = pl.BlockSpec(memory_space=pltpu.VMEM), pl.BlockSpec(memory_space=pl.ANY)
    shapes = [(D, PAIR), (D, PAIR), (240, D), (320, 240), (320, 240), (240, D), (240, FF), (240, FF), (D, 640), (240,), (240,), (240,)]
    return pl.pallas_call(
        finish_kernel,
        name="finish",
        out_shape=tuple(jax.ShapeDtypeStruct(shape, F32) for shape in shapes),
        in_specs=[hbm] * 5 + [vmem] * 6,
        out_specs=(hbm,) * 9 + (vmem,) * 3,
        scratch_shapes=[
            pltpu.VMEM((2, 240, WIDE), BF),
            pltpu.VMEM((240, WIDE), BF),
            pltpu.VMEM((240, REST), BF),
            pltpu.VMEM((240, 640), BF),
            pltpu.VMEM((2, 240, WIDE), F32),
            pltpu.VMEM((2, 240, D), F32),
            pltpu.VMEM((D, 640), F32),
            pltpu.VMEM((2, 320, 240), F32),
            pltpu.VMEM((2, D, PAIR), F32),
            pltpu.SemaphoreType.DMA((10,)),
            pltpu.SemaphoreType.DMA((14,)),
        ],
        compiler_params=pltpu.CompilerParams(vmem_limit_bytes=VMEM_LIMIT),
        cost_estimate=pl.CostEstimate(flops=0, bytes_accessed=16_000_000, transcendentals=0),
    )(*args)


def shard_of(me, k):
    ylo, core = me[0], me[1]
    return (ylo if k < 2 else 1 - ylo) * 2 + (core if k % 2 == 0 else 1 - core)


def our_order(me, p):
    core, ylo = me[1] == 1, me[0] == 1
    p = [jnp.where(core, p[k ^ 1], p[k]) for k in range(4)]
    return [jnp.where(ylo, p[k ^ 2], p[k]) for k in range(4)]


def cut_four(ref):
    return [ref[:, 240 * k : 240 * (k + 1)] for k in range(4)]


def norm_back_rows(z, r, gain, dy):
    dz = r * (gain * dy) - z * (r * r * r) * jnp.mean(gain * dy * z, axis=-1, keepdims=True)
    return dz, jnp.sum(dy * z * r, axis=0, keepdims=True)


def everyone_steps(sends, pieces):
    half = T // 2
    arrived, last = [], []
    for kind, source, whole, relay in pieces:
        near = source if kind == "all" else source[1]
        last.append(sends.start(near, whole.at[pl.ds(T, T)], "core", 1))
    for step, at in ((1, 0), (-1, half)):
        r = pl.ds(at, half)
        for kind, source, whole, relay in pieces:
            far = source if kind == "all" else source[2]
            arrived.append((sends.start(far.at[r], whole.at[pl.ds(2 * T + at, half)], "y", step), None))
            if kind == "all":
                arrived[-1] = (arrived[-1][0], (whole.at[pl.ds(2 * T + at, half)], whole.at[pl.ds(3 * T + at, half)]))
            else:
                copy = sends.start(source[3].at[r], relay.at[r], "y", step)
                arrived.append((copy, (relay.at[r], whole.at[pl.ds(3 * T + at, half)])))
    yield
    for copy, onward in arrived:
        copy.wait_recv()
        if onward is not None:
            last.append(sends.start(onward[0], onward[1], "core", 1))
    yield
    for copy in last:
        copy.wait_recv()


def dense_kernel(
    mix_ref, q_ref, prob_in, kv_in, h_ref, up_ref, vec_ref,
    wo_ref, wg_ref, wu_ref, wd_ref, wos_ref, wgs_ref, wus_ref, wds_ref,
    dq_ref, dkv_out, g_out, sums_ref, d_attn_ref, mixture_ref, d_mid_ref, out_ref, logit_ref, vec_out_ref,
    wo, wg, wu, wd, mixf, gate_s, up_s, inner, dgu, dffn, xs, do_s, d_mix_s,
    dgu_all, dffn_all, xs_all, inner_all, xs_relay, inner_relay,
    prob_ref, kv_ref, dkv_ref, g_ref, g_down, low, out_b, full,
    load_sems, store_sems, send_sems, recv_sems,
):
    me = here()
    loads = []
    for k, (own, rest, to) in enumerate(
        ((wo_ref, wos_ref, wo), (wg_ref, wgs_ref, wg), (wu_ref, wus_ref, wu), (wd_ref, wds_ref, wd))
    ):
        there = to.at[pl.ds(1, 3)] if k < 3 else to.at[pl.ds(2, 1)]
        pair = (
            pltpu.make_async_copy(own, to.at[0], load_sems.at[2 * k]),
            pltpu.make_async_copy(rest, there, load_sems.at[2 * k + 1]),
        )
        for copy in pair:
            copy.start()
        loads.append(pair)
    loads.append(
        (
            pltpu.make_async_copy(prob_in, prob_ref, load_sems.at[8]),
            pltpu.make_async_copy(kv_in, kv_ref, load_sems.at[9]),
        )
    )
    for copy in loads[4]:
        copy.start()
    hail(me, NEAR[:4] + WEIGHT)
    sends = Sends(me, send_sems, recv_sems)
    shards = [shard_of(me, k) for k in range(4)]

    def run640(k):
        return pl.ds(pl.multiple_of(shards[k] * 640, 128), 640)

    def loaded(k):
        for copy in loads[k]:
            copy.wait()

    for j in range(KV_HEADS):
        for g in range(GROUPS):
            h = GROUPS * j + g
            mixf[:, HEAD_DIM * h : HEAD_DIM * (h + 1)] = mix_ref[j, g * T : (g + 1) * T, HEAD_DIM:]
    mixture_ref[...] = mixf[...].astype(BF)
    mix_k = our_order(me, cut_four(mixture_ref))
    loaded(0)
    attn_out = sum(dot(mix_k[k], wo[k]) for k in range(4))
    hidden = h_ref[...]
    gain_f = vec_ref[1:2, :D]
    route_w = vec_ref[2:3, :D]
    middle = hidden + attn_out
    r2 = lax.rsqrt(jnp.mean(middle * middle, axis=-1, keepdims=True) + EPS)
    x2 = middle * r2 * gain_f
    x2_k = our_order(me, [x2[:, 240 * k : 240 * (k + 1)].astype(BF) for k in range(4)])
    xs[...] = jnp.zeros_like(xs)
    for k in range(4):
        xs[k, :, :240] = x2_k[k]
    meet(NEAR[:4] + WEIGHT)
    down = [
        sends.start(wd_ref, wd.at[1], "core", 1),
        sends.start(wds_ref.at[0], wd.at[3], "core", 1),
    ]
    shares = [everyone_steps(sends, (("one", [xs.at[k] for k in range(4)], xs_all, xs_relay),))]
    next(shares[0])
    loaded(1)
    gate_s[...] = sum(dot(x2_k[k], wg[k]) for k in range(4))
    loaded(2)
    up_s[...] = sum(dot(x2_k[k], wu[k]) for k in range(4))
    gate = gate_s[...]
    inner[...] = (gate * jax.nn.sigmoid(gate) * up_s[...]).astype(BF)
    loaded(3)
    shares.append(
        everyone_steps(sends, (("one", [inner.at[:, run640(k)] for k in range(4)], inner_all, inner_relay),))
    )
    next(shares[1])
    for copy in down:
        copy.wait_recv()
    ffn_out = sum(dot(inner[:, run640(k)], wd[k], NT) for k in range(4))
    route = jax.nn.sigmoid(jnp.sum(hidden * route_w, axis=-1, keepdims=True))
    branch = attn_out + ffn_out
    odd = lax.rem(me[4], 2)
    keep = pl.ds(pl.multiple_of(odd * T, T), T)
    out_ref[keep] = (route * branch).astype(BF)
    swap = sends.start(out_ref.at[keep], out_ref.at[keep], "pair", 1)
    upstream = up_ref[...]
    d_branch = upstream * route
    d_logit = route * (1.0 - route) * jnp.sum(upstream * branch, axis=-1, keepdims=True)
    logit_ref[...] = jnp.broadcast_to(d_logit, logit_ref.shape)
    vec_out_ref[...] = jnp.zeros_like(vec_out_ref)
    vec_out_ref[2:3, :D] = jnp.sum(d_logit * hidden, axis=0, keepdims=True)
    d_ffn = d_branch.astype(BF)
    own = pl.ds(0, T)
    dffn[...] = jnp.zeros_like(dffn)
    for k in range(4):
        dffn[:, 256 * k : 256 * k + 240] = d_branch[:, 240 * k : 240 * (k + 1)].astype(BF)
    shares.append(everyone_steps(sends, (("all", dffn, dffn_all, None),)))
    next(shares[2])
    dffn_all[own], xs_all[own], inner_all[own] = dffn[...], xs[0], inner[:, run640(0)]
    late = []
    for p in range(2):
        first = 2 * lax.rem(me[0] + p, 2)
        for b in range(2):
            at = (2 * p + (me[1] if b == 0 else 1 - me[1])) * 640
            run, run_up = (pl.ds(pl.multiple_of(c + at, 128), 640) for c in (0, FF))
            d_inner = dot(d_ffn, wd[first + b])
            gate, up = gate_s[:, run], up_s[:, run]
            sg = jax.nn.sigmoid(gate)
            dgu[:, run] = (d_inner * up * (sg + gate * sg * (1.0 - sg))).astype(BF)
            dgu[:, run_up] = (d_inner * (gate * sg)).astype(BF)
        cols = [pl.ds(c + 1280 * p, 1280) for c in (0, FF)]
        late.append(everyone_steps(sends, tuple(("all", dgu.at[:, c], dgu_all.at[:, c], None) for c in cols)))
        next(late[-1])
    for share in shares:
        next(share)
    dgu_all[own] = dgu[...]
    d_gate, d_up = dgu[:, :FF], dgu[:, FF:]
    d_x2 = jnp.concatenate(
        our_order(me, [dot(d_gate, wg[k], NT) + dot(d_up, wu[k], NT) for k in range(4)]), axis=1
    )
    d_mid, g_gain_f = norm_back_rows(middle, r2, gain_f, d_x2)
    d_mid_ref[...] = d_mid
    vec_out_ref[1:2, :D] = g_gain_f
    d_attn = (d_branch + d_mid).astype(BF)
    d_attn_ref[...] = d_attn
    d_mix_s[...] = jnp.concatenate(our_order(me, [dot(d_attn, wo[k], NT) for k in range(4)]), axis=1)
    do_s[...] = jnp.zeros_like(do_s)
    for j in range(KV_HEADS):
        for g in range(GROUPS):
            h = GROUPS * j + g
            do_s[j, g * T : (g + 1) * T, HEAD_DIM:] = d_mix_s[:, HEAD_DIM * h : HEAD_DIM * (h + 1)].astype(BF)

    stores = []

    def store(a, b):
        stores.append(pltpu.make_async_copy(a, b, store_sems.at[len(stores)]))
        stores[-1].start()

    together(*shares)
    for k in range(4):
        c = pl.ds(640 * k, 640)
        g_down[:, c] = dot(dffn_all[:, 256 * k : 256 * (k + 1)], inner_all[...], TN).astype(BF)
    wide = wide_steps(me, sends, g_down, low, out_b, full, sums_ref)
    next(wide)
    loaded(4)
    for j in range(KV_HEADS):
        c = pl.ds(j * 128, 128)
        tile = kv_ref[:, :, :, :, c].reshape(KEYS, 128)
        prob, d_out = prob_ref[j], do_s[j]
        d_prob = dot(d_out, tile, NT)
        delta = jnp.sum(d_out.astype(F32) * mix_ref[j], axis=-1, keepdims=True)
        d_score = (prob.astype(F32) * (d_prob - delta)).astype(BF)
        dq_ref[j] = dot(d_score, tile) * SCALE
        grad = dot(d_score, q_ref[j], TN) * SCALE + dot(prob, d_out, TN)
        dkv_ref[:, :, :, :, c] = grad.astype(BF).reshape(2, 4, 4, T, 128)
        store(dkv_ref.at[:, :, :, :, c], dkv_out.at[:, :, :, :, c])
        if j == 3:
            next(wide)
            next(wide)
    together(*late)
    for at in range(0, 2 * FF, 1280):
        c = pl.ds(at, 1280)
        g_ref[:, c] = dot(xs_all[...], dgu_all[:, c], TN).astype(BF)
        store(g_ref.at[:, c], g_out.at[:, c])
    together(wide)
    swap.wait_recv()
    for copy in stores:
        copy.wait()
    sends.finish()


def dense(mix, q, prob, kv, h, up_c, vec, own, rest):
    vmem, hbm = pl.BlockSpec(memory_space=pltpu.VMEM), pl.BlockSpec(memory_space=pl.ANY)
    rows = GROUPS * T
    return pl.pallas_call(
        dense_kernel,
        name="dense",
        out_shape=(
            jax.ShapeDtypeStruct((KV_HEADS, rows, 128), F32),
            jax.ShapeDtypeStruct((2, 4, 4, T, 640), BF),
            jax.ShapeDtypeStruct((ROWS, 2 * FF), BF),
            jax.ShapeDtypeStruct((ROWS, FF // 4), BF),
            jax.ShapeDtypeStruct((T, D), BF),
            jax.ShapeDtypeStruct((T, D), BF),
            jax.ShapeDtypeStruct((T, D), F32),
            jax.ShapeDtypeStruct((PAIR, D), BF),
            jax.ShapeDtypeStruct((T, 128), F32),
            jax.ShapeDtypeStruct((8, 1024), F32),
        ),
        in_specs=[vmem] * 2 + [hbm] * 2 + [vmem] * 3 + [hbm] * 8,
        out_specs=(vmem,) + (hbm,) * 2 + (vmem,) * 7,
        scratch_shapes=[
            pltpu.VMEM((4, 240, D), BF),
            pltpu.VMEM((4, 240, FF), BF),
            pltpu.VMEM((4, 240, FF), BF),
            pltpu.VMEM((4, D, 640), BF),
            pltpu.VMEM((T, D), F32),
            pltpu.VMEM((T, FF), F32),
            pltpu.VMEM((T, FF), F32),
            pltpu.VMEM((T, FF), BF),
            pltpu.VMEM((T, 2 * FF), BF),
            pltpu.VMEM((T, 1024), BF),
            pltpu.VMEM((4, T, 256), BF),
            pltpu.VMEM((KV_HEADS, rows, 128), BF),
            pltpu.VMEM((T, D), F32),
            pltpu.VMEM((4 * T, 2 * FF), BF),
            pltpu.VMEM((4 * T, 1024), BF),
            pltpu.VMEM((4 * T, 256), BF),
            pltpu.VMEM((4 * T, 640), BF),
            pltpu.VMEM((T, 256), BF),
            pltpu.VMEM((T, 640), BF),
            pltpu.VMEM((KV_HEADS, rows, KEYS), BF),
            pltpu.VMEM((2, 4, 4, T, 640), BF),
            pltpu.VMEM((2, 4, 4, T, 640), BF),
            pltpu.VMEM((ROWS, 2 * FF), BF),
            pltpu.VMEM((ROWS, FF), BF),
            *sum_scratch(FF, HALF)[:3],
            pltpu.SemaphoreType.DMA((10,)),
            pltpu.SemaphoreType.DMA((13,)),
        ]
        + sems(57),
        compiler_params=pltpu.CompilerParams(
            collective_id=4, has_side_effects=True, vmem_limit_bytes=VMEM_LIMIT
        ),
        cost_estimate=pl.CostEstimate(
            flops=20_000_000_000, bytes_accessed=40_000_000, transcendentals=0
        ),
    )(mix, q, prob, kv, h, up_c, vec, *own, *rest)


def per_device(hidden, chosen, positions, w_query, w_key, w_value, w_output, w_gate, w_up, w_down, gain_attn, gain_ffn, router, d_out):
    tokens, upstream = hidden[0], d_out[0]
    own_w = (w_output, w_gate, w_up, w_down.T)
    frequency = (THETA ** (-np.arange(0, HEAD_DIM // 2) * 2.0 / HEAD_DIM)).astype(np.float32)
    (
        mix_heads, prob, q_heads, kv_all, h, up_c, x1, cosine, sine, place, vec_in, wq, wk, wv, *rest_w
    ) = front(
        tokens.T, upstream.T, chosen, positions, np.tile(frequency, 4)[None, :], gain_attn, gain_ffn, router,
        w_query, w_key.T, w_value.T, *own_w
    )
    d_q_heads, d_kv, g_one, sums_down, d_attn, mixture, d_mid, out_c, d_logit, vec_out = dense(
        mix_heads, q_heads, prob, kv_all, h, up_c, vec_in, own_w, rest_w
    )
    s_gate, s_up, s_down, s_two, s_three, vector, d_rows = back(
        d_kv, g_one, sums_down, d_q_heads, d_attn, mixture, x1, h, d_mid, d_logit, vec_in, vec_out, cosine, sine, wq, wk, wv
    )
    output, d_tokens, g_query, g_key, g_value, g_output, g_gate, g_up, g_down, *vectors = finish(
        s_gate, s_up, s_down, s_two, s_three, vector, out_c, d_rows, place, tokens.T, upstream.T
    )
    return (
        output.T[None],
        d_tokens.T[None],
        g_query,
        g_key.T,
        g_value.T,
        g_output,
        g_gate,
        g_up,
        g_down.T,
        vectors[0],
        vectors[1],
        vectors[2],
    )


def solution(mesh):
    finer = Mesh(mesh.devices.reshape(DIMS), AX)
    shard, blk = ("ylo", "core"), ("yhi", "z", "x")
    act, row, weight, vec = P(shard, blk, None), P(shard, blk), P(shard, None), P(shard)
    return jax.shard_map(
        per_device,
        mesh=finer,
        in_specs=(act, row, row) + (weight,) * 7 + (vec,) * 3 + (act,),
        out_specs=(act, act) + (weight,) * 7 + (vec,) * 3,
        check_vma=False,
    )
```

```python
import functools

import jax
import jax.numpy as jnp
import numpy as np
from jax import lax
from jax.experimental import pallas as pl
from jax.experimental.pallas import tpu as pltpu
from jax.sharding import Mesh
from jax.sharding import PartitionSpec as P

D = 960
HEADS = 15
KV_HEADS = 5
GROUPS = 3
HEAD_DIM = 64
FF = 2560
EPS = 1e-05
THETA = 10000.0
SCALE = HEAD_DIM ** (-0.5)
T = 64
PAIR = 128
SLOTS = 32
KEYS = SLOTS * T
AX = ("ylo", "core", "yhi", "z", "x")
DIMS = (2, 2, 2, 4, 4)
MESH = pl.DeviceIdType.MESH
BF = jnp.bfloat16
F32 = jnp.float32
VMEM_LIMIT = 56 * 2**20


def dot(a, b, dims=(((1,), (0,)), ((), ()))):
    return lax.dot_general(a, b, dims, preferred_element_type=F32)


NT = (((1,), (1,)), ((), ()))
TN = (((0,), (0,)), ((), ()))


def here():
    return tuple(lax.axis_index(a) for a in AX)


def neighbour(me, axis, step):
    ylo, core, yhi, z, x = me
    if axis == "z":
        z = lax.rem(z + step + 4, 4)
    elif axis == "x":
        x = lax.rem(x + step + 4, 4)
    elif axis == "pair":
        x = x + 1 - 2 * lax.rem(x, 2)
    elif axis == "yhi":
        yhi = 1 - yhi
    elif axis == "ylo":
        ylo = 1 - ylo
    elif axis == "core":
        core = 1 - core
    else:
        y = lax.rem(yhi * 2 + ylo + step + 4, 4)
        ylo, yhi = lax.rem(y, 2), y // 2
    return (ylo, core, yhi, z, x)


NEAR = (("x", 1), ("x", -1), ("z", 1), ("z", -1), ("yhi", 1))
WEIGHT = (("y", 1), ("y", -1), ("core", 1))
FAR = (("x", 2), ("z", 2))


def hail(me, partners):
    barrier = pltpu.get_barrier_semaphore()
    for axis, step in partners:
        pl.semaphore_signal(
            barrier, inc=1, device_id=neighbour(me, axis, step), device_id_type=MESH
        )


def meet(partners):
    pl.semaphore_wait(pltpu.get_barrier_semaphore(), len(partners))


class Sends:
    def __init__(self, me, send_sems, recv_sems):
        self.me, self.send_sems, self.recv_sems, self.all = me, send_sems, recv_sems, []

    def start(self, src, dst, axis, step):
        k = len(self.all)
        copy = pltpu.make_async_remote_copy(
            src_ref=src,
            dst_ref=dst,
            send_sem=self.send_sems.at[k],
            recv_sem=self.recv_sems.at[k],
            device_id=neighbour(self.me, axis, step),
            device_id_type=MESH,
        )
        copy.start()
        self.all.append(copy)
        return copy

    def finish(self):
        for copy in self.all:
            copy.wait_send()


def together(*steps):
    steps = list(steps)
    while steps:
        for step in list(steps):
            try:
                next(step)
            except StopIteration:
                steps.remove(step)


def run_lanes(lanes, order):
    for c in order:
        next(lanes[c], None)
    together(*lanes.values())


def sems(count):
    return [pltpu.SemaphoreType.DMA((count,)), pltpu.SemaphoreType.DMA((count,))]


def plus(*terms):
    total = terms[0].astype(F32)
    for term in terms[1:]:
        total = total + term.astype(F32)
    return total


class Shards:
    def __init__(self, sends):
        self.sends, self.arrived, self.last = sends, [], []
        self.color = lax.rem(sends.me[3] + sends.me[4], 2)

    def near(self, own, out):
        self.last.append(self.sends.start(own, out.at[out.shape[0] - 3], "core", 1))

    def far(self, own, out, cut):
        for step, row, rows in ((1, 0, cut), (-1, cut, own.shape[0] - cut)):
            r = pl.ds(row, rows)
            ref = out.at[out.shape[0] - 2, r]
            self.arrived.append((ref, out.at[out.shape[0] - 1, r], self.sends.start(own.at[r], ref, "y", step)))

    def relay(self):
        for ref, to, copy in self.arrived:
            copy.wait_recv()
            self.last.append(self.sends.start(ref, to, "core", 1))
        self.arrived = []

    def finish(self):
        self.relay()
        for copy in self.last:
            copy.wait_recv()
        self.last = []

    def half(self, own, out, block, cuts):
        rows, slots = own.shape[0], out.shape[0]
        sub = block // 2
        mine = self.color * (rows - block)
        relay = slots > 1
        other = slots - 2 if relay else 0

        def part(slot, start, count):
            return out.at[slot, pl.ds(pl.multiple_of(start, 16), count)]

        copies = []
        for step, off in ((1, 0), (-1, sub)):
            src = own.at[pl.ds(pl.multiple_of(mine + off, 16), sub)]
            copies.append(self.sends.start(src, part(other, mine + off, sub), "y", step))
        if relay:
            self.near(own, out)
        yield
        for copy in copies:
            copy.wait_recv()
        copies, off = [], 0
        for (axis, step), count in zip((("x", 1), ("x", -1), ("z", 1), ("z", -1)), cuts):
            ref = part(other, self.color * block + off, count)
            copies.append(self.sends.start(ref, ref, axis, step))
            off += count
        if relay:
            self.last.append(self.sends.start(part(other, mine, block), part(slots - 1, mine, block), "core", 1))
        yield
        for copy in copies:
            copy.wait_recv()
        rest = (1 - self.color) * block
        if relay:
            self.last.append(
                self.sends.start(part(other, rest, rows - block), part(slots - 1, rest, rows - block), "core", 1)
            )


def gather_steps(me, sends, kv_ref, out_ref):
    _, _, yh, z, x = me
    oy = 1 - yh
    half, quarter = T // 2, T // 4
    streams = (("x", "z", 0), ("z", "x", half))

    def slot(y, axis, step, rows, count):
        zz = lax.rem(z + step + 4, 4) if axis == "z" else z
        xx = lax.rem(x + step + 4, 4) if axis == "x" else x
        return out_ref.at[y, zz, xx, pl.ds(rows, count)]

    def line(y, axis, step, rows, count):
        if axis == "z":
            return out_ref.at[y, lax.rem(z + step + 4, 4), :, pl.ds(rows, count)]
        return out_ref.at[y, :, lax.rem(x + step + 4, 4), pl.ds(rows, count)]

    own = out_ref.at[yh, z, x]
    own[...] = kv_ref[...]
    first = sends.start(kv_ref, own, "yhi", 1)
    got = {}
    for y, tag in ((yh, 0), (oy, 1)):
        if tag:
            yield
            first.wait_recv()
        for axis, _, row in streams:
            src = slot(y, axis, 0, row, half)
            for step in (1, -1):
                got[tag, row, step] = sends.start(src, src, axis, step)
    far = {}
    for y, tag in ((yh, 0), (oy, 1)):
        yield
        for axis, _, row in streams:
            for step, off in ((1, 0), (-1, quarter)):
                got[tag, row, step].wait_recv()
                src = slot(y, axis, -step, row + off, quarter)
                far[tag, row, step] = sends.start(src, src, axis, step)
    wide = {}
    for y, tag in ((yh, 0), (oy, 1)):
        yield
        for _, axis, row in streams:
            for step in (1, -1):
                far[tag, row, step].wait_recv()
            src = line(y, axis, 0, row, half)
            for step in (1, -1):
                wide[tag, row, step] = sends.start(src, src, axis, step)
    last = []
    for y, tag in ((yh, 0), (oy, 1)):
        yield
        for _, axis, row in streams:
            for step, off in ((1, 0), (-1, quarter)):
                wide[tag, row, step].wait_recv()
                src = line(y, axis, -step, row + off, quarter)
                last.append(sends.start(src, src, axis, step))
    yield
    for copy in last:
        copy.wait_recv()


def swapped(x):
    lane = lax.broadcasted_iota(jnp.int32, x.shape, 1)
    return jnp.where(lane < HEAD_DIM // 2, pltpu.roll(x, 96, 1), pltpu.roll(x, 32, 1))


def front_kernel(
    hidden_ref, d_out_ref, chosen_ref, pos_ref, freq_ref, gain_a_ref, gain_f_ref, router_ref, wq_ref, wk_ref, wv_ref,
    wo_ref, wg_ref, wu_ref, wd_ref,
    mix_ref, prob_out, q_ref, kv_out, h_ref, up_ref, x1_ref, cos_ref, sin_ref, place_ref, vec_out_ref,
    wq_out, wk_out, wv_out, wos_ref, wgs_ref, wus_ref, wds_ref,
    compact_h, compact_d, compact_p, got_h, got_d, got_p, vecs, q_pre, kv_own,
    prob_ref, kv_ref, wq, wk, wv,
    load_sems, store_sems, send_sems, recv_sems,
):
    me = here()
    yhi, z, x = me[2:]
    loads = []
    for k, (own, to) in enumerate(((wq_ref, wq), (wk_ref, wk), (wv_ref, wv))):
        loads.append(pltpu.make_async_copy(own, to.at[0], load_sems.at[k]))
        loads[-1].start()
    hail(me, NEAR + WEIGHT)
    sends = Sends(me, send_sems, recv_sems)
    early, query, late = Shards(sends), Shards(sends), Shards(sends)
    odd = lax.rem(x, 2)
    give = pl.ds(pl.multiple_of((1 - odd) * T, T), T)
    keep = pl.ds(pl.multiple_of(odd * T, T), T)
    limit = ((yhi * 16 + z * 4 + x) // 2 + 1) * PAIR
    stores = []

    def store(a, b):
        stores.append(pltpu.make_async_copy(a, b, store_sems.at[len(stores)]))
        stores[-1].start()

    def main():
        flag = jnp.where(chosen_ref[...] > 0, 1.0, 0.0)
        token = lax.broadcasted_iota(jnp.int32, (PAIR, PAIR), 0)
        lane = lax.broadcasted_iota(jnp.int32, (PAIR, PAIR), 1)
        upto = jnp.where(token <= lane, 1.0, 0.0).astype(BF)
        count = dot(jnp.broadcast_to(flag, (16, PAIR)).astype(BF), upto)[0:1]
        total = jnp.sum(flag, axis=1, keepdims=True)
        rank = count - 1.0 + jnp.where(odd == 1, PAIR - total, 0.0)
        place = jnp.where(token.astype(F32) == rank, flag, 0.0)
        place_low = place.astype(BF)
        place_ref[...] = place_low
        compact_p[...] = jnp.broadcast_to(
            jnp.sum(place * pos_ref[...].astype(F32), axis=1, keepdims=True), (PAIR, PAIR)
        )
        compact_h[...] = dot(place_low, hidden_ref[...].astype(BF), NT).astype(BF)
        vecs[0] = jnp.zeros((8, 256), F32)
        for k, ref in enumerate((gain_a_ref, gain_f_ref, router_ref)):
            vecs[0, k : k + 1, :240] = ref[...].astype(F32).reshape(1, 240)
        meet(NEAR + WEIGHT)
        vec_far = sends.start(vecs.at[0], vecs.at[2], "y", 1)
        early.far(wk_ref, wk, 160)
        early.far(wv_ref, wv, 160)
        vec_near = sends.start(vecs.at[0], vecs.at[1], "core", 1)
        early.near(wk_ref, wk)
        early.near(wv_ref, wv)
        query.far(wq_ref, wq, 128)
        query.near(wq_ref, wq)
        swaps = [sends.start(c.at[give], g, "pair", 1) for c, g in ((compact_h, got_h), (compact_p, got_p))]
        yield
        compact_d[...] = dot(place_low, d_out_ref[...].astype(BF), NT).astype(BF)
        vec_far.wait_recv()
        vec_last = sends.start(vecs.at[2], vecs.at[3], "core", 1)
        early.relay()
        yield
        swaps[0].wait_recv()
        h = plus(compact_h[keep], got_h[...])
        h_ref[...] = h
        swaps.append(sends.start(compact_d.at[give], got_d, "pair", 1))
        swaps[1].wait_recv()
        angle = (compact_p[keep] + got_p[...]) * freq_ref[...]
        turn = lax.broadcasted_iota(jnp.int32, (T, PAIR), 1)
        cosine = jnp.where(turn < HEAD_DIM, jnp.cos(angle), 1.0)
        sine = jnp.sin(angle)
        sine = jnp.where(turn < HEAD_DIM // 2, -sine, jnp.where(turn < HEAD_DIM, sine, 0.0))
        cos_ref[...], sin_ref[...] = cosine, sine
        vec_near.wait_recv()
        vec_last.wait_recv()
        vec_out_ref[...] = jnp.zeros_like(vec_out_ref)
        for k, v in enumerate(our_order(me, [vecs[k, :, :240] for k in range(4)])):
            vec_out_ref[:, 240 * k : 240 * (k + 1)] = v
        r1 = lax.rsqrt(jnp.mean(h * h, axis=-1, keepdims=True) + EPS)
        x1_ref[...] = (h * r1 * vec_out_ref[0:1, :D]).astype(BF)
        x1_k = our_order(me, cut_four(x1_ref))
        for copy in loads:
            copy.wait()
        early.finish()
        k_pre = sum(dot(x1_k[k], wk[k], NT) for k in range(4))
        v_pre = sum(dot(x1_k[k], wv[k], NT) for k in range(4))
        for j in range(KV_HEADS):
            run = slice(HEAD_DIM * j, HEAD_DIM * (j + 1))
            tile = jnp.concatenate([k_pre[:, run], v_pre[:, run]], axis=1)
            kv_own[:, 128 * j : 128 * (j + 1)] = (tile * cosine + swapped(tile) * sine).astype(BF)
        gather = gather_steps(me, sends, kv_own, kv_ref)
        next(gather)
        yield
        next(gather)
        yield
        query.relay()
        yield
        query.finish()
        swaps[2].wait_recv()
        up_ref[...] = plus(compact_d[keep], got_d[...])
        q_pre[...] = sum(dot(x1_k[k], wq[k]) for k in range(4))
        zero = jnp.zeros((T, HEAD_DIM), F32)
        for j in range(KV_HEADS):
            for g in range(GROUPS):
                at = HEAD_DIM * (GROUPS * j + g)
                tile = jnp.concatenate([q_pre[:, at : at + HEAD_DIM], zero], axis=1)
                q_ref[j, g * T : (g + 1) * T] = ((tile * cosine + swapped(tile) * sine) * SCALE).astype(BF)
        yield
        yield from gather
        for a, b in ((kv_ref, kv_out), (wq, wq_out), (wk, wk_out), (wv, wv_out)):
            store(a, b)
        for j in range(KV_HEADS):
            tile = kv_ref[:, :, :, :, 128 * j : 128 * (j + 1)].reshape(KEYS, 128)
            scores = dot(q_ref[j], tile, NT)
            column = lax.broadcasted_iota(jnp.int32, scores.shape, 1)
            scores = jnp.where(column < limit, scores, -1e30)
            exponent = jnp.exp(scores - jnp.max(scores, axis=-1, keepdims=True))
            prob = (exponent * (1.0 / jnp.sum(exponent, axis=-1, keepdims=True))).astype(BF)
            prob_ref[j] = prob
            store(prob_ref.at[j], prob_out.at[j])
            mix_ref[j] = dot(prob, tile)
            yield

    small, large = (128, (32, 32, 32, 16)), (480, (128, 128, 112, 112))
    lanes = {
        "m": main(),
        "o": late.half(wo_ref, wos_ref, *small),
        "t": late.half(wg_ref, wgs_ref, *small),
        "u": late.half(wu_ref, wus_ref, *small),
        "d": late.half(wd_ref, wds_ref, *large),
    }
    run_lanes(lanes, "".join(FRONT_ORDER))
    late.finish()
    for copy in stores:
        copy.wait()
    sends.finish()


FRONT_ORDER = (
    "mmmotmmmmmomummdmotummtdmmumdm",
)


def front(hidden, d_out, chosen, pos, freq, gain_a, gain_f, router, w_query, w_key, w_value, *later):
    vmem, hbm = pl.BlockSpec(memory_space=pltpu.VMEM), pl.BlockSpec(memory_space=pl.ANY)
    rows = GROUPS * T
    return pl.pallas_call(
        front_kernel,
        name="front",
        out_shape=(
            jax.ShapeDtypeStruct((KV_HEADS, rows, 128), F32),
            jax.ShapeDtypeStruct((KV_HEADS, rows, KEYS), BF),
            jax.ShapeDtypeStruct((KV_HEADS, rows, 128), BF),
            jax.ShapeDtypeStruct((2, 4, 4, T, 640), BF),
            jax.ShapeDtypeStruct((T, D), F32),
            jax.ShapeDtypeStruct((T, D), F32),
            jax.ShapeDtypeStruct((T, D), BF),
            jax.ShapeDtypeStruct((T, 128), F32),
            jax.ShapeDtypeStruct((T, 128), F32),
            jax.ShapeDtypeStruct((PAIR, PAIR), BF),
            jax.ShapeDtypeStruct((8, 1024), F32),
            jax.ShapeDtypeStruct((4, 240, 960), BF),
            jax.ShapeDtypeStruct((4, 320, 240), BF),
            jax.ShapeDtypeStruct((4, 320, 240), BF),
        )
        + tuple(jax.ShapeDtypeStruct((3,) + w.shape, BF) for w in later[:3])
        + (jax.ShapeDtypeStruct((1,) + later[3].shape, BF),),
        in_specs=[vmem] * 8 + [hbm] * 7,
        out_specs=(vmem, hbm, vmem, hbm) + (vmem,) * 7 + (hbm,) * 7,
        scratch_shapes=[
            pltpu.VMEM((PAIR, D), BF),
            pltpu.VMEM((PAIR, D), BF),
            pltpu.VMEM((PAIR, PAIR), F32),
            pltpu.VMEM((T, D), BF),
            pltpu.VMEM((T, D), BF),
            pltpu.VMEM((T, PAIR), F32),
            pltpu.VMEM((4, 8, 256), F32),
            pltpu.VMEM((T, D), F32),
            pltpu.VMEM((T, 640), BF),
            pltpu.VMEM((KV_HEADS, rows, KEYS), BF),
            pltpu.VMEM((2, 4, 4, T, 640), BF),
            pltpu.VMEM((4, 240, 960), BF),
            pltpu.VMEM((4, 320, 240), BF),
            pltpu.VMEM((4, 320, 240), BF),
            pltpu.SemaphoreType.DMA((3,)),
            pltpu.SemaphoreType.DMA((9,)),
        ]
        + sems(90),
        compiler_params=pltpu.CompilerParams(
            collective_id=1, has_side_effects=True, vmem_limit_bytes=VMEM_LIMIT
        ),
        cost_estimate=pl.CostEstimate(flops=5_000_000_000, bytes_accessed=90_000_000, transcendentals=0),
    )(hidden, d_out, chosen, pos, freq, gain_a, gain_f, router, w_query, w_key, w_value, *later)


def key_steps(me, sends, part_ref, out_ref, low, out_b, full, sums, nlow, nout, nfull, mine, y_in):
    _, _, yh, z, x = me
    half, quarter = T // 2, T // 4
    streams = (("x", "z", 0), ("z", "x", half))

    def line(axis, step, row, count):
        if axis == "z":
            return part_ref.at[:, lax.rem(z + step + 4, 4), :, pl.ds(row, count)]
        return part_ref.at[:, :, lax.rem(x + step + 4, 4), pl.ds(row, count)]

    near = {}
    for s, (axis, _, row) in enumerate(streams):
        near[s, 1] = sends.start(line(axis, 2, row, quarter), low.at[s, 0], axis, 1)
        near[s, -1] = sends.start(line(axis, 2, row + quarter, quarter), low.at[s, 1], axis, -1)
    whole = {}
    for s, (axis, _, row) in enumerate(streams):
        yield
        for d, step in enumerate((1, -1)):
            near[s, step].wait_recv()
            lo, hi = (0, quarter) if step == 1 else (quarter, 0)
            out_b[s, d, :, :, pl.ds(lo, quarter)] = plus(
                line(axis, step, row + lo, quarter)[...], low[s, d]
            ).astype(BF)
            out_b[s, d, :, :, pl.ds(hi, quarter)] = line(axis, step, row + hi, quarter)[...]
            whole[s, step] = sends.start(out_b.at[s, d], full.at[s, d], axis, step)
    near = {}
    for s, (axis, other, row) in enumerate(streams):
        yield
        for step in (1, -1):
            whole[s, step].wait_recv()
        sums[s] = plus(line(axis, 0, row, half)[...], full[s, 0], full[s, 1]).astype(BF)
        far = lax.rem((z if other == "z" else x) + 2, 4)
        near[s, 1] = sends.start(sums.at[s, :, far, pl.ds(0, quarter)], nlow.at[s, 0], other, 1)
        near[s, -1] = sends.start(
            sums.at[s, :, far, pl.ds(quarter, quarter)], nlow.at[s, 1], other, -1
        )
    for s, (axis, other, row) in enumerate(streams):
        yield
        at = z if other == "z" else x
        for d, step in enumerate((1, -1)):
            near[s, step].wait_recv()
            to = lax.rem(at + step + 4, 4)
            lo, hi = (0, quarter) if step == 1 else (quarter, 0)
            nout[s, d, :, pl.ds(lo, quarter)] = plus(
                sums[s, :, to, pl.ds(lo, quarter)], nlow[s, d]
            ).astype(BF)
            nout[s, d, :, pl.ds(hi, quarter)] = sums[s, :, to, pl.ds(hi, quarter)]
            whole[s, step] = sends.start(nout.at[s, d], nfull.at[s, d], other, step)
    swap = {}
    for s, (axis, other, row) in enumerate(streams):
        yield
        at = z if other == "z" else x
        for step in (1, -1):
            whole[s, step].wait_recv()
        mine[s] = plus(sums[s, :, at], nfull[s, 0], nfull[s, 1]).astype(BF)
        swap[s] = sends.start(mine.at[s, 1 - yh], y_in.at[s], "yhi", 1)
    yield
    for s, (axis, other, row) in enumerate(streams):
        swap[s].wait_recv()
        out_ref[pl.ds(row, half)] = plus(mine[s, yh], y_in[s])


def key_scratch():
    half, quarter, w = T // 2, T // 4, 640
    return [
        pltpu.VMEM((2, 2, 2, 4, quarter, w), BF),
        pltpu.VMEM((2, 2, 2, 4, half, w), BF),
        pltpu.VMEM((2, 2, 2, 4, half, w), BF),
        pltpu.VMEM((2, 2, 4, half, w), BF),
        pltpu.VMEM((2, 2, 2, quarter, w), BF),
        pltpu.VMEM((2, 2, 2, half, w), BF),
        pltpu.VMEM((2, 2, 2, half, w), BF),
        pltpu.VMEM((2, 2, half, w), BF),
        pltpu.VMEM((2, half, w), BF),
    ]


ROWS = 256
HALF = ROWS // 2
STREAMS = (("x", "z"), ("z", "x"))


def spots(me):
    return {"z": me[3], "x": me[4]}


def around(me, axis, step):
    return lax.rem(spots(me)[axis] + step + 4, 4)


def columns(me, axis, step, big):
    return pl.ds(pl.multiple_of(around(me, axis, step) * big, 128), big)


def halves(big):
    cut = (big // 2 + 127) // 128 * 128
    return (0, cut), (cut, big - cut)


def wide_steps(me, sends, g_ref, low, out_b, full, sums):
    h, big = sums.shape[0] // 2, sums.shape[1]
    cut = h // 2
    near, whole = {}, {}

    def parts(step):
        return (0, cut) if step == 1 else (cut, 0)

    for s, (axis, _) in enumerate(STREAMS):
        c = columns(me, axis, 2, big)
        for step in (1, -1):
            r = pl.ds(s * h + parts(step)[0], cut)
            near[s, step] = sends.start(g_ref.at[r, c], low.at[r], axis, step)
    for s, (axis, _) in enumerate(STREAMS):
        yield
        for d, step in enumerate((1, -1)):
            near[s, step].wait_recv()
            add, keep = (pl.ds(s * h + p, cut) for p in parts(step))
            c = columns(me, axis, step, big)
            out_b[d, add] = plus(g_ref[add, c], low[add]).astype(BF)
            out_b[d, keep] = g_ref[keep, c]
            r = pl.ds(s * h, h)
            whole[s, step] = sends.start(out_b.at[d, r], full.at[d, r], axis, step)

    for s, (axis, _) in enumerate(STREAMS):
        yield
        for step in (1, -1):
            whole[s, step].wait_recv()
        r = pl.ds(s * h, h)
        sums[r] = plus(g_ref[r, columns(me, axis, 0, big)], full[0, r], full[1, r]).astype(BF)


def narrow_steps(me, sends, sums, mine, swap_y, nlow, nout, nfull, y_in):
    run, big = mine.shape[-2:]
    h = 4 * run
    near, whole = {}, {}

    def rows(s, other, step):
        return pl.ds(pl.multiple_of(s * h + around(me, other, step) * run, 16), run)

    for s, (axis, other) in enumerate(STREAMS):
        for d, step in enumerate((1, -1)):
            c = pl.ds(*halves(big)[d])
            near[s, step] = sends.start(sums.at[rows(s, other, 2), c], nlow.at[s, :, c], other, step)
    for s, (axis, other) in enumerate(STREAMS):
        yield
        for d, step in enumerate((1, -1)):
            near[s, step].wait_recv()
            add, keep = pl.ds(*halves(big)[d]), pl.ds(*halves(big)[1 - d])
            r = rows(s, other, step)
            nout[s, d, :, add] = plus(sums[r, add], nlow[s, :, add]).astype(BF)
            nout[s, d, :, keep] = sums[r, keep]
            whole[s, step] = sends.start(nout.at[s, d], nfull.at[s, d], other, step)
    swap = {}
    for s, (axis, other) in enumerate(STREAMS):
        yield
        for step in (1, -1):
            whole[s, step].wait_recv()
        total = plus(sums[rows(s, other, 0)], nfull[s, 0], nfull[s, 1]).astype(BF)
        if swap_y:
            y_in[0, s] = total
            swap[s] = sends.start(y_in.at[0, s], y_in.at[1, s], "yhi", 1)
        else:
            mine[s] = total
    if swap_y:
        for s in range(2):
            yield
            swap[s].wait_recv()
            mine[s] = plus(y_in[0, s], y_in[1, s]).astype(BF)


def sum_steps(me, sends, g_ref, mine, swap_y, low, out_b, full, sums, *narrow):
    yield from wide_steps(me, sends, g_ref, low, out_b, full, sums)
    yield from narrow_steps(me, sends, sums, mine, swap_y, *narrow)


def sum_scratch(width, h):
    big, run = width // 4, h // 4
    return [
        pltpu.VMEM((2 * h, big), BF),
        pltpu.VMEM((2, 2 * h, big), BF),
        pltpu.VMEM((2, 2 * h, big), BF),
        pltpu.VMEM((2 * h, big), BF),
        pltpu.VMEM((2, run, big), BF),
        pltpu.VMEM((2, 2, run, big), BF),
        pltpu.VMEM((2, 2, run, big), BF),
        pltpu.VMEM((2, 2, run, big), BF),
    ]


def spread_steps(me, sends, mine, out_ref, store_sems, to_y):
    run, big = mine.shape[-2:]
    h = 4 * run
    cut = h // 2
    near, whole, stored, last, over = {}, {}, [], {}, []

    def base(s):
        return s * HALF + (me[2] * h if to_y else 0)

    def rows(s, off, count):
        return pl.ds(pl.multiple_of(base(s) + off, 16), count)

    def block(s, axis, step, off, count):
        return out_ref.at[rows(s, off, count), columns(me, axis, step, big)]

    def on(ref):
        if to_y:
            over.append(sends.start(ref, ref, "yhi", 1))

    for s, (axis, other) in enumerate(STREAMS):
        ref = block(s, axis, 0, around(me, other, 0) * run, run)
        for step in (1, -1):
            near[s, step] = sends.start(mine.at[s], ref, other, step)
        stored.append(pltpu.make_async_copy(mine.at[s], ref, store_sems.at[s]))
        stored[-1].start()

    def narrow(s, axis, other, step, d):
        c0, n = halves(big)[d]
        c = pl.ds(pl.multiple_of(around(me, axis, 0) * big + c0, 128), n)
        return out_ref.at[rows(s, around(me, other, step) * run, run), c]

    for s, (axis, other) in enumerate(STREAMS):
        yield
        for d, step in enumerate((1, -1)):
            near[s, step].wait_recv()
            ref = narrow(s, axis, other, -step, d)
            whole[s, step] = sends.start(ref, ref, other, step)
    for s, (axis, other) in enumerate(STREAMS):
        yield
        for step in (1, -1):
            whole[s, step].wait_recv()
        stored[s].wait()
        ref = block(s, axis, 0, 0, h)
        for step in (1, -1):
            near[s, step] = sends.start(ref, ref, axis, step)
        on(ref)
    for s, (axis, other) in enumerate(STREAMS):
        yield
        for d, step in enumerate((1, -1)):
            near[s, step].wait_recv()
            ref = block(s, axis, -step, d * cut, cut)
            last[s, step] = sends.start(ref, ref, axis, step)
            on(block(s, axis, -step, 0, h))
    for s, (axis, other) in enumerate(STREAMS):
        yield
        for step in (1, -1):
            last[s, step].wait_recv()
        on(block(s, axis, 2, 0, h))
    if to_y:
        yield
        for copy in over:
            copy.wait_recv()


def halved_steps(me, sends, g_ref, mine, kept, got, out_ref, store_sems, *scratch):
    h = HALF // 2
    yh = me[2]
    copies = []
    for s in range(2):
        give = pl.ds(pl.multiple_of(s * HALF + (1 - yh) * h, 16), h)
        copies.append(sends.start(g_ref.at[give], got.at[pl.ds(s * h, h)], "yhi", 1))
    for s in range(2):
        yield
        copies[s].wait_recv()
        r = pl.ds(s * h, h)
        kept[r] = plus(g_ref[pl.ds(pl.multiple_of(s * HALF + yh * h, 16), h)], got[r]).astype(BF)
    yield
    yield from sum_steps(me, sends, kept, mine, False, *scratch)
    yield from spread_steps(me, sends, mine, out_ref, store_sems, True)


def vector_steps(sends, vec_ref, out_ref, keep, got):
    rounds = ((("core", 1),), (("ylo", 1),), (("x", 1), ("x", -1), ("x", 2)), (("z", 1), ("z", -1), ("z", 2)), (("yhi", 1),))
    keep[0] = vec_ref[...]
    k = 0
    for at, partners in enumerate(rounds):
        copies = []
        for axis, step in partners:
            copies.append((k, sends.start(keep.at[at], got.at[k], axis, step)))
            k += 1
        yield
        total = keep[at]
        for slot, copy in copies:
            copy.wait_recv()
            total = total + got[slot]
        keep[at + 1] = total
    out_ref[...] = keep[len(rounds)]


def small_steps(me, sends, g_ref, out_ref, got_x, got_z, got_y, sum_z, sum_y):
    x, z = me[3], me[4]
    steps = (1, -1, 2)

    def rows(at, step, count, base=0):
        return pl.ds(pl.multiple_of(base + lax.rem(at + step + 4, 4) * count, 16), count)

    copies = [
        sends.start(g_ref.at[rows(x, step, 64)], got_x.at[k], "z", step) for k, step in enumerate(steps)
    ]
    yield
    for copy in copies:
        copy.wait_recv()
    sum_z[...] = plus(g_ref[rows(x, 0, 64)], got_x[0], got_x[1], got_x[2]).astype(BF)
    copies = [
        sends.start(sum_z.at[rows(z, step, 16)], got_z.at[k], "x", step) for k, step in enumerate(steps)
    ]
    yield
    for copy in copies:
        copy.wait_recv()
    sum_y[...] = plus(sum_z[rows(z, 0, 16)], got_z[0], got_z[1], got_z[2]).astype(BF)
    copy = sends.start(sum_y, got_y, "yhi", 1)
    yield
    copy.wait_recv()
    ref = out_ref.at[rows(z, 0, 16, x * 64)]
    ref[...] = plus(sum_y[...], got_y[...]).astype(BF)
    copies = [sends.start(ref, ref, "x", step) for step in steps]
    yield
    for copy in copies:
        copy.wait_recv()
    ref = out_ref.at[rows(x, 0, 64)]
    copies = [sends.start(ref, ref, "z", step) for step in steps]
    yield
    for copy in copies:
        copy.wait_recv()


KEY_N, SUM_N = 9, 8
WIDE, REST = FF, 2048


def back_kernel(
    part_ref, g_in, sums_ref, dq_ref, d_attn_ref, mixture_ref, x1_ref, h_ref, d_mid_ref, logit_ref, vec_ref, vec_part_ref,
    cos_ref, sin_ref, wq_in, wk_in, wv_in,
    gate_ref, up_ref, down_ref, two_ref, three_ref, vec_out_ref, both_ref,
    own, ra, rb, xs, ra_all, rb_all, xs_all, xs_relay, g_two, g_three, d_x1_s, vec_all, keep_v, got_v,
    mine_gate, mine_up, mine_down, mine_two, got_x, got_z, got_y, sum_z, sum_y,
    g_gate, g_up, kept, got_gate, wq, wk, wv, load_sems, store_sems,
    *scratch,
):
    me = here()
    key_scr, rest = scratch[:KEY_N], scratch[KEY_N:-2]
    gate_scr, up_scr, two_scr, down_scr = (rest[SUM_N * k : SUM_N * (k + 1)] for k in range(4))
    loads = [
        pltpu.make_async_copy(a, b, load_sems.at[k])
        for k, (a, b) in enumerate(
            (
                (g_in.at[:, pl.ds(0, WIDE)], g_gate),
                (g_in.at[:, pl.ds(WIDE, WIDE)], g_up),
                (wq_in, wq),
                (wk_in, wk),
                (wv_in, wv),
            )
        )
    ]
    for copy in loads:
        copy.start()
    hail(me, NEAR + WEIGHT + FAR)
    sends = Sends(me, *scratch[-2:])
    odd = lax.rem(me[4], 2)
    keep = pl.ds(pl.multiple_of(odd * T, T), T)
    cosine, sine = cos_ref[...], sin_ref[...]
    mine = pl.ds(0, T)

    def turned_back(tile):
        return tile * cosine - swapped(tile) * sine

    for j in range(KV_HEADS):
        for g in range(GROUPS):
            at = HEAD_DIM * (GROUPS * j + g)
            ra[:, at : at + HEAD_DIM] = turned_back(dq_ref[j, g * T : (g + 1) * T]).astype(BF)[:, :HEAD_DIM]
    ra[:, D:] = d_attn_ref[...]
    xs[...] = jnp.zeros_like(xs)
    for k, (a, b) in enumerate(zip(our_order(me, cut_four(x1_ref)), our_order(me, cut_four(mixture_ref)))):
        xs[k, :, :240] = a
        xs[k, :, 256:496] = b
    meet(NEAR + WEIGHT + FAR)

    def keys():
        yield from key_steps(me, sends, part_ref, own, *key_scr)
        for j in range(KV_HEADS):
            tile = turned_back(own[:, 128 * j : 128 * (j + 1)]).astype(BF)
            rb[:, HEAD_DIM * j : HEAD_DIM * (j + 1)] = tile[:, :HEAD_DIM]
            rb[:, 320 + HEAD_DIM * j : 320 + HEAD_DIM * (j + 1)] = tile[:, HEAD_DIM:]
        share = everyone_steps(sends, (("all", rb, rb_all, None),))
        next(share)
        rb_all[mine] = rb[...]
        d_k, d_v = rb[:, :320], rb[:, 320:]
        d_x1 = d_x1_s[...] + jnp.concatenate(
            our_order(me, [dot(d_k, wk[k]) + dot(d_v, wv[k]) for k in range(4)]), axis=1
        )
        h = h_ref[...]
        r1 = lax.rsqrt(jnp.mean(h * h, axis=-1, keepdims=True) + EPS)
        d_first, g_gain_a = norm_back_rows(h, r1, vec_ref[0:1, :D], d_x1)
        d_h = d_mid_ref[...] + d_first + logit_ref[:, 0:1] * vec_ref[2:3, :D]
        both_ref[keep] = d_h.astype(BF)
        swap = sends.start(both_ref.at[keep], both_ref.at[keep], "pair", 1)
        vec_all[...] = vec_part_ref[...]
        vec_all[0:1, :D] = g_gain_a
        vectors = vector_steps(sends, vec_all, vec_out_ref, keep_v, got_v)
        next(vectors)
        yield
        next(share)
        yield
        together(share)
        g_three[...] = dot(xs_all[:, :256], rb_all[...], TN).astype(BF)
        small = small_steps(me, sends, g_three, three_ref, got_x, got_z, got_y, sum_z, sum_y)
        while True:
            for step in (small, vectors):
                next(step, None)
            if small.gi_frame is None and vectors.gi_frame is None:
                break
            yield
        swap.wait_recv()

    def queries():
        share = everyone_steps(
            sends, (("all", ra, ra_all, None), ("one", [xs.at[k] for k in range(4)], xs_all, xs_relay))
        )
        next(share)
        ra_all[mine] = ra[...]
        xs_all[mine] = xs[0]
        d_q = ra[:, :D]
        for copy in loads[2:]:
            copy.wait()
        d_x1_s[...] = jnp.concatenate(our_order(me, [dot(d_q, wq[k], NT) for k in range(4)]), axis=1)
        g_two[:, 2 * D :] = jnp.zeros((ROWS, 128), BF)
        yield
        next(share)
        yield
        together(share)
        g_two[:, :D] = dot(xs_all[:, :256], ra_all[:, :D], TN).astype(BF)
        g_two[:, D : 2 * D] = dot(xs_all[:, 256:], ra_all[:, D:], TN).astype(BF)
        yield from sum_steps(me, sends, g_two, mine_two, True, *two_scr)
        yield from spread_steps(me, sends, mine_two, two_ref, store_sems.at[pl.ds(6, 2)], False)

    def gate():
        loads[0].wait()
        yield from halved_steps(
            me, sends, g_gate, mine_gate, kept, got_gate, gate_ref, store_sems.at[pl.ds(0, 2)], *gate_scr
        )

    def up():
        loads[1].wait()
        yield from sum_steps(me, sends, g_up, mine_up, True, *up_scr)
        yield from spread_steps(me, sends, mine_up, up_ref, store_sems.at[pl.ds(2, 2)], False)

    def down():
        yield from narrow_steps(me, sends, sums_ref, mine_down, True, *down_scr)
        yield from spread_steps(me, sends, mine_down, down_ref, store_sems.at[pl.ds(4, 2)], False)

    run_lanes({"k": keys(), "g": gate(), "u": up(), "d": down(), "q": queries()}, "".join(ORDER))
    sends.finish()


ORDER = (
    "kgdukkquugkkgddguukkqdqgdukgkdqudqggkqdk",
    "qgkguqgdqugddqqgukguqqgugdudqqkuguqqdkuu",
    "gdgkuuqgqgqqk",
)


def back(*args):
    vmem, hbm = pl.BlockSpec(memory_space=pltpu.VMEM), pl.BlockSpec(memory_space=pl.ANY)
    return pl.pallas_call(
        back_kernel,
        name="back",
        out_shape=(
            jax.ShapeDtypeStruct((ROWS, WIDE), BF),
            jax.ShapeDtypeStruct((ROWS, WIDE), BF),
            jax.ShapeDtypeStruct((ROWS, WIDE), BF),
            jax.ShapeDtypeStruct((ROWS, REST), BF),
            jax.ShapeDtypeStruct((ROWS, 640), BF),
            jax.ShapeDtypeStruct((8, 1024), F32),
            jax.ShapeDtypeStruct((PAIR, D), BF),
        ),
        in_specs=[vmem, hbm] + [vmem] * (len(args) - 5) + [hbm] * 3,
        out_specs=(hbm,) * 4 + (vmem,) * 3,
        scratch_shapes=[
            pltpu.VMEM((T, 640), F32),
            pltpu.VMEM((T, 2 * D), BF),
            pltpu.VMEM((T, 640), BF),
            pltpu.VMEM((4, T, 512), BF),
            pltpu.VMEM((4 * T, 2 * D), BF),
            pltpu.VMEM((4 * T, 640), BF),
            pltpu.VMEM((4 * T, 512), BF),
            pltpu.VMEM((T, 512), BF),
            pltpu.VMEM((ROWS, REST), BF),
            pltpu.VMEM((ROWS, 640), BF),
            pltpu.VMEM((T, D), F32),
            pltpu.VMEM((8, 1024), F32),
            pltpu.VMEM((6, 8, 1024), F32),
            pltpu.VMEM((9, 8, 1024), F32),
            pltpu.VMEM((2, HALF // 8, WIDE // 4), BF),
            pltpu.VMEM((2, HALF // 4, WIDE // 4), BF),
            pltpu.VMEM((2, HALF // 4, WIDE // 4), BF),
            pltpu.VMEM((2, HALF // 4, REST // 4), BF),
            pltpu.VMEM((3, 64, 640), BF),
            pltpu.VMEM((3, 16, 640), BF),
            pltpu.VMEM((16, 640), BF),
            pltpu.VMEM((64, 640), BF),
            pltpu.VMEM((16, 640), BF),
            pltpu.VMEM((ROWS, WIDE), BF),
            pltpu.VMEM((ROWS, WIDE), BF),
            pltpu.VMEM((HALF, WIDE), BF),
            pltpu.VMEM((HALF, WIDE), BF),
            pltpu.VMEM((4, 240, 960), BF),
            pltpu.VMEM((4, 320, 240), BF),
            pltpu.VMEM((4, 320, 240), BF),
            pltpu.SemaphoreType.DMA((6,)),
            pltpu.SemaphoreType.DMA((8,)),
        ]
        + key_scratch()
        + sum_scratch(WIDE, HALF // 2)
        + sum_scratch(WIDE, HALF)
        + sum_scratch(REST, HALF)
        + sum_scratch(WIDE, HALF)[4:]
        + sems(230),
        compiler_params=pltpu.CompilerParams(
            collective_id=2, has_side_effects=True, vmem_limit_bytes=VMEM_LIMIT
        ),
        cost_estimate=pl.CostEstimate(flops=2_000_000_000, bytes_accessed=200_000_000, transcendentals=0),
    )(*args)


def finish_kernel(
    g_gate_ref, g_up_ref, g_down_ref, two_ref, three_ref, vec_ref, out_rows_ref, d_rows_ref, place_ref, hidden_ref, d_out_ref,
    out_ref, d_hidden_ref, query_ref, key_ref, value_ref, output_ref, gate_ref, up_ref, down_ref, vec_a_ref, vec_f_ref, vec_r_ref,
    low_one, low_down, low_two, low_three, wide_one, wide_two, wide_down, wide_kv, rows, ranked, load_sems, store_sems,
):
    keep = pl.ds(0, 240)
    runs_one = [pl.ds(1280 * k, 1280) for k in range(2)]
    runs_down = [pl.ds(640 * k, 640) for k in range(4)]
    loads = []
    for src, dst, runs in (
        (g_gate_ref, low_one.at[0], runs_one),
        (g_up_ref, low_one.at[1], runs_one),
        (g_down_ref, low_down, runs_down),
        (two_ref, low_two, [pl.ds(0, 2 * D)]),
        (three_ref, low_three, [pl.ds(0, 640)]),
    ):
        for c in runs:
            loads.append(pltpu.make_async_copy(src.at[keep, c], dst.at[:, c], load_sems.at[len(loads)]))
            loads[-1].start()
    for k, (base, at_rank) in enumerate(((hidden_ref, out_rows_ref), (d_out_ref, d_rows_ref))):
        for src, dst in ((base, rows.at[k]), (at_rank, ranked.at[k])):
            loads.append(pltpu.make_async_copy(src, dst, load_sems.at[len(loads)]))
            loads[-1].start()
    stores = []

    def store(a, b):
        stores.append(pltpu.make_async_copy(a, b, store_sems.at[len(stores)]))
        stores[-1].start()

    for k in range(4):
        loads[k].wait()
        c = runs_one[k % 2]
        wide_one[k // 2, :, c] = low_one[k // 2, :, c].astype(F32)
        store(wide_one.at[k // 2, :, c], (gate_ref, up_ref)[k // 2].at[:, c])
    for k in range(4):
        loads[4 + k].wait()
        r = pl.ds(240 * k, 240)
        wide_down[r] = low_down[:, runs_down[k]].astype(F32)
        store(wide_down.at[r], down_ref.at[r])
    loads[8].wait()
    for k, to in enumerate((query_ref, output_ref)):
        wide_two[k] = low_two[:, D * k : D * (k + 1)].astype(F32)
        store(wide_two.at[k], to)
    loads[9].wait()
    for k, to in enumerate((key_ref, value_ref)):
        wide_kv[k] = low_three[:, 320 * k : 320 * (k + 1)].astype(F32).T
        store(wide_kv.at[k], to)
    for k, to in enumerate((out_ref, d_hidden_ref)):
        loads[10 + 2 * k].wait()
        loads[11 + 2 * k].wait()
        rows[k] = rows[k] + dot(ranked[k], place_ref[...], TN)
        store(rows.at[k], to)
    core, ylo = lax.axis_index("core") == 1, lax.axis_index("ylo") == 1
    p = [vec_ref[:, 240 * k : 240 * (k + 1)] for k in range(4)]
    p = jnp.where(ylo, jnp.where(core, p[3], p[2]), jnp.where(core, p[1], p[0]))
    for k, ref in enumerate((vec_a_ref, vec_f_ref, vec_r_ref)):
        ref[...] = p[k : k + 1].reshape(240)
    for copy in stores:
        copy.wait()


def finish(*args):
    vmem, hbm = pl.BlockSpec(memory_space=pltpu.VMEM), pl.BlockSpec(memory_space=pl.ANY)
    shapes = [(D, PAIR), (D, PAIR), (240, D), (320, 240), (320, 240), (240, D), (240, FF), (240, FF), (D, 640), (240,), (240,), (240,)]
    return pl.pallas_call(
        finish_kernel,
        name="finish",
        out_shape=tuple(jax.ShapeDtypeStruct(shape, F32) for shape in shapes),
        in_specs=[hbm] * 5 + [vmem] + [hbm] * 2 + [vmem] + [hbm] * 2,
        out_specs=(hbm,) * 9 + (vmem,) * 3,
        scratch_shapes=[
            pltpu.VMEM((2, 240, WIDE), BF),
            pltpu.VMEM((240, WIDE), BF),
            pltpu.VMEM((240, REST), BF),
            pltpu.VMEM((240, 640), BF),
            pltpu.VMEM((2, 240, WIDE), F32),
            pltpu.VMEM((2, 240, D), F32),
            pltpu.VMEM((D, 640), F32),
            pltpu.VMEM((2, 320, 240), F32),
            pltpu.VMEM((2, D, PAIR), F32),
            pltpu.VMEM((2, PAIR, D), BF),
            pltpu.SemaphoreType.DMA((14,)),
            pltpu.SemaphoreType.DMA((14,)),
        ],
        compiler_params=pltpu.CompilerParams(vmem_limit_bytes=VMEM_LIMIT),
        cost_estimate=pl.CostEstimate(flops=0, bytes_accessed=16_000_000, transcendentals=0),
    )(*args)


def shard_of(me, k):
    ylo, core = me[0], me[1]
    return (ylo if k < 2 else 1 - ylo) * 2 + (core if k % 2 == 0 else 1 - core)


def our_order(me, p):
    core, ylo = me[1] == 1, me[0] == 1
    p = [jnp.where(core, p[k ^ 1], p[k]) for k in range(4)]
    return [jnp.where(ylo, p[k ^ 2], p[k]) for k in range(4)]


def cut_four(ref):
    return [ref[:, 240 * k : 240 * (k + 1)] for k in range(4)]


def norm_back_rows(z, r, gain, dy):
    dz = r * (gain * dy) - z * (r * r * r) * jnp.mean(gain * dy * z, axis=-1, keepdims=True)
    return dz, jnp.sum(dy * z * r, axis=0, keepdims=True)


def everyone_steps(sends, pieces):
    half = T // 2
    arrived, last = [], []
    for kind, source, whole, relay in pieces:
        near = source if kind == "all" else source[1]
        last.append(sends.start(near, whole.at[pl.ds(T, T)], "core", 1))
    for step, at in ((1, 0), (-1, half)):
        r = pl.ds(at, half)
        for kind, source, whole, relay in pieces:
            far = source if kind == "all" else source[2]
            arrived.append((sends.start(far.at[r], whole.at[pl.ds(2 * T + at, half)], "y", step), None))
            if kind == "all":
                arrived[-1] = (arrived[-1][0], (whole.at[pl.ds(2 * T + at, half)], whole.at[pl.ds(3 * T + at, half)]))
            else:
                copy = sends.start(source[3].at[r], relay.at[r], "y", step)
                arrived.append((copy, (relay.at[r], whole.at[pl.ds(3 * T + at, half)])))
    yield
    for copy, onward in arrived:
        copy.wait_recv()
        if onward is not None:
            last.append(sends.start(onward[0], onward[1], "core", 1))
    yield
    for copy in last:
        copy.wait_recv()


def dense_kernel(
    mix_ref, q_ref, prob_in, kv_in, h_ref, up_ref, vec_ref,
    wo_ref, wg_ref, wu_ref, wd_ref, wos_ref, wgs_ref, wus_ref, wds_ref,
    dq_ref, dkv_out, g_out, sums_ref, d_attn_ref, mixture_ref, d_mid_ref, out_ref, logit_ref, vec_out_ref,
    wo, wg, wu, wd, mixf, gate_s, up_s, inner, dgu, dffn, xs, do_s, d_mix_s,
    dgu_all, dffn_all, xs_all, inner_all, xs_relay, inner_relay,
    prob_ref, kv_ref, dkv_ref, g_ref, g_down, low, out_b, full,
    load_sems, store_sems, send_sems, recv_sems,
):
    me = here()
    loads = []
    for k, (own, rest, to) in enumerate(
        ((wo_ref, wos_ref, wo), (wg_ref, wgs_ref, wg), (wu_ref, wus_ref, wu), (wd_ref, wds_ref, wd))
    ):
        there = to.at[pl.ds(1, 3)] if k < 3 else to.at[pl.ds(2, 1)]
        pair = (
            pltpu.make_async_copy(own, to.at[0], load_sems.at[2 * k]),
            pltpu.make_async_copy(rest, there, load_sems.at[2 * k + 1]),
        )
        for copy in pair:
            copy.start()
        loads.append(pair)
    loads.append(
        (
            pltpu.make_async_copy(prob_in, prob_ref, load_sems.at[8]),
            pltpu.make_async_copy(kv_in, kv_ref, load_sems.at[9]),
        )
    )
    for copy in loads[4]:
        copy.start()
    hail(me, NEAR[:4] + WEIGHT)
    sends = Sends(me, send_sems, recv_sems)
    shards = [shard_of(me, k) for k in range(4)]

    def run640(k):
        return pl.ds(pl.multiple_of(shards[k] * 640, 128), 640)

    def loaded(k):
        for copy in loads[k]:
            copy.wait()

    for j in range(KV_HEADS):
        for g in range(GROUPS):
            h = GROUPS * j + g
            mixf[:, HEAD_DIM * h : HEAD_DIM * (h + 1)] = mix_ref[j, g * T : (g + 1) * T, HEAD_DIM:]
    mixture_ref[...] = mixf[...].astype(BF)
    mix_k = our_order(me, cut_four(mixture_ref))
    loaded(0)
    attn_out = sum(dot(mix_k[k], wo[k]) for k in range(4))
    hidden = h_ref[...]
    gain_f = vec_ref[1:2, :D]
    route_w = vec_ref[2:3, :D]
    middle = hidden + attn_out
    r2 = lax.rsqrt(jnp.mean(middle * middle, axis=-1, keepdims=True) + EPS)
    x2 = middle * r2 * gain_f
    x2_k = our_order(me, [x2[:, 240 * k : 240 * (k + 1)].astype(BF) for k in range(4)])
    xs[...] = jnp.zeros_like(xs)
    for k in range(4):
        xs[k, :, :240] = x2_k[k]
    meet(NEAR[:4] + WEIGHT)
    down = [
        sends.start(wd_ref, wd.at[1], "core", 1),
        sends.start(wds_ref.at[0], wd.at[3], "core", 1),
    ]
    shares = [everyone_steps(sends, (("one", [xs.at[k] for k in range(4)], xs_all, xs_relay),))]
    next(shares[0])
    loaded(1)
    gate_s[...] = sum(dot(x2_k[k], wg[k]) for k in range(4))
    loaded(2)
    up_s[...] = sum(dot(x2_k[k], wu[k]) for k in range(4))
    gate = gate_s[...]
    inner[...] = (gate * jax.nn.sigmoid(gate) * up_s[...]).astype(BF)
    loaded(3)
    shares.append(
        everyone_steps(sends, (("one", [inner.at[:, run640(k)] for k in range(4)], inner_all, inner_relay),))
    )
    next(shares[1])
    for copy in down:
        copy.wait_recv()
    ffn_out = sum(dot(inner[:, run640(k)], wd[k], NT) for k in range(4))
    route = jax.nn.sigmoid(jnp.sum(hidden * route_w, axis=-1, keepdims=True))
    branch = attn_out + ffn_out
    odd = lax.rem(me[4], 2)
    keep = pl.ds(pl.multiple_of(odd * T, T), T)
    out_ref[keep] = (route * branch).astype(BF)
    swap = sends.start(out_ref.at[keep], out_ref.at[keep], "pair", 1)
    upstream = up_ref[...]
    d_branch = upstream * route
    d_logit = route * (1.0 - route) * jnp.sum(upstream * branch, axis=-1, keepdims=True)
    logit_ref[...] = jnp.broadcast_to(d_logit, logit_ref.shape)
    vec_out_ref[...] = jnp.zeros_like(vec_out_ref)
    vec_out_ref[2:3, :D] = jnp.sum(d_logit * hidden, axis=0, keepdims=True)
    d_ffn = d_branch.astype(BF)
    own = pl.ds(0, T)
    dffn[...] = jnp.zeros_like(dffn)
    for k in range(4):
        dffn[:, 256 * k : 256 * k + 240] = d_branch[:, 240 * k : 240 * (k + 1)].astype(BF)
    shares.append(everyone_steps(sends, (("all", dffn, dffn_all, None),)))
    next(shares[2])
    dffn_all[own], xs_all[own], inner_all[own] = dffn[...], xs[0], inner[:, run640(0)]
    late = []
    for p in range(2):
        first = 2 * lax.rem(me[0] + p, 2)
        for b in range(2):
            at = (2 * p + (me[1] if b == 0 else 1 - me[1])) * 640
            run, run_up = (pl.ds(pl.multiple_of(c + at, 128), 640) for c in (0, FF))
            d_inner = dot(d_ffn, wd[first + b])
            gate, up = gate_s[:, run], up_s[:, run]
            sg = jax.nn.sigmoid(gate)
            dgu[:, run] = (d_inner * up * (sg + gate * sg * (1.0 - sg))).astype(BF)
            dgu[:, run_up] = (d_inner * (gate * sg)).astype(BF)
        cols = [pl.ds(c + 1280 * p, 1280) for c in (0, FF)]
        late.append(everyone_steps(sends, tuple(("all", dgu.at[:, c], dgu_all.at[:, c], None) for c in cols)))
        next(late[-1])
    for share in shares:
        next(share)
    dgu_all[own] = dgu[...]
    d_gate, d_up = dgu[:, :FF], dgu[:, FF:]
    d_x2 = jnp.concatenate(
        our_order(me, [dot(d_gate, wg[k], NT) + dot(d_up, wu[k], NT) for k in range(4)]), axis=1
    )
    d_mid, g_gain_f = norm_back_rows(middle, r2, gain_f, d_x2)
    d_mid_ref[...] = d_mid
    vec_out_ref[1:2, :D] = g_gain_f
    d_attn = (d_branch + d_mid).astype(BF)
    d_attn_ref[...] = d_attn
    d_mix_s[...] = jnp.concatenate(our_order(me, [dot(d_attn, wo[k], NT) for k in range(4)]), axis=1)
    do_s[...] = jnp.zeros_like(do_s)
    for j in range(KV_HEADS):
        for g in range(GROUPS):
            h = GROUPS * j + g
            do_s[j, g * T : (g + 1) * T, HEAD_DIM:] = d_mix_s[:, HEAD_DIM * h : HEAD_DIM * (h + 1)].astype(BF)

    stores = []

    def store(a, b):
        stores.append(pltpu.make_async_copy(a, b, store_sems.at[len(stores)]))
        stores[-1].start()

    together(*shares)
    for k in range(4):
        c = pl.ds(640 * k, 640)
        g_down[:, c] = dot(dffn_all[:, 256 * k : 256 * (k + 1)], inner_all[...], TN).astype(BF)
    wide = wide_steps(me, sends, g_down, low, out_b, full, sums_ref)
    next(wide)
    loaded(4)
    for j in range(KV_HEADS):
        c = pl.ds(j * 128, 128)
        tile = kv_ref[:, :, :, :, c].reshape(KEYS, 128)
        prob, d_out = prob_ref[j], do_s[j]
        d_prob = dot(d_out, tile, NT)
        delta = jnp.sum(d_out.astype(F32) * mix_ref[j], axis=-1, keepdims=True)
        d_score = (prob.astype(F32) * (d_prob - delta)).astype(BF)
        dq_ref[j] = dot(d_score, tile) * SCALE
        grad = dot(
            jnp.concatenate([d_score, prob], axis=0), jnp.concatenate([q_ref[j], d_out], axis=0), TN
        )
        dkv_ref[:, :, :, :, c] = grad.astype(BF).reshape(2, 4, 4, T, 128)
        store(dkv_ref.at[:, :, :, :, c], dkv_out.at[:, :, :, :, c])
        if j == 3:
            next(wide)
            next(wide)
    together(*late)
    for at in range(0, 2 * FF, 1280):
        c = pl.ds(at, 1280)
        g_ref[:, c] = dot(xs_all[...], dgu_all[:, c], TN).astype(BF)
        store(g_ref.at[:, c], g_out.at[:, c])
    together(wide)
    swap.wait_recv()
    for copy in stores:
        copy.wait()
    sends.finish()


def dense(mix, q, prob, kv, h, up_c, vec, own, rest):
    vmem, hbm = pl.BlockSpec(memory_space=pltpu.VMEM), pl.BlockSpec(memory_space=pl.ANY)
    rows = GROUPS * T
    return pl.pallas_call(
        dense_kernel,
        name="dense",
        out_shape=(
            jax.ShapeDtypeStruct((KV_HEADS, rows, 128), F32),
            jax.ShapeDtypeStruct((2, 4, 4, T, 640), BF),
            jax.ShapeDtypeStruct((ROWS, 2 * FF), BF),
            jax.ShapeDtypeStruct((ROWS, FF // 4), BF),
            jax.ShapeDtypeStruct((T, D), BF),
            jax.ShapeDtypeStruct((T, D), BF),
            jax.ShapeDtypeStruct((T, D), F32),
            jax.ShapeDtypeStruct((PAIR, D), BF),
            jax.ShapeDtypeStruct((T, 128), F32),
            jax.ShapeDtypeStruct((8, 1024), F32),
        ),
        in_specs=[vmem] * 2 + [hbm] * 2 + [vmem] * 3 + [hbm] * 8,
        out_specs=(vmem,) + (hbm,) * 2 + (vmem,) * 7,
        scratch_shapes=[
            pltpu.VMEM((4, 240, D), BF),
            pltpu.VMEM((4, 240, FF), BF),
            pltpu.VMEM((4, 240, FF), BF),
            pltpu.VMEM((4, D, 640), BF),
            pltpu.VMEM((T, D), F32),
            pltpu.VMEM((T, FF), F32),
            pltpu.VMEM((T, FF), F32),
            pltpu.VMEM((T, FF), BF),
            pltpu.VMEM((T, 2 * FF), BF),
            pltpu.VMEM((T, 1024), BF),
            pltpu.VMEM((4, T, 256), BF),
            pltpu.VMEM((KV_HEADS, rows, 128), BF),
            pltpu.VMEM((T, D), F32),
            pltpu.VMEM((4 * T, 2 * FF), BF),
            pltpu.VMEM((4 * T, 1024), BF),
            pltpu.VMEM((4 * T, 256), BF),
            pltpu.VMEM((4 * T, 640), BF),
            pltpu.VMEM((T, 256), BF),
            pltpu.VMEM((T, 640), BF),
            pltpu.VMEM((KV_HEADS, rows, KEYS), BF),
            pltpu.VMEM((2, 4, 4, T, 640), BF),
            pltpu.VMEM((2, 4, 4, T, 640), BF),
            pltpu.VMEM((ROWS, 2 * FF), BF),
            pltpu.VMEM((ROWS, FF), BF),
            *sum_scratch(FF, HALF)[:3],
            pltpu.SemaphoreType.DMA((10,)),
            pltpu.SemaphoreType.DMA((13,)),
        ]
        + sems(57),
        compiler_params=pltpu.CompilerParams(
            collective_id=4, has_side_effects=True, vmem_limit_bytes=VMEM_LIMIT
        ),
        cost_estimate=pl.CostEstimate(
            flops=20_000_000_000, bytes_accessed=40_000_000, transcendentals=0
        ),
    )(mix, q, prob, kv, h, up_c, vec, *own, *rest)


def per_device(hidden, chosen, positions, w_query, w_key, w_value, w_output, w_gate, w_up, w_down, gain_attn, gain_ffn, router, d_out):
    tokens, upstream = hidden[0], d_out[0]
    own_w = (w_output, w_gate, w_up, w_down.T)
    frequency = (THETA ** (-np.arange(0, HEAD_DIM // 2) * 2.0 / HEAD_DIM)).astype(np.float32)
    (
        mix_heads, prob, q_heads, kv_all, h, up_c, x1, cosine, sine, place, vec_in, wq, wk, wv, *rest_w
    ) = front(
        tokens.T, upstream.T, chosen, positions, np.tile(frequency, 4)[None, :], gain_attn, gain_ffn, router,
        w_query, w_key.T, w_value.T, *own_w
    )
    d_q_heads, d_kv, g_one, sums_down, d_attn, mixture, d_mid, out_c, d_logit, vec_out = dense(
        mix_heads, q_heads, prob, kv_all, h, up_c, vec_in, own_w, rest_w
    )
    s_gate, s_up, s_down, s_two, s_three, vector, d_rows = back(
        d_kv, g_one, sums_down, d_q_heads, d_attn, mixture, x1, h, d_mid, d_logit, vec_in, vec_out, cosine, sine, wq, wk, wv
    )
    output, d_tokens, g_query, g_key, g_value, g_output, g_gate, g_up, g_down, *vectors = finish(
        s_gate, s_up, s_down, s_two, s_three, vector, out_c, d_rows, place, tokens.T, upstream.T
    )
    return (
        output.T[None],
        d_tokens.T[None],
        g_query,
        g_key.T,
        g_value.T,
        g_output,
        g_gate,
        g_up,
        g_down.T,
        vectors[0],
        vectors[1],
        vectors[2],
    )


def solution(mesh):
    finer = Mesh(mesh.devices.reshape(DIMS), AX)
    shard, blk = ("ylo", "core"), ("yhi", "z", "x")
    act, row, weight, vec = P(shard, blk, None), P(shard, blk), P(shard, None), P(shard)
    return jax.shard_map(
        per_device,
        mesh=finer,
        in_specs=(act, row, row) + (weight,) * 7 + (vec,) * 3 + (act,),
        out_specs=(act, act) + (weight,) * 7 + (vec,) * 3,
        check_vma=False,
    )
```

```python
import functools

import jax
import jax.numpy as jnp
import numpy as np
from jax import lax
from jax.experimental import pallas as pl
from jax.experimental.pallas import tpu as pltpu
from jax.sharding import Mesh
from jax.sharding import PartitionSpec as P

D = 960
HEADS = 15
KV_HEADS = 5
GROUPS = 3
HEAD_DIM = 64
FF = 2560
EPS = 1e-05
THETA = 10000.0
SCALE = HEAD_DIM ** (-0.5)
T = 64
PAIR = 128
SLOTS = 32
KEYS = SLOTS * T
AX = ("ylo", "core", "yhi", "z", "x")
DIMS = (2, 2, 2, 4, 4)
MESH = pl.DeviceIdType.MESH
BF = jnp.bfloat16
F32 = jnp.float32
VMEM_LIMIT = 56 * 2**20


def dot(a, b, dims=(((1,), (0,)), ((), ()))):
    return lax.dot_general(a, b, dims, preferred_element_type=F32)


NT = (((1,), (1,)), ((), ()))
TN = (((0,), (0,)), ((), ()))


def here():
    return tuple(lax.axis_index(a) for a in AX)


def neighbour(me, axis, step):
    ylo, core, yhi, z, x = me
    if axis == "z":
        z = lax.rem(z + step + 4, 4)
    elif axis == "x":
        x = lax.rem(x + step + 4, 4)
    elif axis == "pair":
        x = x + 1 - 2 * lax.rem(x, 2)
    elif axis == "yhi":
        yhi = 1 - yhi
    elif axis == "ylo":
        ylo = 1 - ylo
    elif axis == "core":
        core = 1 - core
    else:
        y = lax.rem(yhi * 2 + ylo + step + 4, 4)
        ylo, yhi = lax.rem(y, 2), y // 2
    return (ylo, core, yhi, z, x)


NEAR = (("x", 1), ("x", -1), ("z", 1), ("z", -1), ("yhi", 1))
WEIGHT = (("y", 1), ("y", -1), ("core", 1))
FAR = (("x", 2), ("z", 2))


def hail(me, partners):
    barrier = pltpu.get_barrier_semaphore()
    for axis, step in partners:
        pl.semaphore_signal(
            barrier, inc=1, device_id=neighbour(me, axis, step), device_id_type=MESH
        )


def meet(partners):
    pl.semaphore_wait(pltpu.get_barrier_semaphore(), len(partners))


class Sends:
    def __init__(self, me, send_sems, recv_sems):
        self.me, self.send_sems, self.recv_sems, self.all = me, send_sems, recv_sems, []

    def start(self, src, dst, axis, step):
        k = len(self.all)
        copy = pltpu.make_async_remote_copy(
            src_ref=src,
            dst_ref=dst,
            send_sem=self.send_sems.at[k],
            recv_sem=self.recv_sems.at[k],
            device_id=neighbour(self.me, axis, step),
            device_id_type=MESH,
        )
        copy.start()
        self.all.append(copy)
        return copy

    def finish(self):
        for copy in self.all:
            copy.wait_send()


def together(*steps):
    steps = list(steps)
    while steps:
        for step in list(steps):
            try:
                next(step)
            except StopIteration:
                steps.remove(step)


def run_lanes(lanes, order):
    for c in order:
        next(lanes[c], None)
    together(*lanes.values())


def sems(count):
    return [pltpu.SemaphoreType.DMA((count,)), pltpu.SemaphoreType.DMA((count,))]


def plus(*terms):
    total = terms[0].astype(F32)
    for term in terms[1:]:
        total = total + term.astype(F32)
    return total


class Shards:
    def __init__(self, sends):
        self.sends, self.arrived, self.last = sends, [], []
        self.color = lax.rem(sends.me[3] + sends.me[4], 2)

    def near(self, own, out):
        self.last.append(self.sends.start(own, out.at[out.shape[0] - 3], "core", 1))

    def far(self, own, out, cut):
        for step, row, rows in ((1, 0, cut), (-1, cut, own.shape[0] - cut)):
            r = pl.ds(row, rows)
            ref = out.at[out.shape[0] - 2, r]
            self.arrived.append((ref, out.at[out.shape[0] - 1, r], self.sends.start(own.at[r], ref, "y", step)))

    def relay(self):
        for ref, to, copy in self.arrived:
            copy.wait_recv()
            self.last.append(self.sends.start(ref, to, "core", 1))
        self.arrived = []

    def finish(self):
        self.relay()
        for copy in self.last:
            copy.wait_recv()
        self.last = []

    def half(self, own, out, block, cuts):
        rows, slots = own.shape[0], out.shape[0]
        sub = block // 2
        mine = self.color * (rows - block)
        relay = slots > 1
        other = slots - 2 if relay else 0

        def part(slot, start, count):
            return out.at[slot, pl.ds(pl.multiple_of(start, 16), count)]

        copies = []
        for step, off in ((1, 0), (-1, sub)):
            src = own.at[pl.ds(pl.multiple_of(mine + off, 16), sub)]
            copies.append(self.sends.start(src, part(other, mine + off, sub), "y", step))
        if relay:
            self.near(own, out)
        yield
        for copy in copies:
            copy.wait_recv()
        copies, off = [], 0
        for (axis, step), count in zip((("x", 1), ("x", -1), ("z", 1), ("z", -1)), cuts):
            ref = part(other, self.color * block + off, count)
            copies.append(self.sends.start(ref, ref, axis, step))
            off += count
        if relay:
            self.last.append(self.sends.start(part(other, mine, block), part(slots - 1, mine, block), "core", 1))
        yield
        for copy in copies:
            copy.wait_recv()
        rest = (1 - self.color) * block
        if relay:
            self.last.append(
                self.sends.start(part(other, rest, rows - block), part(slots - 1, rest, rows - block), "core", 1)
            )


def gather_steps(me, sends, kv_ref, out_ref):
    _, _, yh, z, x = me
    oy = 1 - yh
    half, quarter = T // 2, T // 4
    streams = (("x", "z", 0), ("z", "x", half))

    def slot(y, axis, step, rows, count):
        zz = lax.rem(z + step + 4, 4) if axis == "z" else z
        xx = lax.rem(x + step + 4, 4) if axis == "x" else x
        return out_ref.at[y, zz, xx, pl.ds(rows, count)]

    def line(y, axis, step, rows, count):
        if axis == "z":
            return out_ref.at[y, lax.rem(z + step + 4, 4), :, pl.ds(rows, count)]
        return out_ref.at[y, :, lax.rem(x + step + 4, 4), pl.ds(rows, count)]

    own = out_ref.at[yh, z, x]
    own[...] = kv_ref[...]
    first = sends.start(kv_ref, own, "yhi", 1)
    got = {}
    for y, tag in ((yh, 0), (oy, 1)):
        if tag:
            yield
            first.wait_recv()
        for axis, _, row in streams:
            src = slot(y, axis, 0, row, half)
            for step in (1, -1):
                got[tag, row, step] = sends.start(src, src, axis, step)
    far = {}
    for y, tag in ((yh, 0), (oy, 1)):
        yield
        for axis, _, row in streams:
            for step, off in ((1, 0), (-1, quarter)):
                got[tag, row, step].wait_recv()
                src = slot(y, axis, -step, row + off, quarter)
                far[tag, row, step] = sends.start(src, src, axis, step)
    wide = {}
    for y, tag in ((yh, 0), (oy, 1)):
        yield
        for _, axis, row in streams:
            for step in (1, -1):
                far[tag, row, step].wait_recv()
            src = line(y, axis, 0, row, half)
            for step in (1, -1):
                wide[tag, row, step] = sends.start(src, src, axis, step)
    last = []
    for y, tag in ((yh, 0), (oy, 1)):
        yield
        for _, axis, row in streams:
            for step, off in ((1, 0), (-1, quarter)):
                wide[tag, row, step].wait_recv()
                src = line(y, axis, -step, row + off, quarter)
                last.append(sends.start(src, src, axis, step))
    yield
    for copy in last:
        copy.wait_recv()


def swapped(x):
    lane = lax.broadcasted_iota(jnp.int32, x.shape, 1)
    return jnp.where(lane < HEAD_DIM // 2, pltpu.roll(x, 96, 1), pltpu.roll(x, 32, 1))


def front_kernel(
    hidden_ref, d_out_ref, chosen_ref, pos_ref, freq_ref, gain_a_ref, gain_f_ref, router_ref, wq_ref, wk_ref, wv_ref,
    wo_ref, wg_ref, wu_ref, wd_ref,
    mix_ref, prob_out, q_ref, kv_out, h_ref, up_ref, x1_ref, cos_ref, sin_ref, place_ref, vec_out_ref,
    wq_out, wk_out, wv_out, wos_ref, wgs_ref, wus_ref, wds_ref,
    compact_h, compact_d, compact_p, got_h, got_d, got_p, vecs, q_pre, kv_own,
    prob_ref, kv_ref, wq, wk, wv,
    load_sems, store_sems, send_sems, recv_sems,
):
    me = here()
    yhi, z, x = me[2:]
    loads = []
    for k, (own, to) in enumerate(((wq_ref, wq), (wk_ref, wk), (wv_ref, wv))):
        loads.append(pltpu.make_async_copy(own, to.at[0], load_sems.at[k]))
        loads[-1].start()
    hail(me, NEAR + WEIGHT)
    sends = Sends(me, send_sems, recv_sems)
    early, query, late = Shards(sends), Shards(sends), Shards(sends)
    odd = lax.rem(x, 2)
    give = pl.ds(pl.multiple_of((1 - odd) * T, T), T)
    keep = pl.ds(pl.multiple_of(odd * T, T), T)
    limit = ((yhi * 16 + z * 4 + x) // 2 + 1) * PAIR
    stores = []

    def store(a, b):
        stores.append(pltpu.make_async_copy(a, b, store_sems.at[len(stores)]))
        stores[-1].start()

    def main():
        flag = jnp.where(chosen_ref[...] > 0, 1.0, 0.0)
        token = lax.broadcasted_iota(jnp.int32, (PAIR, PAIR), 0)
        lane = lax.broadcasted_iota(jnp.int32, (PAIR, PAIR), 1)
        upto = jnp.where(token <= lane, 1.0, 0.0).astype(BF)
        count = dot(jnp.broadcast_to(flag, (16, PAIR)).astype(BF), upto)[0:1]
        total = jnp.sum(flag, axis=1, keepdims=True)
        rank = count - 1.0 + jnp.where(odd == 1, PAIR - total, 0.0)
        place = jnp.where(token.astype(F32) == rank, flag, 0.0)
        place_low = place.astype(BF)
        place_ref[...] = place_low
        compact_p[...] = jnp.broadcast_to(
            jnp.sum(place * pos_ref[...].astype(F32), axis=1, keepdims=True), (PAIR, PAIR)
        )
        compact_h[...] = dot(place_low, hidden_ref[...].astype(BF), NT).astype(BF)
        vecs[0] = jnp.zeros((8, 256), F32)
        for k, ref in enumerate((gain_a_ref, gain_f_ref, router_ref)):
            vecs[0, k : k + 1, :240] = ref[...].astype(F32).reshape(1, 240)
        meet(NEAR + WEIGHT)
        vec_far = sends.start(vecs.at[0], vecs.at[2], "y", 1)
        early.far(wk_ref, wk, 160)
        early.far(wv_ref, wv, 160)
        vec_near = sends.start(vecs.at[0], vecs.at[1], "core", 1)
        early.near(wk_ref, wk)
        early.near(wv_ref, wv)
        query.far(wq_ref, wq, 128)
        query.near(wq_ref, wq)
        swaps = [sends.start(c.at[give], g, "pair", 1) for c, g in ((compact_h, got_h), (compact_p, got_p))]
        yield
        compact_d[...] = dot(place_low, d_out_ref[...].astype(BF), NT).astype(BF)
        vec_far.wait_recv()
        vec_last = sends.start(vecs.at[2], vecs.at[3], "core", 1)
        early.relay()
        yield
        swaps[0].wait_recv()
        h = plus(compact_h[keep], got_h[...])
        h_ref[...] = h
        swaps.append(sends.start(compact_d.at[give], got_d, "pair", 1))
        swaps[1].wait_recv()
        angle = (compact_p[keep] + got_p[...]) * freq_ref[...]
        turn = lax.broadcasted_iota(jnp.int32, (T, PAIR), 1)
        cosine = jnp.where(turn < HEAD_DIM, jnp.cos(angle), 1.0)
        sine = jnp.sin(angle)
        sine = jnp.where(turn < HEAD_DIM // 2, -sine, jnp.where(turn < HEAD_DIM, sine, 0.0))
        cos_ref[...], sin_ref[...] = cosine, sine
        vec_near.wait_recv()
        vec_last.wait_recv()
        vec_out_ref[...] = jnp.zeros_like(vec_out_ref)
        for k, v in enumerate(our_order(me, [vecs[k, :, :240] for k in range(4)])):
            vec_out_ref[:, 240 * k : 240 * (k + 1)] = v
        r1 = lax.rsqrt(jnp.mean(h * h, axis=-1, keepdims=True) + EPS)
        x1_ref[...] = (h * r1 * vec_out_ref[0:1, :D]).astype(BF)
        x1_k = our_order(me, cut_four(x1_ref))
        for copy in loads:
            copy.wait()
        early.finish()
        k_pre = sum(dot(x1_k[k], wk[k], NT) for k in range(4))
        v_pre = sum(dot(x1_k[k], wv[k], NT) for k in range(4))
        for j in range(KV_HEADS):
            run = slice(HEAD_DIM * j, HEAD_DIM * (j + 1))
            tile = jnp.concatenate([k_pre[:, run], v_pre[:, run]], axis=1)
            kv_own[:, 128 * j : 128 * (j + 1)] = (tile * cosine + swapped(tile) * sine).astype(BF)
        gather = gather_steps(me, sends, kv_own, kv_ref)
        next(gather)
        yield
        next(gather)
        yield
        query.relay()
        yield
        query.finish()
        swaps[2].wait_recv()
        up_ref[...] = plus(compact_d[keep], got_d[...])
        q_pre[...] = sum(dot(x1_k[k], wq[k]) for k in range(4))
        zero = jnp.zeros((T, HEAD_DIM), F32)
        for j in range(KV_HEADS):
            for g in range(GROUPS):
                at = HEAD_DIM * (GROUPS * j + g)
                tile = jnp.concatenate([q_pre[:, at : at + HEAD_DIM], zero], axis=1)
                q_ref[j, g * T : (g + 1) * T] = ((tile * cosine + swapped(tile) * sine) * SCALE).astype(BF)
        yield
        yield from gather
        for a, b in ((kv_ref, kv_out), (wq, wq_out), (wk, wk_out), (wv, wv_out)):
            store(a, b)
        for j in range(KV_HEADS):
            tile = kv_ref[:, :, :, :, 128 * j : 128 * (j + 1)].reshape(KEYS, 128)
            scores = dot(q_ref[j], tile, NT)
            column = lax.broadcasted_iota(jnp.int32, scores.shape, 1)
            scores = jnp.where(column < limit, scores, -1e30)
            exponent = jnp.exp(scores - jnp.max(scores, axis=-1, keepdims=True))
            prob = (exponent * (1.0 / jnp.sum(exponent, axis=-1, keepdims=True))).astype(BF)
            prob_ref[j] = prob
            store(prob_ref.at[j], prob_out.at[j])
            mix_ref[j] = dot(prob, tile)
            yield

    small, large = (128, (32, 32, 32, 16)), (480, (128, 128, 112, 112))
    lanes = {
        "m": main(),
        "o": late.half(wo_ref, wos_ref, *small),
        "t": late.half(wg_ref, wgs_ref, *small),
        "u": late.half(wu_ref, wus_ref, *small),
        "d": late.half(wd_ref, wds_ref, *large),
    }
    run_lanes(lanes, "".join(FRONT_ORDER))
    late.finish()
    for copy in stores:
        copy.wait()
    sends.finish()


FRONT_ORDER = (
    "mmmotmmmmmomummdmotummtdmmumdm",
)


def front(hidden, d_out, chosen, pos, freq, gain_a, gain_f, router, w_query, w_key, w_value, *later):
    vmem, hbm = pl.BlockSpec(memory_space=pltpu.VMEM), pl.BlockSpec(memory_space=pl.ANY)
    rows = GROUPS * T
    return pl.pallas_call(
        front_kernel,
        name="front",
        out_shape=(
            jax.ShapeDtypeStruct((KV_HEADS, rows, 128), F32),
            jax.ShapeDtypeStruct((KV_HEADS, rows, KEYS), BF),
            jax.ShapeDtypeStruct((KV_HEADS, rows, 128), BF),
            jax.ShapeDtypeStruct((2, 4, 4, T, 640), BF),
            jax.ShapeDtypeStruct((T, D), F32),
            jax.ShapeDtypeStruct((T, D), F32),
            jax.ShapeDtypeStruct((T, D), BF),
            jax.ShapeDtypeStruct((T, 128), F32),
            jax.ShapeDtypeStruct((T, 128), F32),
            jax.ShapeDtypeStruct((PAIR, PAIR), BF),
            jax.ShapeDtypeStruct((8, 1024), F32),
            jax.ShapeDtypeStruct((4, 240, 960), BF),
            jax.ShapeDtypeStruct((4, 320, 240), BF),
            jax.ShapeDtypeStruct((4, 320, 240), BF),
        )
        + tuple(jax.ShapeDtypeStruct((3,) + w.shape, BF) for w in later[:3])
        + (jax.ShapeDtypeStruct((1,) + later[3].shape, BF),),
        in_specs=[vmem] * 8 + [hbm] * 7,
        out_specs=(vmem, hbm, vmem, hbm) + (vmem,) * 7 + (hbm,) * 7,
        scratch_shapes=[
            pltpu.VMEM((PAIR, D), BF),
            pltpu.VMEM((PAIR, D), BF),
            pltpu.VMEM((PAIR, PAIR), F32),
            pltpu.VMEM((T, D), BF),
            pltpu.VMEM((T, D), BF),
            pltpu.VMEM((T, PAIR), F32),
            pltpu.VMEM((4, 8, 256), F32),
            pltpu.VMEM((T, D), F32),
            pltpu.VMEM((T, 640), BF),
            pltpu.VMEM((KV_HEADS, rows, KEYS), BF),
            pltpu.VMEM((2, 4, 4, T, 640), BF),
            pltpu.VMEM((4, 240, 960), BF),
            pltpu.VMEM((4, 320, 240), BF),
            pltpu.VMEM((4, 320, 240), BF),
            pltpu.SemaphoreType.DMA((3,)),
            pltpu.SemaphoreType.DMA((9,)),
        ]
        + sems(90),
        compiler_params=pltpu.CompilerParams(
            collective_id=1, has_side_effects=True, vmem_limit_bytes=VMEM_LIMIT
        ),
        cost_estimate=pl.CostEstimate(flops=5_000_000_000, bytes_accessed=90_000_000, transcendentals=0),
    )(hidden, d_out, chosen, pos, freq, gain_a, gain_f, router, w_query, w_key, w_value, *later)


def key_steps(me, sends, part_ref, out_ref, low, out_b, full, sums, nlow, nout, nfull, mine, y_in):
    _, _, yh, z, x = me
    half, quarter = T // 2, T // 4
    streams = (("x", "z", 0), ("z", "x", half))

    def line(axis, step, row, count):
        if axis == "z":
            return part_ref.at[:, lax.rem(z + step + 4, 4), :, pl.ds(row, count)]
        return part_ref.at[:, :, lax.rem(x + step + 4, 4), pl.ds(row, count)]

    near = {}
    for s, (axis, _, row) in enumerate(streams):
        near[s, 1] = sends.start(line(axis, 2, row, quarter), low.at[s, 0], axis, 1)
        near[s, -1] = sends.start(line(axis, 2, row + quarter, quarter), low.at[s, 1], axis, -1)
    whole = {}
    for s, (axis, _, row) in enumerate(streams):
        yield
        for d, step in enumerate((1, -1)):
            near[s, step].wait_recv()
            lo, hi = (0, quarter) if step == 1 else (quarter, 0)
            out_b[s, d, :, :, pl.ds(lo, quarter)] = plus(
                line(axis, step, row + lo, quarter)[...], low[s, d]
            ).astype(BF)
            out_b[s, d, :, :, pl.ds(hi, quarter)] = line(axis, step, row + hi, quarter)[...]
            whole[s, step] = sends.start(out_b.at[s, d], full.at[s, d], axis, step)
    near = {}
    for s, (axis, other, row) in enumerate(streams):
        yield
        for step in (1, -1):
            whole[s, step].wait_recv()
        sums[s] = plus(line(axis, 0, row, half)[...], full[s, 0], full[s, 1]).astype(BF)
        far = lax.rem((z if other == "z" else x) + 2, 4)
        near[s, 1] = sends.start(sums.at[s, :, far, pl.ds(0, quarter)], nlow.at[s, 0], other, 1)
        near[s, -1] = sends.start(
            sums.at[s, :, far, pl.ds(quarter, quarter)], nlow.at[s, 1], other, -1
        )
    for s, (axis, other, row) in enumerate(streams):
        yield
        at = z if other == "z" else x
        for d, step in enumerate((1, -1)):
            near[s, step].wait_recv()
            to = lax.rem(at + step + 4, 4)
            lo, hi = (0, quarter) if step == 1 else (quarter, 0)
            nout[s, d, :, pl.ds(lo, quarter)] = plus(
                sums[s, :, to, pl.ds(lo, quarter)], nlow[s, d]
            ).astype(BF)
            nout[s, d, :, pl.ds(hi, quarter)] = sums[s, :, to, pl.ds(hi, quarter)]
            whole[s, step] = sends.start(nout.at[s, d], nfull.at[s, d], other, step)
    swap = {}
    for s, (axis, other, row) in enumerate(streams):
        yield
        at = z if other == "z" else x
        for step in (1, -1):
            whole[s, step].wait_recv()
        mine[s] = plus(sums[s, :, at], nfull[s, 0], nfull[s, 1]).astype(BF)
        swap[s] = sends.start(mine.at[s, 1 - yh], y_in.at[s], "yhi", 1)
    yield
    for s, (axis, other, row) in enumerate(streams):
        swap[s].wait_recv()
        out_ref[pl.ds(row, half)] = plus(mine[s, yh], y_in[s])


def key_scratch():
    half, quarter, w = T // 2, T // 4, 640
    return [
        pltpu.VMEM((2, 2, 2, 4, quarter, w), BF),
        pltpu.VMEM((2, 2, 2, 4, half, w), BF),
        pltpu.VMEM((2, 2, 2, 4, half, w), BF),
        pltpu.VMEM((2, 2, 4, half, w), BF),
        pltpu.VMEM((2, 2, 2, quarter, w), BF),
        pltpu.VMEM((2, 2, 2, half, w), BF),
        pltpu.VMEM((2, 2, 2, half, w), BF),
        pltpu.VMEM((2, 2, half, w), BF),
        pltpu.VMEM((2, half, w), BF),
    ]


ROWS = 256
HALF = ROWS // 2
STREAMS = (("x", "z"), ("z", "x"))


def spots(me):
    return {"z": me[3], "x": me[4]}


def around(me, axis, step):
    return lax.rem(spots(me)[axis] + step + 4, 4)


def columns(me, axis, step, big):
    return pl.ds(pl.multiple_of(around(me, axis, step) * big, 128), big)


def halves(big):
    cut = (big // 2 + 127) // 128 * 128
    return (0, cut), (cut, big - cut)


def wide_steps(me, sends, g_ref, low, out_b, full, sums):
    h, big = sums.shape[0] // 2, sums.shape[1]
    cut = h // 2
    near, whole = {}, {}

    def parts(step):
        return (0, cut) if step == 1 else (cut, 0)

    for s, (axis, _) in enumerate(STREAMS):
        c = columns(me, axis, 2, big)
        for step in (1, -1):
            r = pl.ds(s * h + parts(step)[0], cut)
            near[s, step] = sends.start(g_ref.at[r, c], low.at[r], axis, step)
    for s, (axis, _) in enumerate(STREAMS):
        yield
        for d, step in enumerate((1, -1)):
            near[s, step].wait_recv()
            add, keep = (pl.ds(s * h + p, cut) for p in parts(step))
            c = columns(me, axis, step, big)
            out_b[d, add] = plus(g_ref[add, c], low[add]).astype(BF)
            out_b[d, keep] = g_ref[keep, c]
            r = pl.ds(s * h, h)
            whole[s, step] = sends.start(out_b.at[d, r], full.at[d, r], axis, step)

    for s, (axis, _) in enumerate(STREAMS):
        yield
        for step in (1, -1):
            whole[s, step].wait_recv()
        r = pl.ds(s * h, h)
        sums[r] = plus(g_ref[r, columns(me, axis, 0, big)], full[0, r], full[1, r]).astype(BF)


def narrow_steps(me, sends, sums, mine, swap_y, nlow, nout, nfull, y_in):
    run, big = mine.shape[-2:]
    h = 4 * run
    near, whole = {}, {}

    def rows(s, other, step):
        return pl.ds(pl.multiple_of(s * h + around(me, other, step) * run, 16), run)

    for s, (axis, other) in enumerate(STREAMS):
        for d, step in enumerate((1, -1)):
            c = pl.ds(*halves(big)[d])
            near[s, step] = sends.start(sums.at[rows(s, other, 2), c], nlow.at[s, :, c], other, step)
    for s, (axis, other) in enumerate(STREAMS):
        yield
        for d, step in enumerate((1, -1)):
            near[s, step].wait_recv()
            add, keep = pl.ds(*halves(big)[d]), pl.ds(*halves(big)[1 - d])
            r = rows(s, other, step)
            nout[s, d, :, add] = plus(sums[r, add], nlow[s, :, add]).astype(BF)
            nout[s, d, :, keep] = sums[r, keep]
            whole[s, step] = sends.start(nout.at[s, d], nfull.at[s, d], other, step)
    swap = {}
    for s, (axis, other) in enumerate(STREAMS):
        yield
        for step in (1, -1):
            whole[s, step].wait_recv()
        total = plus(sums[rows(s, other, 0)], nfull[s, 0], nfull[s, 1]).astype(BF)
        if swap_y:
            y_in[0, s] = total
            swap[s] = sends.start(y_in.at[0, s], y_in.at[1, s], "yhi", 1)
        else:
            mine[s] = total
    if swap_y:
        for s in range(2):
            yield
            swap[s].wait_recv()
            mine[s] = plus(y_in[0, s], y_in[1, s]).astype(BF)


def sum_steps(me, sends, g_ref, mine, swap_y, low, out_b, full, sums, *narrow):
    yield from wide_steps(me, sends, g_ref, low, out_b, full, sums)
    yield from narrow_steps(me, sends, sums, mine, swap_y, *narrow)


def sum_scratch(width, h):
    big, run = width // 4, h // 4
    return [
        pltpu.VMEM((2 * h, big), BF),
        pltpu.VMEM((2, 2 * h, big), BF),
        pltpu.VMEM((2, 2 * h, big), BF),
        pltpu.VMEM((2 * h, big), BF),
        pltpu.VMEM((2, run, big), BF),
        pltpu.VMEM((2, 2, run, big), BF),
        pltpu.VMEM((2, 2, run, big), BF),
        pltpu.VMEM((2, 2, run, big), BF),
    ]


def spread_steps(me, sends, mine, out_ref, store_sems, to_y):
    run, big = mine.shape[-2:]
    h = 4 * run
    cut = h // 2
    near, whole, stored, last, over = {}, {}, [], {}, []

    def base(s):
        return s * HALF + (me[2] * h if to_y else 0)

    def rows(s, off, count):
        return pl.ds(pl.multiple_of(base(s) + off, 16), count)

    def block(s, axis, step, off, count):
        return out_ref.at[rows(s, off, count), columns(me, axis, step, big)]

    def on(ref):
        if to_y:
            over.append(sends.start(ref, ref, "yhi", 1))

    for s, (axis, other) in enumerate(STREAMS):
        ref = block(s, axis, 0, around(me, other, 0) * run, run)
        for step in (1, -1):
            near[s, step] = sends.start(mine.at[s], ref, other, step)
        stored.append(pltpu.make_async_copy(mine.at[s], ref, store_sems.at[s]))
        stored[-1].start()

    def narrow(s, axis, other, step, d):
        c0, n = halves(big)[d]
        c = pl.ds(pl.multiple_of(around(me, axis, 0) * big + c0, 128), n)
        return out_ref.at[rows(s, around(me, other, step) * run, run), c]

    for s, (axis, other) in enumerate(STREAMS):
        yield
        for d, step in enumerate((1, -1)):
            near[s, step].wait_recv()
            ref = narrow(s, axis, other, -step, d)
            whole[s, step] = sends.start(ref, ref, other, step)
    for s, (axis, other) in enumerate(STREAMS):
        yield
        for step in (1, -1):
            whole[s, step].wait_recv()
        stored[s].wait()
        ref = block(s, axis, 0, 0, h)
        for step in (1, -1):
            near[s, step] = sends.start(ref, ref, axis, step)
        on(ref)
    for s, (axis, other) in enumerate(STREAMS):
        yield
        for d, step in enumerate((1, -1)):
            near[s, step].wait_recv()
            ref = block(s, axis, -step, d * cut, cut)
            last[s, step] = sends.start(ref, ref, axis, step)
            on(block(s, axis, -step, 0, h))
    for s, (axis, other) in enumerate(STREAMS):
        yield
        for step in (1, -1):
            last[s, step].wait_recv()
        on(block(s, axis, 2, 0, h))
    if to_y:
        yield
        for copy in over:
            copy.wait_recv()


def halved_steps(me, sends, g_ref, mine, kept, got, out_ref, store_sems, *scratch):
    h = HALF // 2
    yh = me[2]
    copies = []
    for s in range(2):
        give = pl.ds(pl.multiple_of(s * HALF + (1 - yh) * h, 16), h)
        copies.append(sends.start(g_ref.at[give], got.at[pl.ds(s * h, h)], "yhi", 1))
    for s in range(2):
        yield
        copies[s].wait_recv()
        r = pl.ds(s * h, h)
        kept[r] = plus(g_ref[pl.ds(pl.multiple_of(s * HALF + yh * h, 16), h)], got[r]).astype(BF)
    yield
    yield from sum_steps(me, sends, kept, mine, False, *scratch)
    yield from spread_steps(me, sends, mine, out_ref, store_sems, True)


def vector_steps(sends, vec_ref, out_ref, keep, got):
    rounds = ((("core", 1),), (("ylo", 1),), (("x", 1), ("x", -1), ("x", 2)), (("z", 1), ("z", -1), ("z", 2)), (("yhi", 1),))
    keep[0] = vec_ref[...]
    k = 0
    for at, partners in enumerate(rounds):
        copies = []
        for axis, step in partners:
            copies.append((k, sends.start(keep.at[at], got.at[k], axis, step)))
            k += 1
        yield
        total = keep[at]
        for slot, copy in copies:
            copy.wait_recv()
            total = total + got[slot]
        keep[at + 1] = total
    out_ref[...] = keep[len(rounds)]


def small_steps(me, sends, g_ref, out_ref, got_x, got_z, got_y, sum_z, sum_y):
    x, z = me[3], me[4]
    steps = (1, -1, 2)

    def rows(at, step, count, base=0):
        return pl.ds(pl.multiple_of(base + lax.rem(at + step + 4, 4) * count, 16), count)

    copies = [
        sends.start(g_ref.at[rows(x, step, 64)], got_x.at[k], "z", step) for k, step in enumerate(steps)
    ]
    yield
    for copy in copies:
        copy.wait_recv()
    sum_z[...] = plus(g_ref[rows(x, 0, 64)], got_x[0], got_x[1], got_x[2]).astype(BF)
    copies = [
        sends.start(sum_z.at[rows(z, step, 16)], got_z.at[k], "x", step) for k, step in enumerate(steps)
    ]
    yield
    for copy in copies:
        copy.wait_recv()
    sum_y[...] = plus(sum_z[rows(z, 0, 16)], got_z[0], got_z[1], got_z[2]).astype(BF)
    copy = sends.start(sum_y, got_y, "yhi", 1)
    yield
    copy.wait_recv()
    ref = out_ref.at[rows(z, 0, 16, x * 64)]
    ref[...] = plus(sum_y[...], got_y[...]).astype(BF)
    copies = [sends.start(ref, ref, "x", step) for step in steps]
    yield
    for copy in copies:
        copy.wait_recv()
    ref = out_ref.at[rows(x, 0, 64)]
    copies = [sends.start(ref, ref, "z", step) for step in steps]
    yield
    for copy in copies:
        copy.wait_recv()


KEY_N, SUM_N = 9, 8
WIDE, REST = FF, 2048


def back_kernel(
    part_ref, g_in, sums_ref, dq_ref, d_attn_ref, mixture_ref, x1_ref, h_ref, d_mid_ref, logit_ref, vec_ref, vec_part_ref,
    cos_ref, sin_ref, wq_in, wk_in, wv_in,
    gate_ref, up_ref, down_ref, two_ref, three_ref, vec_out_ref, both_ref,
    own, ra, rb, xs, ra_all, rb_all, xs_all, xs_relay, g_two, g_three, d_x1_s, vec_all, keep_v, got_v,
    mine_gate, mine_up, mine_down, mine_two, got_x, got_z, got_y, sum_z, sum_y,
    g_gate, g_up, kept, got_gate, wq, wk, wv, load_sems, store_sems,
    *scratch,
):
    me = here()
    key_scr, rest = scratch[:KEY_N], scratch[KEY_N:-2]
    gate_scr, up_scr, two_scr, down_scr = (rest[SUM_N * k : SUM_N * (k + 1)] for k in range(4))
    loads = [
        pltpu.make_async_copy(a, b, load_sems.at[k])
        for k, (a, b) in enumerate(
            (
                (g_in.at[:, pl.ds(0, WIDE)], g_gate),
                (g_in.at[:, pl.ds(WIDE, WIDE)], g_up),
                (wq_in, wq),
                (wk_in, wk),
                (wv_in, wv),
            )
        )
    ]
    for copy in loads:
        copy.start()
    hail(me, NEAR + WEIGHT + FAR)
    sends = Sends(me, *scratch[-2:])
    odd = lax.rem(me[4], 2)
    keep = pl.ds(pl.multiple_of(odd * T, T), T)
    cosine, sine = cos_ref[...], sin_ref[...]
    mine = pl.ds(0, T)

    def turned_back(tile):
        return tile * cosine - swapped(tile) * sine

    for j in range(KV_HEADS):
        for g in range(GROUPS):
            at = HEAD_DIM * (GROUPS * j + g)
            ra[:, at : at + HEAD_DIM] = turned_back(dq_ref[j, g * T : (g + 1) * T]).astype(BF)[:, :HEAD_DIM]
    ra[:, D:] = d_attn_ref[...]
    xs[...] = jnp.zeros_like(xs)
    for k, (a, b) in enumerate(zip(our_order(me, cut_four(x1_ref)), our_order(me, cut_four(mixture_ref)))):
        xs[k, :, :240] = a
        xs[k, :, 256:496] = b
    meet(NEAR + WEIGHT + FAR)

    def keys():
        yield from key_steps(me, sends, part_ref, own, *key_scr)
        for j in range(KV_HEADS):
            tile = turned_back(own[:, 128 * j : 128 * (j + 1)]).astype(BF)
            rb[:, HEAD_DIM * j : HEAD_DIM * (j + 1)] = tile[:, :HEAD_DIM]
            rb[:, 320 + HEAD_DIM * j : 320 + HEAD_DIM * (j + 1)] = tile[:, HEAD_DIM:]
        share = everyone_steps(sends, (("all", rb, rb_all, None),))
        next(share)
        rb_all[mine] = rb[...]
        d_k, d_v = rb[:, :320], rb[:, 320:]
        d_x1 = d_x1_s[...] + jnp.concatenate(
            our_order(me, [dot(d_k, wk[k]) + dot(d_v, wv[k]) for k in range(4)]), axis=1
        )
        h = h_ref[...]
        r1 = lax.rsqrt(jnp.mean(h * h, axis=-1, keepdims=True) + EPS)
        d_first, g_gain_a = norm_back_rows(h, r1, vec_ref[0:1, :D], d_x1)
        d_h = d_mid_ref[...] + d_first + logit_ref[:, 0:1] * vec_ref[2:3, :D]
        both_ref[keep] = d_h.astype(BF)
        swap = sends.start(both_ref.at[keep], both_ref.at[keep], "pair", 1)
        vec_all[...] = jnp.zeros_like(vec_all)
        for k, row in enumerate((g_gain_a, vec_part_ref[1:2, :D], vec_part_ref[2:3, :D])):
            for i in range(2):
                vec_all[2 * k + i : 2 * k + i + 1, :480] = row[:, 480 * i : 480 * (i + 1)]
        vectors = vector_steps(sends, vec_all, vec_out_ref, keep_v, got_v)
        next(vectors)
        yield
        next(share)
        yield
        together(share)
        g_three[...] = dot(xs_all[:, :256], rb_all[...], TN).astype(BF)
        small = small_steps(me, sends, g_three, three_ref, got_x, got_z, got_y, sum_z, sum_y)
        while True:
            for step in (small, vectors):
                next(step, None)
            if small.gi_frame is None and vectors.gi_frame is None:
                break
            yield
        swap.wait_recv()

    def queries():
        share = everyone_steps(
            sends, (("all", ra, ra_all, None), ("one", [xs.at[k] for k in range(4)], xs_all, xs_relay))
        )
        next(share)
        ra_all[mine] = ra[...]
        xs_all[mine] = xs[0]
        d_q = ra[:, :D]
        for copy in loads[2:]:
            copy.wait()
        d_x1_s[...] = jnp.concatenate(our_order(me, [dot(d_q, wq[k], NT) for k in range(4)]), axis=1)
        g_two[:, 2 * D :] = jnp.zeros((ROWS, 128), BF)
        yield
        next(share)
        yield
        together(share)
        g_two[:, :D] = dot(xs_all[:, :256], ra_all[:, :D], TN).astype(BF)
        g_two[:, D : 2 * D] = dot(xs_all[:, 256:], ra_all[:, D:], TN).astype(BF)
        yield from sum_steps(me, sends, g_two, mine_two, True, *two_scr)
        yield from spread_steps(me, sends, mine_two, two_ref, store_sems.at[pl.ds(6, 2)], False)

    def gate():
        loads[0].wait()
        yield from halved_steps(
            me, sends, g_gate, mine_gate, kept, got_gate, gate_ref, store_sems.at[pl.ds(0, 2)], *gate_scr
        )

    def up():
        loads[1].wait()
        yield from sum_steps(me, sends, g_up, mine_up, True, *up_scr)
        yield from spread_steps(me, sends, mine_up, up_ref, store_sems.at[pl.ds(2, 2)], False)

    def down():
        yield from narrow_steps(me, sends, sums_ref, mine_down, True, *down_scr)
        yield from spread_steps(me, sends, mine_down, down_ref, store_sems.at[pl.ds(4, 2)], False)

    run_lanes({"k": keys(), "g": gate(), "u": up(), "d": down(), "q": queries()}, "".join(ORDER))
    sends.finish()


ORDER = (
    "kgdukkquugkkgddguukkqdqgdukgkdqudqggkqdk",
    "qgkguqgdqugddqqgukguqqgugdudqqkuguqqdkuu",
    "gdgkuuqgqgqqk",
)


def back(*args):
    vmem, hbm = pl.BlockSpec(memory_space=pltpu.VMEM), pl.BlockSpec(memory_space=pl.ANY)
    return pl.pallas_call(
        back_kernel,
        name="back",
        out_shape=(
            jax.ShapeDtypeStruct((ROWS, WIDE), BF),
            jax.ShapeDtypeStruct((ROWS, WIDE), BF),
            jax.ShapeDtypeStruct((ROWS, WIDE), BF),
            jax.ShapeDtypeStruct((ROWS, REST), BF),
            jax.ShapeDtypeStruct((ROWS, 640), BF),
            jax.ShapeDtypeStruct((8, 512), F32),
            jax.ShapeDtypeStruct((PAIR, D), BF),
        ),
        in_specs=[vmem, hbm] + [vmem] * (len(args) - 5) + [hbm] * 3,
        out_specs=(hbm,) * 4 + (vmem,) * 3,
        scratch_shapes=[
            pltpu.VMEM((T, 640), F32),
            pltpu.VMEM((T, 2 * D), BF),
            pltpu.VMEM((T, 640), BF),
            pltpu.VMEM((4, T, 512), BF),
            pltpu.VMEM((4 * T, 2 * D), BF),
            pltpu.VMEM((4 * T, 640), BF),
            pltpu.VMEM((4 * T, 512), BF),
            pltpu.VMEM((T, 512), BF),
            pltpu.VMEM((ROWS, REST), BF),
            pltpu.VMEM((ROWS, 640), BF),
            pltpu.VMEM((T, D), F32),
            pltpu.VMEM((8, 512), F32),
            pltpu.VMEM((6, 8, 512), F32),
            pltpu.VMEM((9, 8, 512), F32),
            pltpu.VMEM((2, HALF // 8, WIDE // 4), BF),
            pltpu.VMEM((2, HALF // 4, WIDE // 4), BF),
            pltpu.VMEM((2, HALF // 4, WIDE // 4), BF),
            pltpu.VMEM((2, HALF // 4, REST // 4), BF),
            pltpu.VMEM((3, 64, 640), BF),
            pltpu.VMEM((3, 16, 640), BF),
            pltpu.VMEM((16, 640), BF),
            pltpu.VMEM((64, 640), BF),
            pltpu.VMEM((16, 640), BF),
            pltpu.VMEM((ROWS, WIDE), BF),
            pltpu.VMEM((ROWS, WIDE), BF),
            pltpu.VMEM((HALF, WIDE), BF),
            pltpu.VMEM((HALF, WIDE), BF),
            pltpu.VMEM((4, 240, 960), BF),
            pltpu.VMEM((4, 320, 240), BF),
            pltpu.VMEM((4, 320, 240), BF),
            pltpu.SemaphoreType.DMA((6,)),
            pltpu.SemaphoreType.DMA((8,)),
        ]
        + key_scratch()
        + sum_scratch(WIDE, HALF // 2)
        + sum_scratch(WIDE, HALF)
        + sum_scratch(REST, HALF)
        + sum_scratch(WIDE, HALF)[4:]
        + sems(230),
        compiler_params=pltpu.CompilerParams(
            collective_id=2, has_side_effects=True, vmem_limit_bytes=VMEM_LIMIT
        ),
        cost_estimate=pl.CostEstimate(flops=2_000_000_000, bytes_accessed=200_000_000, transcendentals=0),
    )(*args)


def finish_kernel(
    g_gate_ref, g_up_ref, g_down_ref, two_ref, three_ref, vec_ref, out_rows_ref, d_rows_ref, place_ref, hidden_ref, d_out_ref,
    out_ref, d_hidden_ref, query_ref, key_ref, value_ref, output_ref, gate_ref, up_ref, down_ref, vec_a_ref, vec_f_ref, vec_r_ref,
    low_one, low_down, low_two, low_three, wide_one, wide_two, wide_down, wide_kv, rows, ranked, load_sems, store_sems,
):
    keep = pl.ds(0, 240)
    runs_one = [pl.ds(1280 * k, 1280) for k in range(2)]
    runs_down = [pl.ds(640 * k, 640) for k in range(4)]
    loads = []
    for src, dst, runs in (
        (g_gate_ref, low_one.at[0], runs_one),
        (g_up_ref, low_one.at[1], runs_one),
        (g_down_ref, low_down, runs_down),
        (two_ref, low_two, [pl.ds(0, 2 * D)]),
        (three_ref, low_three, [pl.ds(0, 640)]),
    ):
        for c in runs:
            loads.append(pltpu.make_async_copy(src.at[keep, c], dst.at[:, c], load_sems.at[len(loads)]))
            loads[-1].start()
    for k, (base, at_rank) in enumerate(((hidden_ref, out_rows_ref), (d_out_ref, d_rows_ref))):
        for src, dst in ((base, rows.at[k]), (at_rank, ranked.at[k])):
            loads.append(pltpu.make_async_copy(src, dst, load_sems.at[len(loads)]))
            loads[-1].start()
    stores = []

    def store(a, b):
        stores.append(pltpu.make_async_copy(a, b, store_sems.at[len(stores)]))
        stores[-1].start()

    for k in range(4):
        loads[k].wait()
        c = runs_one[k % 2]
        wide_one[k // 2, :, c] = low_one[k // 2, :, c].astype(F32)
        store(wide_one.at[k // 2, :, c], (gate_ref, up_ref)[k // 2].at[:, c])
    for k in range(4):
        loads[4 + k].wait()
        r = pl.ds(240 * k, 240)
        wide_down[r] = low_down[:, runs_down[k]].astype(F32)
        store(wide_down.at[r], down_ref.at[r])
    loads[8].wait()
    for k, to in enumerate((query_ref, output_ref)):
        wide_two[k] = low_two[:, D * k : D * (k + 1)].astype(F32)
        store(wide_two.at[k], to)
    loads[9].wait()
    for k, to in enumerate((key_ref, value_ref)):
        wide_kv[k] = low_three[:, 320 * k : 320 * (k + 1)].astype(F32).T
        store(wide_kv.at[k], to)
    for k, to in enumerate((out_ref, d_hidden_ref)):
        loads[10 + 2 * k].wait()
        loads[11 + 2 * k].wait()
        rows[k] = rows[k] + dot(ranked[k], place_ref[...], TN)
        store(rows.at[k], to)
    core, ylo = lax.axis_index("core") == 1, lax.axis_index("ylo") == 1
    for v, ref in enumerate((vec_a_ref, vec_f_ref, vec_r_ref)):
        p = [vec_ref[2 * v + k // 2 : 2 * v + k // 2 + 1, 240 * (k % 2) : 240 * (k % 2 + 1)] for k in range(4)]
        row = jnp.where(ylo, jnp.where(core, p[3], p[2]), jnp.where(core, p[1], p[0]))
        ref[...] = row.reshape(240)
    for copy in stores:
        copy.wait()


def finish(*args):
    vmem, hbm = pl.BlockSpec(memory_space=pltpu.VMEM), pl.BlockSpec(memory_space=pl.ANY)
    shapes = [(D, PAIR), (D, PAIR), (240, D), (320, 240), (320, 240), (240, D), (240, FF), (240, FF), (D, 640), (240,), (240,), (240,)]
    return pl.pallas_call(
        finish_kernel,
        name="finish",
        out_shape=tuple(jax.ShapeDtypeStruct(shape, F32) for shape in shapes),
        in_specs=[hbm] * 5 + [vmem] + [hbm] * 2 + [vmem] + [hbm] * 2,
        out_specs=(hbm,) * 9 + (vmem,) * 3,
        scratch_shapes=[
            pltpu.VMEM((2, 240, WIDE), BF),
            pltpu.VMEM((240, WIDE), BF),
            pltpu.VMEM((240, REST), BF),
            pltpu.VMEM((240, 640), BF),
            pltpu.VMEM((2, 240, WIDE), F32),
            pltpu.VMEM((2, 240, D), F32),
            pltpu.VMEM((D, 640), F32),
            pltpu.VMEM((2, 320, 240), F32),
            pltpu.VMEM((2, D, PAIR), F32),
            pltpu.VMEM((2, PAIR, D), BF),
            pltpu.SemaphoreType.DMA((14,)),
            pltpu.SemaphoreType.DMA((14,)),
        ],
        compiler_params=pltpu.CompilerParams(vmem_limit_bytes=VMEM_LIMIT),
        cost_estimate=pl.CostEstimate(flops=0, bytes_accessed=16_000_000, transcendentals=0),
    )(*args)


def shard_of(me, k):
    ylo, core = me[0], me[1]
    return (ylo if k < 2 else 1 - ylo) * 2 + (core if k % 2 == 0 else 1 - core)


def our_order(me, p):
    core, ylo = me[1] == 1, me[0] == 1
    p = [jnp.where(core, p[k ^ 1], p[k]) for k in range(4)]
    return [jnp.where(ylo, p[k ^ 2], p[k]) for k in range(4)]


def cut_four(ref):
    return [ref[:, 240 * k : 240 * (k + 1)] for k in range(4)]


def norm_back_rows(z, r, gain, dy):
    dz = r * (gain * dy) - z * (r * r * r) * jnp.mean(gain * dy * z, axis=-1, keepdims=True)
    return dz, jnp.sum(dy * z * r, axis=0, keepdims=True)


def everyone_steps(sends, pieces):
    half = T // 2
    arrived, last = [], []
    for kind, source, whole, relay in pieces:
        near = source if kind == "all" else source[1]
        last.append(sends.start(near, whole.at[pl.ds(T, T)], "core", 1))
    for step, at in ((1, 0), (-1, half)):
        r = pl.ds(at, half)
        for kind, source, whole, relay in pieces:
            far = source if kind == "all" else source[2]
            arrived.append((sends.start(far.at[r], whole.at[pl.ds(2 * T + at, half)], "y", step), None))
            if kind == "all":
                arrived[-1] = (arrived[-1][0], (whole.at[pl.ds(2 * T + at, half)], whole.at[pl.ds(3 * T + at, half)]))
            else:
                copy = sends.start(source[3].at[r], relay.at[r], "y", step)
                arrived.append((copy, (relay.at[r], whole.at[pl.ds(3 * T + at, half)])))
    yield
    for copy, onward in arrived:
        copy.wait_recv()
        if onward is not None:
            last.append(sends.start(onward[0], onward[1], "core", 1))
    yield
    for copy in last:
        copy.wait_recv()


def dense_kernel(
    mix_ref, q_ref, prob_in, kv_in, h_ref, up_ref, vec_ref,
    wo_ref, wg_ref, wu_ref, wd_ref, wos_ref, wgs_ref, wus_ref, wds_ref,
    dq_ref, dkv_out, g_out, sums_ref, d_attn_ref, mixture_ref, d_mid_ref, out_ref, logit_ref, vec_out_ref,
    wo, wg, wu, wd, mixf, gate_s, up_s, inner, dgu, dffn, xs, do_s, d_mix_s,
    dgu_all, dffn_all, xs_all, inner_all, xs_relay, inner_relay,
    prob_ref, kv_ref, dkv_ref, g_ref, g_down, low, out_b, full,
    load_sems, store_sems, send_sems, recv_sems,
):
    me = here()
    loads = []
    for k, (own, rest, to) in enumerate(
        ((wo_ref, wos_ref, wo), (wg_ref, wgs_ref, wg), (wu_ref, wus_ref, wu), (wd_ref, wds_ref, wd))
    ):
        there = to.at[pl.ds(1, 3)] if k < 3 else to.at[pl.ds(2, 1)]
        pair = (
            pltpu.make_async_copy(own, to.at[0], load_sems.at[2 * k]),
            pltpu.make_async_copy(rest, there, load_sems.at[2 * k + 1]),
        )
        for copy in pair:
            copy.start()
        loads.append(pair)
    loads.append(
        (
            pltpu.make_async_copy(prob_in, prob_ref, load_sems.at[8]),
            pltpu.make_async_copy(kv_in, kv_ref, load_sems.at[9]),
        )
    )
    for copy in loads[4]:
        copy.start()
    hail(me, NEAR[:4] + WEIGHT)
    sends = Sends(me, send_sems, recv_sems)
    shards = [shard_of(me, k) for k in range(4)]

    def run640(k):
        return pl.ds(pl.multiple_of(shards[k] * 640, 128), 640)

    def loaded(k):
        for copy in loads[k]:
            copy.wait()

    for j in range(KV_HEADS):
        for g in range(GROUPS):
            h = GROUPS * j + g
            mixf[:, HEAD_DIM * h : HEAD_DIM * (h + 1)] = mix_ref[j, g * T : (g + 1) * T, HEAD_DIM:]
    mixture_ref[...] = mixf[...].astype(BF)
    mix_k = our_order(me, cut_four(mixture_ref))
    loaded(0)
    attn_out = sum(dot(mix_k[k], wo[k]) for k in range(4))
    hidden = h_ref[...]
    gain_f = vec_ref[1:2, :D]
    route_w = vec_ref[2:3, :D]
    middle = hidden + attn_out
    r2 = lax.rsqrt(jnp.mean(middle * middle, axis=-1, keepdims=True) + EPS)
    x2 = middle * r2 * gain_f
    x2_k = our_order(me, [x2[:, 240 * k : 240 * (k + 1)].astype(BF) for k in range(4)])
    xs[...] = jnp.zeros_like(xs)
    for k in range(4):
        xs[k, :, :240] = x2_k[k]
    meet(NEAR[:4] + WEIGHT)
    down = [
        sends.start(wd_ref, wd.at[1], "core", 1),
        sends.start(wds_ref.at[0], wd.at[3], "core", 1),
    ]
    shares = [everyone_steps(sends, (("one", [xs.at[k] for k in range(4)], xs_all, xs_relay),))]
    next(shares[0])
    loaded(1)
    gate_s[...] = sum(dot(x2_k[k], wg[k]) for k in range(4))
    loaded(2)
    up_s[...] = sum(dot(x2_k[k], wu[k]) for k in range(4))
    gate = gate_s[...]
    inner[...] = (gate * jax.nn.sigmoid(gate) * up_s[...]).astype(BF)
    loaded(3)
    shares.append(
        everyone_steps(sends, (("one", [inner.at[:, run640(k)] for k in range(4)], inner_all, inner_relay),))
    )
    next(shares[1])
    for copy in down:
        copy.wait_recv()
    ffn_out = sum(dot(inner[:, run640(k)], wd[k], NT) for k in range(4))
    route = jax.nn.sigmoid(jnp.sum(hidden * route_w, axis=-1, keepdims=True))
    branch = attn_out + ffn_out
    odd = lax.rem(me[4], 2)
    keep = pl.ds(pl.multiple_of(odd * T, T), T)
    out_ref[keep] = (route * branch).astype(BF)
    swap = sends.start(out_ref.at[keep], out_ref.at[keep], "pair", 1)
    upstream = up_ref[...]
    d_branch = upstream * route
    d_logit = route * (1.0 - route) * jnp.sum(upstream * branch, axis=-1, keepdims=True)
    logit_ref[...] = jnp.broadcast_to(d_logit, logit_ref.shape)
    vec_out_ref[...] = jnp.zeros_like(vec_out_ref)
    vec_out_ref[2:3, :D] = jnp.sum(d_logit * hidden, axis=0, keepdims=True)
    d_ffn = d_branch.astype(BF)
    own = pl.ds(0, T)
    dffn[...] = jnp.zeros_like(dffn)
    for k in range(4):
        dffn[:, 256 * k : 256 * k + 240] = d_branch[:, 240 * k : 240 * (k + 1)].astype(BF)
    shares.append(everyone_steps(sends, (("all", dffn, dffn_all, None),)))
    next(shares[2])
    dffn_all[own], xs_all[own], inner_all[own] = dffn[...], xs[0], inner[:, run640(0)]
    late = []
    for p in range(2):
        first = 2 * lax.rem(me[0] + p, 2)
        for b in range(2):
            at = (2 * p + (me[1] if b == 0 else 1 - me[1])) * 640
            run, run_up = (pl.ds(pl.multiple_of(c + at, 128), 640) for c in (0, FF))
            d_inner = dot(d_ffn, wd[first + b])
            gate, up = gate_s[:, run], up_s[:, run]
            sg = jax.nn.sigmoid(gate)
            dgu[:, run] = (d_inner * up * (sg + gate * sg * (1.0 - sg))).astype(BF)
            dgu[:, run_up] = (d_inner * (gate * sg)).astype(BF)
        cols = [pl.ds(c + 1280 * p, 1280) for c in (0, FF)]
        late.append(everyone_steps(sends, tuple(("all", dgu.at[:, c], dgu_all.at[:, c], None) for c in cols)))
        next(late[-1])
    for share in shares:
        next(share)
    dgu_all[own] = dgu[...]
    d_gate, d_up = dgu[:, :FF], dgu[:, FF:]
    d_x2 = jnp.concatenate(
        our_order(me, [dot(d_gate, wg[k], NT) + dot(d_up, wu[k], NT) for k in range(4)]), axis=1
    )
    d_mid, g_gain_f = norm_back_rows(middle, r2, gain_f, d_x2)
    d_mid_ref[...] = d_mid
    vec_out_ref[1:2, :D] = g_gain_f
    d_attn = (d_branch + d_mid).astype(BF)
    d_attn_ref[...] = d_attn
    d_mix_s[...] = jnp.concatenate(our_order(me, [dot(d_attn, wo[k], NT) for k in range(4)]), axis=1)
    do_s[...] = jnp.zeros_like(do_s)
    for j in range(KV_HEADS):
        for g in range(GROUPS):
            h = GROUPS * j + g
            do_s[j, g * T : (g + 1) * T, HEAD_DIM:] = d_mix_s[:, HEAD_DIM * h : HEAD_DIM * (h + 1)].astype(BF)

    stores = []

    def store(a, b):
        stores.append(pltpu.make_async_copy(a, b, store_sems.at[len(stores)]))
        stores[-1].start()

    together(*shares)
    for k in range(4):
        c = pl.ds(640 * k, 640)
        g_down[:, c] = dot(dffn_all[:, 256 * k : 256 * (k + 1)], inner_all[...], TN).astype(BF)
    wide = wide_steps(me, sends, g_down, low, out_b, full, sums_ref)
    next(wide)
    loaded(4)
    for j in range(KV_HEADS):
        c = pl.ds(j * 128, 128)
        tile = kv_ref[:, :, :, :, c].reshape(KEYS, 128)
        prob, d_out = prob_ref[j], do_s[j]
        d_prob = dot(d_out, tile, NT)
        delta = jnp.sum(d_out.astype(F32) * mix_ref[j], axis=-1, keepdims=True)
        d_score = (prob.astype(F32) * (d_prob - delta)).astype(BF)
        dq_ref[j] = dot(d_score, tile) * SCALE
        grad = dot(
            jnp.concatenate([d_score, prob], axis=0), jnp.concatenate([q_ref[j], d_out], axis=0), TN
        )
        dkv_ref[:, :, :, :, c] = grad.astype(BF).reshape(2, 4, 4, T, 128)
        store(dkv_ref.at[:, :, :, :, c], dkv_out.at[:, :, :, :, c])
        if j == 3:
            next(wide)
            next(wide)
    together(*late)
    for at in range(0, 2 * FF, 1280):
        c = pl.ds(at, 1280)
        g_ref[:, c] = dot(xs_all[...], dgu_all[:, c], TN).astype(BF)
        store(g_ref.at[:, c], g_out.at[:, c])
    together(wide)
    swap.wait_recv()
    for copy in stores:
        copy.wait()
    sends.finish()


def dense(mix, q, prob, kv, h, up_c, vec, own, rest):
    vmem, hbm = pl.BlockSpec(memory_space=pltpu.VMEM), pl.BlockSpec(memory_space=pl.ANY)
    rows = GROUPS * T
    return pl.pallas_call(
        dense_kernel,
        name="dense",
        out_shape=(
            jax.ShapeDtypeStruct((KV_HEADS, rows, 128), F32),
            jax.ShapeDtypeStruct((2, 4, 4, T, 640), BF),
            jax.ShapeDtypeStruct((ROWS, 2 * FF), BF),
            jax.ShapeDtypeStruct((ROWS, FF // 4), BF),
            jax.ShapeDtypeStruct((T, D), BF),
            jax.ShapeDtypeStruct((T, D), BF),
            jax.ShapeDtypeStruct((T, D), F32),
            jax.ShapeDtypeStruct((PAIR, D), BF),
            jax.ShapeDtypeStruct((T, 128), F32),
            jax.ShapeDtypeStruct((8, 1024), F32),
        ),
        in_specs=[vmem] * 2 + [hbm] * 2 + [vmem] * 3 + [hbm] * 8,
        out_specs=(vmem,) + (hbm,) * 2 + (vmem,) * 7,
        scratch_shapes=[
            pltpu.VMEM((4, 240, D), BF),
            pltpu.VMEM((4, 240, FF), BF),
            pltpu.VMEM((4, 240, FF), BF),
            pltpu.VMEM((4, D, 640), BF),
            pltpu.VMEM((T, D), F32),
            pltpu.VMEM((T, FF), F32),
            pltpu.VMEM((T, FF), F32),
            pltpu.VMEM((T, FF), BF),
            pltpu.VMEM((T, 2 * FF), BF),
            pltpu.VMEM((T, 1024), BF),
            pltpu.VMEM((4, T, 256), BF),
            pltpu.VMEM((KV_HEADS, rows, 128), BF),
            pltpu.VMEM((T, D), F32),
            pltpu.VMEM((4 * T, 2 * FF), BF),
            pltpu.VMEM((4 * T, 1024), BF),
            pltpu.VMEM((4 * T, 256), BF),
            pltpu.VMEM((4 * T, 640), BF),
            pltpu.VMEM((T, 256), BF),
            pltpu.VMEM((T, 640), BF),
            pltpu.VMEM((KV_HEADS, rows, KEYS), BF),
            pltpu.VMEM((2, 4, 4, T, 640), BF),
            pltpu.VMEM((2, 4, 4, T, 640), BF),
            pltpu.VMEM((ROWS, 2 * FF), BF),
            pltpu.VMEM((ROWS, FF), BF),
            *sum_scratch(FF, HALF)[:3],
            pltpu.SemaphoreType.DMA((10,)),
            pltpu.SemaphoreType.DMA((13,)),
        ]
        + sems(57),
        compiler_params=pltpu.CompilerParams(
            collective_id=4, has_side_effects=True, vmem_limit_bytes=VMEM_LIMIT
        ),
        cost_estimate=pl.CostEstimate(
            flops=20_000_000_000, bytes_accessed=40_000_000, transcendentals=0
        ),
    )(mix, q, prob, kv, h, up_c, vec, *own, *rest)


def per_device(hidden, chosen, positions, w_query, w_key, w_value, w_output, w_gate, w_up, w_down, gain_attn, gain_ffn, router, d_out):
    tokens, upstream = hidden[0], d_out[0]
    own_w = (w_output, w_gate, w_up, w_down.T)
    frequency = (THETA ** (-np.arange(0, HEAD_DIM // 2) * 2.0 / HEAD_DIM)).astype(np.float32)
    (
        mix_heads, prob, q_heads, kv_all, h, up_c, x1, cosine, sine, place, vec_in, wq, wk, wv, *rest_w
    ) = front(
        tokens.T, upstream.T, chosen, positions, np.tile(frequency, 4)[None, :], gain_attn, gain_ffn, router,
        w_query, w_key.T, w_value.T, *own_w
    )
    d_q_heads, d_kv, g_one, sums_down, d_attn, mixture, d_mid, out_c, d_logit, vec_out = dense(
        mix_heads, q_heads, prob, kv_all, h, up_c, vec_in, own_w, rest_w
    )
    s_gate, s_up, s_down, s_two, s_three, vector, d_rows = back(
        d_kv, g_one, sums_down, d_q_heads, d_attn, mixture, x1, h, d_mid, d_logit, vec_in, vec_out, cosine, sine, wq, wk, wv
    )
    output, d_tokens, g_query, g_key, g_value, g_output, g_gate, g_up, g_down, *vectors = finish(
        s_gate, s_up, s_down, s_two, s_three, vector, out_c, d_rows, place, tokens.T, upstream.T
    )
    return (
        output.T[None],
        d_tokens.T[None],
        g_query,
        g_key.T,
        g_value.T,
        g_output,
        g_gate,
        g_up,
        g_down.T,
        vectors[0],
        vectors[1],
        vectors[2],
    )


def solution(mesh):
    finer = Mesh(mesh.devices.reshape(DIMS), AX)
    shard, blk = ("ylo", "core"), ("yhi", "z", "x")
    act, row, weight, vec = P(shard, blk, None), P(shard, blk), P(shard, None), P(shard)
    return jax.shard_map(
        per_device,
        mesh=finer,
        in_specs=(act, row, row) + (weight,) * 7 + (vec,) * 3 + (act,),
        out_specs=(act, act) + (weight,) * 7 + (vec,) * 3,
        check_vma=False,
    )
```

```python
import functools

import jax
import jax.numpy as jnp
import numpy as np
from jax import lax
from jax.experimental import pallas as pl
from jax.experimental.pallas import tpu as pltpu
from jax.sharding import Mesh
from jax.sharding import PartitionSpec as P

D = 960
HEADS = 15
KV_HEADS = 5
GROUPS = 3
HEAD_DIM = 64
FF = 2560
EPS = 1e-05
THETA = 10000.0
SCALE = HEAD_DIM ** (-0.5)
T = 64
PAIR = 128
SLOTS = 32
KEYS = SLOTS * T
AX = ("ylo", "core", "yhi", "z", "x")
DIMS = (2, 2, 2, 4, 4)
MESH = pl.DeviceIdType.MESH
BF = jnp.bfloat16
F32 = jnp.float32
VMEM_LIMIT = 56 * 2**20


def dot(a, b, dims=(((1,), (0,)), ((), ()))):
    return lax.dot_general(a, b, dims, preferred_element_type=F32)


NT = (((1,), (1,)), ((), ()))
TN = (((0,), (0,)), ((), ()))


def here():
    return tuple(lax.axis_index(a) for a in AX)


def neighbour(me, axis, step):
    ylo, core, yhi, z, x = me
    if axis == "z":
        z = lax.rem(z + step + 4, 4)
    elif axis == "x":
        x = lax.rem(x + step + 4, 4)
    elif axis == "pair":
        x = x + 1 - 2 * lax.rem(x, 2)
    elif axis == "yhi":
        yhi = 1 - yhi
    elif axis == "ylo":
        ylo = 1 - ylo
    elif axis == "core":
        core = 1 - core
    else:
        y = lax.rem(yhi * 2 + ylo + step + 4, 4)
        ylo, yhi = lax.rem(y, 2), y // 2
    return (ylo, core, yhi, z, x)


NEAR = (("x", 1), ("x", -1), ("z", 1), ("z", -1), ("yhi", 1))
WEIGHT = (("y", 1), ("y", -1), ("core", 1))
FAR = (("x", 2), ("z", 2))


def hail(me, partners):
    barrier = pltpu.get_barrier_semaphore()
    for axis, step in partners:
        pl.semaphore_signal(
            barrier, inc=1, device_id=neighbour(me, axis, step), device_id_type=MESH
        )


def meet(partners):
    pl.semaphore_wait(pltpu.get_barrier_semaphore(), len(partners))


class Sends:
    def __init__(self, me, send_sems, recv_sems):
        self.me, self.send_sems, self.recv_sems, self.all = me, send_sems, recv_sems, []

    def start(self, src, dst, axis, step):
        k = len(self.all)
        copy = pltpu.make_async_remote_copy(
            src_ref=src,
            dst_ref=dst,
            send_sem=self.send_sems.at[k],
            recv_sem=self.recv_sems.at[k],
            device_id=neighbour(self.me, axis, step),
            device_id_type=MESH,
        )
        copy.start()
        self.all.append(copy)
        return copy

    def finish(self):
        for copy in self.all:
            copy.wait_send()


def together(*steps):
    steps = list(steps)
    while steps:
        for step in list(steps):
            try:
                next(step)
            except StopIteration:
                steps.remove(step)


def run_lanes(lanes, order):
    for c in order:
        next(lanes[c], None)
    together(*lanes.values())


def sems(count):
    return [pltpu.SemaphoreType.DMA((count,)), pltpu.SemaphoreType.DMA((count,))]


def plus(*terms):
    total = terms[0].astype(F32)
    for term in terms[1:]:
        total = total + term.astype(F32)
    return total


class Shards:
    def __init__(self, sends):
        self.sends, self.arrived, self.last = sends, [], []
        self.color = lax.rem(sends.me[3] + sends.me[4], 2)

    def near(self, own, out):
        self.last.append(self.sends.start(own, out.at[out.shape[0] - 3], "core", 1))

    def far(self, own, out, cut):
        for step, row, rows in ((1, 0, cut), (-1, cut, own.shape[0] - cut)):
            r = pl.ds(row, rows)
            ref = out.at[out.shape[0] - 2, r]
            self.arrived.append((ref, out.at[out.shape[0] - 1, r], self.sends.start(own.at[r], ref, "y", step)))

    def relay(self):
        for ref, to, copy in self.arrived:
            copy.wait_recv()
            self.last.append(self.sends.start(ref, to, "core", 1))
        self.arrived = []

    def finish(self):
        self.relay()
        for copy in self.last:
            copy.wait_recv()
        self.last = []

    def half(self, own, out, block, cuts):
        rows, slots = own.shape[0], out.shape[0]
        sub = block // 2
        mine = self.color * (rows - block)
        relay = slots > 1
        other = slots - 2 if relay else 0

        def part(slot, start, count):
            return out.at[slot, pl.ds(pl.multiple_of(start, 16), count)]

        copies = []
        for step, off in ((1, 0), (-1, sub)):
            src = own.at[pl.ds(pl.multiple_of(mine + off, 16), sub)]
            copies.append(self.sends.start(src, part(other, mine + off, sub), "y", step))
        if relay:
            self.near(own, out)
        yield
        for copy in copies:
            copy.wait_recv()
        copies, off = [], 0
        for (axis, step), count in zip((("x", 1), ("x", -1), ("z", 1), ("z", -1)), cuts):
            ref = part(other, self.color * block + off, count)
            copies.append(self.sends.start(ref, ref, axis, step))
            off += count
        if relay:
            self.last.append(self.sends.start(part(other, mine, block), part(slots - 1, mine, block), "core", 1))
        yield
        for copy in copies:
            copy.wait_recv()
        rest = (1 - self.color) * block
        if relay:
            self.last.append(
                self.sends.start(part(other, rest, rows - block), part(slots - 1, rest, rows - block), "core", 1)
            )


def gather_steps(me, sends, kv_ref, out_ref):
    _, _, yh, z, x = me
    oy = 1 - yh
    half, quarter = T // 2, T // 4
    streams = (("x", "z", 0), ("z", "x", half))

    def slot(y, axis, step, rows, count):
        zz = lax.rem(z + step + 4, 4) if axis == "z" else z
        xx = lax.rem(x + step + 4, 4) if axis == "x" else x
        return out_ref.at[y, zz, xx, pl.ds(rows, count)]

    def line(y, axis, step, rows, count):
        if axis == "z":
            return out_ref.at[y, lax.rem(z + step + 4, 4), :, pl.ds(rows, count)]
        return out_ref.at[y, :, lax.rem(x + step + 4, 4), pl.ds(rows, count)]

    own = out_ref.at[yh, z, x]
    own[...] = kv_ref[...]
    first = sends.start(kv_ref, own, "yhi", 1)
    got = {}
    for y, tag in ((yh, 0), (oy, 1)):
        if tag:
            yield
            first.wait_recv()
        for axis, _, row in streams:
            src = slot(y, axis, 0, row, half)
            for step in (1, -1):
                got[tag, row, step] = sends.start(src, src, axis, step)
    far = {}
    for y, tag in ((yh, 0), (oy, 1)):
        yield
        for axis, _, row in streams:
            for step, off in ((1, 0), (-1, quarter)):
                got[tag, row, step].wait_recv()
                src = slot(y, axis, -step, row + off, quarter)
                far[tag, row, step] = sends.start(src, src, axis, step)
    wide = {}
    for y, tag in ((yh, 0), (oy, 1)):
        yield
        for _, axis, row in streams:
            for step in (1, -1):
                far[tag, row, step].wait_recv()
            src = line(y, axis, 0, row, half)
            for step in (1, -1):
                wide[tag, row, step] = sends.start(src, src, axis, step)
    last = []
    for y, tag in ((yh, 0), (oy, 1)):
        yield
        for _, axis, row in streams:
            for step, off in ((1, 0), (-1, quarter)):
                wide[tag, row, step].wait_recv()
                src = line(y, axis, -step, row + off, quarter)
                last.append(sends.start(src, src, axis, step))
    yield
    for copy in last:
        copy.wait_recv()


def swapped(x):
    lane = lax.broadcasted_iota(jnp.int32, x.shape, 1)
    return jnp.where(lane < HEAD_DIM // 2, pltpu.roll(x, 96, 1), pltpu.roll(x, 32, 1))


def front_kernel(
    hidden_ref, d_out_ref, chosen_ref, pos_ref, freq_ref, gain_a_ref, gain_f_ref, router_ref, wq_ref, wk_ref, wv_ref,
    wo_ref, wg_ref, wu_ref, wd_ref,
    mix_ref, prob_out, q_ref, kv_out, h_ref, up_ref, x1_ref, cos_ref, sin_ref, place_ref, vec_out_ref,
    wq_out, wk_out, wv_out, wos_ref, wgs_ref, wus_ref, wds_ref,
    compact_h, compact_d, compact_p, got_h, got_d, got_p, vecs, q_pre, kv_own,
    prob_ref, kv_ref, wq, wk, wv,
    load_sems, store_sems, send_sems, recv_sems,
):
    me = here()
    yhi, z, x = me[2:]
    loads = []
    for k, (own, to) in enumerate(((wq_ref, wq), (wk_ref, wk), (wv_ref, wv))):
        loads.append(pltpu.make_async_copy(own, to.at[0], load_sems.at[k]))
        loads[-1].start()
    hail(me, NEAR + WEIGHT)
    sends = Sends(me, send_sems, recv_sems)
    early, query, late = Shards(sends), Shards(sends), Shards(sends)
    odd = lax.rem(x, 2)
    give = pl.ds(pl.multiple_of((1 - odd) * T, T), T)
    keep = pl.ds(pl.multiple_of(odd * T, T), T)
    limit = ((yhi * 16 + z * 4 + x) // 2 + 1) * PAIR
    stores = []

    def store(a, b):
        stores.append(pltpu.make_async_copy(a, b, store_sems.at[len(stores)]))
        stores[-1].start()

    def main():
        flag = jnp.where(chosen_ref[...] > 0, 1.0, 0.0)
        token = lax.broadcasted_iota(jnp.int32, (PAIR, PAIR), 0)
        lane = lax.broadcasted_iota(jnp.int32, (PAIR, PAIR), 1)
        upto = jnp.where(token <= lane, 1.0, 0.0).astype(BF)
        count = dot(jnp.broadcast_to(flag, (16, PAIR)).astype(BF), upto)[0:1]
        total = jnp.sum(flag, axis=1, keepdims=True)
        rank = count - 1.0 + jnp.where(odd == 1, PAIR - total, 0.0)
        place = jnp.where(token.astype(F32) == rank, flag, 0.0)
        place_low = place.astype(BF)
        place_ref[...] = place_low
        compact_p[...] = jnp.broadcast_to(
            jnp.sum(place * pos_ref[...].astype(F32), axis=1, keepdims=True), (PAIR, PAIR)
        )
        compact_h[...] = dot(place_low, hidden_ref[...].astype(BF), NT).astype(BF)
        vecs[0] = jnp.zeros((8, 256), F32)
        for k, ref in enumerate((gain_a_ref, gain_f_ref, router_ref)):
            vecs[0, k : k + 1, :240] = ref[...].astype(F32).reshape(1, 240)
        meet(NEAR + WEIGHT)
        vec_far = sends.start(vecs.at[0], vecs.at[2], "y", 1)
        early.far(wk_ref, wk, 160)
        early.far(wv_ref, wv, 160)
        vec_near = sends.start(vecs.at[0], vecs.at[1], "core", 1)
        early.near(wk_ref, wk)
        early.near(wv_ref, wv)
        query.far(wq_ref, wq, 128)
        query.near(wq_ref, wq)
        swaps = [sends.start(c.at[give], g, "pair", 1) for c, g in ((compact_h, got_h), (compact_p, got_p))]
        yield
        compact_d[...] = dot(place_low, d_out_ref[...].astype(BF), NT).astype(BF)
        vec_far.wait_recv()
        vec_last = sends.start(vecs.at[2], vecs.at[3], "core", 1)
        early.relay()
        yield
        swaps[0].wait_recv()
        h = plus(compact_h[keep], got_h[...])
        h_ref[...] = h
        swaps.append(sends.start(compact_d.at[give], got_d, "pair", 1))
        swaps[1].wait_recv()
        angle = (compact_p[keep] + got_p[...]) * freq_ref[...]
        turn = lax.broadcasted_iota(jnp.int32, (T, PAIR), 1)
        cosine = jnp.where(turn < HEAD_DIM, jnp.cos(angle), 1.0)
        sine = jnp.sin(angle)
        sine = jnp.where(turn < HEAD_DIM // 2, -sine, jnp.where(turn < HEAD_DIM, sine, 0.0))
        cos_ref[...], sin_ref[...] = cosine, sine
        vec_near.wait_recv()
        vec_last.wait_recv()
        vec_out_ref[...] = jnp.zeros_like(vec_out_ref)
        for k, v in enumerate(our_order(me, [vecs[k, :, :240] for k in range(4)])):
            vec_out_ref[:, 240 * k : 240 * (k + 1)] = v
        r1 = lax.rsqrt(jnp.mean(h * h, axis=-1, keepdims=True) + EPS)
        x1_ref[...] = (h * r1 * vec_out_ref[0:1, :D]).astype(BF)
        x1_k = our_order(me, cut_four(x1_ref))
        for copy in loads:
            copy.wait()
        early.finish()
        k_pre = sum(dot(x1_k[k], wk[k], NT) for k in range(4))
        v_pre = sum(dot(x1_k[k], wv[k], NT) for k in range(4))
        for j in range(KV_HEADS):
            run = slice(HEAD_DIM * j, HEAD_DIM * (j + 1))
            tile = jnp.concatenate([k_pre[:, run], v_pre[:, run]], axis=1)
            kv_own[:, 128 * j : 128 * (j + 1)] = (tile * cosine + swapped(tile) * sine).astype(BF)
        gather = gather_steps(me, sends, kv_own, kv_ref)
        next(gather)
        yield
        next(gather)
        yield
        query.relay()
        yield
        query.finish()
        swaps[2].wait_recv()
        up_ref[...] = plus(compact_d[keep], got_d[...])
        q_pre[...] = sum(dot(x1_k[k], wq[k]) for k in range(4))
        zero = jnp.zeros((T, HEAD_DIM), F32)
        for j in range(KV_HEADS):
            for g in range(GROUPS):
                at = HEAD_DIM * (GROUPS * j + g)
                tile = jnp.concatenate([q_pre[:, at : at + HEAD_DIM], zero], axis=1)
                q_ref[j, g * T : (g + 1) * T] = ((tile * cosine + swapped(tile) * sine) * SCALE).astype(BF)
        yield
        yield from gather
        for a, b in ((kv_ref, kv_out), (wq, wq_out), (wk, wk_out), (wv, wv_out)):
            store(a, b)
        for j in range(KV_HEADS):
            tile = kv_ref[:, :, :, :, 128 * j : 128 * (j + 1)].reshape(KEYS, 128)
            scores = dot(q_ref[j], tile, NT)
            column = lax.broadcasted_iota(jnp.int32, scores.shape, 1)
            scores = jnp.where(column < limit, scores, -1e30)
            exponent = jnp.exp(scores - jnp.max(scores, axis=-1, keepdims=True))
            prob = (exponent * (1.0 / jnp.sum(exponent, axis=-1, keepdims=True))).astype(BF)
            prob_ref[j] = prob
            store(prob_ref.at[j], prob_out.at[j])
            mix_ref[j] = dot(prob, tile)
            yield

    small, large = (128, (32, 32, 32, 16)), (480, (128, 128, 112, 112))
    lanes = {
        "m": main(),
        "o": late.half(wo_ref, wos_ref, *small),
        "t": late.half(wg_ref, wgs_ref, *small),
        "u": late.half(wu_ref, wus_ref, *small),
        "d": late.half(wd_ref, wds_ref, *large),
    }
    run_lanes(lanes, "".join(FRONT_ORDER))
    late.finish()
    for copy in stores:
        copy.wait()
    sends.finish()


FRONT_ORDER = (
    "mmmotmmmmmomummdmotummtdmmumdm",
)


def front(hidden, d_out, chosen, pos, freq, gain_a, gain_f, router, w_query, w_key, w_value, *later):
    vmem, hbm = pl.BlockSpec(memory_space=pltpu.VMEM), pl.BlockSpec(memory_space=pl.ANY)
    rows = GROUPS * T
    return pl.pallas_call(
        front_kernel,
        name="front",
        out_shape=(
            jax.ShapeDtypeStruct((KV_HEADS, rows, 128), F32),
            jax.ShapeDtypeStruct((KV_HEADS, rows, KEYS), BF),
            jax.ShapeDtypeStruct((KV_HEADS, rows, 128), BF),
            jax.ShapeDtypeStruct((2, 4, 4, T, 640), BF),
            jax.ShapeDtypeStruct((T, D), F32),
            jax.ShapeDtypeStruct((T, D), F32),
            jax.ShapeDtypeStruct((T, D), BF),
            jax.ShapeDtypeStruct((T, 128), F32),
            jax.ShapeDtypeStruct((T, 128), F32),
            jax.ShapeDtypeStruct((PAIR, PAIR), BF),
            jax.ShapeDtypeStruct((8, 1024), F32),
            jax.ShapeDtypeStruct((4, 240, 960), BF),
            jax.ShapeDtypeStruct((4, 320, 240), BF),
            jax.ShapeDtypeStruct((4, 320, 240), BF),
        )
        + tuple(jax.ShapeDtypeStruct((3,) + w.shape, BF) for w in later[:3])
        + (jax.ShapeDtypeStruct((1,) + later[3].shape, BF),),
        in_specs=[vmem] * 8 + [hbm] * 7,
        out_specs=(vmem, hbm, vmem, hbm) + (vmem,) * 7 + (hbm,) * 7,
        scratch_shapes=[
            pltpu.VMEM((PAIR, D), BF),
            pltpu.VMEM((PAIR, D), BF),
            pltpu.VMEM((PAIR, PAIR), F32),
            pltpu.VMEM((T, D), BF),
            pltpu.VMEM((T, D), BF),
            pltpu.VMEM((T, PAIR), F32),
            pltpu.VMEM((4, 8, 256), F32),
            pltpu.VMEM((T, D), F32),
            pltpu.VMEM((T, 640), BF),
            pltpu.VMEM((KV_HEADS, rows, KEYS), BF),
            pltpu.VMEM((2, 4, 4, T, 640), BF),
            pltpu.VMEM((4, 240, 960), BF),
            pltpu.VMEM((4, 320, 240), BF),
            pltpu.VMEM((4, 320, 240), BF),
            pltpu.SemaphoreType.DMA((3,)),
            pltpu.SemaphoreType.DMA((9,)),
        ]
        + sems(90),
        compiler_params=pltpu.CompilerParams(
            collective_id=1, has_side_effects=True, vmem_limit_bytes=VMEM_LIMIT
        ),
        cost_estimate=pl.CostEstimate(flops=5_000_000_000, bytes_accessed=90_000_000, transcendentals=0),
    )(hidden, d_out, chosen, pos, freq, gain_a, gain_f, router, w_query, w_key, w_value, *later)


def key_steps(me, sends, part_ref, out_ref, low, out_b, full, sums, nlow, nout, nfull, mine, y_in):
    _, _, yh, z, x = me
    half, quarter = T // 2, T // 4
    streams = (("x", "z", 0), ("z", "x", half))

    def line(axis, step, row, count):
        if axis == "z":
            return part_ref.at[:, lax.rem(z + step + 4, 4), :, pl.ds(row, count)]
        return part_ref.at[:, :, lax.rem(x + step + 4, 4), pl.ds(row, count)]

    near = {}
    for s, (axis, _, row) in enumerate(streams):
        near[s, 1] = sends.start(line(axis, 2, row, quarter), low.at[s, 0], axis, 1)
        near[s, -1] = sends.start(line(axis, 2, row + quarter, quarter), low.at[s, 1], axis, -1)
    whole = {}
    for s, (axis, _, row) in enumerate(streams):
        yield
        for d, step in enumerate((1, -1)):
            near[s, step].wait_recv()
            lo, hi = (0, quarter) if step == 1 else (quarter, 0)
            out_b[s, d, :, :, pl.ds(lo, quarter)] = plus(
                line(axis, step, row + lo, quarter)[...], low[s, d]
            ).astype(BF)
            out_b[s, d, :, :, pl.ds(hi, quarter)] = line(axis, step, row + hi, quarter)[...]
            whole[s, step] = sends.start(out_b.at[s, d], full.at[s, d], axis, step)
    near = {}
    for s, (axis, other, row) in enumerate(streams):
        yield
        for step in (1, -1):
            whole[s, step].wait_recv()
        sums[s] = plus(line(axis, 0, row, half)[...], full[s, 0], full[s, 1]).astype(BF)
        far = lax.rem((z if other == "z" else x) + 2, 4)
        near[s, 1] = sends.start(sums.at[s, :, far, pl.ds(0, quarter)], nlow.at[s, 0], other, 1)
        near[s, -1] = sends.start(
            sums.at[s, :, far, pl.ds(quarter, quarter)], nlow.at[s, 1], other, -1
        )
    for s, (axis, other, row) in enumerate(streams):
        yield
        at = z if other == "z" else x
        for d, step in enumerate((1, -1)):
            near[s, step].wait_recv()
            to = lax.rem(at + step + 4, 4)
            lo, hi = (0, quarter) if step == 1 else (quarter, 0)
            nout[s, d, :, pl.ds(lo, quarter)] = plus(
                sums[s, :, to, pl.ds(lo, quarter)], nlow[s, d]
            ).astype(BF)
            nout[s, d, :, pl.ds(hi, quarter)] = sums[s, :, to, pl.ds(hi, quarter)]
            whole[s, step] = sends.start(nout.at[s, d], nfull.at[s, d], other, step)
    swap = {}
    for s, (axis, other, row) in enumerate(streams):
        yield
        at = z if other == "z" else x
        for step in (1, -1):
            whole[s, step].wait_recv()
        mine[s] = plus(sums[s, :, at], nfull[s, 0], nfull[s, 1]).astype(BF)
        swap[s] = sends.start(mine.at[s, 1 - yh], y_in.at[s], "yhi", 1)
    yield
    for s, (axis, other, row) in enumerate(streams):
        swap[s].wait_recv()
        out_ref[pl.ds(row, half)] = plus(mine[s, yh], y_in[s])


def key_scratch():
    half, quarter, w = T // 2, T // 4, 640
    return [
        pltpu.VMEM((2, 2, 2, 4, quarter, w), BF),
        pltpu.VMEM((2, 2, 2, 4, half, w), BF),
        pltpu.VMEM((2, 2, 2, 4, half, w), BF),
        pltpu.VMEM((2, 2, 4, half, w), BF),
        pltpu.VMEM((2, 2, 2, quarter, w), BF),
        pltpu.VMEM((2, 2, 2, half, w), BF),
        pltpu.VMEM((2, 2, 2, half, w), BF),
        pltpu.VMEM((2, 2, half, w), BF),
        pltpu.VMEM((2, half, w), BF),
    ]


ROWS = 256
HALF = ROWS // 2
STREAMS = (("x", "z"), ("z", "x"))


def spots(me):
    return {"z": me[3], "x": me[4]}


def around(me, axis, step):
    return lax.rem(spots(me)[axis] + step + 4, 4)


def columns(me, axis, step, big):
    return pl.ds(pl.multiple_of(around(me, axis, step) * big, 128), big)


def halves(big):
    cut = (big // 2 + 127) // 128 * 128
    return (0, cut), (cut, big - cut)


def wide_steps(me, sends, g_ref, low, out_b, full, sums):
    h, big = sums.shape[0] // 2, sums.shape[1]
    cut = h // 2
    near, whole = {}, {}

    def parts(step):
        return (0, cut) if step == 1 else (cut, 0)

    for s, (axis, _) in enumerate(STREAMS):
        c = columns(me, axis, 2, big)
        for step in (1, -1):
            r = pl.ds(s * h + parts(step)[0], cut)
            near[s, step] = sends.start(g_ref.at[r, c], low.at[r], axis, step)
    for s, (axis, _) in enumerate(STREAMS):
        yield
        for d, step in enumerate((1, -1)):
            near[s, step].wait_recv()
            add, keep = (pl.ds(s * h + p, cut) for p in parts(step))
            c = columns(me, axis, step, big)
            out_b[d, add] = plus(g_ref[add, c], low[add]).astype(BF)
            out_b[d, keep] = g_ref[keep, c]
            r = pl.ds(s * h, h)
            whole[s, step] = sends.start(out_b.at[d, r], full.at[d, r], axis, step)

    for s, (axis, _) in enumerate(STREAMS):
        yield
        for step in (1, -1):
            whole[s, step].wait_recv()
        r = pl.ds(s * h, h)
        sums[r] = plus(g_ref[r, columns(me, axis, 0, big)], full[0, r], full[1, r]).astype(BF)


def narrow_steps(me, sends, sums, mine, swap_y, nlow, nout, nfull, y_in):
    run, big = mine.shape[-2:]
    h = 4 * run
    near, whole = {}, {}

    def rows(s, other, step):
        return pl.ds(pl.multiple_of(s * h + around(me, other, step) * run, 16), run)

    for s, (axis, other) in enumerate(STREAMS):
        for d, step in enumerate((1, -1)):
            c = pl.ds(*halves(big)[d])
            near[s, step] = sends.start(sums.at[rows(s, other, 2), c], nlow.at[s, :, c], other, step)
    for s, (axis, other) in enumerate(STREAMS):
        yield
        for d, step in enumerate((1, -1)):
            near[s, step].wait_recv()
            add, keep = pl.ds(*halves(big)[d]), pl.ds(*halves(big)[1 - d])
            r = rows(s, other, step)
            nout[s, d, :, add] = plus(sums[r, add], nlow[s, :, add]).astype(BF)
            nout[s, d, :, keep] = sums[r, keep]
            whole[s, step] = sends.start(nout.at[s, d], nfull.at[s, d], other, step)
    swap = {}
    for s, (axis, other) in enumerate(STREAMS):
        yield
        for step in (1, -1):
            whole[s, step].wait_recv()
        total = plus(sums[rows(s, other, 0)], nfull[s, 0], nfull[s, 1]).astype(BF)
        if swap_y:
            y_in[0, s] = total
            swap[s] = sends.start(y_in.at[0, s], y_in.at[1, s], "yhi", 1)
        else:
            mine[s] = total
    if swap_y:
        for s in range(2):
            yield
            swap[s].wait_recv()
            mine[s] = plus(y_in[0, s], y_in[1, s]).astype(BF)


def sum_steps(me, sends, g_ref, mine, swap_y, low, out_b, full, sums, *narrow):
    yield from wide_steps(me, sends, g_ref, low, out_b, full, sums)
    yield from narrow_steps(me, sends, sums, mine, swap_y, *narrow)


def sum_scratch(width, h):
    big, run = width // 4, h // 4
    return [
        pltpu.VMEM((2 * h, big), BF),
        pltpu.VMEM((2, 2 * h, big), BF),
        pltpu.VMEM((2, 2 * h, big), BF),
        pltpu.VMEM((2 * h, big), BF),
        pltpu.VMEM((2, run, big), BF),
        pltpu.VMEM((2, 2, run, big), BF),
        pltpu.VMEM((2, 2, run, big), BF),
        pltpu.VMEM((2, 2, run, big), BF),
    ]


def spread_steps(me, sends, mine, out_ref, store_sems, to_y):
    run, big = mine.shape[-2:]
    h = 4 * run
    cut = h // 2
    near, whole, stored, last, over = {}, {}, [], {}, []

    def base(s):
        return s * HALF + (me[2] * h if to_y else 0)

    def rows(s, off, count):
        return pl.ds(pl.multiple_of(base(s) + off, 16), count)

    def block(s, axis, step, off, count):
        return out_ref.at[rows(s, off, count), columns(me, axis, step, big)]

    def on(ref):
        if to_y:
            over.append(sends.start(ref, ref, "yhi", 1))

    for s, (axis, other) in enumerate(STREAMS):
        ref = block(s, axis, 0, around(me, other, 0) * run, run)
        for step in (1, -1):
            near[s, step] = sends.start(mine.at[s], ref, other, step)
        stored.append(pltpu.make_async_copy(mine.at[s], ref, store_sems.at[s]))
        stored[-1].start()

    def narrow(s, axis, other, step, d):
        c0, n = halves(big)[d]
        c = pl.ds(pl.multiple_of(around(me, axis, 0) * big + c0, 128), n)
        return out_ref.at[rows(s, around(me, other, step) * run, run), c]

    for s, (axis, other) in enumerate(STREAMS):
        yield
        for d, step in enumerate((1, -1)):
            near[s, step].wait_recv()
            ref = narrow(s, axis, other, -step, d)
            whole[s, step] = sends.start(ref, ref, other, step)
    for s, (axis, other) in enumerate(STREAMS):
        yield
        for step in (1, -1):
            whole[s, step].wait_recv()
        stored[s].wait()
        ref = block(s, axis, 0, 0, h)
        for step in (1, -1):
            near[s, step] = sends.start(ref, ref, axis, step)
        on(ref)
    for s, (axis, other) in enumerate(STREAMS):
        yield
        for d, step in enumerate((1, -1)):
            near[s, step].wait_recv()
            ref = block(s, axis, -step, d * cut, cut)
            last[s, step] = sends.start(ref, ref, axis, step)
            on(block(s, axis, -step, 0, h))
    for s, (axis, other) in enumerate(STREAMS):
        yield
        for step in (1, -1):
            last[s, step].wait_recv()
        on(block(s, axis, 2, 0, h))
    if to_y:
        yield
        for copy in over:
            copy.wait_recv()


def halved_steps(me, sends, g_ref, mine, kept, got, out_ref, store_sems, *scratch):
    h = HALF // 2
    yh = me[2]
    copies = []
    for s in range(2):
        give = pl.ds(pl.multiple_of(s * HALF + (1 - yh) * h, 16), h)
        copies.append(sends.start(g_ref.at[give], got.at[pl.ds(s * h, h)], "yhi", 1))
    for s in range(2):
        yield
        copies[s].wait_recv()
        r = pl.ds(s * h, h)
        kept[r] = plus(g_ref[pl.ds(pl.multiple_of(s * HALF + yh * h, 16), h)], got[r]).astype(BF)
    yield
    yield from sum_steps(me, sends, kept, mine, False, *scratch)
    yield from spread_steps(me, sends, mine, out_ref, store_sems, True)


def vector_steps(sends, vec_ref, out_ref, keep, got):
    rounds = ((("core", 1),), (("ylo", 1),), (("x", 1), ("x", -1), ("x", 2)), (("z", 1), ("z", -1), ("z", 2)), (("yhi", 1),))
    keep[0] = vec_ref[...]
    k = 0
    for at, partners in enumerate(rounds):
        copies = []
        for axis, step in partners:
            copies.append((k, sends.start(keep.at[at], got.at[k], axis, step)))
            k += 1
        yield
        total = keep[at]
        for slot, copy in copies:
            copy.wait_recv()
            total = total + got[slot]
        keep[at + 1] = total
    out_ref[...] = keep[len(rounds)]


def small_steps(me, sends, g_ref, out_ref, got_x, got_z, got_y, sum_z, sum_y):
    x, z = me[3], me[4]
    steps = (1, -1, 2)

    def rows(at, step, count, base=0):
        return pl.ds(pl.multiple_of(base + lax.rem(at + step + 4, 4) * count, 16), count)

    copies = [
        sends.start(g_ref.at[rows(x, step, 64)], got_x.at[k], "z", step) for k, step in enumerate(steps)
    ]
    yield
    for copy in copies:
        copy.wait_recv()
    sum_z[...] = plus(g_ref[rows(x, 0, 64)], got_x[0], got_x[1], got_x[2]).astype(BF)
    copies = [
        sends.start(sum_z.at[rows(z, step, 16)], got_z.at[k], "x", step) for k, step in enumerate(steps)
    ]
    yield
    for copy in copies:
        copy.wait_recv()
    sum_y[...] = plus(sum_z[rows(z, 0, 16)], got_z[0], got_z[1], got_z[2]).astype(BF)
    copy = sends.start(sum_y, got_y, "yhi", 1)
    yield
    copy.wait_recv()
    ref = out_ref.at[rows(z, 0, 16, x * 64)]
    ref[...] = plus(sum_y[...], got_y[...]).astype(BF)
    copies = [sends.start(ref, ref, "x", step) for step in steps]
    yield
    for copy in copies:
        copy.wait_recv()
    ref = out_ref.at[rows(x, 0, 64)]
    copies = [sends.start(ref, ref, "z", step) for step in steps]
    yield
    for copy in copies:
        copy.wait_recv()


KEY_N, SUM_N = 9, 8
WIDE, REST = FF, 2048


def back_kernel(
    part_ref, g_in, sums_ref, dq_ref, d_attn_ref, mixture_ref, x1_ref, h_ref, d_mid_ref, logit_ref, vec_ref, vec_part_ref,
    cos_ref, sin_ref, wq_in, wk_in, wv_in,
    gate_ref, up_ref, down_ref, two_ref, three_ref, vec_out_ref, both_ref,
    own, ra, rb, xs, ra_all, rb_all, xs_all, xs_relay, g_two, g_three, d_x1_s, vec_all, keep_v, got_v,
    mine_gate, mine_up, mine_down, mine_two, got_x, got_z, got_y, sum_z, sum_y,
    g_gate, g_up, kept, got_gate, wq, wk, wv, load_sems, store_sems,
    *scratch,
):
    me = here()
    key_scr, rest = scratch[:KEY_N], scratch[KEY_N:-2]
    gate_scr, up_scr, two_scr, down_scr = (rest[SUM_N * k : SUM_N * (k + 1)] for k in range(4))
    loads = [
        pltpu.make_async_copy(a, b, load_sems.at[k])
        for k, (a, b) in enumerate(
            (
                (g_in.at[:, pl.ds(0, WIDE)], g_gate),
                (g_in.at[:, pl.ds(WIDE, WIDE)], g_up),
                (wq_in, wq),
                (wk_in, wk),
                (wv_in, wv),
            )
        )
    ]
    for copy in loads:
        copy.start()
    hail(me, NEAR + WEIGHT + FAR)
    sends = Sends(me, *scratch[-2:])
    odd = lax.rem(me[4], 2)
    keep = pl.ds(pl.multiple_of(odd * T, T), T)
    cosine, sine = cos_ref[...], sin_ref[...]
    mine = pl.ds(0, T)

    def turned_back(tile):
        return tile * cosine - swapped(tile) * sine

    for j in range(KV_HEADS):
        for g in range(GROUPS):
            at = HEAD_DIM * (GROUPS * j + g)
            ra[:, at : at + HEAD_DIM] = turned_back(dq_ref[j, g * T : (g + 1) * T]).astype(BF)[:, :HEAD_DIM]
    ra[:, D:] = d_attn_ref[...]
    xs[...] = jnp.zeros_like(xs)
    for k, (a, b) in enumerate(zip(our_order(me, cut_four(x1_ref)), our_order(me, cut_four(mixture_ref)))):
        xs[k, :, :240] = a
        xs[k, :, 256:496] = b
    meet(NEAR + WEIGHT + FAR)

    def keys():
        yield from key_steps(me, sends, part_ref, own, *key_scr)
        for j in range(KV_HEADS):
            tile = turned_back(own[:, 128 * j : 128 * (j + 1)]).astype(BF)
            rb[:, HEAD_DIM * j : HEAD_DIM * (j + 1)] = tile[:, :HEAD_DIM]
            rb[:, 320 + HEAD_DIM * j : 320 + HEAD_DIM * (j + 1)] = tile[:, HEAD_DIM:]
        share = everyone_steps(sends, (("all", rb, rb_all, None),))
        next(share)
        rb_all[mine] = rb[...]
        d_k, d_v = rb[:, :320], rb[:, 320:]
        d_x1 = d_x1_s[...] + jnp.concatenate(
            our_order(me, [dot(d_k, wk[k]) + dot(d_v, wv[k]) for k in range(4)]), axis=1
        )
        h = h_ref[...]
        r1 = lax.rsqrt(jnp.mean(h * h, axis=-1, keepdims=True) + EPS)
        d_first, g_gain_a = norm_back_rows(h, r1, vec_ref[0:1, :D], d_x1)
        d_h = d_mid_ref[...] + d_first + logit_ref[:, 0:1] * vec_ref[2:3, :D]
        both_ref[keep] = d_h.astype(BF)
        swap = sends.start(both_ref.at[keep], both_ref.at[keep], "pair", 1)
        vec_all[...] = jnp.zeros_like(vec_all)
        for k, row in enumerate((g_gain_a, vec_part_ref[1:2, :D], vec_part_ref[2:3, :D])):
            for i in range(2):
                vec_all[2 * k + i : 2 * k + i + 1, :480] = row[:, 480 * i : 480 * (i + 1)]
        vectors = vector_steps(sends, vec_all, vec_out_ref, keep_v, got_v)
        next(vectors)
        yield
        next(share)
        yield
        together(share)
        g_three[...] = dot(xs_all[:, :256], rb_all[...], TN).astype(BF)
        small = small_steps(me, sends, g_three, three_ref, got_x, got_z, got_y, sum_z, sum_y)
        while True:
            for step in (small, vectors):
                next(step, None)
            if small.gi_frame is None and vectors.gi_frame is None:
                break
            yield
        swap.wait_recv()

    def queries():
        share = everyone_steps(
            sends, (("all", ra, ra_all, None), ("one", [xs.at[k] for k in range(4)], xs_all, xs_relay))
        )
        next(share)
        ra_all[mine] = ra[...]
        xs_all[mine] = xs[0]
        d_q = ra[:, :D]
        for copy in loads[2:]:
            copy.wait()
        d_x1_s[...] = jnp.concatenate(our_order(me, [dot(d_q, wq[k], NT) for k in range(4)]), axis=1)
        g_two[:, 2 * D :] = jnp.zeros((ROWS, 128), BF)
        yield
        next(share)
        yield
        together(share)
        g_two[:, :D] = dot(xs_all[:, :256], ra_all[:, :D], TN).astype(BF)
        g_two[:, D : 2 * D] = dot(xs_all[:, 256:], ra_all[:, D:], TN).astype(BF)
        yield from sum_steps(me, sends, g_two, mine_two, True, *two_scr)
        yield from spread_steps(me, sends, mine_two, two_ref, store_sems.at[pl.ds(6, 2)], False)

    def gate():
        loads[0].wait()
        yield from halved_steps(
            me, sends, g_gate, mine_gate, kept, got_gate, gate_ref, store_sems.at[pl.ds(0, 2)], *gate_scr
        )

    def up():
        loads[1].wait()
        yield from sum_steps(me, sends, g_up, mine_up, True, *up_scr)
        yield from spread_steps(me, sends, mine_up, up_ref, store_sems.at[pl.ds(2, 2)], False)

    def down():
        yield from narrow_steps(me, sends, sums_ref, mine_down, True, *down_scr)
        yield from spread_steps(me, sends, mine_down, down_ref, store_sems.at[pl.ds(4, 2)], False)

    run_lanes({"k": keys(), "g": gate(), "u": up(), "d": down(), "q": queries()}, "".join(ORDER))
    sends.finish()


ORDER = (
    "kgdukkquugkkgddguukkqdqgdukgkdqudqggkqdk",
    "qgkguqgdqugddqqgukguqqgugdudqqkuguqqdkuu",
    "gdgkuuqgqgqqk",
)


def back(*args):
    vmem, hbm = pl.BlockSpec(memory_space=pltpu.VMEM), pl.BlockSpec(memory_space=pl.ANY)
    return pl.pallas_call(
        back_kernel,
        name="back",
        out_shape=(
            jax.ShapeDtypeStruct((ROWS, WIDE), BF),
            jax.ShapeDtypeStruct((ROWS, WIDE), BF),
            jax.ShapeDtypeStruct((ROWS, WIDE), BF),
            jax.ShapeDtypeStruct((ROWS, REST), BF),
            jax.ShapeDtypeStruct((ROWS, 640), BF),
            jax.ShapeDtypeStruct((8, 512), F32),
            jax.ShapeDtypeStruct((PAIR, D), BF),
        ),
        in_specs=[vmem, hbm] + [vmem] * (len(args) - 5) + [hbm] * 3,
        out_specs=(hbm,) * 4 + (vmem,) * 3,
        scratch_shapes=[
            pltpu.VMEM((T, 640), F32),
            pltpu.VMEM((T, 2 * D), BF),
            pltpu.VMEM((T, 640), BF),
            pltpu.VMEM((4, T, 512), BF),
            pltpu.VMEM((4 * T, 2 * D), BF),
            pltpu.VMEM((4 * T, 640), BF),
            pltpu.VMEM((4 * T, 512), BF),
            pltpu.VMEM((T, 512), BF),
            pltpu.VMEM((ROWS, REST), BF),
            pltpu.VMEM((ROWS, 640), BF),
            pltpu.VMEM((T, D), F32),
            pltpu.VMEM((8, 512), F32),
            pltpu.VMEM((6, 8, 512), F32),
            pltpu.VMEM((9, 8, 512), F32),
            pltpu.VMEM((2, HALF // 8, WIDE // 4), BF),
            pltpu.VMEM((2, HALF // 4, WIDE // 4), BF),
            pltpu.VMEM((2, HALF // 4, WIDE // 4), BF),
            pltpu.VMEM((2, HALF // 4, REST // 4), BF),
            pltpu.VMEM((3, 64, 640), BF),
            pltpu.VMEM((3, 16, 640), BF),
            pltpu.VMEM((16, 640), BF),
            pltpu.VMEM((64, 640), BF),
            pltpu.VMEM((16, 640), BF),
            pltpu.VMEM((ROWS, WIDE), BF),
            pltpu.VMEM((ROWS, WIDE), BF),
            pltpu.VMEM((HALF, WIDE), BF),
            pltpu.VMEM((HALF, WIDE), BF),
            pltpu.VMEM((4, 240, 960), BF),
            pltpu.VMEM((4, 320, 240), BF),
            pltpu.VMEM((4, 320, 240), BF),
            pltpu.SemaphoreType.DMA((6,)),
            pltpu.SemaphoreType.DMA((8,)),
        ]
        + key_scratch()
        + sum_scratch(WIDE, HALF // 2)
        + sum_scratch(WIDE, HALF)
        + sum_scratch(REST, HALF)
        + sum_scratch(WIDE, HALF)[4:]
        + sems(230),
        compiler_params=pltpu.CompilerParams(
            collective_id=2, has_side_effects=True, vmem_limit_bytes=VMEM_LIMIT
        ),
        cost_estimate=pl.CostEstimate(flops=2_000_000_000, bytes_accessed=200_000_000, transcendentals=0),
    )(*args)


def finish_kernel(
    g_gate_ref, g_up_ref, g_down_ref, two_ref, three_ref, vec_ref, out_rows_ref, d_rows_ref, place_ref, hidden_ref, d_out_ref,
    out_ref, d_hidden_ref, query_ref, key_ref, value_ref, output_ref, gate_ref, up_ref, down_ref, vec_a_ref, vec_f_ref, vec_r_ref,
    low_one, low_down, low_two, low_three, wide_one, wide_two, wide_down, wide_kv, rows, ranked, load_sems, store_sems,
):
    keep = pl.ds(0, 240)
    runs_one = [pl.ds(1280 * k, 1280) for k in range(2)]
    runs_down = [pl.ds(640 * k, 640) for k in range(4)]
    loads = []
    for src, dst, runs in (
        (g_gate_ref, low_one.at[0], runs_one),
        (g_up_ref, low_one.at[1], runs_one),
        (g_down_ref, low_down, runs_down),
        (two_ref, low_two, [pl.ds(0, 2 * D)]),
        (three_ref, low_three, [pl.ds(0, 640)]),
    ):
        for c in runs:
            loads.append(pltpu.make_async_copy(src.at[keep, c], dst.at[:, c], load_sems.at[len(loads)]))
            loads[-1].start()
    for k, (base, at_rank) in enumerate(((hidden_ref, out_rows_ref), (d_out_ref, d_rows_ref))):
        for src, dst in ((base, rows.at[k]), (at_rank, ranked.at[k])):
            loads.append(pltpu.make_async_copy(src, dst, load_sems.at[len(loads)]))
            loads[-1].start()
    stores = []

    def store(a, b):
        stores.append(pltpu.make_async_copy(a, b, store_sems.at[len(stores)]))
        stores[-1].start()

    for k in range(4):
        loads[k].wait()
        c = runs_one[k % 2]
        wide_one[k // 2, :, c] = low_one[k // 2, :, c].astype(F32)
        store(wide_one.at[k // 2, :, c], (gate_ref, up_ref)[k // 2].at[:, c])
    for k in range(4):
        loads[4 + k].wait()
        r = pl.ds(240 * k, 240)
        wide_down[r] = low_down[:, runs_down[k]].astype(F32)
        store(wide_down.at[r], down_ref.at[r])
    loads[8].wait()
    for k, to in enumerate((query_ref, output_ref)):
        wide_two[k] = low_two[:, D * k : D * (k + 1)].astype(F32)
        store(wide_two.at[k], to)
    loads[9].wait()
    for k, to in enumerate((key_ref, value_ref)):
        wide_kv[k] = low_three[:, 320 * k : 320 * (k + 1)].astype(F32).T
        store(wide_kv.at[k], to)
    for k, to in enumerate((out_ref, d_hidden_ref)):
        loads[10 + 2 * k].wait()
        loads[11 + 2 * k].wait()
        rows[k] = rows[k] + dot(ranked[k], place_ref[...], TN)
        store(rows.at[k], to)
    core, ylo = lax.axis_index("core") == 1, lax.axis_index("ylo") == 1
    for v, ref in enumerate((vec_a_ref, vec_f_ref, vec_r_ref)):
        p = [vec_ref[2 * v + k // 2 : 2 * v + k // 2 + 1, 240 * (k % 2) : 240 * (k % 2 + 1)] for k in range(4)]
        row = jnp.where(ylo, jnp.where(core, p[3], p[2]), jnp.where(core, p[1], p[0]))
        ref[...] = row.reshape(240)
    for copy in stores:
        copy.wait()


def finish(*args):
    vmem, hbm = pl.BlockSpec(memory_space=pltpu.VMEM), pl.BlockSpec(memory_space=pl.ANY)
    shapes = [(D, PAIR), (D, PAIR), (240, D), (320, 240), (320, 240), (240, D), (240, FF), (240, FF), (D, 640), (240,), (240,), (240,)]
    return pl.pallas_call(
        finish_kernel,
        name="finish",
        out_shape=tuple(jax.ShapeDtypeStruct(shape, F32) for shape in shapes),
        in_specs=[hbm] * 5 + [vmem] + [hbm] * 2 + [vmem] + [hbm] * 2,
        out_specs=(hbm,) * 9 + (vmem,) * 3,
        scratch_shapes=[
            pltpu.VMEM((2, 240, WIDE), BF),
            pltpu.VMEM((240, WIDE), BF),
            pltpu.VMEM((240, REST), BF),
            pltpu.VMEM((240, 640), BF),
            pltpu.VMEM((2, 240, WIDE), F32),
            pltpu.VMEM((2, 240, D), F32),
            pltpu.VMEM((D, 640), F32),
            pltpu.VMEM((2, 320, 240), F32),
            pltpu.VMEM((2, D, PAIR), F32),
            pltpu.VMEM((2, PAIR, D), BF),
            pltpu.SemaphoreType.DMA((14,)),
            pltpu.SemaphoreType.DMA((14,)),
        ],
        compiler_params=pltpu.CompilerParams(vmem_limit_bytes=VMEM_LIMIT),
        cost_estimate=pl.CostEstimate(flops=0, bytes_accessed=16_000_000, transcendentals=0),
    )(*args)


def shard_of(me, k):
    ylo, core = me[0], me[1]
    return (ylo if k < 2 else 1 - ylo) * 2 + (core if k % 2 == 0 else 1 - core)


def our_order(me, p):
    core, ylo = me[1] == 1, me[0] == 1
    p = [jnp.where(core, p[k ^ 1], p[k]) for k in range(4)]
    return [jnp.where(ylo, p[k ^ 2], p[k]) for k in range(4)]


def cut_four(ref):
    return [ref[:, 240 * k : 240 * (k + 1)] for k in range(4)]


def norm_back_rows(z, r, gain, dy):
    dz = r * (gain * dy) - z * (r * r * r) * jnp.mean(gain * dy * z, axis=-1, keepdims=True)
    return dz, jnp.sum(dy * z * r, axis=0, keepdims=True)


def everyone_steps(sends, pieces):
    half = T // 2
    arrived, last = [], []
    for kind, source, whole, relay in pieces:
        near = source if kind == "all" else source[1]
        last.append(sends.start(near, whole.at[pl.ds(T, T)], "core", 1))
    for step, at in ((1, 0), (-1, half)):
        r = pl.ds(at, half)
        for kind, source, whole, relay in pieces:
            far = source if kind == "all" else source[2]
            arrived.append((sends.start(far.at[r], whole.at[pl.ds(2 * T + at, half)], "y", step), None))
            if kind == "all":
                arrived[-1] = (arrived[-1][0], (whole.at[pl.ds(2 * T + at, half)], whole.at[pl.ds(3 * T + at, half)]))
            else:
                copy = sends.start(source[3].at[r], relay.at[r], "y", step)
                arrived.append((copy, (relay.at[r], whole.at[pl.ds(3 * T + at, half)])))
    yield
    for copy, onward in arrived:
        copy.wait_recv()
        if onward is not None:
            last.append(sends.start(onward[0], onward[1], "core", 1))
    yield
    for copy in last:
        copy.wait_recv()


def dense_kernel(
    mix_ref, q_ref, prob_in, kv_in, h_ref, up_ref, vec_ref,
    wo_ref, wg_ref, wu_ref, wd_ref, wos_ref, wgs_ref, wus_ref, wds_ref,
    dq_ref, dkv_out, g_out, sums_ref, d_attn_ref, mixture_ref, d_mid_ref, out_ref, logit_ref, vec_out_ref,
    wo, wg, wu, wd, mixf, gate_s, up_s, inner, dgu, dffn, xs, do_s, d_mix_s,
    dgu_all, dffn_all, xs_all, inner_all, xs_relay, inner_relay,
    prob_ref, kv_ref, dkv_ref, g_ref, g_down, low, out_b, full,
    load_sems, store_sems, send_sems, recv_sems,
):
    me = here()
    loads = []
    for k, (own, rest, to) in enumerate(
        ((wo_ref, wos_ref, wo), (wg_ref, wgs_ref, wg), (wu_ref, wus_ref, wu), (wd_ref, wds_ref, wd))
    ):
        there = to.at[pl.ds(1, 3)] if k < 3 else to.at[pl.ds(2, 1)]
        pair = (
            pltpu.make_async_copy(own, to.at[0], load_sems.at[2 * k]),
            pltpu.make_async_copy(rest, there, load_sems.at[2 * k + 1]),
        )
        for copy in pair:
            copy.start()
        loads.append(pair)
    loads.append(
        (
            pltpu.make_async_copy(prob_in, prob_ref, load_sems.at[8]),
            pltpu.make_async_copy(kv_in, kv_ref, load_sems.at[9]),
        )
    )
    for copy in loads[4]:
        copy.start()
    hail(me, NEAR[:4] + WEIGHT)
    sends = Sends(me, send_sems, recv_sems)
    shards = [shard_of(me, k) for k in range(4)]

    def run640(k):
        return pl.ds(pl.multiple_of(shards[k] * 640, 128), 640)

    def loaded(k):
        for copy in loads[k]:
            copy.wait()

    for j in range(KV_HEADS):
        for g in range(GROUPS):
            h = GROUPS * j + g
            mixf[:, HEAD_DIM * h : HEAD_DIM * (h + 1)] = mix_ref[j, g * T : (g + 1) * T, HEAD_DIM:]
    mixture_ref[...] = mixf[...].astype(BF)
    mix_k = our_order(me, cut_four(mixture_ref))
    loaded(0)
    attn_out = sum(dot(mix_k[k], wo[k]) for k in range(4))
    hidden = h_ref[...]
    gain_f = vec_ref[1:2, :D]
    route_w = vec_ref[2:3, :D]
    middle = hidden + attn_out
    r2 = lax.rsqrt(jnp.mean(middle * middle, axis=-1, keepdims=True) + EPS)
    x2 = middle * r2 * gain_f
    x2_k = our_order(me, [x2[:, 240 * k : 240 * (k + 1)].astype(BF) for k in range(4)])
    xs[...] = jnp.zeros_like(xs)
    for k in range(4):
        xs[k, :, :240] = x2_k[k]
    meet(NEAR[:4] + WEIGHT)
    down = [
        sends.start(wd_ref, wd.at[1], "core", 1),
        sends.start(wds_ref.at[0], wd.at[3], "core", 1),
    ]
    shares = [everyone_steps(sends, (("one", [xs.at[k] for k in range(4)], xs_all, xs_relay),))]
    next(shares[0])
    loaded(1)
    gate_s[...] = sum(dot(x2_k[k], wg[k]) for k in range(4))
    loaded(2)
    up_s[...] = sum(dot(x2_k[k], wu[k]) for k in range(4))
    gate = gate_s[...]
    inner[...] = (gate * jax.nn.sigmoid(gate) * up_s[...]).astype(BF)
    loaded(3)
    shares.append(
        everyone_steps(sends, (("one", [inner.at[:, run640(k)] for k in range(4)], inner_all, inner_relay),))
    )
    next(shares[1])
    for copy in down:
        copy.wait_recv()
    ffn_out = sum(dot(inner[:, run640(k)], wd[k], NT) for k in range(4))
    route = jax.nn.sigmoid(jnp.sum(hidden * route_w, axis=-1, keepdims=True))
    branch = attn_out + ffn_out
    odd = lax.rem(me[4], 2)
    keep = pl.ds(pl.multiple_of(odd * T, T), T)
    out_ref[keep] = (route * branch).astype(BF)
    swap = sends.start(out_ref.at[keep], out_ref.at[keep], "pair", 1)
    upstream = up_ref[...]
    d_branch = upstream * route
    d_logit = route * (1.0 - route) * jnp.sum(upstream * branch, axis=-1, keepdims=True)
    logit_ref[...] = jnp.broadcast_to(d_logit, logit_ref.shape)
    vec_out_ref[...] = jnp.zeros_like(vec_out_ref)
    vec_out_ref[2:3, :D] = jnp.sum(d_logit * hidden, axis=0, keepdims=True)
    d_ffn = d_branch.astype(BF)
    own = pl.ds(0, T)
    dffn[...] = jnp.zeros_like(dffn)
    for k in range(4):
        dffn[:, 256 * k : 256 * k + 240] = d_branch[:, 240 * k : 240 * (k + 1)].astype(BF)
    shares.append(everyone_steps(sends, (("all", dffn, dffn_all, None),)))
    next(shares[2])
    dffn_all[own], xs_all[own], inner_all[own] = dffn[...], xs[0], inner[:, run640(0)]
    late = []
    for p in range(2):
        first = 2 * lax.rem(me[0] + p, 2)
        for b in range(2):
            at = (2 * p + (me[1] if b == 0 else 1 - me[1])) * 640
            run, run_up = (pl.ds(pl.multiple_of(c + at, 128), 640) for c in (0, FF))
            d_inner = dot(d_ffn, wd[first + b])
            gate, up = gate_s[:, run], up_s[:, run]
            sg = jax.nn.sigmoid(gate)
            dgu[:, run] = (d_inner * up * (sg + gate * sg * (1.0 - sg))).astype(BF)
            dgu[:, run_up] = (d_inner * (gate * sg)).astype(BF)
        cols = [pl.ds(c + 1280 * p, 1280) for c in (0, FF)]
        late.append(everyone_steps(sends, tuple(("all", dgu.at[:, c], dgu_all.at[:, c], None) for c in cols)))
        next(late[-1])
    for share in shares:
        next(share)
    dgu_all[own] = dgu[...]
    d_gate, d_up = dgu[:, :FF], dgu[:, FF:]
    d_x2 = jnp.concatenate(
        our_order(me, [dot(d_gate, wg[k], NT) + dot(d_up, wu[k], NT) for k in range(4)]), axis=1
    )
    d_mid, g_gain_f = norm_back_rows(middle, r2, gain_f, d_x2)
    d_mid_ref[...] = d_mid
    vec_out_ref[1:2, :D] = g_gain_f
    d_attn = (d_branch + d_mid).astype(BF)
    d_attn_ref[...] = d_attn
    d_mix_s[...] = jnp.concatenate(our_order(me, [dot(d_attn, wo[k], NT) for k in range(4)]), axis=1)
    do_s[...] = jnp.zeros_like(do_s)
    for j in range(KV_HEADS):
        for g in range(GROUPS):
            h = GROUPS * j + g
            do_s[j, g * T : (g + 1) * T, HEAD_DIM:] = d_mix_s[:, HEAD_DIM * h : HEAD_DIM * (h + 1)].astype(BF)

    stores = []

    def store(a, b):
        stores.append(pltpu.make_async_copy(a, b, store_sems.at[len(stores)]))
        stores[-1].start()

    together(*shares)
    for k in range(4):
        c = pl.ds(640 * k, 640)
        g_down[:, c] = dot(dffn_all[:, 256 * k : 256 * (k + 1)], inner_all[...], TN).astype(BF)
    wide = wide_steps(me, sends, g_down, low, out_b, full, sums_ref)
    next(wide)
    loaded(4)
    for j in range(KV_HEADS):
        c = pl.ds(j * 128, 128)
        tile = kv_ref[:, :, :, :, c].reshape(KEYS, 128)
        prob, d_out = prob_ref[j], do_s[j]
        d_prob = dot(d_out, tile, NT)
        delta = jnp.sum(d_out.astype(F32) * mix_ref[j], axis=-1, keepdims=True)
        d_score = (prob.astype(F32) * (d_prob - delta)).astype(BF)
        dq_ref[j] = dot(d_score, tile) * SCALE
        grad = dot(
            jnp.concatenate([d_score, prob], axis=0), jnp.concatenate([q_ref[j], d_out], axis=0), TN
        )
        dkv_ref[:, :, :, :, c] = grad.astype(BF).reshape(2, 4, 4, T, 128)
        store(dkv_ref.at[:, :, :, :, c], dkv_out.at[:, :, :, :, c])
        if j == 2:
            next(wide)
            next(wide)
    together(*late)
    for at in range(0, 2 * FF, 1280):
        c = pl.ds(at, 1280)
        g_ref[:, c] = dot(xs_all[...], dgu_all[:, c], TN).astype(BF)
        store(g_ref.at[:, c], g_out.at[:, c])
    together(wide)
    swap.wait_recv()
    for copy in stores:
        copy.wait()
    sends.finish()


def dense(mix, q, prob, kv, h, up_c, vec, own, rest):
    vmem, hbm = pl.BlockSpec(memory_space=pltpu.VMEM), pl.BlockSpec(memory_space=pl.ANY)
    rows = GROUPS * T
    return pl.pallas_call(
        dense_kernel,
        name="dense",
        out_shape=(
            jax.ShapeDtypeStruct((KV_HEADS, rows, 128), F32),
            jax.ShapeDtypeStruct((2, 4, 4, T, 640), BF),
            jax.ShapeDtypeStruct((ROWS, 2 * FF), BF),
            jax.ShapeDtypeStruct((ROWS, FF // 4), BF),
            jax.ShapeDtypeStruct((T, D), BF),
            jax.ShapeDtypeStruct((T, D), BF),
            jax.ShapeDtypeStruct((T, D), F32),
            jax.ShapeDtypeStruct((PAIR, D), BF),
            jax.ShapeDtypeStruct((T, 128), F32),
            jax.ShapeDtypeStruct((8, 1024), F32),
        ),
        in_specs=[vmem] * 2 + [hbm] * 2 + [vmem] * 3 + [hbm] * 8,
        out_specs=(vmem,) + (hbm,) * 2 + (vmem,) * 7,
        scratch_shapes=[
            pltpu.VMEM((4, 240, D), BF),
            pltpu.VMEM((4, 240, FF), BF),
            pltpu.VMEM((4, 240, FF), BF),
            pltpu.VMEM((4, D, 640), BF),
            pltpu.VMEM((T, D), F32),
            pltpu.VMEM((T, FF), F32),
            pltpu.VMEM((T, FF), F32),
            pltpu.VMEM((T, FF), BF),
            pltpu.VMEM((T, 2 * FF), BF),
            pltpu.VMEM((T, 1024), BF),
            pltpu.VMEM((4, T, 256), BF),
            pltpu.VMEM((KV_HEADS, rows, 128), BF),
            pltpu.VMEM((T, D), F32),
            pltpu.VMEM((4 * T, 2 * FF), BF),
            pltpu.VMEM((4 * T, 1024), BF),
            pltpu.VMEM((4 * T, 256), BF),
            pltpu.VMEM((4 * T, 640), BF),
            pltpu.VMEM((T, 256), BF),
            pltpu.VMEM((T, 640), BF),
            pltpu.VMEM((KV_HEADS, rows, KEYS), BF),
            pltpu.VMEM((2, 4, 4, T, 640), BF),
            pltpu.VMEM((2, 4, 4, T, 640), BF),
            pltpu.VMEM((ROWS, 2 * FF), BF),
            pltpu.VMEM((ROWS, FF), BF),
            *sum_scratch(FF, HALF)[:3],
            pltpu.SemaphoreType.DMA((10,)),
            pltpu.SemaphoreType.DMA((13,)),
        ]
        + sems(57),
        compiler_params=pltpu.CompilerParams(
            collective_id=4, has_side_effects=True, vmem_limit_bytes=VMEM_LIMIT
        ),
        cost_estimate=pl.CostEstimate(
            flops=20_000_000_000, bytes_accessed=40_000_000, transcendentals=0
        ),
    )(mix, q, prob, kv, h, up_c, vec, *own, *rest)


def per_device(hidden, chosen, positions, w_query, w_key, w_value, w_output, w_gate, w_up, w_down, gain_attn, gain_ffn, router, d_out):
    tokens, upstream = hidden[0], d_out[0]
    own_w = (w_output, w_gate, w_up, w_down.T)
    frequency = (THETA ** (-np.arange(0, HEAD_DIM // 2) * 2.0 / HEAD_DIM)).astype(np.float32)
    (
        mix_heads, prob, q_heads, kv_all, h, up_c, x1, cosine, sine, place, vec_in, wq, wk, wv, *rest_w
    ) = front(
        tokens.T, upstream.T, chosen, positions, np.tile(frequency, 4)[None, :], gain_attn, gain_ffn, router,
        w_query, w_key.T, w_value.T, *own_w
    )
    d_q_heads, d_kv, g_one, sums_down, d_attn, mixture, d_mid, out_c, d_logit, vec_out = dense(
        mix_heads, q_heads, prob, kv_all, h, up_c, vec_in, own_w, rest_w
    )
    s_gate, s_up, s_down, s_two, s_three, vector, d_rows = back(
        d_kv, g_one, sums_down, d_q_heads, d_attn, mixture, x1, h, d_mid, d_logit, vec_in, vec_out, cosine, sine, wq, wk, wv
    )
    output, d_tokens, g_query, g_key, g_value, g_output, g_gate, g_up, g_down, *vectors = finish(
        s_gate, s_up, s_down, s_two, s_three, vector, out_c, d_rows, place, tokens.T, upstream.T
    )
    return (
        output.T[None],
        d_tokens.T[None],
        g_query,
        g_key.T,
        g_value.T,
        g_output,
        g_gate,
        g_up,
        g_down.T,
        vectors[0],
        vectors[1],
        vectors[2],
    )


def solution(mesh):
    finer = Mesh(mesh.devices.reshape(DIMS), AX)
    shard, blk = ("ylo", "core"), ("yhi", "z", "x")
    act, row, weight, vec = P(shard, blk, None), P(shard, blk), P(shard, None), P(shard)
    return jax.shard_map(
        per_device,
        mesh=finer,
        in_specs=(act, row, row) + (weight,) * 7 + (vec,) * 3 + (act,),
        out_specs=(act, act) + (weight,) * 7 + (vec,) * 3,
        check_vma=False,
    )
```
